128 devices in a mesh: section: 2 (over core), depth: 16 (over y, x), row: 4 (over z).
Axes of the slice: x: 4, y: 4, z: 4, core: 2. Of those that a mesh axis runs over, the one named last changes fastest.
Arguments:
- latent: bfloat16 [2, 32, 16, 16, 128], P(None, 'depth', 'row'), may hold values from -6 to 6
- noise_field: bfloat16 [2, 32, 16, 16, 128], P(None, 'depth', 'row'), may hold values from -6 to 6
- timestep: int32 [2], replicated, may hold values from 0 to 899
- embed_weight: bfloat16 [128, 3072], replicated, may hold values from -0.5 to 0.5
- modulate_weight: bfloat16 [2, 256, 9216], P('section', None, 'row'), may hold values from -5 to 5
- attend_weight: bfloat16 [2, 3, 3072, 1536], P('section', None, None, 'row'), may hold values from -0.109375 to 0.109375
- query_gain: float32 [2, 128], P('section'), may hold values from 1.8 to 2.4
- key_gain: float32 [2, 128], P('section'), may hold values from 1.8 to 2.4
- output_weight: bfloat16 [2, 1536, 3072], P('section', 'row'), may hold values from -0.15625 to 0.15625
Outputs:
- activations: bfloat16 [2, 2, 32, 16, 16, 3072], P('section', None, 'depth', 'row')
The draws below stay inside these ranges and needn't reach their ends.
Inputs may be any that keep to these rules, and one draw needn't show every extreme that they name: `timestep`: one diffusion step index a micro-batch.
All inputs are finite; a program needn't handle non-finite values.
Results may differ from the reference program's by a relative error of at most 0.028.
Values may be sent and summed in bfloat16 or wider, within the bound.
No kernel may reach another device: no remote copies, remote signals or barrier semaphores. Data moves between devices by JAX's collectives and lax.ppermute only.
A program may use at most 256 MiB of HBM per device.

```python
import math
import jax
import jax.numpy as jnp
from jax import lax

D = 3072
HEADS = 12
HEAD_DIM = 128
FREQ_DIM = 256
PATCH = 128
MICRO = 2
XC = 16
SECTIONS = 2
GROUPS = 4
NZ = 32
NY = 16


def draw_modulate_weight(key, part):
    key = jax.random.fold_in(key, 11)
    base_key, amount_key, sign_key = jax.random.split(key, 3)
    full_shape = (SECTIONS, FREQ_DIM, 3 * D)
    half_count = FREQ_DIM // 2
    steady = max(half_count // 8, 1)
    base = jnp.clip(jax.random.normal(base_key, full_shape, jnp.float32), -6.0, 6.0) / math.sqrt(FREQ_DIM)
    amount = jax.random.uniform(amount_key, (SECTIONS, 1, D), jnp.float32, 1.0, 2.5)
    signs = (jax.random.randint(sign_key, (SECTIONS, 1, D), 0, 2) * 2 - 1).astype(jnp.float32)
    positions = jnp.arange(FREQ_DIM, dtype=jnp.int32)
    steady_rows = jnp.logical_and(positions >= half_count - steady, positions < half_count).astype(jnp.float32)[None, :, None]
    gate_part = steady_rows * (signs * amount / steady)
    empty = jnp.zeros((SECTIONS, FREQ_DIM, 2 * D), jnp.float32)
    return (base + jnp.concatenate([empty, gate_part], axis=2)).astype(jnp.bfloat16)


def block_scale(stream_key, dims, cuts, smallest, largest):
    level = 1.0
    for dim, shards_of in cuts:
        draws = jax.random.uniform(jax.random.fold_in(jax.random.fold_in(stream_key, 6), dim), (shards_of,), jnp.float32, smallest / len(cuts), largest / len(cuts))
        level = level * jnp.repeat(jnp.exp(draws), dims[dim] // shards_of).reshape((-1,) + (1,) * (len(dims) - 1 - dim))
    return level


def scatter_about(key, shape, deviation, reach, cuts=(), kind=jnp.bfloat16):
    drawn = jax.random.normal(key, shape, jnp.float32) * deviation
    if len(cuts) > 0:
        drawn = block_scale(key, shape, cuts, -0.22, 0.18) * drawn
    return jnp.clip(drawn, min=-reach, max=reach).astype(kind)


def setup_inputs(seed: int = 0) -> dict:
    seeds = jax.random.split(jax.random.key(seed), 10)
    return {
        "latent": scatter_about(seeds[0], (MICRO, NZ, NY, XC, PATCH), 1.0, 6.0, ((1, 16), (2, 4))),
        "noise_field": scatter_about(seeds[1], (MICRO, NZ, NY, XC, PATCH), 1.0, 6.0, ((1, 16), (2, 4))),
        "timestep": jax.random.randint(seeds[2], (MICRO,), 0, 900).astype(jnp.int32),
        "embed_weight": scatter_about(seeds[3], (PATCH, D), PATCH ** -0.5, 0.5),
        "modulate_weight": draw_modulate_weight(jax.random.fold_in(seeds[9], 71), 0),
        "attend_weight": scatter_about(seeds[5], (SECTIONS, 3, D, HEADS * HEAD_DIM), D ** -0.5, 0.109375, ((0, 2), (3, 4))),
        "query_gain": jnp.clip(jnp.exp(math.log(2.4) - 0.28768214 * jax.random.uniform(seeds[6], (SECTIONS, HEAD_DIM), jnp.float32) ** block_scale(seeds[6], (SECTIONS, HEAD_DIM), ((0, 2),), -0.2, 0.2)), 1.8, 2.4),
        "key_gain": jnp.clip(jnp.exp(math.log(2.4) - 0.28768214 * jax.random.uniform(seeds[7], (SECTIONS, HEAD_DIM), jnp.float32) ** block_scale(seeds[7], (SECTIONS, HEAD_DIM), ((0, 2),), -0.2, 0.2)), 1.8, 2.4),
        "output_weight": scatter_about(seeds[8], (SECTIONS, HEADS * HEAD_DIM, D), (HEADS * HEAD_DIM) ** -0.5, 0.15625, ((0, 2), (1, 4))),
    }


norm_eps = 1e-06
plan_steps = 1000.0

def signal_level(timestep):
    phase = (timestep.astype(jnp.float32) / plan_steps + 0.008) / 1.008 * (math.pi / 2)
    return jnp.cos(phase) ** 2

def time_features(timestep, count):
    half = count // 2
    frequency = jnp.exp(-math.log(10000.0) * jnp.arange(half, dtype=jnp.float32) / half)
    angles = timestep.astype(jnp.float32)[:, None] * frequency[None, :]
    return jnp.concatenate([jnp.cos(angles), jnp.sin(angles)], axis=1)

def head_norm(values, gain, head_size):
    rows = values.shape[0]
    shaped = values.reshape(rows, -1, head_size)
    factor = lax.rsqrt(lax.optimization_barrier(jnp.mean(shaped * shaped, axis=-1, keepdims=True)) + norm_eps)
    return (shaped * factor * gain).reshape(rows, -1).astype(jnp.bfloat16)

def rounded(values):
    return lax.optimization_barrier(values.astype(jnp.bfloat16)).astype(jnp.float32)

def layer(tokens, modulation, attend_weight, query_gain, key_gain, output_weight):
    width = tokens.shape[1]
    length = tokens.shape[0]
    values = tokens.astype(jnp.float32)
    center = lax.optimization_barrier(jnp.mean(values, axis=1, keepdims=True))
    spread = lax.optimization_barrier(jnp.mean((values - center) ** 2, axis=1, keepdims=True))
    shift = modulation[:width]
    scale = modulation[width:2 * width]
    gate = modulation[2 * width:]
    normed = ((values - center) * lax.rsqrt(spread + norm_eps) * (1.0 + scale) + shift).astype(jnp.bfloat16)
    projected = jnp.einsum('td,jdc->jtc', normed.astype(jnp.float32), attend_weight.astype(jnp.float32))
    queries = head_norm(projected[0], query_gain, HEAD_DIM)
    keys = head_norm(projected[1], key_gain, HEAD_DIM)
    value_rows = projected[2].astype(jnp.bfloat16)
    query_heads = queries.reshape(length, HEADS, HEAD_DIM).transpose(1, 0, 2)
    key_heads = keys.reshape(length, HEADS, HEAD_DIM).transpose(1, 0, 2)
    value_heads = value_rows.reshape(length, HEADS, HEAD_DIM).transpose(1, 0, 2)

    def one_head(group):
        query_head, key_head, value_head = group
        scores = jnp.einsum('qe,ke->qk', query_head.astype(jnp.float32), key_head.astype(jnp.float32)) / math.sqrt(HEAD_DIM)
        weights = jnp.exp(scores)
        total = lax.optimization_barrier(jnp.sum(weights, axis=1, keepdims=True))
        mixed = jnp.einsum('qk,ke->qe', rounded(weights), value_head.astype(jnp.float32))
        return mixed / total
    attended = lax.map(one_head, (query_heads, key_heads, value_heads))
    attended = attended.transpose(1, 0, 2).reshape(length, HEADS * HEAD_DIM).astype(jnp.bfloat16)
    group_width = HEADS * HEAD_DIM // GROUPS
    partials = jnp.einsum('tng,ngd->ntd', attended.astype(jnp.float32).reshape(length, GROUPS, group_width), output_weight.astype(jnp.float32).reshape(GROUPS, group_width, width))
    update = lax.optimization_barrier(jnp.sum(rounded(partials), axis=0))
    return (values + gate * update).astype(jnp.bfloat16)

def reference(latent, noise_field, timestep, embed_weight, modulate_weight, attend_weight, query_gain, key_gain, output_weight):
    batches = latent.shape[0]
    level = signal_level(timestep)[:, None, None, None, None]
    noisy = (jnp.sqrt(level) * latent.astype(jnp.float32) + jnp.sqrt(1.0 - level) * noise_field.astype(jnp.float32)).astype(jnp.bfloat16)
    flat = noisy.reshape(batches, -1, noisy.shape[-1])
    tokens = jnp.einsum('mtp,pd->mtd', flat.astype(jnp.float32), embed_weight.astype(jnp.float32)).astype(jnp.bfloat16)
    features = time_features(timestep, FREQ_DIM).astype(jnp.bfloat16)

    def segment_step(current, params):
        modulation = jnp.dot(features, params[0], preferred_element_type=jnp.float32)
        following = jnp.stack([layer(current[batch_index], modulation[batch_index], params[1], params[2], params[3], params[4]) for batch_index in range(batches)])
        return (following, following)
    unused, stacked = lax.scan(segment_step, tokens, (modulate_weight, attend_weight, query_gain, key_gain, output_weight))
    return stacked.reshape(stacked.shape[0], batches, latent.shape[1], latent.shape[2], latent.shape[3], -1)
```

```python
import math

import jax
import jax.numpy as jnp
from jax import lax
from jax.experimental import pallas as pl
from jax.experimental.pallas import tpu as pltpu
from jax.sharding import PartitionSpec as P

HEAD_DIM = 128
BF = jnp.bfloat16
F32 = jnp.float32
VMEM_BYTES = 48 * 1024 * 1024

norm_eps = 1e-06
plan_steps = 1000.0
QUERY_SCALE = math.log2(math.e) / math.sqrt(HEAD_DIM)
SWAP = [(0, 1), (1, 0)]
STEPS = (0, 1, -1, 2)


def signal_level(timestep):
    phase = (timestep.astype(F32) / plan_steps + 0.008) / 1.008 * (math.pi / 2)
    return jnp.cos(phase) ** 2


def time_features(timestep, count):
    half = count // 2
    frequency = jnp.exp(-math.log(10000.0) * jnp.arange(half, dtype=F32) / half)
    angles = timestep.astype(F32)[:, None] * frequency[None, :]
    return jnp.concatenate([jnp.cos(angles), jnp.sin(angles)], axis=1)


def shift_x(array, by):
    return lax.ppermute(
        array, "depth", [(y * 4 + x, y * 4 + (x + by) % 4) for y in range(4) for x in range(4)]
    )


def shift_y(array, by):
    return lax.ppermute(
        array, "depth", [(y * 4 + x, (y + by) % 4 * 4 + x) for y in range(4) for x in range(4)]
    )


def shift_z(array, by):
    return lax.ppermute(array, "row", [(z, (z + by) % 4) for z in range(4)])


def gather(array, shift):
    return [array] + [shift(array, by) for by in STEPS[1:]]


def give_back(blocks, shift):
    return [blocks[0]] + [shift(block, -by) for block, by in zip(blocks[1:], STEPS[1:])]


def params(**more):
    return pltpu.CompilerParams(vmem_limit_bytes=VMEM_BYTES, **more)


def head_norm(values, gain):
    factor = lax.rsqrt(jnp.mean(values * values, axis=1, keepdims=True) + norm_eps)
    return (values * factor * gain).astype(BF)


def first_projection(noisy, gram, weight, bias, gains):
    rows = noisy.shape[0]
    heads = weight.shape[1] // HEAD_DIM
    normed_heads = gains.shape[0]
    block = 512

    def kernel(noisy_ref, gram_ref, weight_ref, bias_ref, gains_ref, out_ref):
        values = noisy_ref[...].astype(F32)
        spread = jnp.sum(
            jnp.dot(
                values, gram_ref[...], preferred_element_type=F32, precision=lax.Precision.HIGHEST
            )
            * values,
            axis=1,
            keepdims=True,
        )
        scaled = (values * lax.rsqrt(spread + norm_eps)).astype(BF)
        projected = jnp.dot(scaled, weight_ref[...], preferred_element_type=F32) + bias_ref[...]
        for h in range(heads):
            part = projected[:, h * HEAD_DIM : (h + 1) * HEAD_DIM]
            if h < normed_heads:
                out_ref[h] = head_norm(part, gains_ref[h : h + 1])
            else:
                out_ref[h] = part.astype(BF)

    return pl.pallas_call(
        kernel,
        grid=(rows // block,),
        in_specs=[
            pl.BlockSpec((block, noisy.shape[1]), lambda i: (i, 0)),
            pl.BlockSpec(gram.shape, lambda i: (0, 0)),
            pl.BlockSpec(weight.shape, lambda i: (0, 0)),
            pl.BlockSpec(bias.shape, lambda i: (0, 0)),
            pl.BlockSpec(gains.shape, lambda i: (0, 0)),
        ],
        out_specs=pl.BlockSpec((heads, block, HEAD_DIM), lambda i: (0, i, 0)),
        out_shape=jax.ShapeDtypeStruct((heads, rows, HEAD_DIM), BF),
        compiler_params=params(),
    )(noisy, gram, weight, bias, gains)


def attend(queries, key_values):
    heads = queries[0].shape[0]
    rows = queries[0].shape[1]
    key_rows = key_values[0].shape[1]
    keys_total = key_rows * len(key_values)
    count = len(queries)
    chunk = 512

    def kernel(*refs):
        query_refs = refs[:count]
        key_refs = refs[count : count + len(key_values)]
        value_refs = refs[count + len(key_values) : count + 2 * len(key_values)]
        out_refs = refs[count + 2 * len(key_values) : -1]
        wide_ref = refs[-1]
        for i, ref in enumerate(value_refs):
            wide_ref[i * key_rows : (i + 1) * key_rows, :HEAD_DIM] = ref[0]
            wide_ref[i * key_rows : (i + 1) * key_rows, HEAD_DIM:] = jnp.ones(
                (key_rows, HEAD_DIM), BF
            )
        diagonal = lax.broadcasted_iota(jnp.int32, (HEAD_DIM, HEAD_DIM), 0) == lax.broadcasted_iota(
            jnp.int32, (HEAD_DIM, HEAD_DIM), 1
        )
        for q in range(count):
            query = query_refs[q][0]
            sums = jnp.zeros((rows, 2 * HEAD_DIM), F32)
            for start in range(0, keys_total, chunk):
                which, inner = divmod(start, key_rows)
                key = key_refs[which][0, inner : inner + chunk]
                scores = lax.dot_general(
                    query, key, (((1,), (1,)), ((), ())), preferred_element_type=F32
                )
                weights = jnp.exp2(scores).astype(BF)
                sums = sums + jnp.dot(
                    weights, wide_ref[start : start + chunk], preferred_element_type=F32
                )
            out_refs[q][0, :rows] = sums[:, :HEAD_DIM].astype(BF)
            lines = []
            for part in range(rows // HEAD_DIM):
                square = sums[part * HEAD_DIM : (part + 1) * HEAD_DIM, HEAD_DIM:]
                lines.append(jnp.sum(jnp.where(diagonal, square, 0.0), axis=0, keepdims=True))
            total = jnp.concatenate(lines, axis=0)
            upper = total.astype(BF)
            lower = (total - upper.astype(F32)).astype(BF)
            out_refs[q][0, rows : rows + 16] = jnp.concatenate(
                [upper.astype(F32), lower.astype(F32), jnp.zeros((8, HEAD_DIM), F32)], axis=0
            ).astype(BF)

    return pl.pallas_call(
        kernel,
        grid=(heads,),
        in_specs=[pl.BlockSpec((1, rows, HEAD_DIM), lambda h: (h, 0, 0))] * count
        + [pl.BlockSpec((1, key_rows, HEAD_DIM), lambda h: (h, 0, 0))] * len(key_values)
        + [pl.BlockSpec((1, key_rows, HEAD_DIM), lambda h: (h + heads, 0, 0))] * len(key_values),
        out_specs=[pl.BlockSpec((1, rows + 16, HEAD_DIM), lambda h: (h, 0, 0))] * count,
        out_shape=[jax.ShapeDtypeStruct((heads, rows + 16, HEAD_DIM), BF)] * count,
        scratch_shapes=[pltpu.VMEM((keys_total, 2 * HEAD_DIM), BF)],
        compiler_params=params(),
    )(*queries, *key_values, *key_values)


def combine(parts):
    heads, packed, _ = parts[0].shape
    rows = packed - 16
    lines = rows // HEAD_DIM

    def kernel(*refs):
        out_ref = refs[-1]
        diagonal = lax.broadcasted_iota(jnp.int32, (HEAD_DIM, HEAD_DIM), 0) == lax.broadcasted_iota(
            jnp.int32, (HEAD_DIM, HEAD_DIM), 1
        )
        tails = [ref[0, rows : rows + 16].astype(F32) for ref in refs[:-1]]
        tail = tails[0]
        for more in tails[1:]:
            tail = tail + more
        for part in range(lines):
            place = slice(part * HEAD_DIM, (part + 1) * HEAD_DIM)
            numerator = refs[0][0, place].astype(F32)
            for ref in refs[1:-1]:
                numerator = numerator + ref[0, place].astype(F32)
            total = tail[part : part + 1] + tail[lines + part : lines + part + 1]
            column = jnp.sum(jnp.where(diagonal, 1.0 / total, 0.0), axis=1, keepdims=True)
            out_ref[place] = (numerator * column).astype(BF)

    return pl.pallas_call(
        kernel,
        grid=(heads,),
        in_specs=[pl.BlockSpec((1, packed, HEAD_DIM), lambda h: (h, 0, 0))] * len(parts),
        out_specs=pl.BlockSpec((rows, HEAD_DIM), lambda h: (0, h)),
        out_shape=jax.ShapeDtypeStruct((rows, heads * HEAD_DIM), BF),
        compiler_params=params(),
    )(*parts)


def output_step(places, blocks, weights, base, gate):
    rows, part = blocks[0].shape
    width = gate.shape[1]
    count = len(blocks)
    depth = count * part
    half = weights[0].shape[1]
    block = 512
    per_half = half // block

    def kernel(places_ref, *refs):
        block_refs = refs[:count]
        weight_refs = refs[count : count + 2]
        base_ref, gate_ref, out_ref, side_ref = refs[count + 2 :]
        n = pl.program_id(0)

        @pl.when(n == 0)
        def _():
            for k in range(count):
                side_ref[:, pl.ds(pl.multiple_of(places_ref[k] * part, HEAD_DIM), part)] = (
                    block_refs[k][...]
                )

        for which in range(2):

            @pl.when(n // per_half == which)
            def _():
                update = jnp.dot(
                    side_ref[...], weight_refs[which][...], preferred_element_type=F32
                )
                out_ref[...] = (base_ref[...].astype(F32) + gate_ref[...] * update).astype(BF)

    return pl.pallas_call(
        kernel,
        grid_spec=pltpu.PrefetchScalarGridSpec(
            num_scalar_prefetch=1,
            grid=(width // block,),
            in_specs=[pl.BlockSpec((rows, part), lambda n, p: (0, 0))] * count
            + [
                pl.BlockSpec((depth, block), lambda n, p: (0, jnp.minimum(n, per_half - 1))),
                pl.BlockSpec((depth, block), lambda n, p: (0, jnp.maximum(n - per_half, 0))),
                pl.BlockSpec((rows, block), lambda n, p: (0, n)),
                pl.BlockSpec((gate.shape[0], block), lambda n, p: (0, n)),
            ],
            out_specs=pl.BlockSpec((rows, block), lambda n, p: (0, n)),
            scratch_shapes=[pltpu.VMEM((rows, depth), BF)],
        ),
        out_shape=jax.ShapeDtypeStruct((rows, width), BF),
        compiler_params=params(),
    )(places, *blocks, *weights, base, gate)


def second_projection(tokens, scale, shift, weight, query_gain, key_gain):
    rows, width = tokens.shape
    heads = weight.shape[2] // HEAD_DIM
    step = 128

    def kernel(tokens_ref, scale_ref, shift_ref, weight_ref, qg_ref, kg_ref, q_ref, kv_ref, normed_ref):
        j = pl.program_id(0)

        @pl.when(j == 0)
        def _():
            for start in range(0, rows, step):
                values = tokens_ref[start : start + step].astype(F32)
                values = values - jnp.mean(values, axis=1, keepdims=True)
                spread = jnp.mean(values * values, axis=1, keepdims=True)
                normed_ref[start : start + step] = (
                    values * lax.rsqrt(spread + norm_eps) * (1.0 + scale_ref[...]) + shift_ref[...]
                ).astype(BF)

        projected = jnp.dot(normed_ref[...], weight_ref[0], preferred_element_type=F32)
        for h in range(heads):
            part = projected[:, h * HEAD_DIM : (h + 1) * HEAD_DIM]

            @pl.when(j == 0)
            def _():
                q_ref[h] = head_norm(part, qg_ref[...])

            @pl.when(j == 1)
            def _():
                kv_ref[h] = head_norm(part, kg_ref[...])

            @pl.when(j == 2)
            def _():
                kv_ref[h] = part.astype(BF)

    return pl.pallas_call(
        kernel,
        grid=(3,),
        in_specs=[
            pl.BlockSpec((rows, width), lambda j: (0, 0)),
            pl.BlockSpec((1, width), lambda j: (0, 0)),
            pl.BlockSpec((1, width), lambda j: (0, 0)),
            pl.BlockSpec((1, width, heads * HEAD_DIM), lambda j: (j, 0, 0)),
            pl.BlockSpec((1, HEAD_DIM), lambda j: (0, 0)),
            pl.BlockSpec((1, HEAD_DIM), lambda j: (0, 0)),
        ],
        out_specs=[
            pl.BlockSpec((heads, rows, HEAD_DIM), lambda j: (0, 0, 0)),
            pl.BlockSpec((heads, rows, HEAD_DIM), lambda j: (jnp.maximum(j - 1, 0), 0, 0)),
        ],
        out_shape=[
            jax.ShapeDtypeStruct((heads, rows, HEAD_DIM), BF),
            jax.ShapeDtypeStruct((2 * heads, rows, HEAD_DIM), BF),
        ],
        scratch_shapes=[pltpu.VMEM((rows, width), BF)],
        compiler_params=params(),
    )(tokens, scale, shift, weight, query_gain, key_gain)


def per_device(
    latent,
    noise_field,
    timestep,
    embed_weight,
    modulate_weight,
    attend_weight,
    query_gain,
    key_gain,
    output_weight,
):
    batches = latent.shape[0]
    patch, width = embed_weight.shape
    local = latent.shape[1] * latent.shape[2] * latent.shape[3]
    section = lax.axis_index("section")
    row = lax.axis_index("row")
    first = section == 0
    half = width // 2

    def by_section(of_first, of_second):
        return jnp.where(first, of_first, of_second)

    def swapped(array):
        return lax.ppermute(array, "section", SWAP)

    timestep_here = lax.dynamic_slice_in_dim(timestep, section, 1)
    level = signal_level(timestep_here)
    noisy = (
        jnp.sqrt(level) * lax.dynamic_index_in_dim(latent, section, 0, False).astype(F32)
        + jnp.sqrt(1.0 - level) * lax.dynamic_index_in_dim(noise_field, section, 0, False).astype(F32)
    ).astype(BF)
    noisy = noisy.reshape(local, patch)
    features = time_features(timestep, modulate_weight.shape[1]).astype(BF)
    mod_part = jnp.dot(features, modulate_weight[0], preferred_element_type=F32)

    mod_rows = mod_part.size // patch
    packed = jnp.concatenate(
        [noisy.astype(F32), mod_part.reshape(mod_rows, patch), jnp.zeros((-mod_rows % 8, patch), F32)]
    )
    packed = gather(packed, shift_z)
    noisy_row = jnp.concatenate([block[:local] for block in packed]).astype(BF)
    mods = jnp.stack([block[local : local + mod_rows].reshape(batches, -1) for block in packed])
    ordered = [
        lax.dynamic_index_in_dim(mods, jnp.array([0, 2, 3, 1])[(b - row) % 4], 0, False)
        for b in range(4)
    ]
    modulation = jnp.concatenate(ordered, axis=1)
    shift_own = modulation[:, :width]
    scale_own = modulation[:, width : 2 * width]

    noisy_keys = jnp.concatenate(gather(noisy_row, shift_x))
    noisy_queries = jnp.concatenate(gather(noisy_row, shift_y))

    centered = embed_weight.astype(F32)
    centered = centered - jnp.mean(centered, axis=1, keepdims=True)
    gram = (
        jnp.dot(centered, centered.T, preferred_element_type=F32, precision=lax.Precision.HIGHEST)
        / width
    )
    sides = jnp.concatenate(
        [centered[None] * (1.0 + scale_own[:, None, :]), shift_own[:, None, :]], axis=1
    )
    sides = jnp.concatenate([sides, jnp.zeros((batches, 15, width), F32)], axis=1)
    sides = sides.astype(BF).reshape(-1, width)
    mapped = jnp.einsum("pd,jdc->pjc", sides, attend_weight[0], preferred_element_type=F32)
    mapped = mapped.reshape(batches, patch + 16, -1)
    bias = mapped[:, patch : patch + 1]
    upper = bias.astype(BF)
    lower = (bias - upper.astype(F32)).astype(BF)
    mapped = jnp.concatenate(
        [mapped[:, :patch].astype(BF), upper, lower, jnp.zeros((batches, 14, mapped.shape[2]), BF)],
        axis=1,
    )
    mapped_other = lax.ppermute(mapped[1], "section", [(0, 1)])
    mapped = by_section(mapped[0], mapped_other)
    bias = mapped[patch : patch + 1].astype(F32) + mapped[patch + 1 : patch + 2].astype(F32)
    mapped = mapped[:patch]

    gains = jnp.concatenate([query_gain, key_gain])
    small = jnp.concatenate([modulation.reshape(-1, patch), gains, jnp.zeros((6, patch), F32)])
    small_other = swapped(small)
    small_first = by_section(small, small_other)
    small_second = by_section(small_other, small)
    mod_rows_all = modulation.size // patch

    def unpack(array):
        mod = lax.dynamic_slice_in_dim(array[:mod_rows_all].reshape(batches, -1), section, 1)
        qg = array[mod_rows_all : mod_rows_all + 1] * QUERY_SCALE
        kg = array[mod_rows_all + 1 : mod_rows_all + 2]
        return mod[:, :width], mod[:, width : 2 * width], mod[:, 2 * width :], qg, kg

    _, _, gate_first, qg_first, kg_first = unpack(small_first)
    shift_second, scale_second, _, qg_second, kg_second = unpack(small_second)
    attend_other = lax.ppermute(attend_weight[0], "section", [(1, 0)])

    keep = lax.dynamic_slice_in_dim(output_weight[0], section * half, half, 1)
    give = lax.dynamic_slice_in_dim(output_weight[0], (1 - section) * half, half, 1)
    got = swapped(give)
    out_first = lax.all_gather(by_section(keep, got), "row", axis=0, tiled=True)
    second_part, out_first = lax.optimization_barrier((by_section(got, keep), out_first))
    out_second = lax.all_gather(second_part, "row", axis=0, tiled=True)
    out_first_other = swapped(out_first)

    channels = mapped.shape[1] // 3
    heads = channels // HEAD_DIM
    queries = first_projection(
        noisy_queries,
        gram,
        mapped[:, :channels],
        bias[:, :channels],
        jnp.broadcast_to(qg_first, (heads, HEAD_DIM)),
    )
    key_values = first_projection(
        noisy_keys,
        gram,
        mapped[:, channels:],
        bias[:, channels:],
        jnp.broadcast_to(kg_first, (heads, HEAD_DIM)),
    )
    count = noisy_row.shape[0]
    queries = [queries[:, i * count : (i + 1) * count] for i in range(4)]
    attended = combine(give_back(attend(queries, [key_values]), shift_y))

    embedded = jnp.dot(noisy_row, embed_weight, preferred_element_type=F32).astype(BF)
    blocks = gather(attended, shift_z)
    turned = []
    for block, by in zip(blocks, STEPS):
        order = [
            [k for k in range(4) if (by + STEPS[k] - STEPS[mine]) % 4 == 0][0] for mine in range(4)
        ]
        turned.append(jnp.concatenate([block[k * local : (k + 1) * local] for k in order]))
    places = jnp.stack([(row - by) % 4 for by in STEPS]).astype(jnp.int32)

    def step_first(weights):
        return output_step(places, turned, weights, embedded, gate_first)

    tokens = lax.cond(
        first,
        lambda own, other: step_first((own, other)),
        lambda own, other: step_first((other, own)),
        out_first,
        out_first_other,
    )
    result_first = tokens[:local]
    result_other = swapped(result_first)

    def project(weight):
        return second_projection(
            tokens, scale_second, shift_second, weight, qg_second, kg_second
        )

    queries, key_values = lax.cond(
        first, lambda own, other: project(other), lambda own, other: project(own), attend_weight[0], attend_other
    )
    sums = attend(gather(queries, shift_y), gather(key_values, shift_x))
    attended = combine(give_back(sums, shift_y))
    mine = give_back([attended[k * local : (k + 1) * local] for k in range(4)], shift_z)
    mine = jnp.concatenate(mine, axis=1)
    mine_other = lax.ppermute(mine, "section", [(0, 1)])
    out_second_other = swapped(out_second)
    places = jnp.stack([(row + by) % 4 for by in STEPS]).astype(jnp.int32)
    gates = modulation[:, 2 * width :]

    def finish_first():
        return jnp.stack([result_first, result_other])

    def finish_second():
        both = jnp.concatenate([mine_other, mine])
        part = both.shape[1] // 4
        base = jnp.concatenate([result_other, result_first])
        spread_gates = jnp.broadcast_to(gates[:, None, :], (batches, local, width)).reshape(-1, width)
        result = output_step(
            places,
            [both[:, k * part : (k + 1) * part] for k in range(4)],
            (out_second_other, out_second),
            base,
            spread_gates,
        )
        return result.reshape(batches, local, width)

    result = lax.cond(first, finish_first, finish_second)
    return result.reshape(1, batches, latent.shape[1], latent.shape[2], latent.shape[3], width)


def solution(mesh):
    return jax.shard_map(
        per_device,
        mesh=mesh,
        in_specs=(
            P(None, "depth", "row", None, None),
            P(None, "depth", "row", None, None),
            P(),
            P(),
            P("section", None, "row"),
            P("section", None, None, "row"),
            P("section", None),
            P("section", None),
            P("section", "row", None),
        ),
        out_specs=P("section", None, "depth", "row", None, None),
        check_vma=False,
    )
```

```python
import math

import jax
import jax.numpy as jnp
from jax import lax
from jax.experimental import pallas as pl
from jax.experimental.pallas import tpu as pltpu
from jax.sharding import PartitionSpec as P

HEAD_DIM = 128
BF = jnp.bfloat16
F32 = jnp.float32

norm_eps = 1e-06
plan_steps = 1000.0
QUERY_SCALE = math.log2(math.e) / math.sqrt(HEAD_DIM)
SWAP = [(0, 1), (1, 0)]
STEPS = (0, 1, -1, 2)


def signal_level(timestep):
    phase = (timestep.astype(F32) / plan_steps + 0.008) / 1.008 * (math.pi / 2)
    return jnp.cos(phase) ** 2


def time_features(timestep, count):
    half = count // 2
    frequency = jnp.exp(-math.log(10000.0) * jnp.arange(half, dtype=F32) / half)
    angles = timestep.astype(F32)[:, None] * frequency[None, :]
    return jnp.concatenate([jnp.cos(angles), jnp.sin(angles)], axis=1)


def shift_x(array, by):
    return lax.ppermute(
        array, "depth", [(y * 4 + x, y * 4 + (x + by) % 4) for y in range(4) for x in range(4)]
    )


def shift_y(array, by):
    return lax.ppermute(
        array, "depth", [(y * 4 + x, (y + by) % 4 * 4 + x) for y in range(4) for x in range(4)]
    )


def shift_z(array, by):
    return lax.ppermute(array, "row", [(z, (z + by) % 4) for z in range(4)])


def gather(array, shift):
    return [array] + [shift(array, by) for by in STEPS[1:]]


def give_back(blocks, shift):
    return [blocks[0]] + [shift(block, -by) for block, by in zip(blocks[1:], STEPS[1:])]


def params(mib):
    return pltpu.CompilerParams(vmem_limit_bytes=mib * 2**20)


def head_norm(values, gain):
    factor = lax.rsqrt(jnp.mean(values * values, axis=1, keepdims=True) + norm_eps)
    return (values * factor * gain).astype(BF)


def map_weights(sides, weight):
    rows, width = sides.shape
    kinds, _, channels = weight.shape
    heads = channels // HEAD_DIM

    def kernel(sides_ref, weight_ref, out_ref):
        mapped = jnp.dot(sides_ref[...], weight_ref[0], preferred_element_type=F32)
        for h in range(heads):
            out_ref[h] = mapped[:, h * HEAD_DIM : (h + 1) * HEAD_DIM]

    return pl.pallas_call(
        kernel,
        grid=(kinds,),
        in_specs=[
            pl.BlockSpec((rows, width), lambda j: (0, 0)),
            pl.BlockSpec((1, width, channels), lambda j: (j, 0, 0)),
        ],
        out_specs=pl.BlockSpec((heads, rows, HEAD_DIM), lambda j: (j, 0, 0)),
        out_shape=jax.ShapeDtypeStruct((kinds * heads, rows, HEAD_DIM), F32),
        compiler_params=params(24),
    )(sides, weight)


def first_projection(noisy, gram, weight, bias, gains):
    rows = noisy.shape[0]
    heads = weight.shape[1] // HEAD_DIM
    normed_heads = gains.shape[0]

    def kernel(noisy_ref, gram_ref, weight_ref, bias_ref, gains_ref, out_ref):
        values = noisy_ref[...].astype(F32)
        spread = jnp.sum(
            jnp.dot(
                values, gram_ref[...], preferred_element_type=F32, precision=lax.Precision.HIGHEST
            )
            * values,
            axis=1,
            keepdims=True,
        )
        scaled = (values * lax.rsqrt(spread + norm_eps)).astype(BF)
        projected = jnp.dot(scaled, weight_ref[...], preferred_element_type=F32) + bias_ref[...]
        for h in range(heads):
            part = projected[:, h * HEAD_DIM : (h + 1) * HEAD_DIM]
            if h < normed_heads:
                out_ref[h] = head_norm(part, gains_ref[h : h + 1])
            else:
                out_ref[h] = part.astype(BF)

    return pl.pallas_call(
        kernel,
        out_shape=jax.ShapeDtypeStruct((heads, rows, HEAD_DIM), BF),
        compiler_params=params(16),
    )(noisy, gram, weight, bias, gains)


ALONG_X = ((1, 0), (1, 2), (0, 1), (2, 0), (2, 2))
ALONG_Y = ((0, 0), (0, 2), (1, 1), (2, 1))
HEADS_BY = ((1, 0), (0, 0), (1, 1))


def attend(queries, blocks, after):
    rows = queries[0].shape[1]
    key_rows = blocks[0][0].shape[1]
    count = len(blocks[0])
    keys_total = key_rows * count
    places = (ALONG_X, ALONG_Y)

    def kernel(*refs):
        query_refs = refs[:2]
        block_refs = (refs[2 : 2 + count], refs[2 + count : 2 + 2 * count])
        out_refs = refs[-3:-1]
        wide_ref = refs[-1]
        diagonal = lax.broadcasted_iota(jnp.int32, (HEAD_DIM, HEAD_DIM), 0) == lax.broadcasted_iota(
            jnp.int32, (HEAD_DIM, HEAD_DIM), 1
        )
        for h, (along, out_place) in enumerate(HEADS_BY):
            query = query_refs[along][places[along].index((0, h))]
            key_at = places[1 - along].index((1, h))
            value_at = places[1 - along].index((2, h))
            sums = jnp.zeros((rows, 2 * HEAD_DIM), F32)
            for i, ref in enumerate(block_refs[1 - along]):
                wide_ref[h, i * key_rows : (i + 1) * key_rows, :HEAD_DIM] = ref[value_at]
                wide_ref[h, i * key_rows : (i + 1) * key_rows, HEAD_DIM:] = jnp.ones(
                    (key_rows, HEAD_DIM), BF
                )
            for i, ref in enumerate(block_refs[1 - along]):
                scores = lax.dot_general(
                    query, ref[key_at], (((1,), (1,)), ((), ())), preferred_element_type=F32
                )
                weights = jnp.exp2(scores).astype(BF)
                sums = sums + jnp.dot(
                    weights,
                    wide_ref[h, i * key_rows : (i + 1) * key_rows],
                    preferred_element_type=F32,
                )
            out_ref = out_refs[1 - along]
            out_ref[out_place, :rows] = sums[:, :HEAD_DIM].astype(BF)
            lines = []
            for part in range(rows // HEAD_DIM):
                square = sums[part * HEAD_DIM : (part + 1) * HEAD_DIM, HEAD_DIM:]
                lines.append(jnp.sum(jnp.where(diagonal, square, 0.0), axis=0, keepdims=True))
            total = jnp.concatenate(lines, axis=0)
            upper = total.astype(BF)
            lower = (total - upper.astype(F32)).astype(BF)
            out_ref[out_place, rows : rows + 16] = jnp.concatenate(
                [upper.astype(F32), lower.astype(F32), jnp.zeros((8, HEAD_DIM), F32)], axis=0
            ).astype(BF)

    whole = pl.BlockSpec(memory_space=pltpu.VMEM)
    return pl.pallas_call(
        kernel,
        in_specs=[whole] * (2 + 2 * count) + [pl.BlockSpec(memory_space=pl.ANY)] * len(after),
        out_specs=[whole] * 2,
        out_shape=[
            jax.ShapeDtypeStruct((2, rows + 16, HEAD_DIM), BF),
            jax.ShapeDtypeStruct((1, rows + 16, HEAD_DIM), BF),
        ],
        scratch_shapes=[pltpu.VMEM((len(HEADS_BY), keys_total, 2 * HEAD_DIM), BF)],
        compiler_params=params(32),
        cost_estimate=pl.CostEstimate(
            flops=len(HEADS_BY) * rows * keys_total * HEAD_DIM * 8,
            bytes_accessed=8 * 2**20,
            transcendentals=len(HEADS_BY) * rows * keys_total,
        ),
    )(*queries, *blocks[0], *blocks[1], *after)


def combine(parts_y, parts_x):
    packed = parts_y[0].shape[1]
    rows = packed - 16
    lines = rows // HEAD_DIM
    count = len(parts_y)
    heads = len(HEADS_BY)

    def kernel(*refs):
        out_ref = refs[-1]
        diagonal = lax.broadcasted_iota(jnp.int32, (HEAD_DIM, HEAD_DIM), 0) == lax.broadcasted_iota(
            jnp.int32, (HEAD_DIM, HEAD_DIM), 1
        )
        for h, (along, at) in enumerate(HEADS_BY):
            sources = refs[:count] if along == 1 else refs[count : 2 * count]
            tail = sources[0][at, rows : rows + 16].astype(F32)
            for ref in sources[1:]:
                tail = tail + ref[at, rows : rows + 16].astype(F32)
            for part in range(lines):
                place = slice(part * HEAD_DIM, (part + 1) * HEAD_DIM)
                numerator = sources[0][at, place].astype(F32)
                for ref in sources[1:]:
                    numerator = numerator + ref[at, place].astype(F32)
                total = tail[part : part + 1] + tail[lines + part : lines + part + 1]
                column = jnp.sum(jnp.where(diagonal, 1.0 / total, 0.0), axis=1, keepdims=True)
                out_ref[place, h * HEAD_DIM : (h + 1) * HEAD_DIM] = (numerator * column).astype(BF)

    return pl.pallas_call(
        kernel,
        out_shape=jax.ShapeDtypeStruct((rows, heads * HEAD_DIM), BF),
        compiler_params=params(16),
    )(*parts_y, *parts_x)


def attention(xs, ys):
    parts_y, parts_x = [None] * 4, [None] * 4
    after = []
    for k in (3, 2, 1, 0):
        sums_y, sums_x = attend((xs[k], ys[k]), (xs, ys), after)
        after = [sums_x]
        by = STEPS[k]
        parts_y[k] = shift_y(sums_y, -by) if by else sums_y
        parts_x[k] = shift_x(sums_x, -by) if by else sums_x
    return combine(parts_y, parts_x), after[0]


def output_step(places, blocks, weights, base, gate):
    rows, part = blocks[0].shape
    width = gate.shape[1]
    count = len(blocks)
    depth = count * part
    half = weights[0].shape[1]
    block = 512
    per_half = half // block

    def kernel(places_ref, *refs):
        block_refs = refs[:count]
        weight_refs = refs[count : count + 2]
        base_ref, gate_ref, out_ref, side_ref = refs[count + 2 :]
        n = pl.program_id(0)

        @pl.when(n == 0)
        def _():
            for k in range(count):
                side_ref[:, pl.ds(pl.multiple_of(places_ref[k] * part, HEAD_DIM), part)] = (
                    block_refs[k][...]
                )

        for which in range(2):

            @pl.when(n // per_half == which)
            def _():
                update = jnp.dot(
                    side_ref[...], weight_refs[which][...], preferred_element_type=F32
                )
                out_ref[...] = (base_ref[...].astype(F32) + gate_ref[...] * update).astype(BF)

    return pl.pallas_call(
        kernel,
        grid_spec=pltpu.PrefetchScalarGridSpec(
            num_scalar_prefetch=1,
            grid=(width // block,),
            in_specs=[pl.BlockSpec((rows, part), lambda n, p: (0, 0))] * count
            + [
                pl.BlockSpec((depth, block), lambda n, p: (0, jnp.minimum(n, per_half - 1))),
                pl.BlockSpec((depth, block), lambda n, p: (0, jnp.maximum(n - per_half, 0))),
                pl.BlockSpec((rows, block), lambda n, p: (0, n)),
                pl.BlockSpec((gate.shape[0], block), lambda n, p: (0, n)),
            ],
            out_specs=pl.BlockSpec((rows, block), lambda n, p: (0, n)),
            scratch_shapes=[pltpu.VMEM((rows, depth), BF)],
        ),
        out_shape=jax.ShapeDtypeStruct((rows, width), BF),
        compiler_params=params(32),
    )(places, *blocks, *weights, base, gate)


def second_projection(tokens, scale, shift, weight, query_gain, key_gain):
    rows, width = tokens.shape
    heads = weight.shape[2] // HEAD_DIM
    step = 128

    def kernel(tokens_ref, scale_ref, shift_ref, weight_ref, qg_ref, kg_ref, x_ref, y_ref, normed_ref):
        j = pl.program_id(0)

        @pl.when(j == 0)
        def _():
            for start in range(0, rows, step):
                values = tokens_ref[start : start + step].astype(F32)
                values = values - jnp.mean(values, axis=1, keepdims=True)
                spread = jnp.mean(values * values, axis=1, keepdims=True)
                normed_ref[start : start + step] = (
                    values * lax.rsqrt(spread + norm_eps) * (1.0 + scale_ref[...]) + shift_ref[...]
                ).astype(BF)

        projected = jnp.dot(normed_ref[...], weight_ref[0], preferred_element_type=F32)
        for kind in range(3):

            @pl.when(j == kind)
            def _():
                for h in range(heads):
                    part = projected[:, h * HEAD_DIM : (h + 1) * HEAD_DIM]
                    if kind < 2:
                        part = head_norm(part, (qg_ref, kg_ref)[kind][...])
                    else:
                        part = part.astype(BF)
                    if (kind, h) in ALONG_X:
                        x_ref[ALONG_X.index((kind, h))] = part
                    else:
                        y_ref[ALONG_Y.index((kind, h))] = part

    return pl.pallas_call(
        kernel,
        grid=(3,),
        in_specs=[
            pl.BlockSpec((rows, width), lambda j: (0, 0)),
            pl.BlockSpec((1, width), lambda j: (0, 0)),
            pl.BlockSpec((1, width), lambda j: (0, 0)),
            pl.BlockSpec((1, width, heads * HEAD_DIM), lambda j: (j, 0, 0)),
            pl.BlockSpec((1, HEAD_DIM), lambda j: (0, 0)),
            pl.BlockSpec((1, HEAD_DIM), lambda j: (0, 0)),
        ],
        out_specs=[
            pl.BlockSpec((len(ALONG_X), rows, HEAD_DIM), lambda j: (0, 0, 0)),
            pl.BlockSpec((len(ALONG_Y), rows, HEAD_DIM), lambda j: (0, 0, 0)),
        ],
        out_shape=[
            jax.ShapeDtypeStruct((len(ALONG_X), rows, HEAD_DIM), BF),
            jax.ShapeDtypeStruct((len(ALONG_Y), rows, HEAD_DIM), BF),
        ],
        scratch_shapes=[pltpu.VMEM((rows, width), BF)],
        compiler_params=params(32),
    )(tokens, scale, shift, weight, query_gain, key_gain)


def per_device(
    latent,
    noise_field,
    timestep,
    embed_weight,
    modulate_weight,
    attend_weight,
    query_gain,
    key_gain,
    output_weight,
):
    batches = latent.shape[0]
    patch, width = embed_weight.shape
    local = latent.shape[1] * latent.shape[2] * latent.shape[3]
    section = lax.axis_index("section")
    row = lax.axis_index("row")
    first = section == 0
    half = width // 2

    def by_section(of_first, of_second):
        return jnp.where(first, of_first, of_second)

    def swapped(array):
        return lax.ppermute(array, "section", SWAP)

    timestep_here = lax.dynamic_slice_in_dim(timestep, section, 1)
    level = signal_level(timestep_here)
    noisy = (
        jnp.sqrt(level) * lax.dynamic_index_in_dim(latent, section, 0, False).astype(F32)
        + jnp.sqrt(1.0 - level) * lax.dynamic_index_in_dim(noise_field, section, 0, False).astype(F32)
    ).astype(BF)
    noisy = noisy.reshape(local, patch)
    features = time_features(timestep, modulate_weight.shape[1]).astype(BF)
    mod_part = jnp.dot(features, modulate_weight[0], preferred_element_type=F32)

    mod_rows = mod_part.size // patch
    packed = jnp.concatenate(
        [noisy.astype(F32), mod_part.reshape(mod_rows, patch), jnp.zeros((-mod_rows % 8, patch), F32)]
    )
    packed = gather(packed, shift_z)
    noisy_row = jnp.concatenate([block[:local] for block in packed]).astype(BF)
    mods = jnp.stack([block[local : local + mod_rows].reshape(batches, -1) for block in packed])
    ordered = [
        lax.dynamic_index_in_dim(mods, jnp.array([0, 2, 3, 1])[(b - row) % 4], 0, False)
        for b in range(4)
    ]
    modulation = jnp.concatenate(ordered, axis=1)
    shift_own = modulation[:, :width]
    scale_own = modulation[:, width : 2 * width]

    noisy_x = gather(noisy_row, shift_x)
    noisy_y = gather(noisy_row, shift_y)

    centered = embed_weight.astype(F32)
    centered = centered - jnp.mean(centered, axis=1, keepdims=True)
    gram = (
        jnp.dot(centered, centered.T, preferred_element_type=F32, precision=lax.Precision.HIGHEST)
        / width
    )
    sides = jnp.concatenate(
        [centered[None] * (1.0 + scale_own[:, None, :]), shift_own[:, None, :]], axis=1
    )
    sides = jnp.concatenate([sides, jnp.zeros((batches, 15, width), F32)], axis=1)
    sides = sides.astype(BF).reshape(-1, width)
    mapped = map_weights(sides, attend_weight[0])
    kinds = mapped.shape[0]
    mapped = mapped.reshape(kinds, batches, patch + 16, HEAD_DIM)
    bias = mapped[:, :, patch : patch + 1]
    upper = bias.astype(BF)
    lower = (bias - upper.astype(F32)).astype(BF)
    mapped = jnp.concatenate(
        [mapped[:, :, :patch].astype(BF), upper, lower, jnp.zeros((kinds, batches, 14, HEAD_DIM), BF)],
        axis=2,
    )
    mapped_other = lax.ppermute(mapped[:, 1], "section", [(0, 1)])
    mapped = by_section(mapped[:, 0], mapped_other)
    bias = mapped[:, patch : patch + 1].astype(F32) + mapped[:, patch + 1 : patch + 2].astype(F32)
    mapped = mapped[:, :patch]

    gains = jnp.concatenate([query_gain, key_gain])
    small = jnp.concatenate([modulation.reshape(-1, patch), gains, jnp.zeros((6, patch), F32)])
    small_other = swapped(small)
    small_first = by_section(small, small_other)
    small_second = by_section(small_other, small)
    mod_rows_all = modulation.size // patch

    def unpack(array):
        mod = lax.dynamic_slice_in_dim(array[:mod_rows_all].reshape(batches, -1), section, 1)
        qg = array[mod_rows_all : mod_rows_all + 1] * QUERY_SCALE
        kg = array[mod_rows_all + 1 : mod_rows_all + 2]
        return mod[:, :width], mod[:, width : 2 * width], mod[:, 2 * width :], qg, kg

    _, _, gate_first, qg_first, kg_first = unpack(small_first)
    shift_second, scale_second, _, qg_second, kg_second = unpack(small_second)
    attend_given, noisy_x[3] = lax.optimization_barrier((attend_weight[0], noisy_x[3]))
    attend_other = lax.ppermute(attend_given, "section", [(1, 0)])

    keep = lax.dynamic_slice_in_dim(output_weight[0], section * half, half, 1)
    give = lax.dynamic_slice_in_dim(output_weight[0], (1 - section) * half, half, 1)
    got = swapped(give)
    out_first = lax.all_gather(by_section(keep, got), "row", axis=0, tiled=True)

    heads = kinds // 3
    gain_of = (qg_first, kg_first)

    def first_heads(blocks, along):
        weight = jnp.concatenate([mapped[kind * heads + h] for kind, h in along], axis=1)
        bias_row = jnp.concatenate([bias[kind * heads + h] for kind, h in along], axis=1)
        gains_here = jnp.concatenate([gain_of[kind] for kind, h in along if kind < 2])
        return [first_projection(block, gram, weight, bias_row, gains_here) for block in blocks]

    attended, last = attention(first_heads(noisy_x, ALONG_X), first_heads(noisy_y, ALONG_Y))
    out_first, second_part, last = lax.optimization_barrier((out_first, by_section(got, keep), last))
    out_first_other = swapped(out_first)
    out_second = lax.all_gather(second_part, "row", axis=0, tiled=True)

    embedded = jnp.dot(noisy_row, embed_weight, preferred_element_type=F32).astype(BF)
    blocks = gather(attended, shift_z)
    turned = []
    for block, by in zip(blocks, STEPS):
        order = [
            [k for k in range(4) if (by + STEPS[k] - STEPS[mine]) % 4 == 0][0] for mine in range(4)
        ]
        turned.append(jnp.concatenate([block[k * local : (k + 1) * local] for k in order]))
    places = jnp.stack([(row - by) % 4 for by in STEPS]).astype(jnp.int32)

    def step_first(weights):
        return output_step(places, turned, weights, embedded, gate_first)

    tokens = lax.cond(
        first,
        lambda own, other: step_first((own, other)),
        lambda own, other: step_first((other, own)),
        out_first,
        out_first_other,
    )
    result_first = tokens[:local]
    result_other = swapped(result_first)

    def project(weight):
        return second_projection(
            tokens, scale_second, shift_second, weight, qg_second, kg_second
        )

    along_x, along_y = lax.cond(
        first,
        lambda own, other: project(other),
        lambda own, other: project(own),
        attend_weight[0],
        attend_other,
    )
    attended, last = attention(gather(along_x, shift_x), gather(along_y, shift_y))
    out_second, last = lax.optimization_barrier((out_second, last))
    mine = give_back([attended[k * local : (k + 1) * local] for k in range(4)], shift_z)
    mine = jnp.concatenate(mine, axis=1)
    mine_other = lax.ppermute(mine, "section", [(0, 1)])
    out_second_other = swapped(out_second)
    places = jnp.stack([(row + by) % 4 for by in STEPS]).astype(jnp.int32)
    gates = modulation[:, 2 * width :]

    def finish_first():
        return jnp.stack([result_first, result_other])

    def finish_second():
        both = jnp.concatenate([mine_other, mine])
        part = both.shape[1] // 4
        base = jnp.concatenate([result_other, result_first])
        spread_gates = jnp.broadcast_to(gates[:, None, :], (batches, local, width)).reshape(-1, width)
        result = output_step(
            places,
            [both[:, k * part : (k + 1) * part] for k in range(4)],
            (out_second_other, out_second),
            base,
            spread_gates,
        )
        return result.reshape(batches, local, width)

    result = lax.cond(first, finish_first, finish_second)
    return result.reshape(1, batches, latent.shape[1], latent.shape[2], latent.shape[3], width)


def solution(mesh):
    return jax.shard_map(
        per_device,
        mesh=mesh,
        in_specs=(
            P(None, "depth", "row", None, None),
            P(None, "depth", "row", None, None),
            P(),
            P(),
            P("section", None, "row"),
            P("section", None, None, "row"),
            P("section", None),
            P("section", None),
            P("section", "row", None),
        ),
        out_specs=P("section", None, "depth", "row", None, None),
        check_vma=False,
    )
```

```python
import math

import jax
import jax.numpy as jnp
from jax import lax
from jax.experimental import pallas as pl
from jax.experimental.pallas import tpu as pltpu
from jax.sharding import PartitionSpec as P

HEAD_DIM = 128
BF = jnp.bfloat16
F32 = jnp.float32

norm_eps = 1e-06
plan_steps = 1000.0
QUERY_SCALE = math.log2(math.e) / math.sqrt(HEAD_DIM)
SWAP = [(0, 1), (1, 0)]
STEPS = (0, 1, -1, 2)


def signal_level(timestep):
    phase = (timestep.astype(F32) / plan_steps + 0.008) / 1.008 * (math.pi / 2)
    return jnp.cos(phase) ** 2


def time_features(timestep, count):
    half = count // 2
    frequency = jnp.exp(-math.log(10000.0) * jnp.arange(half, dtype=F32) / half)
    angles = timestep.astype(F32)[:, None] * frequency[None, :]
    return jnp.concatenate([jnp.cos(angles), jnp.sin(angles)], axis=1)


def shift_x(array, by):
    return lax.ppermute(
        array, "depth", [(y * 4 + x, y * 4 + (x + by) % 4) for y in range(4) for x in range(4)]
    )


def shift_y(array, by):
    return lax.ppermute(
        array, "depth", [(y * 4 + x, (y + by) % 4 * 4 + x) for y in range(4) for x in range(4)]
    )


def shift_z(array, by):
    return lax.ppermute(array, "row", [(z, (z + by) % 4) for z in range(4)])


def gather(array, shift):
    return [array] + [shift(array, by) for by in STEPS[1:]]


def give_back(blocks, shift):
    return [blocks[0]] + [shift(block, -by) for block, by in zip(blocks[1:], STEPS[1:])]


def params(mib):
    return pltpu.CompilerParams(vmem_limit_bytes=mib * 2**20)


def head_norm(values, gain):
    factor = lax.rsqrt(jnp.mean(values * values, axis=1, keepdims=True) + norm_eps)
    return (values * factor * gain).astype(BF)


def map_weights(sides, weight):
    rows, width = sides.shape
    kinds, _, channels = weight.shape
    heads = channels // HEAD_DIM

    def kernel(sides_ref, weight_ref, out_ref):
        mapped = jnp.dot(sides_ref[...], weight_ref[0], preferred_element_type=F32)
        for h in range(heads):
            out_ref[h] = mapped[:, h * HEAD_DIM : (h + 1) * HEAD_DIM]

    return pl.pallas_call(
        kernel,
        grid=(kinds,),
        in_specs=[
            pl.BlockSpec((rows, width), lambda j: (0, 0)),
            pl.BlockSpec((1, width, channels), lambda j: (j, 0, 0)),
        ],
        out_specs=pl.BlockSpec((heads, rows, HEAD_DIM), lambda j: (j, 0, 0)),
        out_shape=jax.ShapeDtypeStruct((kinds * heads, rows, HEAD_DIM), F32),
        compiler_params=params(24),
    )(sides, weight)


def first_projection(noisy, gram, weight, bias, gains):
    rows = noisy.shape[0]
    heads = weight.shape[1] // HEAD_DIM
    normed_heads = gains.shape[0]

    def kernel(noisy_ref, gram_ref, weight_ref, bias_ref, gains_ref, out_ref):
        values = noisy_ref[...].astype(F32)
        spread = jnp.sum(
            jnp.dot(
                values, gram_ref[...], preferred_element_type=F32, precision=lax.Precision.HIGHEST
            )
            * values,
            axis=1,
            keepdims=True,
        )
        scaled = (values * lax.rsqrt(spread + norm_eps)).astype(BF)
        projected = jnp.dot(scaled, weight_ref[...], preferred_element_type=F32) + bias_ref[...]
        for h in range(heads):
            part = projected[:, h * HEAD_DIM : (h + 1) * HEAD_DIM]
            if h < normed_heads:
                out_ref[h] = head_norm(part, gains_ref[h : h + 1])
            else:
                out_ref[h] = part.astype(BF)

    return pl.pallas_call(
        kernel,
        out_shape=jax.ShapeDtypeStruct((heads, rows, HEAD_DIM), BF),
        compiler_params=params(16),
    )(noisy, gram, weight, bias, gains)


ALONG_X = ((1, 0), (1, 2), (0, 1), (2, 0), (2, 2))
ALONG_Y = ((0, 0), (0, 2), (1, 1), (2, 1))
HEADS_BY = ((1, 0), (0, 0), (1, 1))


def attend(queries, blocks, after):
    rows = queries[0].shape[1]
    key_rows = blocks[0][0].shape[1]
    count = len(blocks[0])
    keys_total = key_rows * count
    places = (ALONG_X, ALONG_Y)

    def kernel(*refs):
        query_refs = refs[:2]
        block_refs = (refs[2 : 2 + count], refs[2 + count : 2 + 2 * count])
        out_refs = refs[-3:-1]
        wide_ref = refs[-1]
        diagonal = lax.broadcasted_iota(jnp.int32, (HEAD_DIM, HEAD_DIM), 0) == lax.broadcasted_iota(
            jnp.int32, (HEAD_DIM, HEAD_DIM), 1
        )
        for h, (along, out_place) in enumerate(HEADS_BY):
            query = query_refs[along][places[along].index((0, h))]
            key_at = places[1 - along].index((1, h))
            value_at = places[1 - along].index((2, h))
            sums = jnp.zeros((rows, 2 * HEAD_DIM), F32)
            for i, ref in enumerate(block_refs[1 - along]):
                wide_ref[h, i * key_rows : (i + 1) * key_rows, :HEAD_DIM] = ref[value_at]
                wide_ref[h, i * key_rows : (i + 1) * key_rows, HEAD_DIM:] = jnp.ones(
                    (key_rows, HEAD_DIM), BF
                )
            for i, ref in enumerate(block_refs[1 - along]):
                scores = lax.dot_general(
                    query, ref[key_at], (((1,), (1,)), ((), ())), preferred_element_type=F32
                )
                weights = jnp.exp2(scores).astype(BF)
                sums = sums + jnp.dot(
                    weights,
                    wide_ref[h, i * key_rows : (i + 1) * key_rows],
                    preferred_element_type=F32,
                )
            out_ref = out_refs[1 - along]
            out_ref[out_place, :rows] = sums[:, :HEAD_DIM].astype(BF)
            lines = []
            for part in range(rows // HEAD_DIM):
                square = sums[part * HEAD_DIM : (part + 1) * HEAD_DIM, HEAD_DIM:]
                lines.append(jnp.sum(jnp.where(diagonal, square, 0.0), axis=0, keepdims=True))
            total = jnp.concatenate(lines, axis=0)
            upper = total.astype(BF)
            lower = (total - upper.astype(F32)).astype(BF)
            out_ref[out_place, rows : rows + 16] = jnp.concatenate(
                [upper.astype(F32), lower.astype(F32), jnp.zeros((8, HEAD_DIM), F32)], axis=0
            ).astype(BF)

    whole = pl.BlockSpec(memory_space=pltpu.VMEM)
    return pl.pallas_call(
        kernel,
        in_specs=[whole] * (2 + 2 * count) + [pl.BlockSpec(memory_space=pl.ANY)] * len(after),
        out_specs=[whole] * 2,
        out_shape=[
            jax.ShapeDtypeStruct((2, rows + 16, HEAD_DIM), BF),
            jax.ShapeDtypeStruct((1, rows + 16, HEAD_DIM), BF),
        ],
        scratch_shapes=[pltpu.VMEM((len(HEADS_BY), keys_total, 2 * HEAD_DIM), BF)],
        compiler_params=params(32),
        cost_estimate=pl.CostEstimate(
            flops=len(HEADS_BY) * rows * keys_total * HEAD_DIM * 8,
            bytes_accessed=8 * 2**20,
            transcendentals=len(HEADS_BY) * rows * keys_total,
        ),
    )(*queries, *blocks[0], *blocks[1], *after)


def combine(parts_y, parts_x):
    packed = parts_y[0].shape[1]
    rows = packed - 16
    lines = rows // HEAD_DIM
    count = len(parts_y)
    heads = len(HEADS_BY)

    def kernel(*refs):
        out_ref = refs[-1]
        diagonal = lax.broadcasted_iota(jnp.int32, (HEAD_DIM, HEAD_DIM), 0) == lax.broadcasted_iota(
            jnp.int32, (HEAD_DIM, HEAD_DIM), 1
        )
        for h, (along, at) in enumerate(HEADS_BY):
            sources = refs[:count] if along == 1 else refs[count : 2 * count]
            tail = sources[0][at, rows : rows + 16].astype(F32)
            for ref in sources[1:]:
                tail = tail + ref[at, rows : rows + 16].astype(F32)
            for part in range(lines):
                place = slice(part * HEAD_DIM, (part + 1) * HEAD_DIM)
                numerator = sources[0][at, place].astype(F32)
                for ref in sources[1:]:
                    numerator = numerator + ref[at, place].astype(F32)
                total = tail[part : part + 1] + tail[lines + part : lines + part + 1]
                column = jnp.sum(jnp.where(diagonal, 1.0 / total, 0.0), axis=1, keepdims=True)
                out_ref[place, h * HEAD_DIM : (h + 1) * HEAD_DIM] = (numerator * column).astype(BF)

    return pl.pallas_call(
        kernel,
        out_shape=jax.ShapeDtypeStruct((rows, heads * HEAD_DIM), BF),
        compiler_params=params(16),
    )(*parts_y, *parts_x)


def attention(xs, ys):
    parts_y, parts_x = [None] * 4, [None] * 4
    after = []
    for k in (3, 2, 1, 0):
        if k == 0:
            after = after + [parts_y[3], parts_x[3]]
        sums_y, sums_x = attend((xs[k], ys[k]), (xs, ys), after)
        after = [sums_x]
        by = STEPS[k]
        parts_y[k] = shift_y(sums_y, -by) if by else sums_y
        parts_x[k] = shift_x(sums_x, -by) if by else sums_x
        if k == 3:
            early = sums_x
    return combine(parts_y, parts_x), early


def output_step(places, blocks, weights, base, gate):
    rows, part = blocks[0].shape
    width = gate.shape[1]
    count = len(blocks)
    depth = count * part
    half = weights[0].shape[1]
    block = 512
    per_half = half // block

    def kernel(places_ref, *refs):
        block_refs = refs[:count]
        weight_refs = refs[count : count + 2]
        base_ref, gate_ref, out_ref, side_ref = refs[count + 2 :]
        n = pl.program_id(0)

        @pl.when(n == 0)
        def _():
            for k in range(count):
                side_ref[:, pl.ds(pl.multiple_of(places_ref[k] * part, HEAD_DIM), part)] = (
                    block_refs[k][...]
                )

        for which in range(2):

            @pl.when(n // per_half == which)
            def _():
                update = jnp.dot(
                    side_ref[...], weight_refs[which][...], preferred_element_type=F32
                )
                out_ref[...] = (base_ref[...].astype(F32) + gate_ref[...] * update).astype(BF)

    return pl.pallas_call(
        kernel,
        grid_spec=pltpu.PrefetchScalarGridSpec(
            num_scalar_prefetch=1,
            grid=(width // block,),
            in_specs=[pl.BlockSpec((rows, part), lambda n, p: (0, 0))] * count
            + [
                pl.BlockSpec((depth, block), lambda n, p: (0, jnp.minimum(n, per_half - 1))),
                pl.BlockSpec((depth, block), lambda n, p: (0, jnp.maximum(n - per_half, 0))),
                pl.BlockSpec((rows, block), lambda n, p: (0, n)),
                pl.BlockSpec((gate.shape[0], block), lambda n, p: (0, n)),
            ],
            out_specs=pl.BlockSpec((rows, block), lambda n, p: (0, n)),
            scratch_shapes=[pltpu.VMEM((rows, depth), BF)],
        ),
        out_shape=jax.ShapeDtypeStruct((rows, width), BF),
        compiler_params=params(32),
    )(places, *blocks, *weights, base, gate)


def second_projection(tokens, scale, shift, weight, query_gain, key_gain):
    rows, width = tokens.shape
    heads = weight.shape[2] // HEAD_DIM
    step = 128

    def kernel(tokens_ref, scale_ref, shift_ref, weight_ref, qg_ref, kg_ref, x_ref, y_ref, normed_ref):
        j = pl.program_id(0)

        @pl.when(j == 0)
        def _():
            for start in range(0, rows, step):
                values = tokens_ref[start : start + step].astype(F32)
                values = values - jnp.mean(values, axis=1, keepdims=True)
                spread = jnp.mean(values * values, axis=1, keepdims=True)
                normed_ref[start : start + step] = (
                    values * lax.rsqrt(spread + norm_eps) * (1.0 + scale_ref[...]) + shift_ref[...]
                ).astype(BF)

        projected = jnp.dot(normed_ref[...], weight_ref[0], preferred_element_type=F32)
        for kind in range(3):

            @pl.when(j == kind)
            def _():
                for h in range(heads):
                    part = projected[:, h * HEAD_DIM : (h + 1) * HEAD_DIM]
                    if kind < 2:
                        part = head_norm(part, (qg_ref, kg_ref)[kind][...])
                    else:
                        part = part.astype(BF)
                    if (kind, h) in ALONG_X:
                        x_ref[ALONG_X.index((kind, h))] = part
                    else:
                        y_ref[ALONG_Y.index((kind, h))] = part

    return pl.pallas_call(
        kernel,
        grid=(3,),
        in_specs=[
            pl.BlockSpec((rows, width), lambda j: (0, 0)),
            pl.BlockSpec((1, width), lambda j: (0, 0)),
            pl.BlockSpec((1, width), lambda j: (0, 0)),
            pl.BlockSpec((1, width, heads * HEAD_DIM), lambda j: (j, 0, 0)),
            pl.BlockSpec((1, HEAD_DIM), lambda j: (0, 0)),
            pl.BlockSpec((1, HEAD_DIM), lambda j: (0, 0)),
        ],
        out_specs=[
            pl.BlockSpec((len(ALONG_X), rows, HEAD_DIM), lambda j: (0, 0, 0)),
            pl.BlockSpec((len(ALONG_Y), rows, HEAD_DIM), lambda j: (0, 0, 0)),
        ],
        out_shape=[
            jax.ShapeDtypeStruct((len(ALONG_X), rows, HEAD_DIM), BF),
            jax.ShapeDtypeStruct((len(ALONG_Y), rows, HEAD_DIM), BF),
        ],
        scratch_shapes=[pltpu.VMEM((rows, width), BF)],
        compiler_params=params(32),
    )(tokens, scale, shift, weight, query_gain, key_gain)


def per_device(
    latent,
    noise_field,
    timestep,
    embed_weight,
    modulate_weight,
    attend_weight,
    query_gain,
    key_gain,
    output_weight,
):
    batches = latent.shape[0]
    patch, width = embed_weight.shape
    local = latent.shape[1] * latent.shape[2] * latent.shape[3]
    section = lax.axis_index("section")
    row = lax.axis_index("row")
    first = section == 0
    half = width // 2

    def by_section(of_first, of_second):
        return jnp.where(first, of_first, of_second)

    def swapped(array):
        return lax.ppermute(array, "section", SWAP)

    level = signal_level(timestep)[:, None, None, None, None]
    noisy = (
        jnp.sqrt(level) * latent.astype(F32) + jnp.sqrt(1.0 - level) * noise_field.astype(F32)
    ).astype(BF)
    noisy = by_section(noisy[0], noisy[1]).reshape(local, patch)
    features = time_features(timestep, modulate_weight.shape[1]).astype(BF)
    mod_part = jnp.dot(features, modulate_weight[0], preferred_element_type=F32)

    mod_rows = mod_part.size // patch
    packed = jnp.concatenate(
        [noisy.astype(F32), mod_part.reshape(mod_rows, patch), jnp.zeros((-mod_rows % 8, patch), F32)]
    )
    packed = gather(packed, shift_z)
    noisy_row = jnp.concatenate([block[:local] for block in packed]).astype(BF)
    mods = [block[local : local + mod_rows].reshape(batches, -1) for block in packed]

    def from_row(b):
        chosen = mods[0]
        for k in (1, 2, 3):
            chosen = jnp.where(row == (b + STEPS[k]) % 4, mods[k], chosen)
        return chosen

    modulation = jnp.concatenate([from_row(b) for b in range(4)], axis=1)
    shift_own = modulation[:, :width]
    scale_own = modulation[:, width : 2 * width]

    noisy_x = gather(noisy_row, shift_x)
    noisy_y = gather(noisy_row, shift_y)

    centered = embed_weight.astype(F32)
    centered = centered - jnp.mean(centered, axis=1, keepdims=True)
    gram = (
        jnp.dot(centered, centered.T, preferred_element_type=F32, precision=lax.Precision.HIGHEST)
        / width
    )
    sides = jnp.concatenate(
        [centered[None] * (1.0 + scale_own[:, None, :]), shift_own[:, None, :]], axis=1
    )
    sides = jnp.concatenate([sides, jnp.zeros((batches, 15, width), F32)], axis=1)
    sides = sides.astype(BF).reshape(-1, width)
    mapped = map_weights(sides, attend_weight[0])
    kinds = mapped.shape[0]
    mapped = mapped.reshape(kinds, batches, patch + 16, HEAD_DIM)
    bias = mapped[:, :, patch : patch + 1]
    upper = bias.astype(BF)
    lower = (bias - upper.astype(F32)).astype(BF)
    mapped = jnp.concatenate(
        [mapped[:, :, :patch].astype(BF), upper, lower, jnp.zeros((kinds, batches, 14, HEAD_DIM), BF)],
        axis=2,
    )
    mapped_other = lax.ppermute(mapped[:, 1], "section", [(0, 1)])
    mapped = by_section(mapped[:, 0], mapped_other)
    bias = mapped[:, patch : patch + 1].astype(F32) + mapped[:, patch + 1 : patch + 2].astype(F32)
    mapped = mapped[:, :patch]

    gains = jnp.concatenate([query_gain, key_gain])
    small = jnp.concatenate([modulation.reshape(-1, patch), gains, jnp.zeros((6, patch), F32)])
    small_other = swapped(small)
    small_first = by_section(small, small_other)
    small_second = by_section(small_other, small)
    mod_rows_all = modulation.size // patch

    def unpack(array):
        mod = array[:mod_rows_all].reshape(batches, -1)
        mod = by_section(mod[:1], mod[1:])
        qg = array[mod_rows_all : mod_rows_all + 1] * QUERY_SCALE
        kg = array[mod_rows_all + 1 : mod_rows_all + 2]
        return mod[:, :width], mod[:, width : 2 * width], mod[:, 2 * width :], qg, kg

    _, _, gate_first, qg_first, kg_first = unpack(small_first)
    shift_second, scale_second, _, qg_second, kg_second = unpack(small_second)

    keep = lax.dynamic_slice_in_dim(output_weight[0], section * half, half, 1)
    give = lax.dynamic_slice_in_dim(output_weight[0], (1 - section) * half, half, 1)
    got = swapped(give)
    out_first = lax.all_gather(by_section(keep, got), "row", axis=0, tiled=True)

    heads = kinds // 3
    gain_of = (qg_first, kg_first)

    def first_heads(blocks, along):
        weight = jnp.concatenate([mapped[kind * heads + h] for kind, h in along], axis=1)
        bias_row = jnp.concatenate([bias[kind * heads + h] for kind, h in along], axis=1)
        gains_here = jnp.concatenate([gain_of[kind] for kind, h in along if kind < 2])
        return [first_projection(block, gram, weight, bias_row, gains_here) for block in blocks]

    attended, early = attention(first_heads(noisy_x, ALONG_X), first_heads(noisy_y, ALONG_Y))
    attend_given, early = lax.optimization_barrier((attend_weight[0], early))
    attend_other = lax.ppermute(attend_given, "section", [(1, 0)])
    out_first, attended = lax.optimization_barrier((out_first, attended))
    out_first_other = swapped(out_first)

    embedded = jnp.dot(noisy_row, embed_weight, preferred_element_type=F32).astype(BF)
    blocks = gather(attended, shift_z)
    turned = []
    for block, by in zip(blocks, STEPS):
        order = [
            [k for k in range(4) if (by + STEPS[k] - STEPS[mine]) % 4 == 0][0] for mine in range(4)
        ]
        turned.append(jnp.concatenate([block[k * local : (k + 1) * local] for k in order]))
    places = jnp.stack([(row - by) & 3 for by in STEPS]).astype(jnp.int32)

    def step_first(weights):
        return output_step(places, turned, weights, embedded, gate_first)

    tokens = lax.cond(
        first,
        lambda own, other: step_first((own, other)),
        lambda own, other: step_first((other, own)),
        out_first,
        out_first_other,
    )
    keep, got, tokens = lax.optimization_barrier((keep, got, tokens))
    out_second = lax.all_gather(by_section(got, keep), "row", axis=0, tiled=True)
    result_first = tokens[:local]
    result_other = swapped(result_first)

    def project(weight):
        return second_projection(
            tokens, scale_second, shift_second, weight, qg_second, kg_second
        )

    along_x, along_y = lax.cond(
        first,
        lambda own, other: project(other),
        lambda own, other: project(own),
        attend_weight[0],
        attend_other,
    )
    attended, early = attention(gather(along_x, shift_x), gather(along_y, shift_y))
    out_second, early = lax.optimization_barrier((out_second, early))
    mine = give_back([attended[k * local : (k + 1) * local] for k in range(4)], shift_z)
    mine = jnp.concatenate(mine, axis=1)
    mine_other = lax.ppermute(mine, "section", [(0, 1)])
    out_second_other = swapped(out_second)
    places = jnp.stack([(row + by) & 3 for by in STEPS]).astype(jnp.int32)
    gates = modulation[:, 2 * width :]

    def finish_first():
        return jnp.stack([result_first, result_other])

    def finish_second():
        both = jnp.concatenate([mine_other, mine])
        part = both.shape[1] // 4
        base = jnp.concatenate([result_other, result_first])
        spread_gates = jnp.broadcast_to(gates[:, None, :], (batches, local, width)).reshape(-1, width)
        result = output_step(
            places,
            [both[:, k * part : (k + 1) * part] for k in range(4)],
            (out_second_other, out_second),
            base,
            spread_gates,
        )
        return result.reshape(batches, local, width)

    result = lax.cond(first, finish_first, finish_second)
    return result.reshape(1, batches, latent.shape[1], latent.shape[2], latent.shape[3], width)


def solution(mesh):
    return jax.shard_map(
        per_device,
        mesh=mesh,
        in_specs=(
            P(None, "depth", "row", None, None),
            P(None, "depth", "row", None, None),
            P(),
            P(),
            P("section", None, "row"),
            P("section", None, None, "row"),
            P("section", None),
            P("section", None),
            P("section", "row", None),
        ),
        out_specs=P("section", None, "depth", "row", None, None),
        check_vma=False,
    )
```

```python
import math

import jax
import jax.numpy as jnp
from jax import lax
from jax.experimental import pallas as pl
from jax.experimental.pallas import tpu as pltpu
from jax.sharding import PartitionSpec as P

HEAD_DIM = 128
BF = jnp.bfloat16
F32 = jnp.float32

norm_eps = 1e-06
plan_steps = 1000.0
QUERY_SCALE = math.log2(math.e) / math.sqrt(HEAD_DIM)
SWAP = [(0, 1), (1, 0)]
STEPS = (0, 1, -1, 2)


def signal_level(timestep):
    phase = (timestep.astype(F32) / plan_steps + 0.008) / 1.008 * (math.pi / 2)
    return jnp.cos(phase) ** 2


def time_features(timestep, count):
    half = count // 2
    frequency = jnp.exp(-math.log(10000.0) * jnp.arange(half, dtype=F32) / half)
    angles = timestep.astype(F32)[:, None] * frequency[None, :]
    return jnp.concatenate([jnp.cos(angles), jnp.sin(angles)], axis=1)


def shift_x(array, by):
    return lax.ppermute(
        array, "depth", [(y * 4 + x, y * 4 + (x + by) % 4) for y in range(4) for x in range(4)]
    )


def shift_y(array, by):
    return lax.ppermute(
        array, "depth", [(y * 4 + x, (y + by) % 4 * 4 + x) for y in range(4) for x in range(4)]
    )


def shift_z(array, by):
    return lax.ppermute(array, "row", [(z, (z + by) % 4) for z in range(4)])


def gather(array, shift):
    return [array] + [shift(array, by) for by in STEPS[1:]]


def give_back(blocks, shift):
    return [blocks[0]] + [shift(block, -by) for block, by in zip(blocks[1:], STEPS[1:])]


def params(mib):
    return pltpu.CompilerParams(vmem_limit_bytes=mib * 2**20)


def head_norm(values, gain):
    factor = lax.rsqrt(jnp.mean(values * values, axis=1, keepdims=True) + norm_eps)
    return (values * factor * gain).astype(BF)


def map_weights(sides, weight):
    rows, width = sides.shape
    kinds, _, channels = weight.shape
    heads = channels // HEAD_DIM

    def kernel(sides_ref, weight_ref, out_ref):
        mapped = jnp.dot(sides_ref[...], weight_ref[0], preferred_element_type=F32)
        for h in range(heads):
            out_ref[h] = mapped[:, h * HEAD_DIM : (h + 1) * HEAD_DIM]

    return pl.pallas_call(
        kernel,
        grid=(kinds,),
        in_specs=[
            pl.BlockSpec((rows, width), lambda j: (0, 0)),
            pl.BlockSpec((1, width, channels), lambda j: (j, 0, 0)),
        ],
        out_specs=pl.BlockSpec((heads, rows, HEAD_DIM), lambda j: (j, 0, 0)),
        out_shape=jax.ShapeDtypeStruct((kinds * heads, rows, HEAD_DIM), F32),
        compiler_params=params(24),
    )(sides, weight)


def first_projection(noisy, gram, weight, bias, gains):
    rows = noisy.shape[0]
    heads = weight.shape[1] // HEAD_DIM
    normed_heads = gains.shape[0]

    def kernel(noisy_ref, gram_ref, weight_ref, bias_ref, gains_ref, out_ref):
        values = noisy_ref[...].astype(F32)
        spread = jnp.sum(
            jnp.dot(
                values, gram_ref[...], preferred_element_type=F32, precision=lax.Precision.HIGHEST
            )
            * values,
            axis=1,
            keepdims=True,
        )
        scaled = (values * lax.rsqrt(spread + norm_eps)).astype(BF)
        projected = jnp.dot(scaled, weight_ref[...], preferred_element_type=F32) + bias_ref[...]
        for h in range(heads):
            part = projected[:, h * HEAD_DIM : (h + 1) * HEAD_DIM]
            if h < normed_heads:
                out_ref[h] = head_norm(part, gains_ref[h : h + 1])
            else:
                out_ref[h] = part.astype(BF)

    return pl.pallas_call(
        kernel,
        out_shape=jax.ShapeDtypeStruct((heads, rows, HEAD_DIM), BF),
        compiler_params=params(16),
    )(noisy, gram, weight, bias, gains)


ALONG_X = ((1, 0), (1, 2), (0, 1), (2, 0), (2, 2))
ALONG_Y = ((0, 0), (0, 2), (1, 1), (2, 1))
HEADS_BY = ((1, 0), (0, 0), (1, 1))


def attend(queries, blocks, after, carry=None, more=False):
    rows = queries[0].shape[1]
    key_rows = blocks[0][0].shape[1]
    count = len(blocks[0])
    keys_total = key_rows * count
    places = (ALONG_X, ALONG_Y)
    carries = [] if carry is None else [carry]

    def kernel(*refs):
        query_refs = refs[:2]
        block_refs = (refs[2 : 2 + count], refs[2 + count : 2 + 2 * count])
        out_refs = refs[-2:-1] if more else refs[-3:-1]
        wide_ref = refs[-1]
        diagonal = lax.broadcasted_iota(jnp.int32, (HEAD_DIM, HEAD_DIM), 0) == lax.broadcasted_iota(
            jnp.int32, (HEAD_DIM, HEAD_DIM), 1
        )
        for h, (along, out_place) in enumerate(HEADS_BY):
            query = query_refs[along][places[along].index((0, h))]
            key_at = places[1 - along].index((1, h))
            value_at = places[1 - along].index((2, h))
            sums = None if carry is None else refs[2 + 2 * count][h]
            for i, ref in enumerate(block_refs[1 - along]):
                wide_ref[h, i * key_rows : (i + 1) * key_rows, :HEAD_DIM] = ref[value_at]
                wide_ref[h, i * key_rows : (i + 1) * key_rows, HEAD_DIM:] = jnp.ones(
                    (key_rows, HEAD_DIM), BF
                )
            for i, ref in enumerate(block_refs[1 - along]):
                scores = lax.dot_general(
                    query, ref[key_at], (((1,), (1,)), ((), ())), preferred_element_type=F32
                )
                weights = jnp.exp2(scores).astype(BF)
                term = jnp.dot(
                    weights,
                    wide_ref[h, i * key_rows : (i + 1) * key_rows],
                    preferred_element_type=F32,
                )
                sums = term if sums is None else sums + term
            if more:
                out_refs[0][h] = sums
                continue
            out_ref = out_refs[1 - along]
            out_ref[out_place, :rows] = sums[:, :HEAD_DIM].astype(BF)
            lines = []
            for part in range(rows // HEAD_DIM):
                square = sums[part * HEAD_DIM : (part + 1) * HEAD_DIM, HEAD_DIM:]
                lines.append(jnp.sum(jnp.where(diagonal, square, 0.0), axis=0, keepdims=True))
            total = jnp.concatenate(lines, axis=0)
            upper = total.astype(BF)
            lower = (total - upper.astype(F32)).astype(BF)
            out_ref[out_place, rows : rows + 16] = jnp.concatenate(
                [upper.astype(F32), lower.astype(F32), jnp.zeros((8, HEAD_DIM), F32)], axis=0
            ).astype(BF)

    whole = pl.BlockSpec(memory_space=pltpu.VMEM)
    return pl.pallas_call(
        kernel,
        in_specs=[whole] * (2 + 2 * count + len(carries))
        + [pl.BlockSpec(memory_space=pl.ANY)] * len(after),
        out_specs=whole if more else [whole] * 2,
        out_shape=jax.ShapeDtypeStruct((len(HEADS_BY), rows, 2 * HEAD_DIM), F32)
        if more
        else [
            jax.ShapeDtypeStruct((2, rows + 16, HEAD_DIM), BF),
            jax.ShapeDtypeStruct((1, rows + 16, HEAD_DIM), BF),
        ],
        scratch_shapes=[pltpu.VMEM((len(HEADS_BY), keys_total, 2 * HEAD_DIM), BF)],
        compiler_params=params(24),
        cost_estimate=pl.CostEstimate(
            flops=len(HEADS_BY) * rows * keys_total * HEAD_DIM * 8,
            bytes_accessed=8 * 2**20,
            transcendentals=len(HEADS_BY) * rows * keys_total,
        ),
    )(*queries, *blocks[0], *blocks[1], *carries, *after)


def combine(parts_y, parts_x):
    packed = parts_y[0].shape[1]
    rows = packed - 16
    lines = rows // HEAD_DIM
    count = len(parts_y)
    heads = len(HEADS_BY)

    def kernel(*refs):
        out_ref = refs[-1]
        diagonal = lax.broadcasted_iota(jnp.int32, (HEAD_DIM, HEAD_DIM), 0) == lax.broadcasted_iota(
            jnp.int32, (HEAD_DIM, HEAD_DIM), 1
        )
        for h, (along, at) in enumerate(HEADS_BY):
            sources = refs[:count] if along == 1 else refs[count : 2 * count]
            tail = sources[0][at, rows : rows + 16].astype(F32)
            for ref in sources[1:]:
                tail = tail + ref[at, rows : rows + 16].astype(F32)
            for part in range(lines):
                place = slice(part * HEAD_DIM, (part + 1) * HEAD_DIM)
                numerator = sources[0][at, place].astype(F32)
                for ref in sources[1:]:
                    numerator = numerator + ref[at, place].astype(F32)
                total = tail[part : part + 1] + tail[lines + part : lines + part + 1]
                column = jnp.sum(jnp.where(diagonal, 1.0 / total, 0.0), axis=1, keepdims=True)
                out_ref[place, h * HEAD_DIM : (h + 1) * HEAD_DIM] = (numerator * column).astype(BF)

    return pl.pallas_call(
        kernel,
        out_shape=jax.ShapeDtypeStruct((rows, heads * HEAD_DIM), BF),
        compiler_params=params(16),
    )(*parts_y, *parts_x)


def attention(xs, ys, near_first):
    parts_y, parts_x = [None] * 4, [None] * 4
    after, carries, early = [], [None] * 4, None
    if near_first:
        for k in (2, 1, 0):
            carries[k] = attend((xs[k], ys[k]), (xs[:3], ys[:3]), after, more=True)
            after = [carries[k]]
            early = after[0] if early is None else early
    for k in (3, 2, 1, 0):
        blocks = (xs, ys) if carries[k] is None else (xs[3:], ys[3:])
        if k == 0:
            after = after + [parts_y[3], parts_x[3]]
        sums_y, sums_x = attend((xs[k], ys[k]), blocks, after, carries[k])
        after = [sums_x]
        early = after[0] if early is None else early
        by = STEPS[k]
        parts_y[k] = shift_y(sums_y, -by) if by else sums_y
        parts_x[k] = shift_x(sums_x, -by) if by else sums_x
    return combine(parts_y, parts_x), early


def weight_copies(weight_refs, held_ref, sems):
    copies = []
    for i, ref in enumerate(weight_refs):
        part, half = ref.shape
        column, k = divmod(i, 4)
        place = held_ref.at[k * part : (k + 1) * part, column * half : (column + 1) * half]
        copies.append(pltpu.make_async_copy(ref, place, sems.at[i]))
    return copies


def between_layers(blocks, weights, noisy, embed, gate, scale, shift, next_weight, query_gain, key_gain):
    rows, part = blocks[0].shape
    width = gate.shape[1]
    depth = 4 * part
    half = width // 2
    block = 512
    local = rows // 4
    kinds, _, channels = next_weight.shape
    heads = channels // HEAD_DIM

    def kernel(*refs):
        block_refs = refs[:4]
        weight_refs = refs[4:12]
        noisy_ref, embed_ref, gate_ref, scale_ref, shift_ref, next_ref, qg_ref, kg_ref = refs[12:20]
        x_ref, y_ref, own_ref = refs[20:23]
        held_ref, next_held_ref, side_ref, tokens_ref, sems = refs[23:]
        copies = weight_copies(weight_refs, held_ref, sems)
        copies += [
            pltpu.make_async_copy(next_ref.at[j], next_held_ref.at[j], sems.at[8 + j])
            for j in range(kinds)
        ]
        for copy in copies:
            copy.start()
        for k in range(4):
            side_ref[:, k * part : (k + 1) * part] = block_refs[k][...]
        for column in range(2):
            for copy in copies[4 * column : 4 * column + 4]:
                copy.wait()

            @pl.loop(0, half // block)
            def _(n):
                place = pl.ds(pl.multiple_of(column * half + n * block, block), block)
                update = jnp.dot(side_ref[...], held_ref[:, place], preferred_element_type=F32)
                base = jnp.dot(noisy_ref[...], embed_ref[:, place], preferred_element_type=F32)
                tokens_ref[:, place] = (
                    base.astype(BF).astype(F32) + gate_ref[:, place] * update
                ).astype(BF)

        own_ref[...] = tokens_ref[:local]

        @pl.loop(0, rows // 128)
        def _(n):
            place = pl.ds(pl.multiple_of(n * 128, 128), 128)
            values = tokens_ref[place].astype(F32)
            values = values - jnp.mean(values, axis=1, keepdims=True)
            spread = jnp.mean(values * values, axis=1, keepdims=True)
            tokens_ref[place] = (
                values * lax.rsqrt(spread + norm_eps) * (1.0 + scale_ref[...]) + shift_ref[...]
            ).astype(BF)

        for kind in range(kinds):
            copies[8 + kind].wait()
            projected = jnp.dot(tokens_ref[...], next_held_ref[kind], preferred_element_type=F32)
            for h in range(heads):
                piece = projected[:, h * HEAD_DIM : (h + 1) * HEAD_DIM]
                if kind < 2:
                    piece = head_norm(piece, (qg_ref, kg_ref)[kind][...])
                else:
                    piece = piece.astype(BF)
                if (kind, h) in ALONG_X:
                    x_ref[ALONG_X.index((kind, h))] = piece
                else:
                    y_ref[ALONG_Y.index((kind, h))] = piece

    whole = pl.BlockSpec(memory_space=pltpu.VMEM)
    left = pl.BlockSpec(memory_space=pl.ANY)
    return pl.pallas_call(
        kernel,
        in_specs=[whole] * 4 + [left] * 8 + [whole] * 5 + [left] + [whole] * 2,
        out_specs=[whole] * 3,
        out_shape=[
            jax.ShapeDtypeStruct((len(ALONG_X), rows, HEAD_DIM), BF),
            jax.ShapeDtypeStruct((len(ALONG_Y), rows, HEAD_DIM), BF),
            jax.ShapeDtypeStruct((local, width), BF),
        ],
        scratch_shapes=[
            pltpu.VMEM((depth, width), BF),
            pltpu.VMEM(next_weight.shape, BF),
            pltpu.VMEM((rows, depth), BF),
            pltpu.VMEM((rows, width), BF),
            pltpu.SemaphoreType.DMA((8 + kinds,)),
        ],
        compiler_params=params(40),
        cost_estimate=pl.CostEstimate(
            flops=2 * rows * width * (depth + kinds * channels),
            bytes_accessed=20 * 2**20,
            transcendentals=0,
        ),
    )(*blocks, *weights, noisy, embed, gate, scale, shift, next_weight, query_gain, key_gain)


def last_step(heads, weights, bases, gates):
    rows, depth = heads[0].shape
    width = gates.shape[1]
    half = width // 2
    block = 512

    def kernel(first_ref, second_ref, *refs):
        weight_refs = refs[:8]
        first_base_ref, second_base_ref, gates_ref, out_ref, held_ref, side_ref, sems = refs[8:]
        copies = weight_copies(weight_refs, held_ref, sems)
        for copy in copies:
            copy.start()
        side_ref[:rows] = first_ref[...]
        side_ref[rows:] = second_ref[...]
        for column in range(2):
            for copy in copies[4 * column : 4 * column + 4]:
                copy.wait()

            @pl.loop(0, half // block)
            def _(n):
                place = pl.ds(pl.multiple_of(column * half + n * block, block), block)
                update = jnp.dot(side_ref[...], held_ref[:, place], preferred_element_type=F32)
                for m, base_ref in enumerate((first_base_ref, second_base_ref)):
                    out_ref[m, :, place] = (
                        base_ref[:, place].astype(F32)
                        + gates_ref[m : m + 1, place] * update[m * rows : (m + 1) * rows]
                    ).astype(BF)

    whole = pl.BlockSpec(memory_space=pltpu.VMEM)
    return pl.pallas_call(
        kernel,
        in_specs=[whole] * 2 + [pl.BlockSpec(memory_space=pl.ANY)] * 8 + [whole] * 3,
        out_specs=whole,
        out_shape=jax.ShapeDtypeStruct((2, rows, width), BF),
        scratch_shapes=[
            pltpu.VMEM((depth, width), BF),
            pltpu.VMEM((2 * rows, depth), BF),
            pltpu.SemaphoreType.DMA((8,)),
        ],
        compiler_params=params(24),
    )(*heads, *weights, *bases, gates)


def per_device(
    latent,
    noise_field,
    timestep,
    embed_weight,
    modulate_weight,
    attend_weight,
    query_gain,
    key_gain,
    output_weight,
):
    batches = latent.shape[0]
    patch, width = embed_weight.shape
    local = latent.shape[1] * latent.shape[2] * latent.shape[3]
    section = lax.axis_index("section")
    row = lax.axis_index("row")
    first = section == 0
    half = width // 2

    def by_section(of_first, of_second):
        return jnp.where(first, of_first, of_second)

    def swapped(array):
        return lax.ppermute(array, "section", SWAP)

    level = signal_level(timestep)[:, None, None, None, None]
    noisy = (
        jnp.sqrt(level) * latent.astype(F32) + jnp.sqrt(1.0 - level) * noise_field.astype(F32)
    ).astype(BF)
    noisy = by_section(noisy[0], noisy[1]).reshape(local, patch)
    features = time_features(timestep, modulate_weight.shape[1]).astype(BF)
    mod_part = jnp.dot(features, modulate_weight[0], preferred_element_type=F32)

    mod_rows = mod_part.size // patch
    packed = jnp.concatenate(
        [noisy.astype(F32), mod_part.reshape(mod_rows, patch), jnp.zeros((-mod_rows % 8, patch), F32)]
    )
    packed = gather(packed, shift_z)
    noisy_row = jnp.concatenate([block[:local] for block in packed]).astype(BF)
    mods = [block[local : local + mod_rows].reshape(batches, -1) for block in packed]

    def from_row(b):
        chosen = mods[0]
        for k in (1, 2, 3):
            chosen = jnp.where(row == (b + STEPS[k]) % 4, mods[k], chosen)
        return chosen

    modulation = jnp.concatenate([from_row(b) for b in range(4)], axis=1)
    shift_own = modulation[:, :width]
    scale_own = modulation[:, width : 2 * width]

    noisy_x = gather(noisy_row, shift_x)
    noisy_y = gather(noisy_row, shift_y)

    centered = embed_weight.astype(F32)
    centered = centered - jnp.mean(centered, axis=1, keepdims=True)
    gram = (
        jnp.dot(centered, centered.T, preferred_element_type=F32, precision=lax.Precision.HIGHEST)
        / width
    )
    sides = jnp.concatenate(
        [centered[None] * (1.0 + scale_own[:, None, :]), shift_own[:, None, :]], axis=1
    )
    sides = jnp.concatenate([sides, jnp.zeros((batches, 15, width), F32)], axis=1)
    sides = sides.astype(BF).reshape(-1, width)
    mapped = map_weights(sides, attend_weight[0])
    kinds = mapped.shape[0]
    mapped = mapped.reshape(kinds, batches, patch + 16, HEAD_DIM)
    bias = mapped[:, :, patch : patch + 1]
    upper = bias.astype(BF)
    lower = (bias - upper.astype(F32)).astype(BF)
    mapped = jnp.concatenate(
        [mapped[:, :, :patch].astype(BF), upper, lower, jnp.zeros((kinds, batches, 14, HEAD_DIM), BF)],
        axis=2,
    )
    mapped_other = lax.ppermute(mapped[:, 1], "section", [(0, 1)])
    mapped = by_section(mapped[:, 0], mapped_other)
    bias = mapped[:, patch : patch + 1].astype(F32) + mapped[:, patch + 1 : patch + 2].astype(F32)
    mapped = mapped[:, :patch]

    gains = jnp.concatenate([query_gain, key_gain])
    small = jnp.concatenate([modulation.reshape(-1, patch), gains, jnp.zeros((6, patch), F32)])
    small_other = swapped(small)
    small_first = by_section(small, small_other)
    small_second = by_section(small_other, small)
    mod_rows_all = modulation.size // patch

    def unpack(array):
        mod = array[:mod_rows_all].reshape(batches, -1)
        mod = by_section(mod[:1], mod[1:])
        qg = array[mod_rows_all : mod_rows_all + 1] * QUERY_SCALE
        kg = array[mod_rows_all + 1 : mod_rows_all + 2]
        return mod[:, :width], mod[:, width : 2 * width], mod[:, 2 * width :], qg, kg

    _, _, gate_first, qg_first, kg_first = unpack(small_first)
    shift_second, scale_second, _, qg_second, kg_second = unpack(small_second)

    keep = lax.dynamic_slice_in_dim(output_weight[0], section * half, half, 1)
    give = lax.dynamic_slice_in_dim(output_weight[0], (1 - section) * half, half, 1)
    got = swapped(give)
    keep, got, packed[3] = lax.optimization_barrier((keep, got, packed[3]))
    out_first = [by_section(keep, got)]
    out_first += [shift_z(out_first[0], by) for by in STEPS[1:3]]
    given, noisy_x[3] = lax.optimization_barrier((out_first[0], noisy_x[3]))
    out_first.append(shift_z(given, STEPS[3]))

    heads = kinds // 3
    gain_of = (qg_first, kg_first)

    def first_heads(blocks, along):
        weight = jnp.concatenate([mapped[kind * heads + h] for kind, h in along], axis=1)
        bias_row = jnp.concatenate([bias[kind * heads + h] for kind, h in along], axis=1)
        gains_here = jnp.concatenate([gain_of[kind] for kind, h in along if kind < 2])
        return [first_projection(block, gram, weight, bias_row, gains_here) for block in blocks]

    attended, early = attention(first_heads(noisy_x, ALONG_X), first_heads(noisy_y, ALONG_Y), False)
    attend_given, early = lax.optimization_barrier((attend_weight[0], early))
    attend_other = lax.ppermute(attend_given, "section", [(1, 0)])
    out_first_other = [swapped(block) for block in out_first]

    blocks = gather(attended, shift_z)
    turned = []
    for block, by in zip(blocks, STEPS):
        order = [
            [k for k in range(4) if (by + STEPS[k] - STEPS[mine]) % 4 == 0][0] for mine in range(4)
        ]
        turned.append(jnp.concatenate([block[k * local : (k + 1) * local] for k in order]))
    keep, got, blocks[3] = lax.optimization_barrier((keep, got, blocks[3]))
    out_second = [by_section(got, keep)]
    out_second += [shift_z(out_second[0], by) for by in STEPS[1:3]]

    def step_first(weights, next_weight):
        return between_layers(
            turned,
            weights,
            noisy_row,
            embed_weight,
            gate_first,
            scale_second,
            shift_second,
            next_weight,
            qg_second,
            kg_second,
        )

    along_x, along_y, result_first = lax.cond(
        first,
        lambda own, other, next_own, next_other: step_first(own + other, next_other),
        lambda own, other, next_own, next_other: step_first(other + own, next_own),
        out_first,
        out_first_other,
        attend_weight[0],
        attend_other,
    )
    given, along_x = lax.optimization_barrier((out_second[0], along_x))
    out_second.append(shift_z(given, STEPS[3]))
    result_other = swapped(result_first)

    attended, early = attention(gather(along_x, shift_x), gather(along_y, shift_y), True)
    out_second, early = lax.optimization_barrier((out_second, early))
    out_second_other = [swapped(block) for block in out_second]
    mine = give_back([attended[k * local : (k + 1) * local] for k in range(4)], shift_z)
    mine = jnp.concatenate([mine[STEPS.index(by if by == 2 else -by)] for by in STEPS], axis=1)
    mine_other = lax.ppermute(mine, "section", [(0, 1)])
    gates = modulation[:, 2 * width :]

    def finish_first():
        return jnp.stack([result_first, result_other])

    def finish_second():
        return last_step(
            (mine_other, mine), out_second_other + out_second, (result_other, result_first), gates
        )

    result = lax.cond(first, finish_first, finish_second)
    return result.reshape(1, batches, latent.shape[1], latent.shape[2], latent.shape[3], width)


def solution(mesh):
    return jax.shard_map(
        per_device,
        mesh=mesh,
        in_specs=(
            P(None, "depth", "row", None, None),
            P(None, "depth", "row", None, None),
            P(),
            P(),
            P("section", None, "row"),
            P("section", None, None, "row"),
            P("section", None),
            P("section", None),
            P("section", "row", None),
        ),
        out_specs=P("section", None, "depth", "row", None, None),
        check_vma=False,
    )
```

```python
import math

import jax
import jax.numpy as jnp
from jax import lax
from jax.experimental import pallas as pl
from jax.experimental.pallas import tpu as pltpu
from jax.sharding import PartitionSpec as P

HEAD_DIM = 128
BF = jnp.bfloat16
F32 = jnp.float32

norm_eps = 1e-06
plan_steps = 1000.0
QUERY_SCALE = math.log2(math.e) / math.sqrt(HEAD_DIM)
SWAP = [(0, 1), (1, 0)]
STEPS = (0, 1, -1, 2)


def signal_level(timestep):
    phase = (timestep.astype(F32) / plan_steps + 0.008) / 1.008 * (math.pi / 2)
    return jnp.cos(phase) ** 2


def time_features(timestep, count):
    half = count // 2
    frequency = jnp.exp(-math.log(10000.0) * jnp.arange(half, dtype=F32) / half)
    angles = timestep.astype(F32)[:, None] * frequency[None, :]
    return jnp.concatenate([jnp.cos(angles), jnp.sin(angles)], axis=1)


def shift_x(array, by):
    return lax.ppermute(
        array, "depth", [(y * 4 + x, y * 4 + (x + by) % 4) for y in range(4) for x in range(4)]
    )


def shift_y(array, by):
    return lax.ppermute(
        array, "depth", [(y * 4 + x, (y + by) % 4 * 4 + x) for y in range(4) for x in range(4)]
    )


def shift_z(array, by):
    return lax.ppermute(array, "row", [(z, (z + by) % 4) for z in range(4)])


def shift_z_in(section, array, by):
    return lax.ppermute(
        array, ("section", "row"), [(section * 4 + z, section * 4 + (z + by) % 4) for z in range(4)]
    )


def gather(array, shift):
    return [array] + [shift(array, by) for by in STEPS[1:]]


def give_back(blocks, shift):
    return [blocks[0]] + [shift(block, -by) for block, by in zip(blocks[1:], STEPS[1:])]


def params(mib):
    return pltpu.CompilerParams(vmem_limit_bytes=mib * 2**20)


def head_norm(values, gain):
    factor = lax.rsqrt(jnp.mean(values * values, axis=1, keepdims=True) + norm_eps)
    return (values * factor * gain).astype(BF)


def map_weights(embed, scale, shift, weight):
    patch, width = embed.shape
    batches = scale.shape[0]
    kinds, _, channels = weight.shape
    heads = channels // HEAD_DIM

    def kernel(embed_ref, scale_ref, shift_ref, weight_ref, out_ref, sides_ref):
        @pl.when(pl.program_id(0) == 0)
        def _():
            values = embed_ref[...].astype(F32)
            values = values - jnp.mean(values, axis=1, keepdims=True)
            for m in range(batches):
                sides_ref[m * patch : (m + 1) * patch] = (
                    values * (1.0 + scale_ref[m : m + 1])
                ).astype(BF)
            sides_ref[batches * patch :] = jnp.concatenate(
                [shift_ref[...], jnp.zeros((16 - batches, width), F32)]
            ).astype(BF)

        mapped = jnp.dot(sides_ref[...], weight_ref[0], preferred_element_type=F32)
        for m in range(batches):
            bias = mapped[batches * patch + m : batches * patch + m + 1]
            upper = bias.astype(BF).astype(F32)
            tail = jnp.concatenate([upper, bias - upper, jnp.zeros((14, channels), F32)]).astype(BF)
            for h in range(heads):
                part = slice(h * HEAD_DIM, (h + 1) * HEAD_DIM)
                out_ref[m, h, :patch] = mapped[m * patch : (m + 1) * patch, part].astype(BF)
                out_ref[m, h, patch:] = tail[:, part]

    return pl.pallas_call(
        kernel,
        grid=(kinds,),
        in_specs=[
            pl.BlockSpec((patch, width), lambda j: (0, 0)),
            pl.BlockSpec((batches, width), lambda j: (0, 0)),
            pl.BlockSpec((batches, width), lambda j: (0, 0)),
            pl.BlockSpec((1, width, channels), lambda j: (j, 0, 0)),
        ],
        out_specs=pl.BlockSpec((batches, heads, patch + 16, HEAD_DIM), lambda j: (0, j, 0, 0)),
        out_shape=jax.ShapeDtypeStruct((batches, kinds * heads, patch + 16, HEAD_DIM), BF),
        scratch_shapes=[pltpu.VMEM((batches * patch + 16, width), BF)],
        compiler_params=params(24),
        cost_estimate=pl.CostEstimate(flops=10**6, bytes_accessed=10**4, transcendentals=0),
    )(embed, scale, shift, weight)


def first_projection(noisy, gram, weight, bias, gains):
    rows = noisy.shape[0]
    heads = weight.shape[1] // HEAD_DIM
    normed_heads = gains.shape[0]

    def kernel(noisy_ref, gram_ref, weight_ref, bias_ref, gains_ref, out_ref):
        values = noisy_ref[...].astype(F32)
        spread = jnp.sum(
            jnp.dot(
                values, gram_ref[...], preferred_element_type=F32, precision=lax.Precision.HIGHEST
            )
            * values,
            axis=1,
            keepdims=True,
        )
        scaled = (values * lax.rsqrt(spread + norm_eps)).astype(BF)
        projected = jnp.dot(scaled, weight_ref[...], preferred_element_type=F32) + bias_ref[...]
        for h in range(heads):
            part = projected[:, h * HEAD_DIM : (h + 1) * HEAD_DIM]
            if h < normed_heads:
                out_ref[h] = head_norm(part, gains_ref[h : h + 1])
            else:
                out_ref[h] = part.astype(BF)

    return pl.pallas_call(
        kernel,
        out_shape=jax.ShapeDtypeStruct((heads, rows, HEAD_DIM), BF),
        compiler_params=params(16),
        cost_estimate=pl.CostEstimate(flops=10**6, bytes_accessed=10**4, transcendentals=0),
    )(noisy, gram, weight, bias, gains)


ALONG_X = ((1, 0), (1, 2), (0, 1), (2, 0), (2, 2))
ALONG_Y = ((0, 0), (0, 2), (1, 1), (2, 1))
HEADS_BY = ((1, 0), (0, 0), (1, 1))


def attend(queries, blocks, after, carry=None, more=False):
    rows = queries[0].shape[1]
    key_rows = blocks[0][0].shape[1]
    count = len(blocks[0])
    keys_total = key_rows * count
    places = (ALONG_X, ALONG_Y)
    carries = [] if carry is None else [carry]

    def kernel(*refs):
        query_refs = refs[:2]
        block_refs = (refs[2 : 2 + count], refs[2 + count : 2 + 2 * count])
        out_refs = refs[-2:-1] if more else refs[-3:-1]
        wide_ref = refs[-1]
        diagonal = lax.broadcasted_iota(jnp.int32, (HEAD_DIM, HEAD_DIM), 0) == lax.broadcasted_iota(
            jnp.int32, (HEAD_DIM, HEAD_DIM), 1
        )
        for h, (along, out_place) in enumerate(HEADS_BY):
            query = query_refs[along][places[along].index((0, h))]
            key_at = places[1 - along].index((1, h))
            value_at = places[1 - along].index((2, h))
            sums = None if carry is None else refs[2 + 2 * count][h]
            for i, ref in enumerate(block_refs[1 - along]):
                wide_ref[h, i * key_rows : (i + 1) * key_rows, :HEAD_DIM] = ref[value_at]
                wide_ref[h, i * key_rows : (i + 1) * key_rows, HEAD_DIM:] = jnp.ones(
                    (key_rows, HEAD_DIM), BF
                )
            for i, ref in enumerate(block_refs[1 - along]):
                scores = lax.dot_general(
                    query, ref[key_at], (((1,), (1,)), ((), ())), preferred_element_type=F32
                )
                weights = jnp.exp2(scores).astype(BF)
                term = jnp.dot(
                    weights,
                    wide_ref[h, i * key_rows : (i + 1) * key_rows],
                    preferred_element_type=F32,
                )
                sums = term if sums is None else sums + term
            if more:
                out_refs[0][h] = sums
                continue
            out_ref = out_refs[1 - along]
            out_ref[out_place, :rows] = sums[:, :HEAD_DIM].astype(BF)
            lines = []
            for part in range(rows // HEAD_DIM):
                square = sums[part * HEAD_DIM : (part + 1) * HEAD_DIM, HEAD_DIM:]
                lines.append(jnp.sum(jnp.where(diagonal, square, 0.0), axis=0, keepdims=True))
            total = jnp.concatenate(lines, axis=0)
            upper = total.astype(BF)
            lower = (total - upper.astype(F32)).astype(BF)
            out_ref[out_place, rows : rows + 16] = jnp.concatenate(
                [upper.astype(F32), lower.astype(F32), jnp.zeros((8, HEAD_DIM), F32)], axis=0
            ).astype(BF)

    whole = pl.BlockSpec(memory_space=pltpu.VMEM)
    return pl.pallas_call(
        kernel,
        in_specs=[whole] * (2 + 2 * count + len(carries))
        + [pl.BlockSpec(memory_space=pl.ANY)] * len(after),
        out_specs=whole if more else [whole] * 2,
        out_shape=jax.ShapeDtypeStruct((len(HEADS_BY), rows, 2 * HEAD_DIM), F32)
        if more
        else [
            jax.ShapeDtypeStruct((2, rows + 16, HEAD_DIM), BF),
            jax.ShapeDtypeStruct((1, rows + 16, HEAD_DIM), BF),
        ],
        scratch_shapes=[pltpu.VMEM((len(HEADS_BY), keys_total, 2 * HEAD_DIM), BF)],
        compiler_params=params(24),
        cost_estimate=pl.CostEstimate(
            flops=len(HEADS_BY) * rows * keys_total * HEAD_DIM * 8,
            bytes_accessed=8 * 2**20,
            transcendentals=len(HEADS_BY) * rows * keys_total,
        ),
    )(*queries, *blocks[0], *blocks[1], *carries, *after)


def combine(parts_y, parts_x):
    packed = parts_y[0].shape[1]
    rows = packed - 16
    lines = rows // HEAD_DIM
    count = len(parts_y)
    heads = len(HEADS_BY)

    def kernel(*refs):
        out_ref = refs[-1]
        diagonal = lax.broadcasted_iota(jnp.int32, (HEAD_DIM, HEAD_DIM), 0) == lax.broadcasted_iota(
            jnp.int32, (HEAD_DIM, HEAD_DIM), 1
        )
        for h, (along, at) in enumerate(HEADS_BY):
            sources = refs[:count] if along == 1 else refs[count : 2 * count]
            tail = sources[0][at, rows : rows + 16].astype(F32)
            for ref in sources[1:]:
                tail = tail + ref[at, rows : rows + 16].astype(F32)
            for part in range(lines):
                place = slice(part * HEAD_DIM, (part + 1) * HEAD_DIM)
                numerator = sources[0][at, place].astype(F32)
                for ref in sources[1:]:
                    numerator = numerator + ref[at, place].astype(F32)
                total = tail[part : part + 1] + tail[lines + part : lines + part + 1]
                column = jnp.sum(jnp.where(diagonal, 1.0 / total, 0.0), axis=1, keepdims=True)
                out_ref[place, h * HEAD_DIM : (h + 1) * HEAD_DIM] = (numerator * column).astype(BF)

    return pl.pallas_call(
        kernel,
        out_shape=jax.ShapeDtypeStruct((rows, heads * HEAD_DIM), BF),
        compiler_params=params(16),
    )(*parts_y, *parts_x)


def attention(xs, ys, near_first, before):
    parts_y, parts_x = [None] * 4, [None] * 4
    after, carries, first_sums, step = [], [None] * 4, None, 0
    if near_first:
        for k in (2, 1, 0):
            carries[k] = attend(
                (xs[k], ys[k]), (xs[:3], ys[:3]), after + before(step, first_sums), more=True
            )
            after = [carries[k]]
            first_sums = after[0] if first_sums is None else first_sums
            step += 1
    for k in (3, 2, 1, 0):
        blocks = (xs, ys) if carries[k] is None else (xs[3:], ys[3:])
        if k == 0:
            after = after + [parts_y[3], parts_x[3]]
        sums_y, sums_x = attend(
            (xs[k], ys[k]), blocks, after + before(step, first_sums), carries[k]
        )
        after = [sums_x]
        first_sums = after[0] if first_sums is None else first_sums
        step += 1
        by = STEPS[k]
        parts_y[k] = shift_y(sums_y, -by) if by else sums_y
        parts_x[k] = shift_x(sums_x, -by) if by else sums_x
    return combine(parts_y, parts_x)


def held_until(array, other):
    return lax.optimization_barrier((array, other))[0]


def weight_copies(weight_refs, held_ref, sems):
    part = weight_refs[0].shape[0]
    return [
        pltpu.make_async_copy(ref, held_ref.at[k * part : (k + 1) * part], sems.at[k])
        for k, ref in enumerate(weight_refs)
    ]


def between_layers(blocks, weights, noisy, embed, gate, scale, shift, next_weight, query_gain, key_gain):
    rows, part = blocks[0].shape
    width = gate.shape[1]
    depth = 4 * part
    block = 512
    local = rows // 4
    kinds, _, channels = next_weight.shape
    heads = channels // HEAD_DIM

    def kernel(*refs):
        block_refs = refs[:4]
        weight_refs = refs[4:8]
        noisy_ref, embed_ref, gate_ref, scale_ref, shift_ref, next_ref, qg_ref, kg_ref = refs[8:16]
        x_ref, y_ref, own_ref = refs[16:19]
        held_ref, next_held_ref, side_ref, tokens_ref, sems = refs[19:]
        copies = weight_copies(weight_refs, held_ref, sems)
        copies += [
            pltpu.make_async_copy(next_ref.at[j], next_held_ref.at[j], sems.at[4 + j])
            for j in range(kinds)
        ]
        for copy in copies:
            copy.start()
        for k in range(4):
            side_ref[:, k * part : (k + 1) * part] = block_refs[k][...]
        for copy in copies[:4]:
            copy.wait()

        @pl.loop(0, width // block)
        def _(n):
            place = pl.ds(pl.multiple_of(n * block, block), block)
            update = jnp.dot(side_ref[...], held_ref[:, place], preferred_element_type=F32)
            base = jnp.dot(noisy_ref[...], embed_ref[:, place], preferred_element_type=F32)
            tokens_ref[:, place] = (
                base.astype(BF).astype(F32) + gate_ref[:, place] * update
            ).astype(BF)

        own_ref[...] = tokens_ref[:local]

        @pl.loop(0, rows // 128)
        def _(n):
            place = pl.ds(pl.multiple_of(n * 128, 128), 128)
            values = tokens_ref[place].astype(F32)
            values = values - jnp.mean(values, axis=1, keepdims=True)
            spread = jnp.mean(values * values, axis=1, keepdims=True)
            tokens_ref[place] = (
                values * lax.rsqrt(spread + norm_eps) * (1.0 + scale_ref[...]) + shift_ref[...]
            ).astype(BF)

        for kind in range(kinds):
            copies[4 + kind].wait()
            projected = jnp.dot(tokens_ref[...], next_held_ref[kind], preferred_element_type=F32)
            for h in range(heads):
                piece = projected[:, h * HEAD_DIM : (h + 1) * HEAD_DIM]
                if kind < 2:
                    piece = head_norm(piece, (qg_ref, kg_ref)[kind][...])
                else:
                    piece = piece.astype(BF)
                if (kind, h) in ALONG_X:
                    x_ref[ALONG_X.index((kind, h))] = piece
                else:
                    y_ref[ALONG_Y.index((kind, h))] = piece

    whole = pl.BlockSpec(memory_space=pltpu.VMEM)
    left = pl.BlockSpec(memory_space=pl.ANY)
    return pl.pallas_call(
        kernel,
        in_specs=[whole] * 4 + [left] * 4 + [whole] * 5 + [left] + [whole] * 2,
        out_specs=[whole] * 3,
        out_shape=[
            jax.ShapeDtypeStruct((len(ALONG_X), rows, HEAD_DIM), BF),
            jax.ShapeDtypeStruct((len(ALONG_Y), rows, HEAD_DIM), BF),
            jax.ShapeDtypeStruct((local, width), BF),
        ],
        scratch_shapes=[
            pltpu.VMEM((depth, width), BF),
            pltpu.VMEM(next_weight.shape, BF),
            pltpu.VMEM((rows, depth), BF),
            pltpu.VMEM((rows, width), BF),
            pltpu.SemaphoreType.DMA((4 + kinds,)),
        ],
        compiler_params=params(40),
        cost_estimate=pl.CostEstimate(
            flops=2 * rows * width * (depth + kinds * channels),
            bytes_accessed=20 * 2**20,
            transcendentals=0,
        ),
    )(*blocks, *weights, noisy, embed, gate, scale, shift, next_weight, query_gain, key_gain)


def last_step(heads, weights, bases, gates):
    rows, depth = heads[0].shape
    width = gates.shape[1]
    block = 512

    def kernel(first_ref, second_ref, *refs):
        weight_refs = refs[:4]
        first_base_ref, second_base_ref, gates_ref, out_ref, held_ref, side_ref, sems = refs[4:]
        copies = weight_copies(weight_refs, held_ref, sems)
        for copy in copies:
            copy.start()
        side_ref[:rows] = first_ref[...]
        side_ref[rows:] = second_ref[...]
        for copy in copies:
            copy.wait()

        @pl.loop(0, width // block)
        def _(n):
            place = pl.ds(pl.multiple_of(n * block, block), block)
            update = jnp.dot(side_ref[...], held_ref[:, place], preferred_element_type=F32)
            for m, base_ref in enumerate((first_base_ref, second_base_ref)):
                out_ref[m, :, place] = (
                    base_ref[:, place].astype(F32)
                    + gates_ref[m : m + 1, place] * update[m * rows : (m + 1) * rows]
                ).astype(BF)

    whole = pl.BlockSpec(memory_space=pltpu.VMEM)
    return pl.pallas_call(
        kernel,
        in_specs=[whole] * 2 + [pl.BlockSpec(memory_space=pl.ANY)] * 4 + [whole] * 3,
        out_specs=whole,
        out_shape=jax.ShapeDtypeStruct((2, rows, width), BF),
        scratch_shapes=[
            pltpu.VMEM((depth, width), BF),
            pltpu.VMEM((2 * rows, depth), BF),
            pltpu.SemaphoreType.DMA((4,)),
        ],
        compiler_params=params(24),
    )(*heads, *weights, *bases, gates)


def per_device(
    latent,
    noise_field,
    timestep,
    embed_weight,
    modulate_weight,
    attend_weight,
    query_gain,
    key_gain,
    output_weight,
):
    batches = latent.shape[0]
    patch, width = embed_weight.shape
    local = latent.shape[1] * latent.shape[2] * latent.shape[3]
    section = lax.axis_index("section")
    row = lax.axis_index("row")
    first = section == 0

    def by_section(of_first, of_second):
        return jnp.where(first, of_first, of_second)

    def swapped(array):
        return lax.ppermute(array, "section", SWAP)

    level = signal_level(timestep)[:, None, None, None, None]
    noisy = (
        jnp.sqrt(level) * latent.astype(F32) + jnp.sqrt(1.0 - level) * noise_field.astype(F32)
    ).astype(BF)
    noisy = by_section(noisy[0], noisy[1]).reshape(local, patch)
    features = time_features(timestep, modulate_weight.shape[1]).astype(BF)
    mod_part = jnp.dot(features, modulate_weight[0], preferred_element_type=F32)

    mod_rows = mod_part.size // patch
    packed = jnp.concatenate(
        [noisy.astype(F32), mod_part.reshape(mod_rows, patch), jnp.zeros((-mod_rows % 8, patch), F32)]
    )
    packed = gather(packed, shift_z)
    noisy_row = jnp.concatenate([block[:local] for block in packed]).astype(BF)
    mods = [block[local : local + mod_rows].reshape(batches, -1) for block in packed]

    def from_row(b):
        chosen = mods[0]
        for k in (1, 2, 3):
            chosen = jnp.where(row == (b + STEPS[k]) % 4, mods[k], chosen)
        return chosen

    modulation = jnp.concatenate([from_row(b) for b in range(4)], axis=1)
    shift_own = modulation[:, :width]
    scale_own = modulation[:, width : 2 * width]

    noisy_x = gather(noisy_row, shift_x)
    noisy_y = gather(noisy_row, shift_y)

    centered = embed_weight.astype(F32)
    centered = centered - jnp.mean(centered, axis=1, keepdims=True)
    gram = (
        jnp.dot(centered, centered.T, preferred_element_type=F32, precision=lax.Precision.HIGHEST)
        / width
    )
    mapped = map_weights(embed_weight, scale_own, shift_own, attend_weight[0])
    kinds = mapped.shape[1]
    mapped_other = lax.ppermute(mapped[1], "section", [(0, 1)])
    mapped = by_section(mapped[0], mapped_other)
    bias = mapped[:, patch : patch + 1].astype(F32) + mapped[:, patch + 1 : patch + 2].astype(F32)
    mapped = mapped[:, :patch]

    gains = jnp.concatenate([query_gain, key_gain])
    small = jnp.concatenate([modulation.reshape(-1, patch), gains, jnp.zeros((6, patch), F32)])
    small_other = swapped(small)
    small_first = by_section(small, small_other)
    small_second = by_section(small_other, small)
    mod_rows_all = modulation.size // patch

    def unpack(array):
        mod = array[:mod_rows_all].reshape(batches, -1)
        mod = by_section(mod[:1], mod[1:])
        qg = array[mod_rows_all : mod_rows_all + 1] * QUERY_SCALE
        kg = array[mod_rows_all + 1 : mod_rows_all + 2]
        return mod[:, :width], mod[:, width : 2 * width], mod[:, 2 * width :], qg, kg

    _, _, gate_first, qg_first, kg_first = unpack(small_first)
    shift_second, scale_second, _, qg_second, kg_second = unpack(small_second)

    out_weight = output_weight[0]
    out_start = held_until(out_weight, packed[3])
    out_first = [out_weight] + [shift_z_in(0, out_start, by) for by in STEPS[1:3]]
    out_first.append(shift_z_in(0, held_until(out_weight, out_first[1]), STEPS[3]))

    def to_second(array):
        return lax.ppermute(array, "section", [(0, 1)])

    out_first_other = [to_second(held_until(out_weight, out_first[1]))]
    out_first_other += [to_second(block) for block in out_first[1:]]

    heads = kinds // 3
    gain_of = (qg_first, kg_first)

    def first_heads(blocks, along):
        weight = jnp.concatenate([mapped[kind * heads + h] for kind, h in along], axis=1)
        bias_row = jnp.concatenate([bias[kind * heads + h] for kind, h in along], axis=1)
        gains_here = jnp.concatenate([gain_of[kind] for kind, h in along if kind < 2])
        return [first_projection(block, gram, weight, bias_row, gains_here) for block in blocks]

    attend_other = []

    def before_first(step, sums):
        if step == 0:
            return out_first[1:3]
        if step == 1:
            attend_given = held_until(attend_weight[0], sums)
            attend_other.append(lax.ppermute(attend_given, "section", [(1, 0)]))
            return out_first_other[:3]
        if step == 3:
            return [out_first[3], attend_other[0]]
        return []

    attended = attention(
        first_heads(noisy_x, ALONG_X), first_heads(noisy_y, ALONG_Y), False, before_first
    )

    blocks = gather(attended, shift_z)
    turned = []
    for block, by in zip(blocks, STEPS):
        order = [
            [k for k in range(4) if (by + STEPS[k] - STEPS[mine]) % 4 == 0][0] for mine in range(4)
        ]
        turned.append(jnp.concatenate([block[k * local : (k + 1) * local] for k in order]))
    out_start = held_until(out_weight, blocks[3])
    out_second = [out_weight] + [shift_z_in(1, out_start, by) for by in STEPS[1:3]]
    out_second.append(shift_z_in(1, held_until(out_weight, out_second[1]), STEPS[3]))

    def step_first(weights, next_weight):
        return between_layers(
            turned,
            weights,
            noisy_row,
            embed_weight,
            gate_first,
            scale_second,
            shift_second,
            next_weight,
            qg_second,
            kg_second,
        )

    along_x, along_y, result_first = lax.cond(
        first,
        lambda own, other, next_own, next_other: step_first(own, next_other),
        lambda own, other, next_own, next_other: step_first(other, next_own),
        out_first,
        [out_first_other[0], out_first_other[1], out_first_other[2], out_first_other[3]],
        attend_weight[0],
        attend_other[0],
    )
    result_other = swapped(result_first)

    def before_second(step, sums):
        return {0: out_second[1:3], 6: [out_second[3], result_other]}.get(step, [])

    attended = attention(gather(along_x, shift_x), gather(along_y, shift_y), True, before_second)
    mine = give_back([attended[k * local : (k + 1) * local] for k in range(4)], shift_z)
    mine = jnp.concatenate([mine[STEPS.index(by if by == 2 else -by)] for by in STEPS], axis=1)
    mine_other = lax.ppermute(mine, "section", [(0, 1)])
    gates = modulation[:, 2 * width :]

    def finish_first():
        return jnp.stack([result_first, result_other])

    def finish_second():
        return last_step(
            (mine_other, mine), out_second, (result_other, result_first), gates
        )

    result = lax.cond(first, finish_first, finish_second)
    return result.reshape(1, batches, latent.shape[1], latent.shape[2], latent.shape[3], width)


def solution(mesh):
    return jax.shard_map(
        per_device,
        mesh=mesh,
        in_specs=(
            P(None, "depth", "row", None, None),
            P(None, "depth", "row", None, None),
            P(),
            P(),
            P("section", None, "row"),
            P("section", None, None, "row"),
            P("section", None),
            P("section", None),
            P("section", "row", None),
        ),
        out_specs=P("section", None, "depth", "row", None, None),
        check_vma=False,
    )
```

```python
import math

import jax
import jax.numpy as jnp
from jax import lax
from jax.experimental import pallas as pl
from jax.experimental.pallas import tpu as pltpu
from jax.sharding import PartitionSpec as P

HEAD_DIM = 128
BF = jnp.bfloat16
F32 = jnp.float32

norm_eps = 1e-06
plan_steps = 1000.0
QUERY_SCALE = math.log2(math.e) / math.sqrt(HEAD_DIM)
SWAP = [(0, 1), (1, 0)]
STEPS = (0, 1, -1, 2)


def signal_level(timestep):
    phase = (timestep.astype(F32) / plan_steps + 0.008) / 1.008 * (math.pi / 2)
    return jnp.cos(phase) ** 2


def time_features(timestep, count):
    half = count // 2
    frequency = jnp.exp(-math.log(10000.0) * jnp.arange(half, dtype=F32) / half)
    angles = timestep.astype(F32)[:, None] * frequency[None, :]
    return jnp.concatenate([jnp.cos(angles), jnp.sin(angles)], axis=1)


def shift_x(array, by):
    return lax.ppermute(
        array, "depth", [(y * 4 + x, y * 4 + (x + by) % 4) for y in range(4) for x in range(4)]
    )


def shift_y(array, by):
    return lax.ppermute(
        array, "depth", [(y * 4 + x, (y + by) % 4 * 4 + x) for y in range(4) for x in range(4)]
    )


def shift_z(array, by):
    return lax.ppermute(array, "row", [(z, (z + by) % 4) for z in range(4)])


def gather(array, shift):
    return [array] + [shift(array, by) for by in STEPS[1:]]


def give_back(blocks, shift):
    return [blocks[0]] + [shift(block, -by) for block, by in zip(blocks[1:], STEPS[1:])]


def params(mib):
    return pltpu.CompilerParams(vmem_limit_bytes=mib * 2**20)


def head_norm(values, gain):
    factor = lax.rsqrt(jnp.mean(values * values, axis=1, keepdims=True) + norm_eps)
    return (values * factor * gain).astype(BF)


def map_weights(embed, scale, shift, weight):
    patch, width = embed.shape
    batches = scale.shape[0]
    kinds, _, channels = weight.shape
    heads = channels // HEAD_DIM

    def kernel(embed_ref, scale_ref, shift_ref, weight_ref, out_ref, sides_ref):
        @pl.when(pl.program_id(0) == 0)
        def _():
            values = embed_ref[...].astype(F32)
            values = values - jnp.mean(values, axis=1, keepdims=True)
            for m in range(batches):
                sides_ref[m * patch : (m + 1) * patch] = (
                    values * (1.0 + scale_ref[m : m + 1])
                ).astype(BF)
            sides_ref[batches * patch :] = jnp.concatenate(
                [shift_ref[...], jnp.zeros((16 - batches, width), F32)]
            ).astype(BF)

        mapped = jnp.dot(sides_ref[...], weight_ref[0], preferred_element_type=F32)
        for m in range(batches):
            bias = mapped[batches * patch + m : batches * patch + m + 1]
            upper = bias.astype(BF).astype(F32)
            tail = jnp.concatenate([upper, bias - upper, jnp.zeros((14, channels), F32)]).astype(BF)
            for h in range(heads):
                part = slice(h * HEAD_DIM, (h + 1) * HEAD_DIM)
                out_ref[m, h, :patch] = mapped[m * patch : (m + 1) * patch, part].astype(BF)
                out_ref[m, h, patch:] = tail[:, part]

    return pl.pallas_call(
        kernel,
        grid=(kinds,),
        in_specs=[
            pl.BlockSpec((patch, width), lambda j: (0, 0)),
            pl.BlockSpec((batches, width), lambda j: (0, 0)),
            pl.BlockSpec((batches, width), lambda j: (0, 0)),
            pl.BlockSpec((1, width, channels), lambda j: (j, 0, 0)),
        ],
        out_specs=pl.BlockSpec((batches, heads, patch + 16, HEAD_DIM), lambda j: (0, j, 0, 0)),
        out_shape=jax.ShapeDtypeStruct((batches, kinds * heads, patch + 16, HEAD_DIM), BF),
        scratch_shapes=[pltpu.VMEM((batches * patch + 16, width), BF)],
        compiler_params=params(24),
        cost_estimate=pl.CostEstimate(flops=10**6, bytes_accessed=10**4, transcendentals=0),
    )(embed, scale, shift, weight)


def first_projection(noisy, gram, weight, bias, gains, after):
    rows = noisy.shape[0]
    heads = weight.shape[1] // HEAD_DIM
    normed_heads = gains.shape[0]

    def kernel(noisy_ref, gram_ref, weight_ref, bias_ref, gains_ref, *refs):
        out_ref = refs[-1]
        values = noisy_ref[...].astype(F32)
        spread = jnp.sum(
            jnp.dot(
                values, gram_ref[...], preferred_element_type=F32, precision=lax.Precision.HIGHEST
            )
            * values,
            axis=1,
            keepdims=True,
        )
        scaled = (values * lax.rsqrt(spread + norm_eps)).astype(BF)
        projected = jnp.dot(scaled, weight_ref[...], preferred_element_type=F32) + bias_ref[...]
        for h in range(heads):
            part = projected[:, h * HEAD_DIM : (h + 1) * HEAD_DIM]
            if h < normed_heads:
                out_ref[h] = head_norm(part, gains_ref[h : h + 1])
            else:
                out_ref[h] = part.astype(BF)

    whole = pl.BlockSpec(memory_space=pltpu.VMEM)
    return pl.pallas_call(
        kernel,
        in_specs=[whole] * 5 + [pl.BlockSpec(memory_space=pl.ANY)] * len(after),
        out_specs=whole,
        out_shape=jax.ShapeDtypeStruct((heads, rows, HEAD_DIM), BF),
        compiler_params=params(16),
        cost_estimate=pl.CostEstimate(flops=10**6, bytes_accessed=10**4, transcendentals=0),
    )(noisy, gram, weight, bias, gains, *after)


ALONG_X = ((1, 0), (1, 2), (0, 1), (2, 0), (2, 2))
ALONG_Y = ((0, 0), (0, 2), (1, 1), (2, 1))
HEADS_BY = ((1, 0), (0, 0), (1, 1))


def attend(queries, blocks, after, carry=None, more=False):
    rows = queries[0].shape[1]
    key_rows = blocks[0][0].shape[1]
    count = len(blocks[0])
    keys_total = key_rows * count
    places = (ALONG_X, ALONG_Y)
    carries = [] if carry is None else [carry]

    def kernel(*refs):
        query_refs = refs[:2]
        block_refs = (refs[2 : 2 + count], refs[2 + count : 2 + 2 * count])
        out_refs = refs[-2:-1] if more else refs[-3:-1]
        wide_ref = refs[-1]
        diagonal = lax.broadcasted_iota(jnp.int32, (HEAD_DIM, HEAD_DIM), 0) == lax.broadcasted_iota(
            jnp.int32, (HEAD_DIM, HEAD_DIM), 1
        )
        for h, (along, out_place) in enumerate(HEADS_BY):
            query = query_refs[along][places[along].index((0, h))]
            key_at = places[1 - along].index((1, h))
            value_at = places[1 - along].index((2, h))
            sums = None if carry is None else refs[2 + 2 * count][h]
            for i, ref in enumerate(block_refs[1 - along]):
                wide_ref[h, i * key_rows : (i + 1) * key_rows, :HEAD_DIM] = ref[value_at]
                wide_ref[h, i * key_rows : (i + 1) * key_rows, HEAD_DIM:] = jnp.ones(
                    (key_rows, HEAD_DIM), BF
                )
            for i, ref in enumerate(block_refs[1 - along]):
                scores = lax.dot_general(
                    query, ref[key_at], (((1,), (1,)), ((), ())), preferred_element_type=F32
                )
                weights = jnp.exp2(scores).astype(BF)
                term = jnp.dot(
                    weights,
                    wide_ref[h, i * key_rows : (i + 1) * key_rows],
                    preferred_element_type=F32,
                )
                sums = term if sums is None else sums + term
            if more:
                out_refs[0][h] = sums
                continue
            out_ref = out_refs[1 - along]
            out_ref[out_place, :rows] = sums[:, :HEAD_DIM].astype(BF)
            lines = []
            for part in range(rows // HEAD_DIM):
                square = sums[part * HEAD_DIM : (part + 1) * HEAD_DIM, HEAD_DIM:]
                lines.append(jnp.sum(jnp.where(diagonal, square, 0.0), axis=0, keepdims=True))
            total = jnp.concatenate(lines, axis=0)
            upper = total.astype(BF)
            lower = (total - upper.astype(F32)).astype(BF)
            out_ref[out_place, rows : rows + 16] = jnp.concatenate(
                [upper.astype(F32), lower.astype(F32), jnp.zeros((8, HEAD_DIM), F32)], axis=0
            ).astype(BF)

    whole = pl.BlockSpec(memory_space=pltpu.VMEM)
    return pl.pallas_call(
        kernel,
        in_specs=[whole] * (2 + 2 * count + len(carries))
        + [pl.BlockSpec(memory_space=pl.ANY)] * len(after),
        out_specs=whole if more else [whole] * 2,
        out_shape=jax.ShapeDtypeStruct((len(HEADS_BY), rows, 2 * HEAD_DIM), F32)
        if more
        else [
            jax.ShapeDtypeStruct((2, rows + 16, HEAD_DIM), BF),
            jax.ShapeDtypeStruct((1, rows + 16, HEAD_DIM), BF),
        ],
        scratch_shapes=[pltpu.VMEM((len(HEADS_BY), keys_total, 2 * HEAD_DIM), BF)],
        compiler_params=params(24),
        cost_estimate=pl.CostEstimate(flops=10**6, bytes_accessed=10**4, transcendentals=0),
    )(*queries, *blocks[0], *blocks[1], *carries, *after)


def combine(parts_y, parts_x):
    packed = parts_y[0].shape[1]
    rows = packed - 16
    lines = rows // HEAD_DIM
    count = len(parts_y)
    heads = len(HEADS_BY)

    def kernel(*refs):
        out_ref = refs[-1]
        diagonal = lax.broadcasted_iota(jnp.int32, (HEAD_DIM, HEAD_DIM), 0) == lax.broadcasted_iota(
            jnp.int32, (HEAD_DIM, HEAD_DIM), 1
        )
        for h, (along, at) in enumerate(HEADS_BY):
            sources = refs[:count] if along == 1 else refs[count : 2 * count]
            tail = sources[0][at, rows : rows + 16].astype(F32)
            for ref in sources[1:]:
                tail = tail + ref[at, rows : rows + 16].astype(F32)
            for part in range(lines):
                place = slice(part * HEAD_DIM, (part + 1) * HEAD_DIM)
                numerator = sources[0][at, place].astype(F32)
                for ref in sources[1:]:
                    numerator = numerator + ref[at, place].astype(F32)
                total = tail[part : part + 1] + tail[lines + part : lines + part + 1]
                column = jnp.sum(jnp.where(diagonal, 1.0 / total, 0.0), axis=1, keepdims=True)
                out_ref[place, h * HEAD_DIM : (h + 1) * HEAD_DIM] = (numerator * column).astype(BF)

    return pl.pallas_call(
        kernel,
        out_shape=jax.ShapeDtypeStruct((rows, heads * HEAD_DIM), BF),
        compiler_params=params(16),
    )(*parts_y, *parts_x)


def attention(xs, ys, near_first, before):
    parts_y, parts_x = [None] * 4, [None] * 4
    after, carries, first_sums, step = [], [None] * 4, None, 0
    if near_first:
        for k in (2, 1, 0):
            carries[k] = attend(
                (xs[k], ys[k]), (xs[:3], ys[:3]), after + before(step, first_sums), more=True
            )
            after = [carries[k]]
            first_sums = after[0] if first_sums is None else first_sums
            step += 1
    for k in (3, 2, 1, 0):
        blocks = (xs, ys) if carries[k] is None else (xs[3:], ys[3:])
        if k == 0:
            after = after + [parts_y[3], parts_x[3]]
        sums_y, sums_x = attend(
            (xs[k], ys[k]), blocks, after + before(step, first_sums), carries[k]
        )
        after = [sums_x]
        first_sums = after[0] if first_sums is None else first_sums
        step += 1
        by = STEPS[k]
        parts_y[k] = shift_y(sums_y, -by) if by else sums_y
        parts_x[k] = shift_x(sums_x, -by) if by else sums_x
    return combine(parts_y, parts_x)


def held_until(array, other):
    return lax.optimization_barrier((array, other))[0]


def weight_copies(weight_refs, held_ref, sems):
    depth, width = held_ref.shape
    part = depth // 8
    half = width // 2
    copies = []
    for column in range(2):
        columns = slice(column * half, (column + 1) * half)
        for k in range(8):
            row, side = divmod(k, 2)
            source = weight_refs[side].at[row * part : (row + 1) * part, columns]
            place = held_ref.at[k * part : (k + 1) * part, columns]
            copies.append(pltpu.make_async_copy(source, place, sems.at[column * 8 + k]))
    return copies


def between_layers(places, blocks, weights, noisy, embed, gate, scale, shift, next_weight, query_gain, key_gain):
    rows, part = blocks[0].shape
    width = gate.shape[1]
    depth = 4 * part
    block = 512
    local = rows // 4
    kinds, _, channels = next_weight.shape
    heads = channels // HEAD_DIM

    def kernel(places_ref, *refs):
        block_refs = refs[:4]
        weight_refs = refs[4:6]
        noisy_ref, embed_ref, gate_ref, scale_ref, shift_ref, next_ref, qg_ref, kg_ref = refs[6:14]
        x_ref, y_ref, own_ref = refs[14:17]
        held_ref, next_held_ref, side_ref, tokens_ref, sems = refs[17:]
        copies = weight_copies(weight_refs, held_ref, sems)
        next_copies = [
            pltpu.make_async_copy(next_ref.at[j], next_held_ref.at[j], sems.at[16 + j])
            for j in range(kinds)
        ]
        for copy in copies:
            copy.start()
        for k in range(4):
            side_ref[:, pl.ds(pl.multiple_of(places_ref[k] * part, HEAD_DIM), part)] = block_refs[k][
                ...
            ]
        for column in range(2):
            for copy in copies[8 * column : 8 * column + 8]:
                copy.wait()
            if column == 0:
                for copy in next_copies:
                    copy.start()

            @pl.loop(0, width // 2 // block)
            def _(n):
                place = pl.ds(pl.multiple_of(column * (width // 2) + n * block, block), block)
                update = jnp.dot(side_ref[...], held_ref[:, place], preferred_element_type=F32)
                base = jnp.dot(noisy_ref[...], embed_ref[:, place], preferred_element_type=F32)
                tokens_ref[:, place] = (
                    base.astype(BF).astype(F32) + gate_ref[:, place] * update
                ).astype(BF)

        own_ref[...] = tokens_ref[:local]

        @pl.loop(0, rows // 128)
        def _(n):
            place = pl.ds(pl.multiple_of(n * 128, 128), 128)
            values = tokens_ref[place].astype(F32)
            values = values - jnp.mean(values, axis=1, keepdims=True)
            spread = jnp.mean(values * values, axis=1, keepdims=True)
            tokens_ref[place] = (
                values * lax.rsqrt(spread + norm_eps) * (1.0 + scale_ref[...]) + shift_ref[...]
            ).astype(BF)

        for kind in range(kinds):
            next_copies[kind].wait()
            projected = jnp.dot(tokens_ref[...], next_held_ref[kind], preferred_element_type=F32)
            for h in range(heads):
                piece = projected[:, h * HEAD_DIM : (h + 1) * HEAD_DIM]
                if kind < 2:
                    piece = head_norm(piece, (qg_ref, kg_ref)[kind][...])
                else:
                    piece = piece.astype(BF)
                if (kind, h) in ALONG_X:
                    x_ref[ALONG_X.index((kind, h))] = piece
                else:
                    y_ref[ALONG_Y.index((kind, h))] = piece

    whole = pl.BlockSpec(memory_space=pltpu.VMEM)
    left = pl.BlockSpec(memory_space=pl.ANY)
    return pl.pallas_call(
        kernel,
        in_specs=[pl.BlockSpec(memory_space=pltpu.SMEM)]
        + [whole] * 4
        + [left] * 2
        + [whole] * 5
        + [left]
        + [whole] * 2,
        out_specs=[whole] * 3,
        out_shape=[
            jax.ShapeDtypeStruct((len(ALONG_X), rows, HEAD_DIM), BF),
            jax.ShapeDtypeStruct((len(ALONG_Y), rows, HEAD_DIM), BF),
            jax.ShapeDtypeStruct((local, width), BF),
        ],
        scratch_shapes=[
            pltpu.VMEM((depth, width), BF),
            pltpu.VMEM(next_weight.shape, BF),
            pltpu.VMEM((rows, depth), BF),
            pltpu.VMEM((rows, width), BF),
            pltpu.SemaphoreType.DMA((16 + kinds,)),
        ],
        compiler_params=params(40),
        cost_estimate=pl.CostEstimate(
            flops=2 * rows * width * (depth + kinds * channels),
            bytes_accessed=20 * 2**20,
            transcendentals=0,
        ),
    )(places, *blocks, *weights, noisy, embed, gate, scale, shift, next_weight, query_gain, key_gain)


def last_step(places, heads, weights, bases, gates):
    rows, depth = heads[0].shape
    width = gates.shape[1]
    block = 512

    part = depth // 4

    def kernel(places_ref, first_ref, second_ref, *refs):
        weight_refs = refs[:2]
        first_base_ref, second_base_ref, gates_ref, out_ref, held_ref, side_ref, sems = refs[2:]
        copies = weight_copies(weight_refs, held_ref, sems)
        for copy in copies:
            copy.start()
        for k in range(4):
            place = pl.ds(pl.multiple_of(places_ref[k] * part, HEAD_DIM), part)
            side_ref[:rows, place] = first_ref[:, k * part : (k + 1) * part]
            side_ref[rows:, place] = second_ref[:, k * part : (k + 1) * part]
        for column in range(2):
            for copy in copies[8 * column : 8 * column + 8]:
                copy.wait()

            @pl.loop(0, width // 2 // block)
            def _(n):
                place = pl.ds(pl.multiple_of(column * (width // 2) + n * block, block), block)
                update = jnp.dot(side_ref[...], held_ref[:, place], preferred_element_type=F32)
                for m, base_ref in enumerate((first_base_ref, second_base_ref)):
                    out_ref[m, :, place] = (
                        base_ref[:, place].astype(F32)
                        + gates_ref[m : m + 1, place] * update[m * rows : (m + 1) * rows]
                    ).astype(BF)

    whole = pl.BlockSpec(memory_space=pltpu.VMEM)
    return pl.pallas_call(
        kernel,
        in_specs=[pl.BlockSpec(memory_space=pltpu.SMEM)]
        + [whole] * 2
        + [pl.BlockSpec(memory_space=pl.ANY)] * 2
        + [whole] * 3,
        out_specs=whole,
        out_shape=jax.ShapeDtypeStruct((2, rows, width), BF),
        scratch_shapes=[
            pltpu.VMEM((depth, width), BF),
            pltpu.VMEM((2 * rows, depth), BF),
            pltpu.SemaphoreType.DMA((16,)),
        ],
        compiler_params=params(24),
    )(places, *heads, *weights, *bases, gates)


def per_device(
    latent,
    noise_field,
    timestep,
    embed_weight,
    modulate_weight,
    attend_weight,
    query_gain,
    key_gain,
    output_weight,
):
    batches = latent.shape[0]
    patch, width = embed_weight.shape
    local = latent.shape[1] * latent.shape[2] * latent.shape[3]
    section = lax.axis_index("section")
    row = lax.axis_index("row")
    first = section == 0

    def by_section(of_first, of_second):
        return jnp.where(first, of_first, of_second)

    def swapped(array):
        return lax.ppermute(array, "section", SWAP)

    level = signal_level(timestep)[:, None, None, None, None]
    noisy = (
        jnp.sqrt(level) * latent.astype(F32) + jnp.sqrt(1.0 - level) * noise_field.astype(F32)
    ).astype(BF)
    noisy = by_section(noisy[0], noisy[1]).reshape(local, patch)
    features = time_features(timestep, modulate_weight.shape[1]).astype(BF)
    mod_part = jnp.dot(features, modulate_weight[0], preferred_element_type=F32)

    mod_rows = mod_part.size // patch
    packed = jnp.concatenate(
        [noisy.astype(F32), mod_part.reshape(mod_rows, patch), jnp.zeros((-mod_rows % 8, patch), F32)]
    )
    packed = gather(packed, shift_z)
    noisy_row = jnp.concatenate([block[:local] for block in packed]).astype(BF)
    mods = [block[local : local + mod_rows].reshape(batches, -1) for block in packed]

    def from_row(b):
        chosen = mods[0]
        for k in (1, 2, 3):
            chosen = jnp.where(row == (b + STEPS[k]) % 4, mods[k], chosen)
        return chosen

    modulation = jnp.concatenate([from_row(b) for b in range(4)], axis=1)
    shift_own = modulation[:, :width]
    scale_own = modulation[:, width : 2 * width]

    noisy_x = gather(noisy_row, shift_x)
    noisy_y = gather(noisy_row, shift_y)

    centered = embed_weight.astype(F32)
    centered = centered - jnp.mean(centered, axis=1, keepdims=True)
    gram = (
        jnp.dot(centered, centered.T, preferred_element_type=F32, precision=lax.Precision.HIGHEST)
        / width
    )
    mapped = map_weights(embed_weight, scale_own, shift_own, attend_weight[0])
    kinds = mapped.shape[1]
    mapped_other = lax.ppermute(mapped[1], "section", [(0, 1)])
    mapped = by_section(mapped[0], mapped_other)
    bias = mapped[:, patch : patch + 1].astype(F32) + mapped[:, patch + 1 : patch + 2].astype(F32)
    mapped = mapped[:, :patch]

    gains = jnp.concatenate([query_gain, key_gain])
    small = jnp.concatenate([modulation.reshape(-1, patch), gains, jnp.zeros((6, patch), F32)])
    small_other = swapped(small)
    small_first = by_section(small, small_other)
    small_second = by_section(small_other, small)
    mod_rows_all = modulation.size // patch

    def unpack(array):
        mod = array[:mod_rows_all].reshape(batches, -1)
        mod = by_section(mod[:1], mod[1:])
        qg = array[mod_rows_all : mod_rows_all + 1] * QUERY_SCALE
        kg = array[mod_rows_all + 1 : mod_rows_all + 2]
        return mod[:, :width], mod[:, width : 2 * width], mod[:, 2 * width :], qg, kg

    _, _, gate_first, qg_first, kg_first = unpack(small_first)
    shift_second, scale_second, _, qg_second, kg_second = unpack(small_second)

    half = output_weight.shape[1] // 2
    keep = lax.dynamic_slice_in_dim(output_weight[0], section * half, half, 0)
    got = swapped(lax.dynamic_slice_in_dim(output_weight[0], (1 - section) * half, half, 0))
    out_part = by_section(keep, got)
    out_first = lax.all_gather(out_part, "row", axis=0, tiled=True)

    heads = kinds // 3
    gain_of = (qg_first, kg_first)

    def first_heads(blocks, along):
        weight = jnp.concatenate([mapped[kind * heads + h] for kind, h in along], axis=1)
        bias_row = jnp.concatenate([bias[kind * heads + h] for kind, h in along], axis=1)
        gains_here = jnp.concatenate([gain_of[kind] for kind, h in along if kind < 2])
        return [
            first_projection(block, gram, weight, bias_row, gains_here, [out_part])
            for block in blocks
        ]

    attend_other = []

    def before_first(step, sums):
        if step == 1:
            attend_given = held_until(attend_weight[0], sums)
            attend_other.append(lax.ppermute(attend_given, "section", [(1, 0)]))
        return [attend_other[0]] if step == 3 else []

    attended = attention(
        first_heads(noisy_x, ALONG_X), first_heads(noisy_y, ALONG_Y), False, before_first
    )
    out_first, attended = lax.optimization_barrier((out_first, attended))
    out_first_other = swapped(out_first)

    blocks = gather(attended, shift_z)
    turned = []
    for block, by in zip(blocks, STEPS):
        order = [
            [k for k in range(4) if (by + STEPS[k] - STEPS[mine]) % 4 == 0][0] for mine in range(4)
        ]
        turned.append(jnp.concatenate([block[k * local : (k + 1) * local] for k in order]))
    keep, got, blocks[3] = lax.optimization_barrier((keep, got, blocks[3]))
    out_second = lax.all_gather(by_section(got, keep), "row", axis=0, tiled=True)
    places = jnp.stack([(row - by) & 3 for by in STEPS]).astype(jnp.int32)

    def step_first(weights, next_weight):
        return between_layers(
            places,
            turned,
            weights,
            noisy_row,
            embed_weight,
            gate_first,
            scale_second,
            shift_second,
            next_weight,
            qg_second,
            kg_second,
        )

    along_x, along_y, result_first = lax.cond(
        first,
        lambda own, other, next_own, next_other: step_first((own, other), next_other),
        lambda own, other, next_own, next_other: step_first((other, own), next_own),
        out_first,
        out_first_other,
        attend_weight[0],
        attend_other[0],
    )
    result_other = swapped(result_first)

    def before_second(step, sums):
        return {5: [out_second], 6: [result_other]}.get(step, [])

    attended = attention(gather(along_x, shift_x), gather(along_y, shift_y), True, before_second)
    mine = give_back([attended[k * local : (k + 1) * local] for k in range(4)], shift_z)
    mine = jnp.concatenate(mine, axis=1)
    mine_other = lax.ppermute(mine, "section", [(0, 1)])
    out_second_other = swapped(out_second)
    places_last = jnp.stack([(row + by) & 3 for by in STEPS]).astype(jnp.int32)
    gates = modulation[:, 2 * width :]

    def finish_first():
        return jnp.stack([result_first, result_other])

    def finish_second():
        return last_step(
            places_last,
            (mine_other, mine),
            (out_second_other, out_second),
            (result_other, result_first),
            gates,
        )

    result = lax.cond(first, finish_first, finish_second)
    return result.reshape(1, batches, latent.shape[1], latent.shape[2], latent.shape[3], width)


def solution(mesh):
    return jax.shard_map(
        per_device,
        mesh=mesh,
        in_specs=(
            P(None, "depth", "row", None, None),
            P(None, "depth", "row", None, None),
            P(),
            P(),
            P("section", None, "row"),
            P("section", None, None, "row"),
            P("section", None),
            P("section", None),
            P("section", "row", None),
        ),
        out_specs=P("section", None, "depth", "row", None, None),
        check_vma=False,
    )
```

```python
import math

import jax
import jax.numpy as jnp
from jax import lax
from jax.experimental import pallas as pl
from jax.experimental.pallas import tpu as pltpu
from jax.sharding import PartitionSpec as P

HEAD_DIM = 128
BF = jnp.bfloat16
F32 = jnp.float32

norm_eps = 1e-06
plan_steps = 1000.0
QUERY_SCALE = math.log2(math.e) / math.sqrt(HEAD_DIM)
SWAP = [(0, 1), (1, 0)]
STEPS = (0, 1, -1, 2)


def signal_level(timestep):
    phase = (timestep.astype(F32) / plan_steps + 0.008) / 1.008 * (math.pi / 2)
    return jnp.cos(phase) ** 2


def time_features(timestep, count):
    half = count // 2
    frequency = jnp.exp(-math.log(10000.0) * jnp.arange(half, dtype=F32) / half)
    angles = timestep.astype(F32)[:, None] * frequency[None, :]
    return jnp.concatenate([jnp.cos(angles), jnp.sin(angles)], axis=1)


def shift_x(array, by):
    return lax.ppermute(
        array, "depth", [(y * 4 + x, y * 4 + (x + by) % 4) for y in range(4) for x in range(4)]
    )


def shift_y(array, by):
    return lax.ppermute(
        array, "depth", [(y * 4 + x, (y + by) % 4 * 4 + x) for y in range(4) for x in range(4)]
    )


def shift_z(array, by):
    return lax.ppermute(array, "row", [(z, (z + by) % 4) for z in range(4)])


def gather(array, shift):
    return [array] + [shift(array, by) for by in STEPS[1:]]


def give_back(blocks, shift):
    return [blocks[0]] + [shift(block, -by) for block, by in zip(blocks[1:], STEPS[1:])]


def params(mib):
    return pltpu.CompilerParams(vmem_limit_bytes=mib * 2**20)


def head_norm(values, gain):
    factor = lax.rsqrt(jnp.mean(values * values, axis=1, keepdims=True) + norm_eps)
    return (values * factor * gain).astype(BF)


def map_weights(embed, scale, shift, weight, after):
    patch, width = embed.shape
    batches = scale.shape[0]
    kinds, _, channels = weight.shape
    heads = channels // HEAD_DIM

    def kernel(embed_ref, scale_ref, shift_ref, weight_ref, *refs):
        out_ref, sides_ref = refs[-2:]

        @pl.when(pl.program_id(0) == 0)
        def _():
            values = embed_ref[...].astype(F32)
            values = values - jnp.mean(values, axis=1, keepdims=True)
            for m in range(batches):
                sides_ref[m * patch : (m + 1) * patch] = (
                    values * (1.0 + scale_ref[m : m + 1])
                ).astype(BF)
            sides_ref[batches * patch :] = jnp.concatenate(
                [shift_ref[...], jnp.zeros((16 - batches, width), F32)]
            ).astype(BF)

        mapped = jnp.dot(sides_ref[...], weight_ref[0], preferred_element_type=F32)
        for m in range(batches):
            bias = mapped[batches * patch + m : batches * patch + m + 1]
            upper = bias.astype(BF).astype(F32)
            tail = jnp.concatenate([upper, bias - upper, jnp.zeros((14, channels), F32)]).astype(BF)
            for h in range(heads):
                part = slice(h * HEAD_DIM, (h + 1) * HEAD_DIM)
                out_ref[m, h, :patch] = mapped[m * patch : (m + 1) * patch, part].astype(BF)
                out_ref[m, h, patch:] = tail[:, part]

    return pl.pallas_call(
        kernel,
        grid=(kinds,),
        in_specs=[
            pl.BlockSpec((patch, width), lambda j: (0, 0)),
            pl.BlockSpec((batches, width), lambda j: (0, 0)),
            pl.BlockSpec((batches, width), lambda j: (0, 0)),
            pl.BlockSpec((1, width, channels), lambda j: (j, 0, 0)),
        ]
        + [pl.BlockSpec(memory_space=pl.ANY)] * len(after),
        out_specs=pl.BlockSpec((batches, heads, patch + 16, HEAD_DIM), lambda j: (0, j, 0, 0)),
        out_shape=jax.ShapeDtypeStruct((batches, kinds * heads, patch + 16, HEAD_DIM), BF),
        scratch_shapes=[pltpu.VMEM((batches * patch + 16, width), BF)],
        compiler_params=params(18),
        cost_estimate=pl.CostEstimate(
            flops=2 * batches * patch * width * kinds * channels,
            bytes_accessed=20 * 2**20,
            transcendentals=0,
        ),
    )(embed, scale, shift, weight, *after)


def first_projection(noisy, gram, weight, bias, gains, after):
    rows = noisy.shape[0]
    heads = weight.shape[1] // HEAD_DIM
    normed_heads = gains.shape[0]

    def kernel(noisy_ref, gram_ref, weight_ref, bias_ref, gains_ref, *refs):
        out_ref = refs[-1]
        values = noisy_ref[...].astype(F32)
        spread = jnp.sum(
            jnp.dot(
                values, gram_ref[...], preferred_element_type=F32, precision=lax.Precision.HIGHEST
            )
            * values,
            axis=1,
            keepdims=True,
        )
        scaled = (values * lax.rsqrt(spread + norm_eps)).astype(BF)
        projected = jnp.dot(scaled, weight_ref[...], preferred_element_type=F32) + bias_ref[...]
        for h in range(heads):
            part = projected[:, h * HEAD_DIM : (h + 1) * HEAD_DIM]
            if h < normed_heads:
                out_ref[h] = head_norm(part, gains_ref[h : h + 1])
            else:
                out_ref[h] = part.astype(BF)

    whole = pl.BlockSpec(memory_space=pltpu.VMEM)
    return pl.pallas_call(
        kernel,
        in_specs=[whole] * 5 + [pl.BlockSpec(memory_space=pl.ANY)] * len(after),
        out_specs=whole,
        out_shape=jax.ShapeDtypeStruct((heads, rows, HEAD_DIM), BF),
        compiler_params=params(16),
        cost_estimate=pl.CostEstimate(flops=10**6, bytes_accessed=10**4, transcendentals=0),
    )(noisy, gram, weight, bias, gains, *after)


ALONG_X = ((1, 0), (1, 2), (0, 1), (2, 0), (2, 2))
ALONG_Y = ((0, 0), (0, 2), (1, 1), (2, 1))
HEADS_BY = ((1, 0), (0, 0), (1, 1))


def attend(queries, blocks, after, carry=None, more=False):
    rows = queries[0].shape[1]
    key_rows = blocks[0][0].shape[1]
    count = len(blocks[0])
    keys_total = key_rows * count
    places = (ALONG_X, ALONG_Y)
    carries = [] if carry is None else [carry]

    def kernel(*refs):
        query_refs = refs[:2]
        block_refs = (refs[2 : 2 + count], refs[2 + count : 2 + 2 * count])
        out_refs = refs[-2:-1] if more else refs[-3:-1]
        wide_ref = refs[-1]
        diagonal = lax.broadcasted_iota(jnp.int32, (HEAD_DIM, HEAD_DIM), 0) == lax.broadcasted_iota(
            jnp.int32, (HEAD_DIM, HEAD_DIM), 1
        )
        for h, (along, out_place) in enumerate(HEADS_BY):
            query = query_refs[along][places[along].index((0, h))]
            key_at = places[1 - along].index((1, h))
            value_at = places[1 - along].index((2, h))
            sums = None if carry is None else refs[2 + 2 * count][h]
            for i, ref in enumerate(block_refs[1 - along]):
                wide_ref[h, i * key_rows : (i + 1) * key_rows, :HEAD_DIM] = ref[value_at]
                wide_ref[h, i * key_rows : (i + 1) * key_rows, HEAD_DIM:] = jnp.ones(
                    (key_rows, HEAD_DIM), BF
                )
            for i, ref in enumerate(block_refs[1 - along]):
                scores = lax.dot_general(
                    query, ref[key_at], (((1,), (1,)), ((), ())), preferred_element_type=F32
                )
                weights = jnp.exp2(scores).astype(BF)
                term = jnp.dot(
                    weights,
                    wide_ref[h, i * key_rows : (i + 1) * key_rows],
                    preferred_element_type=F32,
                )
                sums = term if sums is None else sums + term
            if more:
                out_refs[0][h] = sums
                continue
            out_ref = out_refs[1 - along]
            out_ref[out_place, :rows] = sums[:, :HEAD_DIM].astype(BF)
            lines = []
            for part in range(rows // HEAD_DIM):
                square = sums[part * HEAD_DIM : (part + 1) * HEAD_DIM, HEAD_DIM:]
                lines.append(jnp.sum(jnp.where(diagonal, square, 0.0), axis=0, keepdims=True))
            total = jnp.concatenate(lines, axis=0)
            upper = total.astype(BF)
            lower = (total - upper.astype(F32)).astype(BF)
            out_ref[out_place, rows : rows + 16] = jnp.concatenate(
                [upper.astype(F32), lower.astype(F32), jnp.zeros((8, HEAD_DIM), F32)], axis=0
            ).astype(BF)

    whole = pl.BlockSpec(memory_space=pltpu.VMEM)
    return pl.pallas_call(
        kernel,
        in_specs=[whole] * (2 + 2 * count + len(carries))
        + [pl.BlockSpec(memory_space=pl.ANY)] * len(after),
        out_specs=whole if more else [whole] * 2,
        out_shape=jax.ShapeDtypeStruct((len(HEADS_BY), rows, 2 * HEAD_DIM), F32)
        if more
        else [
            jax.ShapeDtypeStruct((2, rows + 16, HEAD_DIM), BF),
            jax.ShapeDtypeStruct((1, rows + 16, HEAD_DIM), BF),
        ],
        scratch_shapes=[pltpu.VMEM((len(HEADS_BY), keys_total, 2 * HEAD_DIM), BF)],
        compiler_params=params(18),
        cost_estimate=pl.CostEstimate(flops=10**6, bytes_accessed=10**4, transcendentals=0),
    )(*queries, *blocks[0], *blocks[1], *carries, *after)


def combine(parts_y, parts_x):
    packed = parts_y[0].shape[1]
    rows = packed - 16
    lines = rows // HEAD_DIM
    count = len(parts_y)
    heads = len(HEADS_BY)

    def kernel(*refs):
        out_ref = refs[-1]
        diagonal = lax.broadcasted_iota(jnp.int32, (HEAD_DIM, HEAD_DIM), 0) == lax.broadcasted_iota(
            jnp.int32, (HEAD_DIM, HEAD_DIM), 1
        )
        for h, (along, at) in enumerate(HEADS_BY):
            sources = refs[:count] if along == 1 else refs[count : 2 * count]
            tail = sources[0][at, rows : rows + 16].astype(F32)
            for ref in sources[1:]:
                tail = tail + ref[at, rows : rows + 16].astype(F32)
            for part in range(lines):
                place = slice(part * HEAD_DIM, (part + 1) * HEAD_DIM)
                numerator = sources[0][at, place].astype(F32)
                for ref in sources[1:]:
                    numerator = numerator + ref[at, place].astype(F32)
                total = tail[part : part + 1] + tail[lines + part : lines + part + 1]
                column = jnp.sum(jnp.where(diagonal, 1.0 / total, 0.0), axis=1, keepdims=True)
                out_ref[place, h * HEAD_DIM : (h + 1) * HEAD_DIM] = (numerator * column).astype(BF)

    return pl.pallas_call(
        kernel,
        out_shape=jax.ShapeDtypeStruct((rows, heads * HEAD_DIM), BF),
        compiler_params=params(16),
    )(*parts_y, *parts_x)


def attention(xs, ys, near_first, before):
    parts_y, parts_x = [None] * 4, [None] * 4
    after, carries, step = [], [None] * 4, 0
    if near_first:
        for k in (2, 1, 0):
            more = before(step, after[0] if after else None)
            carries[k] = attend((xs[k], ys[k]), (xs[:3], ys[:3]), after + more, more=True)
            after = [carries[k]]
            step += 1
    for k in (3, 2, 1, 0):
        blocks = (xs, ys) if carries[k] is None else (xs[3:], ys[3:])
        more = before(step, after[0] if after else None)
        if k == 0:
            more = more + [parts_y[3], parts_x[3]]
        sums_y, sums_x = attend((xs[k], ys[k]), blocks, after + more, carries[k])
        after = [sums_x]
        step += 1
        by = STEPS[k]
        parts_y[k] = shift_y(sums_y, -by) if by else sums_y
        parts_x[k] = shift_x(sums_x, -by) if by else sums_x
    return combine(parts_y, parts_x)


def held_until(array, other):
    return lax.optimization_barrier((array, other))[0]


def weight_copies(weight_refs, held_ref, sems):
    depth, width = held_ref.shape
    part = depth // 8
    half = width // 2
    copies = []
    for column in range(2):
        columns = slice(column * half, (column + 1) * half)
        for k in range(8):
            row, side = divmod(k, 2)
            source = weight_refs[side].at[row * part : (row + 1) * part, columns]
            place = held_ref.at[k * part : (k + 1) * part, columns]
            copies.append(pltpu.make_async_copy(source, place, sems.at[column * 8 + k]))
    return copies


def between_layers(places, blocks, weights, noisy, embed, gate, scale, shift, next_weight, query_gain, key_gain):
    rows, part = blocks[0].shape
    width = gate.shape[1]
    depth = 4 * part
    block = 512
    local = rows // 4
    kinds, _, channels = next_weight.shape
    heads = channels // HEAD_DIM

    def kernel(places_ref, *refs):
        block_refs = refs[:4]
        weight_refs = refs[4:6]
        noisy_ref, embed_ref, gate_ref, scale_ref, shift_ref, next_ref, qg_ref, kg_ref = refs[6:14]
        x_ref, y_ref, own_ref = refs[14:17]
        held_ref, next_held_ref, side_ref, tokens_ref, sems = refs[17:]
        copies = weight_copies(weight_refs, held_ref, sems)
        next_copies = [
            pltpu.make_async_copy(next_ref.at[j], next_held_ref.at[j], sems.at[16 + j])
            for j in range(kinds)
        ]
        for copy in copies:
            copy.start()
        for k in range(4):
            side_ref[:, pl.ds(pl.multiple_of(places_ref[k] * part, HEAD_DIM), part)] = block_refs[k][
                ...
            ]
        for column in range(2):
            for copy in copies[8 * column : 8 * column + 8]:
                copy.wait()
            if column == 0:
                for copy in next_copies:
                    copy.start()

            @pl.loop(0, width // 2 // block)
            def _(n):
                place = pl.ds(pl.multiple_of(column * (width // 2) + n * block, block), block)
                update = jnp.dot(side_ref[...], held_ref[:, place], preferred_element_type=F32)
                base = jnp.dot(noisy_ref[...], embed_ref[:, place], preferred_element_type=F32)
                tokens_ref[:, place] = (
                    base.astype(BF).astype(F32) + gate_ref[:, place] * update
                ).astype(BF)

        own_ref[...] = tokens_ref[:local]

        @pl.loop(0, rows // 128)
        def _(n):
            place = pl.ds(pl.multiple_of(n * 128, 128), 128)
            values = tokens_ref[place].astype(F32)
            values = values - jnp.mean(values, axis=1, keepdims=True)
            spread = jnp.mean(values * values, axis=1, keepdims=True)
            tokens_ref[place] = (
                values * lax.rsqrt(spread + norm_eps) * (1.0 + scale_ref[...]) + shift_ref[...]
            ).astype(BF)

        for kind in range(kinds):
            next_copies[kind].wait()
            projected = jnp.dot(tokens_ref[...], next_held_ref[kind], preferred_element_type=F32)
            for h in range(heads):
                piece = projected[:, h * HEAD_DIM : (h + 1) * HEAD_DIM]
                if kind < 2:
                    piece = head_norm(piece, (qg_ref, kg_ref)[kind][...])
                else:
                    piece = piece.astype(BF)
                if (kind, h) in ALONG_X:
                    x_ref[ALONG_X.index((kind, h))] = piece
                else:
                    y_ref[ALONG_Y.index((kind, h))] = piece

    whole = pl.BlockSpec(memory_space=pltpu.VMEM)
    left = pl.BlockSpec(memory_space=pl.ANY)
    return pl.pallas_call(
        kernel,
        in_specs=[pl.BlockSpec(memory_space=pltpu.SMEM)]
        + [whole] * 4
        + [left] * 2
        + [whole] * 5
        + [left]
        + [whole] * 2,
        out_specs=[whole] * 3,
        out_shape=[
            jax.ShapeDtypeStruct((len(ALONG_X), rows, HEAD_DIM), BF),
            jax.ShapeDtypeStruct((len(ALONG_Y), rows, HEAD_DIM), BF),
            jax.ShapeDtypeStruct((local, width), BF),
        ],
        scratch_shapes=[
            pltpu.VMEM((depth, width), BF),
            pltpu.VMEM(next_weight.shape, BF),
            pltpu.VMEM((rows, depth), BF),
            pltpu.VMEM((rows, width), BF),
            pltpu.SemaphoreType.DMA((16 + kinds,)),
        ],
        compiler_params=params(32),
        cost_estimate=pl.CostEstimate(
            flops=2 * rows * width * (depth + kinds * channels),
            bytes_accessed=20 * 2**20,
            transcendentals=0,
        ),
    )(places, *blocks, *weights, noisy, embed, gate, scale, shift, next_weight, query_gain, key_gain)


def last_step(places, heads, weights, bases, gates):
    rows, depth = heads[0].shape
    width = gates.shape[1]
    block = 512

    part = depth // 4

    def kernel(places_ref, first_ref, second_ref, *refs):
        weight_refs = refs[:2]
        first_base_ref, second_base_ref, gates_ref, out_ref, held_ref, side_ref, sems = refs[2:]
        copies = weight_copies(weight_refs, held_ref, sems)
        for copy in copies:
            copy.start()
        for k in range(4):
            place = pl.ds(pl.multiple_of(places_ref[k] * part, HEAD_DIM), part)
            side_ref[:rows, place] = first_ref[:, k * part : (k + 1) * part]
            side_ref[rows:, place] = second_ref[:, k * part : (k + 1) * part]
        for column in range(2):
            for copy in copies[8 * column : 8 * column + 8]:
                copy.wait()

            @pl.loop(0, width // 2 // block)
            def _(n):
                place = pl.ds(pl.multiple_of(column * (width // 2) + n * block, block), block)
                update = jnp.dot(side_ref[...], held_ref[:, place], preferred_element_type=F32)
                for m, base_ref in enumerate((first_base_ref, second_base_ref)):
                    out_ref[m, :, place] = (
                        base_ref[:, place].astype(F32)
                        + gates_ref[m : m + 1, place] * update[m * rows : (m + 1) * rows]
                    ).astype(BF)

    whole = pl.BlockSpec(memory_space=pltpu.VMEM)
    return pl.pallas_call(
        kernel,
        in_specs=[pl.BlockSpec(memory_space=pltpu.SMEM)]
        + [whole] * 2
        + [pl.BlockSpec(memory_space=pl.ANY)] * 2
        + [whole] * 3,
        out_specs=whole,
        out_shape=jax.ShapeDtypeStruct((2, rows, width), BF),
        scratch_shapes=[
            pltpu.VMEM((depth, width), BF),
            pltpu.VMEM((2 * rows, depth), BF),
            pltpu.SemaphoreType.DMA((16,)),
        ],
        compiler_params=params(18),
    )(places, *heads, *weights, *bases, gates)


def per_device(
    latent,
    noise_field,
    timestep,
    embed_weight,
    modulate_weight,
    attend_weight,
    query_gain,
    key_gain,
    output_weight,
):
    batches = latent.shape[0]
    patch, width = embed_weight.shape
    local = latent.shape[1] * latent.shape[2] * latent.shape[3]
    section = lax.axis_index("section")
    row = lax.axis_index("row")
    first = section == 0

    def by_section(of_first, of_second):
        return jnp.where(first, of_first, of_second)

    def swapped(array):
        return lax.ppermute(array, "section", SWAP)

    level = signal_level(timestep)[:, None, None, None, None]
    noisy = (
        jnp.sqrt(level) * latent.astype(F32) + jnp.sqrt(1.0 - level) * noise_field.astype(F32)
    ).astype(BF)
    noisy = by_section(noisy[0], noisy[1]).reshape(local, patch)
    features = time_features(timestep, modulate_weight.shape[1]).astype(BF)
    mod_part = jnp.dot(features, modulate_weight[0], preferred_element_type=F32)

    out_own = output_weight[0]
    out_got = swapped(out_own)
    attend_other = lax.ppermute(attend_weight[0], "section", [(1, 0)])
    half = out_own.shape[0] // 2
    out_part = by_section(out_own[:half], out_got[half:])

    mod_rows = mod_part.size // patch
    packed = jnp.concatenate(
        [noisy.astype(F32), mod_part.reshape(mod_rows, patch), jnp.zeros((-mod_rows % 8, patch), F32)]
    )
    packed = gather(packed, shift_z)
    noisy_row = jnp.concatenate([block[:local] for block in packed]).astype(BF)
    mods = [block[local : local + mod_rows].reshape(batches, -1) for block in packed]

    def from_row(b):
        chosen = mods[0]
        for k in (1, 2, 3):
            chosen = jnp.where(row == (b + STEPS[k]) % 4, mods[k], chosen)
        return chosen

    modulation = jnp.concatenate([from_row(b) for b in range(4)], axis=1)
    shift_own = modulation[:, :width]
    scale_own = modulation[:, width : 2 * width]

    out_part, noisy_row = lax.optimization_barrier((out_part, noisy_row))
    out_first = lax.all_gather(out_part, "row", axis=0, tiled=True)

    noisy_x = gather(noisy_row, shift_x)
    noisy_y = gather(noisy_row, shift_y)

    centered = embed_weight.astype(F32)
    centered = centered - jnp.mean(centered, axis=1, keepdims=True)
    gram = (
        jnp.dot(centered, centered.T, preferred_element_type=F32, precision=lax.Precision.HIGHEST)
        / width
    )
    mapped = map_weights(
        embed_weight, scale_own, shift_own, attend_weight[0], [noisy_x[1], noisy_y[1]]
    )
    kinds = mapped.shape[1]
    mapped_other = lax.ppermute(mapped[1], "section", [(0, 1)])
    mapped = by_section(mapped[0], mapped_other)
    bias = mapped[:, patch : patch + 1].astype(F32) + mapped[:, patch + 1 : patch + 2].astype(F32)
    mapped = mapped[:, :patch]

    gains = jnp.concatenate([query_gain, key_gain])
    small = jnp.concatenate([modulation.reshape(-1, patch), gains, jnp.zeros((6, patch), F32)])
    small_other = swapped(small)
    small_first = by_section(small, small_other)
    small_second = by_section(small_other, small)
    mod_rows_all = modulation.size // patch

    def unpack(array):
        mod = array[:mod_rows_all].reshape(batches, -1)
        mod = by_section(mod[:1], mod[1:])
        qg = array[mod_rows_all : mod_rows_all + 1] * QUERY_SCALE
        kg = array[mod_rows_all + 1 : mod_rows_all + 2]
        return mod[:, :width], mod[:, width : 2 * width], mod[:, 2 * width :], qg, kg

    _, _, gate_first, qg_first, kg_first = unpack(small_first)
    shift_second, scale_second, _, qg_second, kg_second = unpack(small_second)

    heads = kinds // 3
    gain_of = (qg_first, kg_first)

    def first_heads(blocks, along):
        weight = jnp.concatenate([mapped[kind * heads + h] for kind, h in along], axis=1)
        bias_row = jnp.concatenate([bias[kind * heads + h] for kind, h in along], axis=1)
        gains_here = jnp.concatenate([gain_of[kind] for kind, h in along if kind < 2])
        return [
            first_projection(block, gram, weight, bias_row, gains_here, [attend_other])
            for block in blocks
        ]

    attended = attention(
        first_heads(noisy_x, ALONG_X), first_heads(noisy_y, ALONG_Y), False, lambda step, sums: []
    )

    blocks = gather(attended, shift_z)
    turned = []
    for block, by in zip(blocks, STEPS):
        order = [
            [k for k in range(4) if (by + STEPS[k] - STEPS[mine]) % 4 == 0][0] for mine in range(4)
        ]
        turned.append(jnp.concatenate([block[k * local : (k + 1) * local] for k in order]))
    out_first, blocks[1] = lax.optimization_barrier((out_first, blocks[1]))
    out_first_other = swapped(out_first)
    out_own, out_got, blocks[3] = lax.optimization_barrier((out_own, out_got, blocks[3]))
    out_part = by_section(out_got[:half], out_own[half:])
    out_second = lax.all_gather(out_part, "row", axis=0, tiled=True)
    places = jnp.stack([(row - by) & 3 for by in STEPS]).astype(jnp.int32)

    def step_first(weights, next_weight):
        return between_layers(
            places,
            turned,
            weights,
            noisy_row,
            embed_weight,
            gate_first,
            scale_second,
            shift_second,
            next_weight,
            qg_second,
            kg_second,
        )

    along_x, along_y, result_first = lax.cond(
        first,
        lambda own, other, next_own, next_other: step_first((own, other), next_other),
        lambda own, other, next_own, next_other: step_first((other, own), next_own),
        out_first,
        out_first_other,
        attend_weight[0],
        attend_other,
    )
    result_other = swapped(result_first)

    out_second_other = []

    def before_second(step, sums):
        if step == 5:
            out_second_other.append(swapped(held_until(out_second, sums)))
        return [result_other] if step == 6 else []

    attended = attention(gather(along_x, shift_x), gather(along_y, shift_y), True, before_second)
    mine = give_back([attended[k * local : (k + 1) * local] for k in range(4)], shift_z)
    mine = jnp.concatenate(mine, axis=1)
    mine_other = lax.ppermute(mine, "section", [(0, 1)])
    places_last = jnp.stack([(row + by) & 3 for by in STEPS]).astype(jnp.int32)
    gates = modulation[:, 2 * width :]

    def finish_first():
        return jnp.stack([result_first, result_other])

    def finish_second():
        return last_step(
            places_last,
            (mine_other, mine),
            (out_second_other[0], out_second),
            (result_other, result_first),
            gates,
        )

    result = lax.cond(first, finish_first, finish_second)
    return result.reshape(1, batches, latent.shape[1], latent.shape[2], latent.shape[3], width)


def solution(mesh):
    return jax.shard_map(
        per_device,
        mesh=mesh,
        in_specs=(
            P(None, "depth", "row", None, None),
            P(None, "depth", "row", None, None),
            P(),
            P(),
            P("section", None, "row"),
            P("section", None, None, "row"),
            P("section", None),
            P("section", None),
            P("section", "row", None),
        ),
        out_specs=P("section", None, "depth", "row", None, None),
        check_vma=False,
    )
```

```python
import math

import jax
import jax.numpy as jnp
from jax import lax
from jax.experimental import pallas as pl
from jax.experimental.pallas import tpu as pltpu
from jax.sharding import PartitionSpec as P

HEAD_DIM = 128
BF = jnp.bfloat16
F32 = jnp.float32

norm_eps = 1e-06
plan_steps = 1000.0
QUERY_SCALE = math.log2(math.e) / math.sqrt(HEAD_DIM)
SWAP = [(0, 1), (1, 0)]
STEPS = (0, 1, -1, 2)


def signal_level(timestep):
    phase = (timestep.astype(F32) / plan_steps + 0.008) / 1.008 * (math.pi / 2)
    return jnp.cos(phase) ** 2


def time_features(timestep, count):
    half = count // 2
    frequency = jnp.exp(-math.log(10000.0) * jnp.arange(half, dtype=F32) / half)
    angles = timestep.astype(F32)[:, None] * frequency[None, :]
    return jnp.concatenate([jnp.cos(angles), jnp.sin(angles)], axis=1)


def shift_x(array, by):
    return lax.ppermute(
        array, "depth", [(y * 4 + x, y * 4 + (x + by) % 4) for y in range(4) for x in range(4)]
    )


def shift_y(array, by):
    return lax.ppermute(
        array, "depth", [(y * 4 + x, (y + by) % 4 * 4 + x) for y in range(4) for x in range(4)]
    )


def shift_z(array, by):
    return lax.ppermute(array, "row", [(z, (z + by) % 4) for z in range(4)])


def gather(array, shift):
    return [array] + [shift(array, by) for by in STEPS[1:]]


def give_back(blocks, shift):
    return [blocks[0]] + [shift(block, -by) for block, by in zip(blocks[1:], STEPS[1:])]


def params(mib):
    return pltpu.CompilerParams(vmem_limit_bytes=mib * 2**20)


def head_norm(values, gain):
    factor = lax.rsqrt(jnp.mean(values * values, axis=1, keepdims=True) + norm_eps)
    return (values * factor * gain).astype(BF)


def map_weights(embed, scale, shift, weight, after):
    patch, width = embed.shape
    batches = scale.shape[0]
    kinds, _, channels = weight.shape
    heads = channels // HEAD_DIM

    def kernel(embed_ref, scale_ref, shift_ref, weight_ref, *refs):
        out_ref, sides_ref = refs[-2:]

        @pl.when(pl.program_id(0) == 0)
        def _():
            values = embed_ref[...].astype(F32)
            values = values - jnp.mean(values, axis=1, keepdims=True)
            for m in range(batches):
                sides_ref[m * patch : (m + 1) * patch] = (
                    values * (1.0 + scale_ref[m : m + 1])
                ).astype(BF)
            sides_ref[batches * patch :] = jnp.concatenate(
                [shift_ref[...], jnp.zeros((16 - batches, width), F32)]
            ).astype(BF)

        mapped = jnp.dot(sides_ref[...], weight_ref[0], preferred_element_type=F32)
        for m in range(batches):
            bias = mapped[batches * patch + m : batches * patch + m + 1]
            upper = bias.astype(BF).astype(F32)
            tail = jnp.concatenate([upper, bias - upper, jnp.zeros((14, channels), F32)]).astype(BF)
            for h in range(heads):
                part = slice(h * HEAD_DIM, (h + 1) * HEAD_DIM)
                out_ref[m, h, :patch] = mapped[m * patch : (m + 1) * patch, part].astype(BF)
                out_ref[m, h, patch:] = tail[:, part]

    return pl.pallas_call(
        kernel,
        grid=(kinds,),
        in_specs=[
            pl.BlockSpec((patch, width), lambda j: (0, 0)),
            pl.BlockSpec((batches, width), lambda j: (0, 0)),
            pl.BlockSpec((batches, width), lambda j: (0, 0)),
            pl.BlockSpec((1, width, channels), lambda j: (j, 0, 0)),
        ]
        + [pl.BlockSpec(memory_space=pl.ANY)] * len(after),
        out_specs=pl.BlockSpec((batches, heads, patch + 16, HEAD_DIM), lambda j: (0, j, 0, 0)),
        out_shape=jax.ShapeDtypeStruct((batches, kinds * heads, patch + 16, HEAD_DIM), BF),
        scratch_shapes=[pltpu.VMEM((batches * patch + 16, width), BF)],
        compiler_params=params(18),
        cost_estimate=pl.CostEstimate(
            flops=2 * batches * patch * width * kinds * channels,
            bytes_accessed=20 * 2**20,
            transcendentals=0,
        ),
    )(embed, scale, shift, weight, *after)


def first_projection(noisy, gram, weight, bias, gains, after):
    rows = noisy.shape[0]
    heads = weight.shape[1] // HEAD_DIM
    normed_heads = gains.shape[0]

    def kernel(noisy_ref, gram_ref, weight_ref, bias_ref, gains_ref, *refs):
        out_ref = refs[-1]
        values = noisy_ref[...].astype(F32)
        spread = jnp.sum(
            jnp.dot(
                values, gram_ref[...], preferred_element_type=F32, precision=lax.Precision.HIGHEST
            )
            * values,
            axis=1,
            keepdims=True,
        )
        scaled = (values * lax.rsqrt(spread + norm_eps)).astype(BF)
        projected = jnp.dot(scaled, weight_ref[...], preferred_element_type=F32) + bias_ref[...]
        for h in range(heads):
            part = projected[:, h * HEAD_DIM : (h + 1) * HEAD_DIM]
            if h < normed_heads:
                out_ref[h] = head_norm(part, gains_ref[h : h + 1])
            else:
                out_ref[h] = part.astype(BF)

    whole = pl.BlockSpec(memory_space=pltpu.VMEM)
    return pl.pallas_call(
        kernel,
        in_specs=[whole] * 5 + [pl.BlockSpec(memory_space=pl.ANY)] * len(after),
        out_specs=whole,
        out_shape=jax.ShapeDtypeStruct((heads, rows, HEAD_DIM), BF),
        compiler_params=params(16),
        cost_estimate=pl.CostEstimate(flops=10**6, bytes_accessed=10**4, transcendentals=0),
    )(noisy, gram, weight, bias, gains, *after)


ALONG_X = ((1, 0), (1, 2), (0, 1), (2, 0), (2, 2))
ALONG_Y = ((0, 0), (0, 2), (1, 1), (2, 1))
HEADS_BY = ((1, 0), (0, 0), (1, 1))


def attend(queries, blocks, after, carry=None, more=False):
    rows = queries[0].shape[1]
    key_rows = blocks[0][0].shape[1]
    count = len(blocks[0])
    keys_total = key_rows * count
    places = (ALONG_X, ALONG_Y)
    carries = [] if carry is None else [carry]

    def kernel(*refs):
        query_refs = refs[:2]
        block_refs = (refs[2 : 2 + count], refs[2 + count : 2 + 2 * count])
        out_refs = refs[-2:-1] if more else refs[-3:-1]
        wide_ref = refs[-1]
        diagonal = lax.broadcasted_iota(jnp.int32, (HEAD_DIM, HEAD_DIM), 0) == lax.broadcasted_iota(
            jnp.int32, (HEAD_DIM, HEAD_DIM), 1
        )
        for h, (along, out_place) in enumerate(HEADS_BY):
            query = query_refs[along][places[along].index((0, h))]
            key_at = places[1 - along].index((1, h))
            value_at = places[1 - along].index((2, h))
            sums = None if carry is None else refs[2 + 2 * count][h]
            for i, ref in enumerate(block_refs[1 - along]):
                wide_ref[h, i * key_rows : (i + 1) * key_rows, :HEAD_DIM] = ref[value_at]
                wide_ref[h, i * key_rows : (i + 1) * key_rows, HEAD_DIM:] = jnp.ones(
                    (key_rows, HEAD_DIM), BF
                )
            for i, ref in enumerate(block_refs[1 - along]):
                scores = lax.dot_general(
                    query, ref[key_at], (((1,), (1,)), ((), ())), preferred_element_type=F32
                )
                weights = jnp.exp2(scores).astype(BF)
                term = jnp.dot(
                    weights,
                    wide_ref[h, i * key_rows : (i + 1) * key_rows],
                    preferred_element_type=F32,
                )
                sums = term if sums is None else sums + term
            if more:
                out_refs[0][h] = sums
                continue
            out_ref = out_refs[1 - along]
            out_ref[out_place, :rows] = sums[:, :HEAD_DIM].astype(BF)
            lines = []
            for part in range(rows // HEAD_DIM):
                square = sums[part * HEAD_DIM : (part + 1) * HEAD_DIM, HEAD_DIM:]
                lines.append(jnp.sum(jnp.where(diagonal, square, 0.0), axis=0, keepdims=True))
            total = jnp.concatenate(lines, axis=0)
            upper = total.astype(BF)
            lower = (total - upper.astype(F32)).astype(BF)
            out_ref[out_place, rows : rows + 16] = jnp.concatenate(
                [upper.astype(F32), lower.astype(F32), jnp.zeros((8, HEAD_DIM), F32)], axis=0
            ).astype(BF)

    whole = pl.BlockSpec(memory_space=pltpu.VMEM)
    return pl.pallas_call(
        kernel,
        in_specs=[whole] * (2 + 2 * count + len(carries))
        + [pl.BlockSpec(memory_space=pl.ANY)] * len(after),
        out_specs=whole if more else [whole] * 2,
        out_shape=jax.ShapeDtypeStruct((len(HEADS_BY), rows, 2 * HEAD_DIM), F32)
        if more
        else [
            jax.ShapeDtypeStruct((2, rows + 16, HEAD_DIM), BF),
            jax.ShapeDtypeStruct((1, rows + 16, HEAD_DIM), BF),
        ],
        scratch_shapes=[pltpu.VMEM((len(HEADS_BY), keys_total, 2 * HEAD_DIM), BF)],
        compiler_params=params(24),
        cost_estimate=pl.CostEstimate(flops=10**6, bytes_accessed=10**4, transcendentals=0),
    )(*queries, *blocks[0], *blocks[1], *carries, *after)


def combine(parts_y, parts_x):
    packed = parts_y[0].shape[1]
    rows = packed - 16
    lines = rows // HEAD_DIM
    count = len(parts_y)
    heads = len(HEADS_BY)

    def kernel(*refs):
        out_ref = refs[-1]
        diagonal = lax.broadcasted_iota(jnp.int32, (HEAD_DIM, HEAD_DIM), 0) == lax.broadcasted_iota(
            jnp.int32, (HEAD_DIM, HEAD_DIM), 1
        )
        for h, (along, at) in enumerate(HEADS_BY):
            sources = refs[:count] if along == 1 else refs[count : 2 * count]
            tail = sources[0][at, rows : rows + 16].astype(F32)
            for ref in sources[1:]:
                tail = tail + ref[at, rows : rows + 16].astype(F32)
            for part in range(lines):
                place = slice(part * HEAD_DIM, (part + 1) * HEAD_DIM)
                numerator = sources[0][at, place].astype(F32)
                for ref in sources[1:]:
                    numerator = numerator + ref[at, place].astype(F32)
                total = tail[part : part + 1] + tail[lines + part : lines + part + 1]
                column = jnp.sum(jnp.where(diagonal, 1.0 / total, 0.0), axis=1, keepdims=True)
                out_ref[place, h * HEAD_DIM : (h + 1) * HEAD_DIM] = (numerator * column).astype(BF)

    return pl.pallas_call(
        kernel,
        out_shape=jax.ShapeDtypeStruct((rows, heads * HEAD_DIM), BF),
        compiler_params=params(16),
    )(*parts_y, *parts_x)


def attention(xs, ys, near_first, before):
    parts_y, parts_x = [None] * 4, [None] * 4
    after, carries, step = [], [None] * 4, 0
    if near_first:
        for k in (2, 1, 0):
            more = before(step, after[0] if after else None)
            carries[k] = attend((xs[k], ys[k]), (xs[:3], ys[:3]), after + more, more=True)
            after = [carries[k]]
            step += 1
    for k in (3, 2, 1, 0):
        blocks = (xs, ys) if carries[k] is None else (xs[3:], ys[3:])
        more = before(step, after[0] if after else None)
        if k == 0:
            more = more + [parts_y[3], parts_x[3]]
        sums_y, sums_x = attend((xs[k], ys[k]), blocks, after + more, carries[k])
        after = [sums_x]
        step += 1
        by = STEPS[k]
        parts_y[k] = shift_y(sums_y, -by) if by else sums_y
        parts_x[k] = shift_x(sums_x, -by) if by else sums_x
    return combine(parts_y, parts_x)


def held_until(array, other):
    return lax.optimization_barrier((array, other))[0]


def weight_copies(weight_refs, held_ref, sems):
    depth, width = held_ref.shape
    part = depth // 8
    half = width // 2
    copies = []
    for column in range(2):
        columns = slice(column * half, (column + 1) * half)
        for k in range(8):
            row, side = divmod(k, 2)
            source = weight_refs[side].at[row * part : (row + 1) * part, columns]
            place = held_ref.at[k * part : (k + 1) * part, columns]
            copies.append(pltpu.make_async_copy(source, place, sems.at[column * 8 + k]))
    return copies


def between_layers(places, blocks, weights, noisy, embed, gate, scale, shift, next_weight, query_gain, key_gain):
    rows, part = blocks[0].shape
    width = gate.shape[1]
    depth = 4 * part
    block = 512
    local = rows // 4
    kinds, _, channels = next_weight.shape
    heads = channels // HEAD_DIM

    def kernel(places_ref, *refs):
        block_refs = refs[:4]
        weight_refs = refs[4:6]
        noisy_ref, embed_ref, gate_ref, scale_ref, shift_ref, next_ref, qg_ref, kg_ref = refs[6:14]
        x_ref, y_ref, own_ref = refs[14:17]
        held_ref, next_held_ref, side_ref, tokens_ref, sems = refs[17:]
        copies = weight_copies(weight_refs, held_ref, sems)
        next_copies = [
            pltpu.make_async_copy(next_ref.at[j], next_held_ref.at[j], sems.at[16 + j])
            for j in range(kinds)
        ]
        for copy in copies:
            copy.start()
        for k in range(4):
            side_ref[:, pl.ds(pl.multiple_of(places_ref[k] * part, HEAD_DIM), part)] = block_refs[k][
                ...
            ]
        for column in range(2):
            for copy in copies[8 * column : 8 * column + 8]:
                copy.wait()
            if column == 0:
                for copy in next_copies:
                    copy.start()

            @pl.loop(0, width // 2 // block)
            def _(n):
                place = pl.ds(pl.multiple_of(column * (width // 2) + n * block, block), block)
                update = jnp.dot(side_ref[...], held_ref[:, place], preferred_element_type=F32)
                base = jnp.dot(noisy_ref[...], embed_ref[:, place], preferred_element_type=F32)
                tokens_ref[:, place] = (
                    base.astype(BF).astype(F32) + gate_ref[:, place] * update
                ).astype(BF)

        own_ref[...] = tokens_ref[:local]

        @pl.loop(0, rows // 128)
        def _(n):
            place = pl.ds(pl.multiple_of(n * 128, 128), 128)
            values = tokens_ref[place].astype(F32)
            values = values - jnp.mean(values, axis=1, keepdims=True)
            spread = jnp.mean(values * values, axis=1, keepdims=True)
            tokens_ref[place] = (
                values * lax.rsqrt(spread + norm_eps) * (1.0 + scale_ref[...]) + shift_ref[...]
            ).astype(BF)

        for kind in range(kinds):
            next_copies[kind].wait()
            projected = jnp.dot(tokens_ref[...], next_held_ref[kind], preferred_element_type=F32)
            for h in range(heads):
                piece = projected[:, h * HEAD_DIM : (h + 1) * HEAD_DIM]
                if kind < 2:
                    piece = head_norm(piece, (qg_ref, kg_ref)[kind][...])
                else:
                    piece = piece.astype(BF)
                if (kind, h) in ALONG_X:
                    x_ref[ALONG_X.index((kind, h))] = piece
                else:
                    y_ref[ALONG_Y.index((kind, h))] = piece

    whole = pl.BlockSpec(memory_space=pltpu.VMEM)
    left = pl.BlockSpec(memory_space=pl.ANY)
    return pl.pallas_call(
        kernel,
        in_specs=[pl.BlockSpec(memory_space=pltpu.SMEM)]
        + [whole] * 4
        + [left] * 2
        + [whole] * 5
        + [left]
        + [whole] * 2,
        out_specs=[whole] * 3,
        out_shape=[
            jax.ShapeDtypeStruct((len(ALONG_X), rows, HEAD_DIM), BF),
            jax.ShapeDtypeStruct((len(ALONG_Y), rows, HEAD_DIM), BF),
            jax.ShapeDtypeStruct((local, width), BF),
        ],
        scratch_shapes=[
            pltpu.VMEM((depth, width), BF),
            pltpu.VMEM(next_weight.shape, BF),
            pltpu.VMEM((rows, depth), BF),
            pltpu.VMEM((rows, width), BF),
            pltpu.SemaphoreType.DMA((16 + kinds,)),
        ],
        compiler_params=params(40),
        cost_estimate=pl.CostEstimate(
            flops=2 * rows * width * (depth + kinds * channels),
            bytes_accessed=20 * 2**20,
            transcendentals=0,
        ),
    )(places, *blocks, *weights, noisy, embed, gate, scale, shift, next_weight, query_gain, key_gain)


def last_step(places, heads, weights, bases, gates):
    rows, depth = heads[0].shape
    width = gates.shape[1]
    block = 512

    part = depth // 4

    def kernel(places_ref, first_ref, second_ref, *refs):
        weight_refs = refs[:2]
        first_base_ref, second_base_ref, gates_ref, out_ref, held_ref, side_ref, sems = refs[2:]
        copies = weight_copies(weight_refs, held_ref, sems)
        for copy in copies:
            copy.start()
        for k in range(4):
            place = pl.ds(pl.multiple_of(places_ref[k] * part, HEAD_DIM), part)
            side_ref[:rows, place] = first_ref[:, k * part : (k + 1) * part]
            side_ref[rows:, place] = second_ref[:, k * part : (k + 1) * part]
        for column in range(2):
            for copy in copies[8 * column : 8 * column + 8]:
                copy.wait()

            @pl.loop(0, width // 2 // block)
            def _(n):
                place = pl.ds(pl.multiple_of(column * (width // 2) + n * block, block), block)
                update = jnp.dot(side_ref[...], held_ref[:, place], preferred_element_type=F32)
                for m, base_ref in enumerate((first_base_ref, second_base_ref)):
                    out_ref[m, :, place] = (
                        base_ref[:, place].astype(F32)
                        + gates_ref[m : m + 1, place] * update[m * rows : (m + 1) * rows]
                    ).astype(BF)

    whole = pl.BlockSpec(memory_space=pltpu.VMEM)
    return pl.pallas_call(
        kernel,
        in_specs=[pl.BlockSpec(memory_space=pltpu.SMEM)]
        + [whole] * 2
        + [pl.BlockSpec(memory_space=pl.ANY)] * 2
        + [whole] * 3,
        out_specs=whole,
        out_shape=jax.ShapeDtypeStruct((2, rows, width), BF),
        scratch_shapes=[
            pltpu.VMEM((depth, width), BF),
            pltpu.VMEM((2 * rows, depth), BF),
            pltpu.SemaphoreType.DMA((16,)),
        ],
        compiler_params=params(18),
    )(places, *heads, *weights, *bases, gates)


def per_device(
    latent,
    noise_field,
    timestep,
    embed_weight,
    modulate_weight,
    attend_weight,
    query_gain,
    key_gain,
    output_weight,
):
    batches = latent.shape[0]
    patch, width = embed_weight.shape
    local = latent.shape[1] * latent.shape[2] * latent.shape[3]
    section = lax.axis_index("section")
    row = lax.axis_index("row")
    first = section == 0

    def by_section(of_first, of_second):
        return jnp.where(first, of_first, of_second)

    def swapped(array):
        return lax.ppermute(array, "section", SWAP)

    level = signal_level(timestep)[:, None, None, None, None]
    noisy = (
        jnp.sqrt(level) * latent.astype(F32) + jnp.sqrt(1.0 - level) * noise_field.astype(F32)
    ).astype(BF)
    noisy = by_section(noisy[0], noisy[1]).reshape(local, patch)
    features = time_features(timestep, modulate_weight.shape[1]).astype(BF)
    mod_part = jnp.dot(features, modulate_weight[0], preferred_element_type=F32)

    out_own = output_weight[0]
    out_got = swapped(out_own)
    attend_other = lax.ppermute(attend_weight[0], "section", [(1, 0)])
    half = out_own.shape[0] // 2
    out_part = by_section(out_own[:half], out_got[half:])

    mod_rows = mod_part.size // patch
    packed = jnp.concatenate(
        [noisy.astype(F32), mod_part.reshape(mod_rows, patch), jnp.zeros((-mod_rows % 8, patch), F32)]
    )
    packed = gather(packed, shift_z)
    noisy_row = jnp.concatenate([block[:local] for block in packed]).astype(BF)
    mods = [block[local : local + mod_rows].reshape(batches, -1) for block in packed]

    def from_row(b):
        chosen = mods[0]
        for k in (1, 2, 3):
            chosen = jnp.where(row == (b + STEPS[k]) % 4, mods[k], chosen)
        return chosen

    modulation = jnp.concatenate([from_row(b) for b in range(4)], axis=1)
    shift_own = modulation[:, :width]
    scale_own = modulation[:, width : 2 * width]

    out_part, noisy_row, scale_own = lax.optimization_barrier((out_part, noisy_row, scale_own))
    out_first = lax.all_gather(out_part, "row", axis=0, tiled=True)

    noisy_x = gather(noisy_row, shift_x)
    noisy_y = gather(noisy_row, shift_y)

    centered = embed_weight.astype(F32)
    centered = centered - jnp.mean(centered, axis=1, keepdims=True)
    gram = (
        jnp.dot(centered, centered.T, preferred_element_type=F32, precision=lax.Precision.HIGHEST)
        / width
    )
    mapped = map_weights(
        embed_weight, scale_own, shift_own, attend_weight[0], []
    )
    kinds = mapped.shape[1]
    mapped_other = lax.ppermute(mapped[1], "section", [(0, 1)])
    mapped = by_section(mapped[0], mapped_other)
    bias = mapped[:, patch : patch + 1].astype(F32) + mapped[:, patch + 1 : patch + 2].astype(F32)
    mapped = mapped[:, :patch]

    gains = jnp.concatenate([query_gain, key_gain])
    small = jnp.concatenate([modulation.reshape(-1, patch), gains, jnp.zeros((6, patch), F32)])
    small_other = swapped(small)
    small_first = by_section(small, small_other)
    small_second = by_section(small_other, small)
    mod_rows_all = modulation.size // patch

    def unpack(array):
        mod = array[:mod_rows_all].reshape(batches, -1)
        mod = by_section(mod[:1], mod[1:])
        qg = array[mod_rows_all : mod_rows_all + 1] * QUERY_SCALE
        kg = array[mod_rows_all + 1 : mod_rows_all + 2]
        return mod[:, :width], mod[:, width : 2 * width], mod[:, 2 * width :], qg, kg

    _, _, gate_first, qg_first, kg_first = unpack(small_first)
    shift_second, scale_second, _, qg_second, kg_second = unpack(small_second)

    heads = kinds // 3
    gain_of = (qg_first, kg_first)

    def first_heads(blocks, along):
        weight = jnp.concatenate([mapped[kind * heads + h] for kind, h in along], axis=1)
        bias_row = jnp.concatenate([bias[kind * heads + h] for kind, h in along], axis=1)
        gains_here = jnp.concatenate([gain_of[kind] for kind, h in along if kind < 2])
        return [
            first_projection(block, gram, weight, bias_row, gains_here, [attend_other])
            for block in blocks
        ]

    attended = attention(
        first_heads(noisy_x, ALONG_X), first_heads(noisy_y, ALONG_Y), False, lambda step, sums: []
    )

    out_first, attended = lax.optimization_barrier((out_first, attended))
    out_first_other = swapped(out_first)
    blocks = gather(attended, shift_z)
    turned = []
    for block, by in zip(blocks, STEPS):
        order = [
            [k for k in range(4) if (by + STEPS[k] - STEPS[mine]) % 4 == 0][0] for mine in range(4)
        ]
        turned.append(jnp.concatenate([block[k * local : (k + 1) * local] for k in order]))
    out_own, out_got, blocks = lax.optimization_barrier((out_own, out_got, blocks))
    out_part = by_section(out_got[:half], out_own[half:])
    out_second = lax.all_gather(out_part, "row", axis=0, tiled=True)
    places = jnp.stack([(row - by) & 3 for by in STEPS]).astype(jnp.int32)

    def step_first(weights, next_weight):
        return between_layers(
            places,
            turned,
            weights,
            noisy_row,
            embed_weight,
            gate_first,
            scale_second,
            shift_second,
            next_weight,
            qg_second,
            kg_second,
        )

    along_x, along_y, result_first = lax.cond(
        first,
        lambda own, other, next_own, next_other: step_first((own, other), next_other),
        lambda own, other, next_own, next_other: step_first((other, own), next_own),
        out_first,
        out_first_other,
        attend_weight[0],
        attend_other,
    )
    result_other = swapped(result_first)

    out_second_other = []

    def before_second(step, sums):
        if step == 5:
            out_second_other.append(swapped(held_until(out_second, sums)))
        return [result_other] if step == 6 else []

    xs = [along_x] + [shift_x(along_x, by) for by in STEPS[1:3]]
    ys = [along_y] + [shift_y(along_y, by) for by in STEPS[1:3]]
    xs, ys = lax.optimization_barrier((xs, ys))
    xs.append(shift_x(xs[0], STEPS[3]))
    ys.append(shift_y(ys[0], STEPS[3]))
    attended = attention(xs, ys, True, before_second)
    mine = give_back([attended[k * local : (k + 1) * local] for k in range(4)], shift_z)
    mine = jnp.concatenate(mine, axis=1)
    mine_other = lax.ppermute(mine, "section", [(0, 1)])
    places_last = jnp.stack([(row + by) & 3 for by in STEPS]).astype(jnp.int32)
    gates = modulation[:, 2 * width :]

    def finish_first():
        return jnp.stack([result_first, result_other])

    def finish_second():
        return last_step(
            places_last,
            (mine_other, mine),
            (out_second_other[0], out_second),
            (result_other, result_first),
            gates,
        )

    result = lax.cond(first, finish_first, finish_second)
    return result.reshape(1, batches, latent.shape[1], latent.shape[2], latent.shape[3], width)


def solution(mesh):
    return jax.shard_map(
        per_device,
        mesh=mesh,
        in_specs=(
            P(None, "depth", "row", None, None),
            P(None, "depth", "row", None, None),
            P(),
            P(),
            P("section", None, "row"),
            P("section", None, None, "row"),
            P("section", None),
            P("section", None),
            P("section", "row", None),
        ),
        out_specs=P("section", None, "depth", "row", None, None),
        check_vma=False,
    )
```

```python
import math

import jax
import jax.numpy as jnp
from jax import lax
from jax.experimental import pallas as pl
from jax.experimental.pallas import tpu as pltpu
from jax.sharding import PartitionSpec as P

HEAD_DIM = 128
BF = jnp.bfloat16
F32 = jnp.float32

norm_eps = 1e-06
plan_steps = 1000.0
QUERY_SCALE = math.log2(math.e) / math.sqrt(HEAD_DIM)
SWAP = [(0, 1), (1, 0)]
STEPS = (0, 1, -1, 2)


def signal_level(timestep):
    phase = (timestep.astype(F32) / plan_steps + 0.008) / 1.008 * (math.pi / 2)
    return jnp.cos(phase) ** 2


def time_features(timestep, count):
    half = count // 2
    frequency = jnp.exp(-math.log(10000.0) * jnp.arange(half, dtype=F32) / half)
    angles = timestep.astype(F32)[:, None] * frequency[None, :]
    return jnp.concatenate([jnp.cos(angles), jnp.sin(angles)], axis=1)


def shift_x(array, by):
    return lax.ppermute(
        array, "depth", [(y * 4 + x, y * 4 + (x + by) % 4) for y in range(4) for x in range(4)]
    )


def shift_y(array, by):
    return lax.ppermute(
        array, "depth", [(y * 4 + x, (y + by) % 4 * 4 + x) for y in range(4) for x in range(4)]
    )


def shift_z(array, by):
    return lax.ppermute(array, "row", [(z, (z + by) % 4) for z in range(4)])


def gather(array, shift):
    return [array] + [shift(array, by) for by in STEPS[1:]]


def give_back(blocks, shift):
    return [blocks[0]] + [shift(block, -by) for block, by in zip(blocks[1:], STEPS[1:])]


def params(mib):
    return pltpu.CompilerParams(vmem_limit_bytes=mib * 2**20)


def head_norm(values, gain):
    factor = lax.rsqrt(jnp.mean(values * values, axis=1, keepdims=True) + norm_eps)
    return (values * factor * gain).astype(BF)


def map_weights(embed, scale, shift, weight, after):
    patch, width = embed.shape
    batches = scale.shape[0]
    kinds, _, channels = weight.shape
    heads = channels // HEAD_DIM

    def kernel(embed_ref, scale_ref, shift_ref, weight_ref, *refs):
        out_ref, sides_ref = refs[-2:]

        @pl.when(pl.program_id(0) == 0)
        def _():
            values = embed_ref[...].astype(F32)
            values = values - jnp.mean(values, axis=1, keepdims=True)
            for m in range(batches):
                sides_ref[m * patch : (m + 1) * patch] = (
                    values * (1.0 + scale_ref[m : m + 1])
                ).astype(BF)
            sides_ref[batches * patch :] = jnp.concatenate(
                [shift_ref[...], jnp.zeros((16 - batches, width), F32)]
            ).astype(BF)

        mapped = jnp.dot(sides_ref[...], weight_ref[0], preferred_element_type=F32)
        for m in range(batches):
            bias = mapped[batches * patch + m : batches * patch + m + 1]
            upper = bias.astype(BF).astype(F32)
            tail = jnp.concatenate([upper, bias - upper, jnp.zeros((14, channels), F32)]).astype(BF)
            for h in range(heads):
                part = slice(h * HEAD_DIM, (h + 1) * HEAD_DIM)
                out_ref[m, h, :patch] = mapped[m * patch : (m + 1) * patch, part].astype(BF)
                out_ref[m, h, patch:] = tail[:, part]

    return pl.pallas_call(
        kernel,
        grid=(kinds,),
        in_specs=[
            pl.BlockSpec((patch, width), lambda j: (0, 0)),
            pl.BlockSpec((batches, width), lambda j: (0, 0)),
            pl.BlockSpec((batches, width), lambda j: (0, 0)),
            pl.BlockSpec((1, width, channels), lambda j: (j, 0, 0)),
        ]
        + [pl.BlockSpec(memory_space=pl.ANY)] * len(after),
        out_specs=pl.BlockSpec((batches, heads, patch + 16, HEAD_DIM), lambda j: (0, j, 0, 0)),
        out_shape=jax.ShapeDtypeStruct((batches, kinds * heads, patch + 16, HEAD_DIM), BF),
        scratch_shapes=[pltpu.VMEM((batches * patch + 16, width), BF)],
        compiler_params=params(18),
        cost_estimate=pl.CostEstimate(
            flops=2 * batches * patch * width * kinds * channels,
            bytes_accessed=20 * 2**20,
            transcendentals=0,
        ),
    )(embed, scale, shift, weight, *after)


def first_projection(noisy, gram, weight, bias, gains, after):
    rows = noisy.shape[0]
    heads = weight.shape[1] // HEAD_DIM
    normed_heads = gains.shape[0]

    def kernel(noisy_ref, gram_ref, weight_ref, bias_ref, gains_ref, *refs):
        out_ref = refs[-1]
        values = noisy_ref[...].astype(F32)
        spread = jnp.sum(
            jnp.dot(
                values, gram_ref[...], preferred_element_type=F32, precision=lax.Precision.HIGHEST
            )
            * values,
            axis=1,
            keepdims=True,
        )
        scaled = (values * lax.rsqrt(spread + norm_eps)).astype(BF)
        projected = jnp.dot(scaled, weight_ref[...], preferred_element_type=F32) + bias_ref[...]
        for h in range(heads):
            part = projected[:, h * HEAD_DIM : (h + 1) * HEAD_DIM]
            if h < normed_heads:
                out_ref[h] = head_norm(part, gains_ref[h : h + 1])
            else:
                out_ref[h] = part.astype(BF)

    whole = pl.BlockSpec(memory_space=pltpu.VMEM)
    return pl.pallas_call(
        kernel,
        in_specs=[whole] * 5 + [pl.BlockSpec(memory_space=pl.ANY)] * len(after),
        out_specs=whole,
        out_shape=jax.ShapeDtypeStruct((heads, rows, HEAD_DIM), BF),
        compiler_params=params(16),
        cost_estimate=pl.CostEstimate(flops=10**6, bytes_accessed=10**4, transcendentals=0),
    )(noisy, gram, weight, bias, gains, *after)


ALONG_X = ((1, 0), (1, 2), (0, 1), (2, 0), (2, 2))
ALONG_Y = ((0, 0), (0, 2), (1, 1), (2, 1))
HEADS_BY = ((1, 0), (0, 0), (1, 1))


def attend(queries, blocks, after, carry=None, more=False, weighty=False):
    rows = queries[0].shape[1]
    key_rows = blocks[0][0].shape[1]
    count = len(blocks[0])
    keys_total = key_rows * count
    places = (ALONG_X, ALONG_Y)
    carries = [] if carry is None else [carry]

    def kernel(*refs):
        query_refs = refs[:2]
        block_refs = (refs[2 : 2 + count], refs[2 + count : 2 + 2 * count])
        out_refs = refs[-2:-1] if more else refs[-3:-1]
        wide_ref = refs[-1]
        diagonal = lax.broadcasted_iota(jnp.int32, (HEAD_DIM, HEAD_DIM), 0) == lax.broadcasted_iota(
            jnp.int32, (HEAD_DIM, HEAD_DIM), 1
        )
        for h, (along, out_place) in enumerate(HEADS_BY):
            query = query_refs[along][places[along].index((0, h))]
            key_at = places[1 - along].index((1, h))
            value_at = places[1 - along].index((2, h))
            sums = None
            for i, ref in enumerate(block_refs[1 - along]):
                wide_ref[h, i * key_rows : (i + 1) * key_rows, :HEAD_DIM] = ref[value_at]
                wide_ref[h, i * key_rows : (i + 1) * key_rows, HEAD_DIM:] = jnp.ones(
                    (key_rows, HEAD_DIM), BF
                )
            for i, ref in enumerate(block_refs[1 - along]):
                scores = lax.dot_general(
                    query, ref[key_at], (((1,), (1,)), ((), ())), preferred_element_type=F32
                )
                weights = jnp.exp2(scores).astype(BF)
                term = jnp.dot(
                    weights,
                    wide_ref[h, i * key_rows : (i + 1) * key_rows],
                    preferred_element_type=F32,
                )
                sums = term if sums is None else sums + term
            numerators = sums[:, :HEAD_DIM]
            lines = []
            for part in range(rows // HEAD_DIM):
                square = sums[part * HEAD_DIM : (part + 1) * HEAD_DIM, HEAD_DIM:]
                lines.append(jnp.sum(jnp.where(diagonal, square, 0.0), axis=0, keepdims=True))
            total = jnp.concatenate(lines, axis=0)
            if carry is not None:
                numerators = numerators + refs[2 + 2 * count][h, :rows]
                total = total + refs[2 + 2 * count][h, rows : rows + 4]
            if more:
                out_refs[0][h, :rows] = numerators
                out_refs[0][h, rows : rows + 8] = jnp.concatenate(
                    [total, jnp.zeros((4, HEAD_DIM), F32)], axis=0
                )
                continue
            out_ref = out_refs[1 - along]
            out_ref[out_place, :rows] = numerators.astype(BF)
            upper = total.astype(BF)
            lower = (total - upper.astype(F32)).astype(BF)
            out_ref[out_place, rows : rows + 16] = jnp.concatenate(
                [upper.astype(F32), lower.astype(F32), jnp.zeros((8, HEAD_DIM), F32)], axis=0
            ).astype(BF)

    whole = pl.BlockSpec(memory_space=pltpu.VMEM)
    return pl.pallas_call(
        kernel,
        in_specs=[whole] * (2 + 2 * count + len(carries))
        + [pl.BlockSpec(memory_space=pl.ANY)] * len(after),
        out_specs=whole if more else [whole] * 2,
        out_shape=jax.ShapeDtypeStruct((len(HEADS_BY), rows + 8, HEAD_DIM), F32)
        if more
        else [
            jax.ShapeDtypeStruct((2, rows + 16, HEAD_DIM), BF),
            jax.ShapeDtypeStruct((1, rows + 16, HEAD_DIM), BF),
        ],
        scratch_shapes=[pltpu.VMEM((len(HEADS_BY), keys_total, 2 * HEAD_DIM), BF)],
        compiler_params=params(24),
        cost_estimate=pl.CostEstimate(
            flops=len(HEADS_BY) * rows * keys_total * HEAD_DIM * 8 if weighty else 10**6,
            bytes_accessed=8 * 2**20 if weighty else 10**4,
            transcendentals=0,
        ),
    )(*queries, *blocks[0], *blocks[1], *carries, *after)


def combine(parts_y, parts_x):
    packed = parts_y[0].shape[1]
    rows = packed - 16
    lines = rows // HEAD_DIM
    count = len(parts_y)
    heads = len(HEADS_BY)

    def kernel(*refs):
        out_ref = refs[-1]
        diagonal = lax.broadcasted_iota(jnp.int32, (HEAD_DIM, HEAD_DIM), 0) == lax.broadcasted_iota(
            jnp.int32, (HEAD_DIM, HEAD_DIM), 1
        )
        for h, (along, at) in enumerate(HEADS_BY):
            sources = refs[:count] if along == 1 else refs[count : 2 * count]
            tail = sources[0][at, rows : rows + 16].astype(F32)
            for ref in sources[1:]:
                tail = tail + ref[at, rows : rows + 16].astype(F32)
            for part in range(lines):
                place = slice(part * HEAD_DIM, (part + 1) * HEAD_DIM)
                numerator = sources[0][at, place].astype(F32)
                for ref in sources[1:]:
                    numerator = numerator + ref[at, place].astype(F32)
                total = tail[part : part + 1] + tail[lines + part : lines + part + 1]
                column = jnp.sum(jnp.where(diagonal, 1.0 / total, 0.0), axis=1, keepdims=True)
                out_ref[place, h * HEAD_DIM : (h + 1) * HEAD_DIM] = (numerator * column).astype(BF)

    return pl.pallas_call(
        kernel,
        out_shape=jax.ShapeDtypeStruct((rows, heads * HEAD_DIM), BF),
        compiler_params=params(16),
    )(*parts_y, *parts_x)


def attention(xs, ys, near_first, before):
    parts_y, parts_x = [None] * 4, [None] * 4
    after, carries, step = [], [None] * 4, 0
    if near_first:
        for k in (2, 1, 0):
            more = before(step, after[0] if after else None)
            carries[k] = attend(
                (xs[k], ys[k]), (xs[:3], ys[:3]), after + more, more=True, weighty=True
            )
            after = [carries[k]]
            step += 1
    for k in (3, 2, 1, 0):
        blocks = (xs, ys) if carries[k] is None else (xs[3:], ys[3:])
        more = before(step, after[0] if after else None)
        if k == 0:
            more = more + [parts_y[3], parts_x[3]]
        sums_y, sums_x = attend(
            (xs[k], ys[k]), blocks, after + more, carries[k], weighty=near_first
        )
        after = [sums_x]
        step += 1
        by = STEPS[k]
        parts_y[k] = shift_y(sums_y, -by) if by else sums_y
        parts_x[k] = shift_x(sums_x, -by) if by else sums_x
    return combine(parts_y, parts_x)


def held_until(array, other):
    return lax.optimization_barrier((array, other))[0]


def weight_copies(weight_refs, held_ref, sems):
    depth, width = held_ref.shape
    part = depth // 8
    half = width // 2
    copies = []
    for column in range(2):
        columns = slice(column * half, (column + 1) * half)
        for k in range(8):
            row, side = divmod(k, 2)
            source = weight_refs[side].at[row * part : (row + 1) * part, columns]
            place = held_ref.at[k * part : (k + 1) * part, columns]
            copies.append(pltpu.make_async_copy(source, place, sems.at[column * 8 + k]))
    return copies


def between_layers(places, blocks, weights, noisy, embed, gate, scale, shift, next_weight, query_gain, key_gain):
    rows, part = blocks[0].shape
    width = gate.shape[1]
    depth = 4 * part
    block = 512
    local = rows // 4
    kinds, _, channels = next_weight.shape
    heads = channels // HEAD_DIM

    def kernel(places_ref, *refs):
        block_refs = refs[:4]
        weight_refs = refs[4:6]
        noisy_ref, embed_ref, gate_ref, scale_ref, shift_ref, next_ref, qg_ref, kg_ref = refs[6:14]
        x_ref, y_ref, own_ref = refs[14:17]
        held_ref, next_held_ref, side_ref, tokens_ref, sems = refs[17:]
        copies = weight_copies(weight_refs, held_ref, sems)
        next_copies = [
            pltpu.make_async_copy(next_ref.at[j], next_held_ref.at[j], sems.at[16 + j])
            for j in range(kinds)
        ]
        for copy in copies:
            copy.start()
        for k in range(4):
            side_ref[:, pl.ds(pl.multiple_of(places_ref[k] * part, HEAD_DIM), part)] = block_refs[k][
                ...
            ]
        for column in range(2):
            for copy in copies[8 * column : 8 * column + 8]:
                copy.wait()
            if column == 0:
                for copy in next_copies:
                    copy.start()

            @pl.loop(0, width // 2 // block)
            def _(n):
                place = pl.ds(pl.multiple_of(column * (width // 2) + n * block, block), block)
                update = jnp.dot(side_ref[...], held_ref[:, place], preferred_element_type=F32)
                base = jnp.dot(noisy_ref[...], embed_ref[:, place], preferred_element_type=F32)
                tokens_ref[:, place] = (
                    base.astype(BF).astype(F32) + gate_ref[:, place] * update
                ).astype(BF)

        own_ref[...] = tokens_ref[:local]

        @pl.loop(0, rows // 128)
        def _(n):
            place = pl.ds(pl.multiple_of(n * 128, 128), 128)
            values = tokens_ref[place].astype(F32)
            values = values - jnp.mean(values, axis=1, keepdims=True)
            spread = jnp.mean(values * values, axis=1, keepdims=True)
            tokens_ref[place] = (
                values * lax.rsqrt(spread + norm_eps) * (1.0 + scale_ref[...]) + shift_ref[...]
            ).astype(BF)

        for kind in range(kinds):
            next_copies[kind].wait()
            projected = jnp.dot(tokens_ref[...], next_held_ref[kind], preferred_element_type=F32)
            for h in range(heads):
                piece = projected[:, h * HEAD_DIM : (h + 1) * HEAD_DIM]
                if kind < 2:
                    piece = head_norm(piece, (qg_ref, kg_ref)[kind][...])
                else:
                    piece = piece.astype(BF)
                if (kind, h) in ALONG_X:
                    x_ref[ALONG_X.index((kind, h))] = piece
                else:
                    y_ref[ALONG_Y.index((kind, h))] = piece

    whole = pl.BlockSpec(memory_space=pltpu.VMEM)
    left = pl.BlockSpec(memory_space=pl.ANY)
    return pl.pallas_call(
        kernel,
        in_specs=[pl.BlockSpec(memory_space=pltpu.SMEM)]
        + [whole] * 4
        + [left] * 2
        + [whole] * 5
        + [left]
        + [whole] * 2,
        out_specs=[whole] * 3,
        out_shape=[
            jax.ShapeDtypeStruct((len(ALONG_X), rows, HEAD_DIM), BF),
            jax.ShapeDtypeStruct((len(ALONG_Y), rows, HEAD_DIM), BF),
            jax.ShapeDtypeStruct((local, width), BF),
        ],
        scratch_shapes=[
            pltpu.VMEM((depth, width), BF),
            pltpu.VMEM(next_weight.shape, BF),
            pltpu.VMEM((rows, depth), BF),
            pltpu.VMEM((rows, width), BF),
            pltpu.SemaphoreType.DMA((16 + kinds,)),
        ],
        compiler_params=params(40),
        cost_estimate=pl.CostEstimate(
            flops=2 * rows * width * (depth + kinds * channels),
            bytes_accessed=20 * 2**20,
            transcendentals=0,
        ),
    )(places, *blocks, *weights, noisy, embed, gate, scale, shift, next_weight, query_gain, key_gain)


def last_step(places, heads, weights, bases, gates):
    rows, depth = heads[0].shape
    width = gates.shape[1]
    block = 512

    part = depth // 4

    def kernel(places_ref, first_ref, second_ref, *refs):
        weight_refs = refs[:2]
        first_base_ref, second_base_ref, gates_ref, out_ref, held_ref, side_ref, sems = refs[2:]
        copies = weight_copies(weight_refs, held_ref, sems)
        for copy in copies:
            copy.start()
        for k in range(4):
            place = pl.ds(pl.multiple_of(places_ref[k] * part, HEAD_DIM), part)
            side_ref[:rows, place] = first_ref[:, k * part : (k + 1) * part]
            side_ref[rows:, place] = second_ref[:, k * part : (k + 1) * part]
        for column in range(2):
            for copy in copies[8 * column : 8 * column + 8]:
                copy.wait()

            @pl.loop(0, width // 2 // block)
            def _(n):
                place = pl.ds(pl.multiple_of(column * (width // 2) + n * block, block), block)
                update = jnp.dot(side_ref[...], held_ref[:, place], preferred_element_type=F32)
                for m, base_ref in enumerate((first_base_ref, second_base_ref)):
                    out_ref[m, :, place] = (
                        base_ref[:, place].astype(F32)
                        + gates_ref[m : m + 1, place] * update[m * rows : (m + 1) * rows]
                    ).astype(BF)

    whole = pl.BlockSpec(memory_space=pltpu.VMEM)
    return pl.pallas_call(
        kernel,
        in_specs=[pl.BlockSpec(memory_space=pltpu.SMEM)]
        + [whole] * 2
        + [pl.BlockSpec(memory_space=pl.ANY)] * 2
        + [whole] * 3,
        out_specs=whole,
        out_shape=jax.ShapeDtypeStruct((2, rows, width), BF),
        scratch_shapes=[
            pltpu.VMEM((depth, width), BF),
            pltpu.VMEM((2 * rows, depth), BF),
            pltpu.SemaphoreType.DMA((16,)),
        ],
        compiler_params=params(18),
    )(places, *heads, *weights, *bases, gates)


def per_device(
    latent,
    noise_field,
    timestep,
    embed_weight,
    modulate_weight,
    attend_weight,
    query_gain,
    key_gain,
    output_weight,
):
    batches = latent.shape[0]
    patch, width = embed_weight.shape
    local = latent.shape[1] * latent.shape[2] * latent.shape[3]
    section = lax.axis_index("section")
    row = lax.axis_index("row")
    first = section == 0

    def by_section(of_first, of_second):
        return jnp.where(first, of_first, of_second)

    def swapped(array):
        return lax.ppermute(array, "section", SWAP)

    level = signal_level(timestep)[:, None, None, None, None]
    noisy = (
        jnp.sqrt(level) * latent.astype(F32) + jnp.sqrt(1.0 - level) * noise_field.astype(F32)
    ).astype(BF)
    noisy = by_section(noisy[0], noisy[1]).reshape(local, patch)
    features = time_features(timestep, modulate_weight.shape[1]).astype(BF)
    mod_part = jnp.dot(features, modulate_weight[0], preferred_element_type=F32)

    out_own = output_weight[0]
    out_got = swapped(out_own)
    attend_other = lax.ppermute(attend_weight[0], "section", [(1, 0)])
    half = out_own.shape[0] // 2
    out_part = by_section(out_own[:half], out_got[half:])

    centered = embed_weight.astype(F32)
    centered = centered - jnp.mean(centered, axis=1, keepdims=True)
    gram = (
        jnp.dot(centered, centered.T, preferred_element_type=F32, precision=lax.Precision.HIGHEST)
        / width
    )
    mod_rows = mod_part.size // patch
    packed = jnp.concatenate(
        [noisy.astype(F32), mod_part.reshape(mod_rows, patch), jnp.zeros((-mod_rows % 8, patch), F32)]
    )
    packed = gather(packed, shift_z)
    noisy_row = jnp.concatenate([block[:local] for block in packed]).astype(BF)
    mods = [block[local : local + mod_rows].reshape(batches, -1) for block in packed]

    def from_row(b):
        chosen = mods[0]
        for k in (1, 2, 3):
            chosen = jnp.where(row == (b + STEPS[k]) % 4, mods[k], chosen)
        return chosen

    modulation = jnp.concatenate([from_row(b) for b in range(4)], axis=1)
    shift_own = modulation[:, :width]
    scale_own = modulation[:, width : 2 * width]

    out_part, gram, noisy_row, scale_own = lax.optimization_barrier(
        (out_part, gram, noisy_row, scale_own)
    )
    out_first = lax.all_gather(out_part, "row", axis=0, tiled=True)

    noisy_x = gather(noisy_row, shift_x)
    noisy_y = gather(noisy_row, shift_y)

    mapped = map_weights(
        embed_weight, scale_own, shift_own, attend_weight[0], [attend_other]
    )
    mapped_all = mapped
    kinds = mapped.shape[1]
    mapped_other = lax.ppermute(mapped[1], "section", [(0, 1)])
    mapped = by_section(mapped[0], mapped_other)
    bias = mapped[:, patch : patch + 1].astype(F32) + mapped[:, patch + 1 : patch + 2].astype(F32)
    mapped = mapped[:, :patch]

    gains = jnp.concatenate([query_gain, key_gain])
    small = jnp.concatenate([modulation.reshape(-1, patch), gains, jnp.zeros((6, patch), F32)])
    small_other = swapped(held_until(small, mapped_all))
    small_first = by_section(small, small_other)
    small_second = by_section(small_other, small)
    mod_rows_all = modulation.size // patch

    def unpack(array):
        mod = array[:mod_rows_all].reshape(batches, -1)
        mod = by_section(mod[:1], mod[1:])
        qg = array[mod_rows_all : mod_rows_all + 1] * QUERY_SCALE
        kg = array[mod_rows_all + 1 : mod_rows_all + 2]
        return mod[:, :width], mod[:, width : 2 * width], mod[:, 2 * width :], qg, kg

    _, _, gate_first, qg_first, kg_first = unpack(small_first)
    shift_second, scale_second, _, qg_second, kg_second = unpack(small_second)

    heads = kinds // 3
    gain_of = (qg_first, kg_first)

    def first_heads(blocks, along):
        weight = jnp.concatenate([mapped[kind * heads + h] for kind, h in along], axis=1)
        bias_row = jnp.concatenate([bias[kind * heads + h] for kind, h in along], axis=1)
        gains_here = jnp.concatenate([gain_of[kind] for kind, h in along if kind < 2])
        return [
            first_projection(block, gram, weight, bias_row, gains_here, [])
            for block in blocks
        ]

    out_first_other = []

    def before_first(step, sums):
        if step == 3:
            out_first_other.append(swapped(held_until(out_first, sums)))
        return []

    attended = attention(
        first_heads(noisy_x, ALONG_X), first_heads(noisy_y, ALONG_Y), False, before_first
    )

    blocks = gather(attended, shift_z)
    turned = []
    for block, by in zip(blocks, STEPS):
        order = [
            [k for k in range(4) if (by + STEPS[k] - STEPS[mine]) % 4 == 0][0] for mine in range(4)
        ]
        turned.append(jnp.concatenate([block[k * local : (k + 1) * local] for k in order]))
    out_own, out_got, blocks = lax.optimization_barrier((out_own, out_got, blocks))
    out_part = by_section(out_got[:half], out_own[half:])
    out_second = lax.all_gather(out_part, "row", axis=0, tiled=True)
    places = jnp.stack([(row - by) & 3 for by in STEPS]).astype(jnp.int32)

    def step_first(weights, next_weight):
        return between_layers(
            places,
            turned,
            weights,
            noisy_row,
            embed_weight,
            gate_first,
            scale_second,
            shift_second,
            next_weight,
            qg_second,
            kg_second,
        )

    along_x, along_y, result_first = lax.cond(
        first,
        lambda own, other, next_own, next_other: step_first((own, other), next_other),
        lambda own, other, next_own, next_other: step_first((other, own), next_own),
        out_first,
        out_first_other[0],
        attend_weight[0],
        attend_other,
    )
    result_other = swapped(result_first)

    out_second_other = []

    def before_second(step, sums):
        if step == 5:
            out_second_other.append(swapped(held_until(out_second, sums)))
        return [result_other] if step == 6 else []

    xs = [along_x] + [shift_x(along_x, by) for by in STEPS[1:3]]
    ys = [along_y] + [shift_y(along_y, by) for by in STEPS[1:3]]
    xs, ys = lax.optimization_barrier((xs, ys))
    xs.append(shift_x(xs[0], STEPS[3]))
    ys.append(shift_y(ys[0], STEPS[3]))
    attended = attention(xs, ys, True, before_second)
    mine = give_back([attended[k * local : (k + 1) * local] for k in range(4)], shift_z)
    mine = jnp.concatenate(mine, axis=1)
    mine_other = lax.ppermute(mine, "section", [(0, 1)])
    places_last = jnp.stack([(row + by) & 3 for by in STEPS]).astype(jnp.int32)
    gates = modulation[:, 2 * width :]

    def finish_first():
        return jnp.stack([result_first, result_other])

    def finish_second():
        return last_step(
            places_last,
            (mine_other, mine),
            (out_second_other[0], out_second),
            (result_other, result_first),
            gates,
        )

    result = lax.cond(first, finish_first, finish_second)
    return result.reshape(1, batches, latent.shape[1], latent.shape[2], latent.shape[3], width)


def solution(mesh):
    return jax.shard_map(
        per_device,
        mesh=mesh,
        in_specs=(
            P(None, "depth", "row", None, None),
            P(None, "depth", "row", None, None),
            P(),
            P(),
            P("section", None, "row"),
            P("section", None, None, "row"),
            P("section", None),
            P("section", None),
            P("section", "row", None),
        ),
        out_specs=P("section", None, "depth", "row", None, None),
        check_vma=False,
    )
```

```python
import math

import jax
import jax.numpy as jnp
from jax import lax
from jax.experimental import pallas as pl
from jax.experimental.pallas import tpu as pltpu
from jax.sharding import PartitionSpec as P

HEAD_DIM = 128
BF = jnp.bfloat16
F32 = jnp.float32

norm_eps = 1e-06
plan_steps = 1000.0
QUERY_SCALE = math.log2(math.e) / math.sqrt(HEAD_DIM)
SWAP = [(0, 1), (1, 0)]
STEPS = (0, 1, -1, 2)


def signal_level(timestep):
    phase = (timestep.astype(F32) / plan_steps + 0.008) / 1.008 * (math.pi / 2)
    return jnp.cos(phase) ** 2


def time_features(timestep, count):
    half = count // 2
    frequency = jnp.exp(-math.log(10000.0) * jnp.arange(half, dtype=F32) / half)
    angles = timestep.astype(F32)[:, None] * frequency[None, :]
    return jnp.concatenate([jnp.cos(angles), jnp.sin(angles)], axis=1)


def shift_x(array, by):
    return lax.ppermute(
        array, "depth", [(y * 4 + x, y * 4 + (x + by) % 4) for y in range(4) for x in range(4)]
    )


def shift_y(array, by):
    return lax.ppermute(
        array, "depth", [(y * 4 + x, (y + by) % 4 * 4 + x) for y in range(4) for x in range(4)]
    )


def shift_z(array, by):
    return lax.ppermute(array, "row", [(z, (z + by) % 4) for z in range(4)])


def gather(array, shift):
    return [array] + [shift(array, by) for by in STEPS[1:]]


def give_back(blocks, shift):
    return [blocks[0]] + [shift(block, -by) for block, by in zip(blocks[1:], STEPS[1:])]


def params(mib):
    return pltpu.CompilerParams(vmem_limit_bytes=mib * 2**20)


def head_norm(values, gain):
    factor = lax.rsqrt(jnp.mean(values * values, axis=1, keepdims=True) + norm_eps)
    return (values * factor * gain).astype(BF)


def map_weights(embed, scale, shift, weight, after):
    patch, width = embed.shape
    batches = scale.shape[0]
    kinds, _, channels = weight.shape
    heads = channels // HEAD_DIM

    def kernel(embed_ref, scale_ref, shift_ref, weight_ref, *refs):
        out_ref, sides_ref = refs[-2:]

        @pl.when(pl.program_id(0) == 0)
        def _():
            values = embed_ref[...].astype(F32)
            values = values - jnp.mean(values, axis=1, keepdims=True)
            for m in range(batches):
                sides_ref[m * patch : (m + 1) * patch] = (
                    values * (1.0 + scale_ref[m : m + 1])
                ).astype(BF)
            sides_ref[batches * patch :] = jnp.concatenate(
                [shift_ref[...], jnp.zeros((16 - batches, width), F32)]
            ).astype(BF)

        mapped = jnp.dot(sides_ref[...], weight_ref[0], preferred_element_type=F32)
        for m in range(batches):
            bias = mapped[batches * patch + m : batches * patch + m + 1]
            upper = bias.astype(BF).astype(F32)
            tail = jnp.concatenate([upper, bias - upper, jnp.zeros((14, channels), F32)]).astype(BF)
            for h in range(heads):
                part = slice(h * HEAD_DIM, (h + 1) * HEAD_DIM)
                out_ref[m, h, :patch] = mapped[m * patch : (m + 1) * patch, part].astype(BF)
                out_ref[m, h, patch:] = tail[:, part]

    return pl.pallas_call(
        kernel,
        grid=(kinds,),
        in_specs=[
            pl.BlockSpec((patch, width), lambda j: (0, 0)),
            pl.BlockSpec((batches, width), lambda j: (0, 0)),
            pl.BlockSpec((batches, width), lambda j: (0, 0)),
            pl.BlockSpec((1, width, channels), lambda j: (j, 0, 0)),
        ]
        + [pl.BlockSpec(memory_space=pl.ANY)] * len(after),
        out_specs=pl.BlockSpec((batches, heads, patch + 16, HEAD_DIM), lambda j: (0, j, 0, 0)),
        out_shape=jax.ShapeDtypeStruct((batches, kinds * heads, patch + 16, HEAD_DIM), BF),
        scratch_shapes=[pltpu.VMEM((batches * patch + 16, width), BF)],
        compiler_params=params(18),
        cost_estimate=pl.CostEstimate(
            flops=2 * batches * patch * width * kinds * channels,
            bytes_accessed=20 * 2**20,
            transcendentals=0,
        ),
    )(embed, scale, shift, weight, *after)


def first_projection(noisy, gram, weight, bias, gains, after):
    rows = noisy.shape[0]
    heads = weight.shape[1] // HEAD_DIM
    normed_heads = gains.shape[0]

    def kernel(noisy_ref, gram_ref, weight_ref, bias_ref, gains_ref, *refs):
        out_ref = refs[-1]
        values = noisy_ref[...].astype(F32)
        spread = jnp.sum(
            jnp.dot(
                values, gram_ref[...], preferred_element_type=F32, precision=lax.Precision.HIGHEST
            )
            * values,
            axis=1,
            keepdims=True,
        )
        scaled = (values * lax.rsqrt(spread + norm_eps)).astype(BF)
        projected = jnp.dot(scaled, weight_ref[...], preferred_element_type=F32) + bias_ref[...]
        for h in range(heads):
            part = projected[:, h * HEAD_DIM : (h + 1) * HEAD_DIM]
            if h < normed_heads:
                out_ref[h] = head_norm(part, gains_ref[h : h + 1])
            else:
                out_ref[h] = part.astype(BF)

    whole = pl.BlockSpec(memory_space=pltpu.VMEM)
    return pl.pallas_call(
        kernel,
        in_specs=[whole] * 5 + [pl.BlockSpec(memory_space=pl.ANY)] * len(after),
        out_specs=whole,
        out_shape=jax.ShapeDtypeStruct((heads, rows, HEAD_DIM), BF),
        compiler_params=params(16),
        cost_estimate=pl.CostEstimate(flops=10**6, bytes_accessed=10**4, transcendentals=0),
    )(noisy, gram, weight, bias, gains, *after)


ALONG_X = ((1, 0), (1, 2), (0, 1), (2, 0), (2, 2))
ALONG_Y = ((0, 0), (0, 2), (1, 1), (2, 1))
HEADS_BY = ((1, 0), (0, 0), (1, 1))


def attend(queries, blocks, after, carry=None, more=False, weighty=False):
    rows = queries[0].shape[1]
    key_rows = blocks[0][0].shape[1]
    count = len(blocks[0])
    keys_total = key_rows * count
    places = (ALONG_X, ALONG_Y)
    carries = [] if carry is None else [carry]

    def kernel(*refs):
        query_refs = refs[:2]
        block_refs = (refs[2 : 2 + count], refs[2 + count : 2 + 2 * count])
        out_refs = refs[-2:-1] if more else refs[-3:-1]
        wide_ref = refs[-1]
        diagonal = lax.broadcasted_iota(jnp.int32, (HEAD_DIM, HEAD_DIM), 0) == lax.broadcasted_iota(
            jnp.int32, (HEAD_DIM, HEAD_DIM), 1
        )
        for h, (along, out_place) in enumerate(HEADS_BY):
            query = query_refs[along][places[along].index((0, h))]
            key_at = places[1 - along].index((1, h))
            value_at = places[1 - along].index((2, h))
            sums = None
            for i, ref in enumerate(block_refs[1 - along]):
                wide_ref[h, i * key_rows : (i + 1) * key_rows, :HEAD_DIM] = ref[value_at]
                wide_ref[h, i * key_rows : (i + 1) * key_rows, HEAD_DIM:] = jnp.ones(
                    (key_rows, HEAD_DIM), BF
                )
            for i, ref in enumerate(block_refs[1 - along]):
                scores = lax.dot_general(
                    query, ref[key_at], (((1,), (1,)), ((), ())), preferred_element_type=F32
                )
                weights = jnp.exp2(scores).astype(BF)
                term = jnp.dot(
                    weights,
                    wide_ref[h, i * key_rows : (i + 1) * key_rows],
                    preferred_element_type=F32,
                )
                sums = term if sums is None else sums + term
            numerators = sums[:, :HEAD_DIM]
            lines = []
            for part in range(rows // HEAD_DIM):
                square = sums[part * HEAD_DIM : (part + 1) * HEAD_DIM, HEAD_DIM:]
                lines.append(jnp.sum(jnp.where(diagonal, square, 0.0), axis=0, keepdims=True))
            total = jnp.concatenate(lines, axis=0)
            if carry is not None:
                numerators = numerators + refs[2 + 2 * count][h, :rows]
                total = total + refs[2 + 2 * count][h, rows : rows + 4]
            if more:
                out_refs[0][h, :rows] = numerators
                out_refs[0][h, rows : rows + 8] = jnp.concatenate(
                    [total, jnp.zeros((4, HEAD_DIM), F32)], axis=0
                )
                continue
            out_ref = out_refs[1 - along]
            out_ref[out_place, :rows] = numerators.astype(BF)
            upper = total.astype(BF)
            lower = (total - upper.astype(F32)).astype(BF)
            out_ref[out_place, rows : rows + 16] = jnp.concatenate(
                [upper.astype(F32), lower.astype(F32), jnp.zeros((8, HEAD_DIM), F32)], axis=0
            ).astype(BF)

    whole = pl.BlockSpec(memory_space=pltpu.VMEM)
    return pl.pallas_call(
        kernel,
        in_specs=[whole] * (2 + 2 * count + len(carries))
        + [pl.BlockSpec(memory_space=pl.ANY)] * len(after),
        out_specs=whole if more else [whole] * 2,
        out_shape=jax.ShapeDtypeStruct((len(HEADS_BY), rows + 8, HEAD_DIM), F32)
        if more
        else [
            jax.ShapeDtypeStruct((2, rows + 16, HEAD_DIM), BF),
            jax.ShapeDtypeStruct((1, rows + 16, HEAD_DIM), BF),
        ],
        scratch_shapes=[pltpu.VMEM((len(HEADS_BY), keys_total, 2 * HEAD_DIM), BF)],
        compiler_params=params(24),
        cost_estimate=pl.CostEstimate(
            flops=len(HEADS_BY) * rows * keys_total * HEAD_DIM * 8 if weighty else 10**6,
            bytes_accessed=8 * 2**20 if weighty else 10**4,
            transcendentals=0,
        ),
    )(*queries, *blocks[0], *blocks[1], *carries, *after)


def combine(parts_y, parts_x):
    packed = parts_y[0].shape[1]
    rows = packed - 16
    lines = rows // HEAD_DIM
    count = len(parts_y)
    heads = len(HEADS_BY)

    def kernel(*refs):
        out_ref = refs[-1]
        diagonal = lax.broadcasted_iota(jnp.int32, (HEAD_DIM, HEAD_DIM), 0) == lax.broadcasted_iota(
            jnp.int32, (HEAD_DIM, HEAD_DIM), 1
        )
        for h, (along, at) in enumerate(HEADS_BY):
            sources = refs[:count] if along == 1 else refs[count : 2 * count]
            tail = sources[0][at, rows : rows + 16].astype(F32)
            for ref in sources[1:]:
                tail = tail + ref[at, rows : rows + 16].astype(F32)
            for part in range(lines):
                place = slice(part * HEAD_DIM, (part + 1) * HEAD_DIM)
                numerator = sources[0][at, place].astype(F32)
                for ref in sources[1:]:
                    numerator = numerator + ref[at, place].astype(F32)
                total = tail[part : part + 1] + tail[lines + part : lines + part + 1]
                column = jnp.sum(jnp.where(diagonal, 1.0 / total, 0.0), axis=1, keepdims=True)
                out_ref[place, h * HEAD_DIM : (h + 1) * HEAD_DIM] = (numerator * column).astype(BF)

    return pl.pallas_call(
        kernel,
        out_shape=jax.ShapeDtypeStruct((rows, heads * HEAD_DIM), BF),
        compiler_params=params(16),
    )(*parts_y, *parts_x)


def attention(xs, ys, near_first, before):
    parts_y, parts_x = [None] * 4, [None] * 4
    after, carries, step = [], [None] * 4, 0
    if near_first:
        for k in (2, 1, 0):
            more = before(step, after[0] if after else None)
            carries[k] = attend(
                (xs[k], ys[k]), (xs[:3], ys[:3]), after + more, more=True, weighty=True
            )
            after = [carries[k]]
            step += 1
    for k in (3, 2, 1, 0):
        blocks = (xs, ys) if carries[k] is None else (xs[3:], ys[3:])
        more = before(step, after[0] if after else None)
        if k == 0:
            more = more + [parts_y[3], parts_x[3]]
        sums_y, sums_x = attend(
            (xs[k], ys[k]), blocks, after + more, carries[k], weighty=near_first
        )
        after = [sums_x]
        step += 1
        by = STEPS[k]
        parts_y[k] = shift_y(sums_y, -by) if by else sums_y
        parts_x[k] = shift_x(sums_x, -by) if by else sums_x
    return combine(parts_y, parts_x)


def held_until(array, other):
    return lax.optimization_barrier((array, other))[0]


def weight_copies(weight_refs, held_ref, sems):
    depth, width = held_ref.shape
    part = depth // 8
    half = width // 2
    copies = []
    for column in range(2):
        columns = slice(column * half, (column + 1) * half)
        for k in range(8):
            row, side = divmod(k, 2)
            source = weight_refs[side].at[row * part : (row + 1) * part, columns]
            place = held_ref.at[k * part : (k + 1) * part, columns]
            copies.append(pltpu.make_async_copy(source, place, sems.at[column * 8 + k]))
    return copies


def between_layers(places, blocks, weights, noisy, embed, gate, scale, shift, next_weight, query_gain, key_gain):
    rows, part = blocks[0].shape
    width = gate.shape[1]
    depth = 4 * part
    block = 512
    local = rows // 4
    kinds, _, channels = next_weight[0].shape
    heads = channels // HEAD_DIM

    def kernel(places_ref, *refs):
        block_refs = refs[:4]
        weight_refs = refs[4:6]
        noisy_ref, embed_ref, gate_ref, scale_ref, shift_ref = refs[6:11]
        next_refs = refs[11:13]
        qg_ref, kg_ref, x_ref, y_ref, own_ref = refs[13:18]
        held_ref, next_held_ref, side_ref, tokens_ref, sems = refs[18:]
        here = places_ref[4]

        def copies_in(section):
            return weight_copies(weight_refs if section == 0 else weight_refs[::-1], held_ref, sems)

        def next_copies_in(section):
            return [
                pltpu.make_async_copy(
                    next_refs[1 - section].at[j], next_held_ref.at[j], sems.at[16 + j]
                )
                for j in range(kinds)
            ]

        copies, next_copies = copies_in(0), next_copies_in(0)
        for section in range(2):

            @pl.when(here == section)
            def _():
                for copy in copies_in(section):
                    copy.start()

        for k in range(4):
            side_ref[:, pl.ds(pl.multiple_of(places_ref[k] * part, HEAD_DIM), part)] = block_refs[k][
                ...
            ]
        for column in range(2):
            for copy in copies[8 * column : 8 * column + 8]:
                copy.wait()
            if column == 0:
                for section in range(2):

                    @pl.when(here == section)
                    def _():
                        for copy in next_copies_in(section):
                            copy.start()

            @pl.loop(0, width // 2 // block)
            def _(n):
                place = pl.ds(pl.multiple_of(column * (width // 2) + n * block, block), block)
                update = jnp.dot(side_ref[...], held_ref[:, place], preferred_element_type=F32)
                base = jnp.dot(noisy_ref[...], embed_ref[:, place], preferred_element_type=F32)
                tokens_ref[:, place] = (
                    base.astype(BF).astype(F32) + gate_ref[:, place] * update
                ).astype(BF)

        own_ref[...] = tokens_ref[:local]

        @pl.loop(0, rows // 128)
        def _(n):
            place = pl.ds(pl.multiple_of(n * 128, 128), 128)
            values = tokens_ref[place].astype(F32)
            values = values - jnp.mean(values, axis=1, keepdims=True)
            spread = jnp.mean(values * values, axis=1, keepdims=True)
            tokens_ref[place] = (
                values * lax.rsqrt(spread + norm_eps) * (1.0 + scale_ref[...]) + shift_ref[...]
            ).astype(BF)

        for kind in range(kinds):
            next_copies[kind].wait()
            projected = jnp.dot(tokens_ref[...], next_held_ref[kind], preferred_element_type=F32)
            for h in range(heads):
                piece = projected[:, h * HEAD_DIM : (h + 1) * HEAD_DIM]
                if kind < 2:
                    piece = head_norm(piece, (qg_ref, kg_ref)[kind][...])
                else:
                    piece = piece.astype(BF)
                if (kind, h) in ALONG_X:
                    x_ref[ALONG_X.index((kind, h))] = piece
                else:
                    y_ref[ALONG_Y.index((kind, h))] = piece

    whole = pl.BlockSpec(memory_space=pltpu.VMEM)
    left = pl.BlockSpec(memory_space=pl.ANY)
    return pl.pallas_call(
        kernel,
        in_specs=[pl.BlockSpec(memory_space=pltpu.SMEM)]
        + [whole] * 4
        + [left] * 2
        + [whole] * 5
        + [left] * 2
        + [whole] * 2,
        out_specs=[whole] * 3,
        out_shape=[
            jax.ShapeDtypeStruct((len(ALONG_X), rows, HEAD_DIM), BF),
            jax.ShapeDtypeStruct((len(ALONG_Y), rows, HEAD_DIM), BF),
            jax.ShapeDtypeStruct((local, width), BF),
        ],
        scratch_shapes=[
            pltpu.VMEM((depth, width), BF),
            pltpu.VMEM(next_weight[0].shape, BF),
            pltpu.VMEM((rows, depth), BF),
            pltpu.VMEM((rows, width), BF),
            pltpu.SemaphoreType.DMA((16 + kinds,)),
        ],
        compiler_params=params(40),
        cost_estimate=pl.CostEstimate(
            flops=2 * rows * width * (depth + kinds * channels),
            bytes_accessed=20 * 2**20,
            transcendentals=0,
        ),
    )(places, *blocks, *weights, noisy, embed, gate, scale, shift, *next_weight, query_gain, key_gain)


def last_step(places, heads, weights, bases, gates):
    rows, depth = heads[0].shape
    width = gates.shape[1]
    block = 512

    part = depth // 4

    def kernel(places_ref, first_ref, second_ref, *refs):
        weight_refs = refs[:2]
        first_base_ref, second_base_ref, gates_ref, out_ref, held_ref, side_ref, sems = refs[2:]
        copies = weight_copies(weight_refs, held_ref, sems)
        for copy in copies:
            copy.start()
        for k in range(4):
            place = pl.ds(pl.multiple_of(places_ref[k] * part, HEAD_DIM), part)
            side_ref[:rows, place] = first_ref[:, k * part : (k + 1) * part]
            side_ref[rows:, place] = second_ref[:, k * part : (k + 1) * part]
        for column in range(2):
            for copy in copies[8 * column : 8 * column + 8]:
                copy.wait()

            @pl.loop(0, width // 2 // block)
            def _(n):
                place = pl.ds(pl.multiple_of(column * (width // 2) + n * block, block), block)
                update = jnp.dot(side_ref[...], held_ref[:, place], preferred_element_type=F32)
                for m, base_ref in enumerate((first_base_ref, second_base_ref)):
                    out_ref[m, :, place] = (
                        base_ref[:, place].astype(F32)
                        + gates_ref[m : m + 1, place] * update[m * rows : (m + 1) * rows]
                    ).astype(BF)

    whole = pl.BlockSpec(memory_space=pltpu.VMEM)
    return pl.pallas_call(
        kernel,
        in_specs=[pl.BlockSpec(memory_space=pltpu.SMEM)]
        + [whole] * 2
        + [pl.BlockSpec(memory_space=pl.ANY)] * 2
        + [whole] * 3,
        out_specs=whole,
        out_shape=jax.ShapeDtypeStruct((2, rows, width), BF),
        scratch_shapes=[
            pltpu.VMEM((depth, width), BF),
            pltpu.VMEM((2 * rows, depth), BF),
            pltpu.SemaphoreType.DMA((16,)),
        ],
        compiler_params=params(18),
    )(places, *heads, *weights, *bases, gates)


def per_device(
    latent,
    noise_field,
    timestep,
    embed_weight,
    modulate_weight,
    attend_weight,
    query_gain,
    key_gain,
    output_weight,
):
    batches = latent.shape[0]
    patch, width = embed_weight.shape
    local = latent.shape[1] * latent.shape[2] * latent.shape[3]
    section = lax.axis_index("section")
    row = lax.axis_index("row")
    first = section == 0

    def by_section(of_first, of_second):
        return jnp.where(first, of_first, of_second)

    def swapped(array):
        return lax.ppermute(array, "section", SWAP)

    level = signal_level(timestep)[:, None, None, None, None]
    noisy = (
        jnp.sqrt(level) * latent.astype(F32) + jnp.sqrt(1.0 - level) * noise_field.astype(F32)
    ).astype(BF)
    noisy = by_section(noisy[0], noisy[1]).reshape(local, patch)
    features = time_features(timestep, modulate_weight.shape[1]).astype(BF)
    mod_part = jnp.dot(features, modulate_weight[0], preferred_element_type=F32)

    out_own = output_weight[0]
    half = out_own.shape[0] // 2
    out_got = swapped(by_section(out_own[half:], out_own[:half]))
    attend_other = lax.ppermute(held_until(attend_weight[0], noisy), "section", [(1, 0)])
    out_part = by_section(out_own[:half], out_got)
    out_part_second = by_section(out_got, out_own[half:])

    centered = embed_weight.astype(F32)
    centered = centered - jnp.mean(centered, axis=1, keepdims=True)
    gram = (
        jnp.dot(centered, centered.T, preferred_element_type=F32, precision=lax.Precision.HIGHEST)
        / width
    )
    mod_rows = mod_part.size // patch
    packed = jnp.concatenate(
        [noisy.astype(F32), mod_part.reshape(mod_rows, patch), jnp.zeros((-mod_rows % 8, patch), F32)]
    )
    packed = gather(packed, shift_z)
    noisy_row = jnp.concatenate([block[:local] for block in packed]).astype(BF)
    mods = [block[local : local + mod_rows].reshape(batches, -1) for block in packed]

    def from_row(b):
        chosen = mods[0]
        for k in (1, 2, 3):
            chosen = jnp.where(row == (b + STEPS[k]) % 4, mods[k], chosen)
        return chosen

    modulation = jnp.concatenate([from_row(b) for b in range(4)], axis=1)
    shift_own = modulation[:, :width]
    scale_own = modulation[:, width : 2 * width]

    out_part, gram, noisy_row, scale_own = lax.optimization_barrier(
        (out_part, gram, noisy_row, scale_own)
    )
    out_first = lax.all_gather(out_part, "row", axis=0, tiled=True)

    noisy_x = gather(noisy_row, shift_x)
    noisy_y = gather(noisy_row, shift_y)

    mapped = map_weights(
        embed_weight, scale_own, shift_own, attend_weight[0], []
    )
    mapped_all = mapped
    kinds = mapped.shape[1]
    mapped_other = lax.ppermute(mapped[1], "section", [(0, 1)])
    mapped = by_section(mapped[0], mapped_other)
    bias = mapped[:, patch : patch + 1].astype(F32) + mapped[:, patch + 1 : patch + 2].astype(F32)
    mapped = mapped[:, :patch]

    gains = jnp.concatenate([query_gain, key_gain])
    small = jnp.concatenate([modulation.reshape(-1, patch), gains, jnp.zeros((6, patch), F32)])
    small_other = swapped(held_until(small, mapped_all))
    small_first = by_section(small, small_other)
    small_second = by_section(small_other, small)
    mod_rows_all = modulation.size // patch

    def unpack(array):
        mod = array[:mod_rows_all].reshape(batches, -1)
        mod = by_section(mod[:1], mod[1:])
        qg = array[mod_rows_all : mod_rows_all + 1] * QUERY_SCALE
        kg = array[mod_rows_all + 1 : mod_rows_all + 2]
        return mod[:, :width], mod[:, width : 2 * width], mod[:, 2 * width :], qg, kg

    _, _, gate_first, qg_first, kg_first = unpack(small_first)
    shift_second, scale_second, _, qg_second, kg_second = unpack(small_second)

    heads = kinds // 3
    gain_of = (qg_first, kg_first)

    def first_heads(blocks, along):
        weight = jnp.concatenate([mapped[kind * heads + h] for kind, h in along], axis=1)
        bias_row = jnp.concatenate([bias[kind * heads + h] for kind, h in along], axis=1)
        gains_here = jnp.concatenate([gain_of[kind] for kind, h in along if kind < 2])
        return [
            first_projection(block, gram, weight, bias_row, gains_here, [])
            for block in blocks
        ]

    out_first_other = []

    def before_first(step, sums):
        if step == 0:
            return [attend_other, out_part_second]
        if step == 3:
            out_first_other.append(swapped(held_until(out_first, sums)))
        return []

    attended = attention(
        first_heads(noisy_x, ALONG_X), first_heads(noisy_y, ALONG_Y), False, before_first
    )

    blocks = gather(attended, shift_z)
    turned = []
    for block, by in zip(blocks, STEPS):
        order = [
            [k for k in range(4) if (by + STEPS[k] - STEPS[mine]) % 4 == 0][0] for mine in range(4)
        ]
        turned.append(jnp.concatenate([block[k * local : (k + 1) * local] for k in order]))
    out_part_second, blocks = lax.optimization_barrier((out_part_second, blocks))
    out_second = lax.all_gather(out_part_second, "row", axis=0, tiled=True)
    places = jnp.stack([(row - by) & 3 for by in STEPS] + [section]).astype(jnp.int32)
    along_x, along_y, result_first = between_layers(
        places,
        turned,
        (out_first, out_first_other[0]),
        noisy_row,
        embed_weight,
        gate_first,
        scale_second,
        shift_second,
        (attend_weight[0], attend_other),
        qg_second,
        kg_second,
    )
    result_other = swapped(result_first)

    out_second_other = []

    def before_second(step, sums):
        if step == 5:
            out_second_other.append(swapped(held_until(out_second, sums)))
        return [result_other] if step == 6 else []

    xs = [along_x] + [shift_x(along_x, by) for by in STEPS[1:3]]
    ys = [along_y] + [shift_y(along_y, by) for by in STEPS[1:3]]
    xs, ys = lax.optimization_barrier((xs, ys))
    xs.append(shift_x(xs[0], STEPS[3]))
    ys.append(shift_y(ys[0], STEPS[3]))
    attended = attention(xs, ys, True, before_second)
    mine = give_back([attended[k * local : (k + 1) * local] for k in range(4)], shift_z)
    mine = jnp.concatenate(mine, axis=1)
    mine_other = lax.ppermute(mine, "section", [(0, 1)])
    places_last = jnp.stack([(row + by) & 3 for by in STEPS]).astype(jnp.int32)
    gates = modulation[:, 2 * width :]

    def finish_first():
        return jnp.stack([result_first, result_other])

    def finish_second():
        return last_step(
            places_last,
            (mine_other, mine),
            (out_second_other[0], out_second),
            (result_other, result_first),
            gates,
        )

    result = lax.cond(first, finish_first, finish_second)
    return result.reshape(1, batches, latent.shape[1], latent.shape[2], latent.shape[3], width)


def solution(mesh):
    return jax.shard_map(
        per_device,
        mesh=mesh,
        in_specs=(
            P(None, "depth", "row", None, None),
            P(None, "depth", "row", None, None),
            P(),
            P(),
            P("section", None, "row"),
            P("section", None, None, "row"),
            P("section", None),
            P("section", None),
            P("section", "row", None),
        ),
        out_specs=P("section", None, "depth", "row", None, None),
        check_vma=False,
    )
```

```python
import math

import jax
import jax.numpy as jnp
from jax import lax
from jax.experimental import pallas as pl
from jax.experimental.pallas import tpu as pltpu
from jax.sharding import PartitionSpec as P

HEAD_DIM = 128
BF = jnp.bfloat16
F32 = jnp.float32

norm_eps = 1e-06
plan_steps = 1000.0
QUERY_SCALE = math.log2(math.e) / math.sqrt(HEAD_DIM)
SWAP = [(0, 1), (1, 0)]
STEPS = (0, 1, -1, 2)


def signal_level(timestep):
    phase = (timestep.astype(F32) / plan_steps + 0.008) / 1.008 * (math.pi / 2)
    return jnp.cos(phase) ** 2


def time_features(timestep, count):
    half = count // 2
    frequency = jnp.exp(-math.log(10000.0) * jnp.arange(half, dtype=F32) / half)
    angles = timestep.astype(F32)[:, None] * frequency[None, :]
    return jnp.concatenate([jnp.cos(angles), jnp.sin(angles)], axis=1)


def shift_x(array, by):
    return lax.ppermute(
        array, "depth", [(y * 4 + x, y * 4 + (x + by) % 4) for y in range(4) for x in range(4)]
    )


def shift_y(array, by):
    return lax.ppermute(
        array, "depth", [(y * 4 + x, (y + by) % 4 * 4 + x) for y in range(4) for x in range(4)]
    )


def shift_z(array, by):
    return lax.ppermute(array, "row", [(z, (z + by) % 4) for z in range(4)])


def gather(array, shift):
    return [array] + [shift(array, by) for by in STEPS[1:]]


def give_back(blocks, shift):
    return [blocks[0]] + [shift(block, -by) for block, by in zip(blocks[1:], STEPS[1:])]


def params(mib):
    return pltpu.CompilerParams(vmem_limit_bytes=mib * 2**20)


def head_norm(values, gain):
    factor = lax.rsqrt(jnp.mean(values * values, axis=1, keepdims=True) + norm_eps)
    return (values * factor * gain).astype(BF)


def map_weights(embed, scale, shift, weight, after):
    patch, width = embed.shape
    batches = scale.shape[0]
    kinds, _, channels = weight.shape
    heads = channels // HEAD_DIM

    def kernel(embed_ref, scale_ref, shift_ref, weight_ref, *refs):
        out_ref, sides_ref = refs[-2:]

        @pl.when(pl.program_id(0) == 0)
        def _():
            values = embed_ref[...].astype(F32)
            values = values - jnp.mean(values, axis=1, keepdims=True)
            for m in range(batches):
                sides_ref[m * patch : (m + 1) * patch] = (
                    values * (1.0 + scale_ref[m : m + 1])
                ).astype(BF)
            sides_ref[batches * patch :] = jnp.concatenate(
                [shift_ref[...], jnp.zeros((16 - batches, width), F32)]
            ).astype(BF)

        mapped = jnp.dot(sides_ref[...], weight_ref[0], preferred_element_type=F32)
        for m in range(batches):
            bias = mapped[batches * patch + m : batches * patch + m + 1]
            upper = bias.astype(BF).astype(F32)
            tail = jnp.concatenate([upper, bias - upper, jnp.zeros((14, channels), F32)]).astype(BF)
            for h in range(heads):
                part = slice(h * HEAD_DIM, (h + 1) * HEAD_DIM)
                out_ref[m, h, :patch] = mapped[m * patch : (m + 1) * patch, part].astype(BF)
                out_ref[m, h, patch:] = tail[:, part]

    return pl.pallas_call(
        kernel,
        grid=(kinds,),
        in_specs=[
            pl.BlockSpec((patch, width), lambda j: (0, 0)),
            pl.BlockSpec((batches, width), lambda j: (0, 0)),
            pl.BlockSpec((batches, width), lambda j: (0, 0)),
            pl.BlockSpec((1, width, channels), lambda j: (j, 0, 0)),
        ]
        + [pl.BlockSpec(memory_space=pl.ANY)] * len(after),
        out_specs=pl.BlockSpec((batches, heads, patch + 16, HEAD_DIM), lambda j: (0, j, 0, 0)),
        out_shape=jax.ShapeDtypeStruct((batches, kinds * heads, patch + 16, HEAD_DIM), BF),
        scratch_shapes=[pltpu.VMEM((batches * patch + 16, width), BF)],
        compiler_params=params(18),
        cost_estimate=pl.CostEstimate(
            flops=2 * batches * patch * width * kinds * channels,
            bytes_accessed=20 * 2**20,
            transcendentals=0,
        ),
    )(embed, scale, shift, weight, *after)


def first_projection(noisy, gram, weight, bias, gains, after):
    rows = noisy.shape[0]
    heads = weight.shape[1] // HEAD_DIM
    normed_heads = gains.shape[0]

    def kernel(noisy_ref, gram_ref, weight_ref, bias_ref, gains_ref, *refs):
        out_ref = refs[-1]
        values = noisy_ref[...].astype(F32)
        spread = jnp.sum(
            jnp.dot(
                values, gram_ref[...], preferred_element_type=F32, precision=lax.Precision.HIGHEST
            )
            * values,
            axis=1,
            keepdims=True,
        )
        scaled = (values * lax.rsqrt(spread + norm_eps)).astype(BF)
        projected = jnp.dot(scaled, weight_ref[...], preferred_element_type=F32) + bias_ref[...]
        for h in range(heads):
            part = projected[:, h * HEAD_DIM : (h + 1) * HEAD_DIM]
            if h < normed_heads:
                out_ref[h] = head_norm(part, gains_ref[h : h + 1])
            else:
                out_ref[h] = part.astype(BF)

    whole = pl.BlockSpec(memory_space=pltpu.VMEM)
    return pl.pallas_call(
        kernel,
        in_specs=[whole] * 5 + [pl.BlockSpec(memory_space=pl.ANY)] * len(after),
        out_specs=whole,
        out_shape=jax.ShapeDtypeStruct((heads, rows, HEAD_DIM), BF),
        compiler_params=params(16),
        cost_estimate=pl.CostEstimate(flops=10**6, bytes_accessed=10**4, transcendentals=0),
    )(noisy, gram, weight, bias, gains, *after)


ALONG_X = ((1, 0), (1, 2), (0, 1), (2, 0), (2, 2))
ALONG_Y = ((0, 0), (0, 2), (1, 1), (2, 1))
HEADS_BY = ((1, 0), (0, 0), (1, 1))


def attend(queries, blocks, after, carry=None, more=False, weighty=False):
    rows = queries[0].shape[1]
    key_rows = blocks[0][0].shape[1]
    count = len(blocks[0])
    keys_total = key_rows * count
    places = (ALONG_X, ALONG_Y)
    carries = [] if carry is None else [carry]

    def kernel(*refs):
        query_refs = refs[:2]
        block_refs = (refs[2 : 2 + count], refs[2 + count : 2 + 2 * count])
        out_refs = refs[-2:-1] if more else refs[-3:-1]
        wide_ref = refs[-1]
        diagonal = lax.broadcasted_iota(jnp.int32, (HEAD_DIM, HEAD_DIM), 0) == lax.broadcasted_iota(
            jnp.int32, (HEAD_DIM, HEAD_DIM), 1
        )
        for h, (along, out_place) in enumerate(HEADS_BY):
            query = query_refs[along][places[along].index((0, h))]
            key_at = places[1 - along].index((1, h))
            value_at = places[1 - along].index((2, h))
            sums = None
            for i, ref in enumerate(block_refs[1 - along]):
                wide_ref[h, i * key_rows : (i + 1) * key_rows, :HEAD_DIM] = ref[value_at]
                wide_ref[h, i * key_rows : (i + 1) * key_rows, HEAD_DIM:] = jnp.ones(
                    (key_rows, HEAD_DIM), BF
                )
            for i, ref in enumerate(block_refs[1 - along]):
                scores = lax.dot_general(
                    query, ref[key_at], (((1,), (1,)), ((), ())), preferred_element_type=F32
                )
                weights = jnp.exp2(scores).astype(BF)
                term = jnp.dot(
                    weights,
                    wide_ref[h, i * key_rows : (i + 1) * key_rows],
                    preferred_element_type=F32,
                )
                sums = term if sums is None else sums + term
            numerators = sums[:, :HEAD_DIM]
            lines = []
            for part in range(rows // HEAD_DIM):
                square = sums[part * HEAD_DIM : (part + 1) * HEAD_DIM, HEAD_DIM:]
                lines.append(jnp.sum(jnp.where(diagonal, square, 0.0), axis=0, keepdims=True))
            total = jnp.concatenate(lines, axis=0)
            if carry is not None:
                numerators = numerators + refs[2 + 2 * count][h, :rows]
                total = total + refs[2 + 2 * count][h, rows : rows + 4]
            if more:
                out_refs[0][h, :rows] = numerators
                out_refs[0][h, rows : rows + 8] = jnp.concatenate(
                    [total, jnp.zeros((4, HEAD_DIM), F32)], axis=0
                )
                continue
            out_ref = out_refs[1 - along]
            out_ref[out_place, :rows] = numerators.astype(BF)
            upper = total.astype(BF)
            lower = (total - upper.astype(F32)).astype(BF)
            out_ref[out_place, rows : rows + 16] = jnp.concatenate(
                [upper.astype(F32), lower.astype(F32), jnp.zeros((8, HEAD_DIM), F32)], axis=0
            ).astype(BF)

    whole = pl.BlockSpec(memory_space=pltpu.VMEM)
    return pl.pallas_call(
        kernel,
        in_specs=[whole] * (2 + 2 * count + len(carries))
        + [pl.BlockSpec(memory_space=pl.ANY)] * len(after),
        out_specs=whole if more else [whole] * 2,
        out_shape=jax.ShapeDtypeStruct((len(HEADS_BY), rows + 8, HEAD_DIM), F32)
        if more
        else [
            jax.ShapeDtypeStruct((2, rows + 16, HEAD_DIM), BF),
            jax.ShapeDtypeStruct((1, rows + 16, HEAD_DIM), BF),
        ],
        scratch_shapes=[pltpu.VMEM((len(HEADS_BY), keys_total, 2 * HEAD_DIM), BF)],
        compiler_params=params(18),
        cost_estimate=pl.CostEstimate(
            flops=len(HEADS_BY) * rows * keys_total * HEAD_DIM * 8 if weighty else 10**6,
            bytes_accessed=8 * 2**20 if weighty else 4 * 2**20,
            transcendentals=0,
        ),
    )(*queries, *blocks[0], *blocks[1], *carries, *after)


def combine(parts_y, parts_x):
    packed = parts_y[0].shape[1]
    rows = packed - 16
    lines = rows // HEAD_DIM
    count = len(parts_y)
    heads = len(HEADS_BY)

    def kernel(*refs):
        out_ref = refs[-1]
        diagonal = lax.broadcasted_iota(jnp.int32, (HEAD_DIM, HEAD_DIM), 0) == lax.broadcasted_iota(
            jnp.int32, (HEAD_DIM, HEAD_DIM), 1
        )
        for h, (along, at) in enumerate(HEADS_BY):
            sources = refs[:count] if along == 1 else refs[count : 2 * count]
            tail = sources[0][at, rows : rows + 16].astype(F32)
            for ref in sources[1:]:
                tail = tail + ref[at, rows : rows + 16].astype(F32)
            for part in range(lines):
                place = slice(part * HEAD_DIM, (part + 1) * HEAD_DIM)
                numerator = sources[0][at, place].astype(F32)
                for ref in sources[1:]:
                    numerator = numerator + ref[at, place].astype(F32)
                total = tail[part : part + 1] + tail[lines + part : lines + part + 1]
                column = jnp.sum(jnp.where(diagonal, 1.0 / total, 0.0), axis=1, keepdims=True)
                out_ref[place, h * HEAD_DIM : (h + 1) * HEAD_DIM] = (numerator * column).astype(BF)

    return pl.pallas_call(
        kernel,
        out_shape=jax.ShapeDtypeStruct((rows, heads * HEAD_DIM), BF),
        compiler_params=params(16),
    )(*parts_y, *parts_x)


def attention(xs, ys, near_first, before):
    parts_y, parts_x = [None] * 4, [None] * 4
    after, carries, step = [], [None] * 4, 0
    if near_first:
        for k in (2, 1, 0):
            more = before(step, after[0] if after else None)
            carries[k] = attend(
                (xs[k], ys[k]), (xs[:3], ys[:3]), after + more, more=True, weighty=True
            )
            after = [carries[k]]
            step += 1
    for k in (3, 2, 1, 0):
        blocks = (xs, ys) if carries[k] is None else (xs[3:], ys[3:])
        more = before(step, after[0] if after else None)
        if k == 0:
            more = more + [parts_y[3], parts_x[3]]
        sums_y, sums_x = attend(
            (xs[k], ys[k]), blocks, after + more, carries[k], weighty=near_first
        )
        after = [sums_x]
        step += 1
        by = STEPS[k]
        parts_y[k] = shift_y(sums_y, -by) if by else sums_y
        parts_x[k] = shift_x(sums_x, -by) if by else sums_x
    return combine(parts_y, parts_x)


def held_until(array, other):
    return lax.optimization_barrier((array, other))[0]


def weight_copies(weight_refs, held_ref, sems, quarter):
    _, depth, columns = held_ref.shape
    part = depth // 8
    slot = quarter % 2
    copies = []
    for k in range(8):
        row, side = divmod(k, 2)
        source = weight_refs[side].at[
            row * part : (row + 1) * part, quarter * columns : (quarter + 1) * columns
        ]
        place = held_ref.at[slot, k * part : (k + 1) * part]
        copies.append(pltpu.make_async_copy(source, place, sems.at[slot * 8 + k]))
    return copies


def between_layers(places, blocks, weights, noisy, embed, gate, scale, shift, next_weight, query_gain, key_gain):
    rows, part = blocks[0].shape
    width = gate.shape[1]
    depth = 4 * part
    block = width // 4
    local = rows // 4
    kinds, _, channels = next_weight[0].shape
    heads = channels // HEAD_DIM

    def kernel(places_ref, *refs):
        block_refs = refs[:4]
        weight_refs = refs[4:6]
        noisy_ref, embed_ref, gate_ref, scale_ref, shift_ref = refs[6:11]
        next_refs = refs[11:13]
        qg_ref, kg_ref, x_ref, y_ref, own_ref = refs[13:18]
        held_ref, next_held_ref, side_ref, tokens_ref, sems = refs[18:]
        here = places_ref[4]

        def start(quarter):
            for section in range(2):

                @pl.when(here == section)
                def _():
                    sources = weight_refs if section == 0 else weight_refs[::-1]
                    for copy in weight_copies(sources, held_ref, sems, quarter):
                        copy.start()

        def next_copy(kind, section):
            slot = kind % 2
            return pltpu.make_async_copy(
                next_refs[1 - section].at[kind], next_held_ref.at[slot], sems.at[16 + slot]
            )

        def start_next(kind):
            for section in range(2):

                @pl.when(here == section)
                def _():
                    next_copy(kind, section).start()

        start(0)
        start(1)
        for k in range(4):
            side_ref[:, pl.ds(pl.multiple_of(places_ref[k] * part, HEAD_DIM), part)] = block_refs[k][
                ...
            ]
        for quarter in range(4):
            for copy in weight_copies(weight_refs, held_ref, sems, quarter):
                copy.wait()
            columns = slice(quarter * block, (quarter + 1) * block)
            update = jnp.dot(side_ref[...], held_ref[quarter % 2], preferred_element_type=F32)
            base = jnp.dot(noisy_ref[...], embed_ref[:, columns], preferred_element_type=F32)
            tokens_ref[:, columns] = (
                base.astype(BF).astype(F32) + gate_ref[:, columns] * update
            ).astype(BF)
            if quarter < 2:
                start(quarter + 2)
                start_next(quarter)

        own_ref[...] = tokens_ref[:local]

        @pl.loop(0, rows // 128)
        def _(n):
            place = pl.ds(pl.multiple_of(n * 128, 128), 128)
            values = tokens_ref[place].astype(F32)
            values = values - jnp.mean(values, axis=1, keepdims=True)
            spread = jnp.mean(values * values, axis=1, keepdims=True)
            tokens_ref[place] = (
                values * lax.rsqrt(spread + norm_eps) * (1.0 + scale_ref[...]) + shift_ref[...]
            ).astype(BF)

        for kind in range(kinds):
            next_copy(kind, 0).wait()
            projected = jnp.dot(
                tokens_ref[...], next_held_ref[kind % 2], preferred_element_type=F32
            )
            if kind == 0:
                start_next(2)
            for h in range(heads):
                piece = projected[:, h * HEAD_DIM : (h + 1) * HEAD_DIM]
                if kind < 2:
                    piece = head_norm(piece, (qg_ref, kg_ref)[kind][...])
                else:
                    piece = piece.astype(BF)
                if (kind, h) in ALONG_X:
                    x_ref[ALONG_X.index((kind, h))] = piece
                else:
                    y_ref[ALONG_Y.index((kind, h))] = piece

    whole = pl.BlockSpec(memory_space=pltpu.VMEM)
    left = pl.BlockSpec(memory_space=pl.ANY)
    return pl.pallas_call(
        kernel,
        in_specs=[pl.BlockSpec(memory_space=pltpu.SMEM)]
        + [whole] * 4
        + [left] * 2
        + [whole] * 5
        + [left] * 2
        + [whole] * 2,
        out_specs=[whole] * 3,
        out_shape=[
            jax.ShapeDtypeStruct((len(ALONG_X), rows, HEAD_DIM), BF),
            jax.ShapeDtypeStruct((len(ALONG_Y), rows, HEAD_DIM), BF),
            jax.ShapeDtypeStruct((local, width), BF),
        ],
        scratch_shapes=[
            pltpu.VMEM((2, depth, block), BF),
            pltpu.VMEM((2,) + next_weight[0].shape[1:], BF),
            pltpu.VMEM((rows, depth), BF),
            pltpu.VMEM((rows, width), BF),
            pltpu.SemaphoreType.DMA((18,)),
        ],
        compiler_params=params(26),
        cost_estimate=pl.CostEstimate(
            flops=2 * rows * width * (depth + kinds * channels),
            bytes_accessed=20 * 2**20,
            transcendentals=0,
        ),
    )(places, *blocks, *weights, noisy, embed, gate, scale, shift, *next_weight, query_gain, key_gain)


def last_step(places, heads, weights, bases, gates):
    rows, depth = heads[0].shape
    width = gates.shape[1]
    block = width // 4
    part = depth // 4

    def kernel(places_ref, first_ref, second_ref, *refs):
        weight_refs = refs[:2]
        first_base_ref, second_base_ref, gates_ref, out_ref, held_ref, side_ref, sems = refs[2:]
        for quarter in range(2):
            for copy in weight_copies(weight_refs, held_ref, sems, quarter):
                copy.start()
        for k in range(4):
            place = pl.ds(pl.multiple_of(places_ref[k] * part, HEAD_DIM), part)
            side_ref[:rows, place] = first_ref[:, k * part : (k + 1) * part]
            side_ref[rows:, place] = second_ref[:, k * part : (k + 1) * part]
        for quarter in range(4):
            for copy in weight_copies(weight_refs, held_ref, sems, quarter):
                copy.wait()
            columns = slice(quarter * block, (quarter + 1) * block)
            update = jnp.dot(side_ref[...], held_ref[quarter % 2], preferred_element_type=F32)
            for m, base_ref in enumerate((first_base_ref, second_base_ref)):
                out_ref[m, :, columns] = (
                    base_ref[:, columns].astype(F32)
                    + gates_ref[m : m + 1, columns] * update[m * rows : (m + 1) * rows]
                ).astype(BF)
            if quarter < 2:
                for copy in weight_copies(weight_refs, held_ref, sems, quarter + 2):
                    copy.start()

    whole = pl.BlockSpec(memory_space=pltpu.VMEM)
    return pl.pallas_call(
        kernel,
        in_specs=[pl.BlockSpec(memory_space=pltpu.SMEM)]
        + [whole] * 2
        + [pl.BlockSpec(memory_space=pl.ANY)] * 2
        + [whole] * 3,
        out_specs=whole,
        out_shape=jax.ShapeDtypeStruct((2, rows, width), BF),
        scratch_shapes=[
            pltpu.VMEM((2, depth, block), BF),
            pltpu.VMEM((2 * rows, depth), BF),
            pltpu.SemaphoreType.DMA((16,)),
        ],
        compiler_params=params(18),
    )(places, *heads, *weights, *bases, gates)


def per_device(
    latent,
    noise_field,
    timestep,
    embed_weight,
    modulate_weight,
    attend_weight,
    query_gain,
    key_gain,
    output_weight,
):
    batches = latent.shape[0]
    patch, width = embed_weight.shape
    local = latent.shape[1] * latent.shape[2] * latent.shape[3]
    section = lax.axis_index("section")
    row = lax.axis_index("row")
    first = section == 0

    def by_section(of_first, of_second):
        return jnp.where(first, of_first, of_second)

    def swapped(array):
        return lax.ppermute(array, "section", SWAP)

    level = signal_level(timestep)[:, None, None, None, None]
    noisy = (
        jnp.sqrt(level) * latent.astype(F32) + jnp.sqrt(1.0 - level) * noise_field.astype(F32)
    ).astype(BF)
    noisy = by_section(noisy[0], noisy[1]).reshape(local, patch)
    features = time_features(timestep, modulate_weight.shape[1]).astype(BF)
    mod_part = jnp.dot(features, modulate_weight[0], preferred_element_type=F32)

    out_own = output_weight[0]
    half = out_own.shape[0] // 2
    out_got = swapped(by_section(out_own[half:], out_own[:half]))
    attend_other = lax.ppermute(held_until(attend_weight[0], noisy), "section", [(1, 0)])
    out_part = by_section(out_own[:half], out_got)
    out_part_second = by_section(out_got, out_own[half:])

    centered = embed_weight.astype(F32)
    centered = centered - jnp.mean(centered, axis=1, keepdims=True)
    gram = (
        jnp.dot(centered, centered.T, preferred_element_type=F32, precision=lax.Precision.HIGHEST)
        / width
    )
    mod_rows = mod_part.size // patch
    packed = jnp.concatenate(
        [noisy.astype(F32), mod_part.reshape(mod_rows, patch), jnp.zeros((-mod_rows % 8, patch), F32)]
    )
    packed = gather(packed, shift_z)
    noisy_row = jnp.concatenate([block[:local] for block in packed]).astype(BF)
    mods = [block[local : local + mod_rows].reshape(batches, -1) for block in packed]

    def from_row(b):
        chosen = mods[0]
        for k in (1, 2, 3):
            chosen = jnp.where(row == (b + STEPS[k]) % 4, mods[k], chosen)
        return chosen

    modulation = jnp.concatenate([from_row(b) for b in range(4)], axis=1)
    shift_own = modulation[:, :width]
    scale_own = modulation[:, width : 2 * width]

    out_part, gram, noisy_row, scale_own = lax.optimization_barrier(
        (out_part, gram, noisy_row, scale_own)
    )
    out_first = lax.all_gather(out_part, "row", axis=0, tiled=True)

    noisy_x = gather(noisy_row, shift_x)
    noisy_y = gather(noisy_row, shift_y)

    mapped = map_weights(
        embed_weight, scale_own, shift_own, attend_weight[0], []
    )
    mapped_all = mapped
    kinds = mapped.shape[1]
    mapped_other = lax.ppermute(mapped[1], "section", [(0, 1)])
    mapped = by_section(mapped[0], mapped_other)
    bias = mapped[:, patch : patch + 1].astype(F32) + mapped[:, patch + 1 : patch + 2].astype(F32)
    mapped = mapped[:, :patch]

    gains = jnp.concatenate([query_gain, key_gain])
    small = jnp.concatenate([modulation.reshape(-1, patch), gains, jnp.zeros((6, patch), F32)])
    small_other = swapped(held_until(small, mapped_all))
    small_first = by_section(small, small_other)
    small_second = by_section(small_other, small)
    mod_rows_all = modulation.size // patch

    def unpack(array):
        mod = array[:mod_rows_all].reshape(batches, -1)
        mod = by_section(mod[:1], mod[1:])
        qg = array[mod_rows_all : mod_rows_all + 1] * QUERY_SCALE
        kg = array[mod_rows_all + 1 : mod_rows_all + 2]
        return mod[:, :width], mod[:, width : 2 * width], mod[:, 2 * width :], qg, kg

    _, _, gate_first, qg_first, kg_first = unpack(small_first)
    shift_second, scale_second, _, qg_second, kg_second = unpack(small_second)

    heads = kinds // 3
    gain_of = (qg_first, kg_first)

    def first_heads(blocks, along):
        weight = jnp.concatenate([mapped[kind * heads + h] for kind, h in along], axis=1)
        bias_row = jnp.concatenate([bias[kind * heads + h] for kind, h in along], axis=1)
        gains_here = jnp.concatenate([gain_of[kind] for kind, h in along if kind < 2])
        return [
            first_projection(block, gram, weight, bias_row, gains_here, [])
            for block in blocks
        ]

    out_first_other = []

    def before_first(step, sums):
        if step == 0:
            return [attend_other, out_part_second]
        if step == 3:
            out_first_other.append(swapped(held_until(out_first, sums)))
        return []

    attended = attention(
        first_heads(noisy_x, ALONG_X), first_heads(noisy_y, ALONG_Y), False, before_first
    )

    blocks = gather(attended, shift_z)
    turned = []
    for block, by in zip(blocks, STEPS):
        order = [
            [k for k in range(4) if (by + STEPS[k] - STEPS[mine]) % 4 == 0][0] for mine in range(4)
        ]
        turned.append(jnp.concatenate([block[k * local : (k + 1) * local] for k in order]))
    out_part_second, blocks = lax.optimization_barrier((out_part_second, blocks))
    out_second = lax.all_gather(out_part_second, "row", axis=0, tiled=True)
    places = jnp.stack([(row - by) & 3 for by in STEPS] + [section]).astype(jnp.int32)
    along_x, along_y, result_first = between_layers(
        places,
        turned,
        (out_first, out_first_other[0]),
        noisy_row,
        embed_weight,
        gate_first,
        scale_second,
        shift_second,
        (attend_weight[0], attend_other),
        qg_second,
        kg_second,
    )
    result_other = swapped(result_first)

    out_second_other = []

    def before_second(step, sums):
        if step == 5:
            out_second_other.append(swapped(held_until(out_second, sums)))
        return [result_other] if step == 6 else []

    xs = [along_x] + [shift_x(along_x, by) for by in STEPS[1:3]]
    ys = [along_y] + [shift_y(along_y, by) for by in STEPS[1:3]]
    xs, ys = lax.optimization_barrier((xs, ys))
    xs.append(shift_x(xs[0], STEPS[3]))
    ys.append(shift_y(ys[0], STEPS[3]))
    attended = attention(xs, ys, True, before_second)
    mine = give_back([attended[k * local : (k + 1) * local] for k in range(4)], shift_z)
    mine = jnp.concatenate(mine, axis=1)
    mine_other = lax.ppermute(mine, "section", [(0, 1)])
    places_last = jnp.stack([(row + by) & 3 for by in STEPS]).astype(jnp.int32)
    gates = modulation[:, 2 * width :]

    def finish_first():
        return jnp.stack([result_first, result_other])

    def finish_second():
        return last_step(
            places_last,
            (mine_other, mine),
            (out_second_other[0], out_second),
            (result_other, result_first),
            gates,
        )

    result = lax.cond(first, finish_first, finish_second)
    return result.reshape(1, batches, latent.shape[1], latent.shape[2], latent.shape[3], width)


def solution(mesh):
    return jax.shard_map(
        per_device,
        mesh=mesh,
        in_specs=(
            P(None, "depth", "row", None, None),
            P(None, "depth", "row", None, None),
            P(),
            P(),
            P("section", None, "row"),
            P("section", None, None, "row"),
            P("section", None),
            P("section", None),
            P("section", "row", None),
        ),
        out_specs=P("section", None, "depth", "row", None, None),
        check_vma=False,
    )
```

```python
import math

import jax
import jax.numpy as jnp
from jax import lax
from jax.experimental import pallas as pl
from jax.experimental.pallas import tpu as pltpu
from jax.sharding import PartitionSpec as P

HEAD_DIM = 128
BF = jnp.bfloat16
F32 = jnp.float32

norm_eps = 1e-06
plan_steps = 1000.0
QUERY_SCALE = math.log2(math.e) / math.sqrt(HEAD_DIM)
SWAP = [(0, 1), (1, 0)]
STEPS = (0, 1, -1, 2)


def signal_level(timestep):
    phase = (timestep.astype(F32) / plan_steps + 0.008) / 1.008 * (math.pi / 2)
    return jnp.cos(phase) ** 2


def time_features(timestep, count):
    half = count // 2
    frequency = jnp.exp(-math.log(10000.0) * jnp.arange(half, dtype=F32) / half)
    angles = timestep.astype(F32)[:, None] * frequency[None, :]
    return jnp.concatenate([jnp.cos(angles), jnp.sin(angles)], axis=1)


def shift_x(array, by):
    return lax.ppermute(
        array, "depth", [(y * 4 + x, y * 4 + (x + by) % 4) for y in range(4) for x in range(4)]
    )


def shift_y(array, by):
    return lax.ppermute(
        array, "depth", [(y * 4 + x, (y + by) % 4 * 4 + x) for y in range(4) for x in range(4)]
    )


def shift_z(array, by):
    return lax.ppermute(array, "row", [(z, (z + by) % 4) for z in range(4)])


def gather(array, shift):
    return [array] + [shift(array, by) for by in STEPS[1:]]


def give_back(blocks, shift):
    return [blocks[0]] + [shift(block, -by) for block, by in zip(blocks[1:], STEPS[1:])]


def params(mib):
    return pltpu.CompilerParams(vmem_limit_bytes=mib * 2**20)


def head_norm(values, gain):
    factor = lax.rsqrt(jnp.mean(values * values, axis=1, keepdims=True) + norm_eps)
    return (values * factor * gain).astype(BF)


def map_weights(embed, scale, shift, weight, after):
    patch, width = embed.shape
    batches = scale.shape[0]
    kinds, _, channels = weight.shape
    heads = channels // HEAD_DIM

    def kernel(embed_ref, scale_ref, shift_ref, weight_ref, *refs):
        out_ref, sides_ref = refs[-2:]

        @pl.when(pl.program_id(0) == 0)
        def _():
            values = embed_ref[...].astype(F32)
            values = values - jnp.mean(values, axis=1, keepdims=True)
            for m in range(batches):
                sides_ref[m * patch : (m + 1) * patch] = (
                    values * (1.0 + scale_ref[m : m + 1])
                ).astype(BF)
            sides_ref[batches * patch :] = jnp.concatenate(
                [shift_ref[...], jnp.zeros((16 - batches, width), F32)]
            ).astype(BF)

        mapped = jnp.dot(sides_ref[...], weight_ref[0], preferred_element_type=F32)
        for m in range(batches):
            bias = mapped[batches * patch + m : batches * patch + m + 1]
            upper = bias.astype(BF).astype(F32)
            tail = jnp.concatenate([upper, bias - upper, jnp.zeros((14, channels), F32)]).astype(BF)
            for h in range(heads):
                part = slice(h * HEAD_DIM, (h + 1) * HEAD_DIM)
                out_ref[m, h, :patch] = mapped[m * patch : (m + 1) * patch, part].astype(BF)
                out_ref[m, h, patch:] = tail[:, part]

    return pl.pallas_call(
        kernel,
        grid=(kinds,),
        in_specs=[
            pl.BlockSpec((patch, width), lambda j: (0, 0)),
            pl.BlockSpec((batches, width), lambda j: (0, 0)),
            pl.BlockSpec((batches, width), lambda j: (0, 0)),
            pl.BlockSpec((1, width, channels), lambda j: (j, 0, 0)),
        ]
        + [pl.BlockSpec(memory_space=pl.ANY)] * len(after),
        out_specs=pl.BlockSpec((batches, heads, patch + 16, HEAD_DIM), lambda j: (0, j, 0, 0)),
        out_shape=jax.ShapeDtypeStruct((batches, kinds * heads, patch + 16, HEAD_DIM), BF),
        scratch_shapes=[pltpu.VMEM((batches * patch + 16, width), BF)],
        compiler_params=params(18),
        cost_estimate=pl.CostEstimate(
            flops=2 * batches * patch * width * kinds * channels,
            bytes_accessed=10**4,
            transcendentals=0,
        ),
    )(embed, scale, shift, weight, *after)


def first_projection(noisy, gram, weight, bias, gains, after):
    rows = noisy.shape[0]
    heads = weight.shape[1] // HEAD_DIM
    normed_heads = gains.shape[0]

    def kernel(noisy_ref, gram_ref, weight_ref, bias_ref, gains_ref, *refs):
        out_ref = refs[-1]
        values = noisy_ref[...].astype(F32)
        spread = jnp.sum(
            jnp.dot(
                values, gram_ref[...], preferred_element_type=F32, precision=lax.Precision.HIGHEST
            )
            * values,
            axis=1,
            keepdims=True,
        )
        scaled = (values * lax.rsqrt(spread + norm_eps)).astype(BF)
        projected = jnp.dot(scaled, weight_ref[...], preferred_element_type=F32) + bias_ref[...]
        for h in range(heads):
            part = projected[:, h * HEAD_DIM : (h + 1) * HEAD_DIM]
            if h < normed_heads:
                out_ref[h] = head_norm(part, gains_ref[h : h + 1])
            else:
                out_ref[h] = part.astype(BF)

    whole = pl.BlockSpec(memory_space=pltpu.VMEM)
    return pl.pallas_call(
        kernel,
        in_specs=[whole] * 5 + [pl.BlockSpec(memory_space=pl.ANY)] * len(after),
        out_specs=whole,
        out_shape=jax.ShapeDtypeStruct((heads, rows, HEAD_DIM), BF),
        compiler_params=params(16),
        cost_estimate=pl.CostEstimate(flops=10**6, bytes_accessed=10**4, transcendentals=0),
    )(noisy, gram, weight, bias, gains, *after)


ALONG_X = ((1, 0), (1, 2), (0, 1), (2, 0), (2, 2))
ALONG_Y = ((0, 0), (0, 2), (1, 1), (2, 1))
HEADS_BY = ((1, 0), (0, 0), (1, 1))


def attend(queries, blocks, after, carry=None, more=False, weighty=False):
    rows = queries[0].shape[1]
    key_rows = blocks[0][0].shape[1]
    count = len(blocks[0])
    keys_total = key_rows * count
    places = (ALONG_X, ALONG_Y)
    carries = [] if carry is None else [carry]

    def kernel(*refs):
        query_refs = refs[:2]
        block_refs = (refs[2 : 2 + count], refs[2 + count : 2 + 2 * count])
        out_refs = refs[-2:-1] if more else refs[-3:-1]
        wide_ref = refs[-1]
        diagonal = lax.broadcasted_iota(jnp.int32, (HEAD_DIM, HEAD_DIM), 0) == lax.broadcasted_iota(
            jnp.int32, (HEAD_DIM, HEAD_DIM), 1
        )
        for h, (along, out_place) in enumerate(HEADS_BY):
            query = query_refs[along][places[along].index((0, h))]
            key_at = places[1 - along].index((1, h))
            value_at = places[1 - along].index((2, h))
            sums = None
            for i, ref in enumerate(block_refs[1 - along]):
                wide_ref[h, i * key_rows : (i + 1) * key_rows, :HEAD_DIM] = ref[value_at]
                wide_ref[h, i * key_rows : (i + 1) * key_rows, HEAD_DIM:] = jnp.ones(
                    (key_rows, HEAD_DIM), BF
                )
            for i, ref in enumerate(block_refs[1 - along]):
                scores = lax.dot_general(
                    query, ref[key_at], (((1,), (1,)), ((), ())), preferred_element_type=F32
                )
                weights = jnp.exp2(scores).astype(BF)
                term = jnp.dot(
                    weights,
                    wide_ref[h, i * key_rows : (i + 1) * key_rows],
                    preferred_element_type=F32,
                )
                sums = term if sums is None else sums + term
            numerators = sums[:, :HEAD_DIM]
            lines = []
            for part in range(rows // HEAD_DIM):
                square = sums[part * HEAD_DIM : (part + 1) * HEAD_DIM, HEAD_DIM:]
                lines.append(jnp.sum(jnp.where(diagonal, square, 0.0), axis=0, keepdims=True))
            total = jnp.concatenate(lines, axis=0)
            if carry is not None:
                numerators = numerators + refs[2 + 2 * count][h, :rows]
                total = total + refs[2 + 2 * count][h, rows : rows + 4]
            if more:
                out_refs[0][h, :rows] = numerators
                out_refs[0][h, rows : rows + 8] = jnp.concatenate(
                    [total, jnp.zeros((4, HEAD_DIM), F32)], axis=0
                )
                continue
            out_ref = out_refs[1 - along]
            out_ref[out_place, :rows] = numerators.astype(BF)
            upper = total.astype(BF)
            lower = (total - upper.astype(F32)).astype(BF)
            out_ref[out_place, rows : rows + 16] = jnp.concatenate(
                [upper.astype(F32), lower.astype(F32), jnp.zeros((8, HEAD_DIM), F32)], axis=0
            ).astype(BF)

    whole = pl.BlockSpec(memory_space=pltpu.VMEM)
    return pl.pallas_call(
        kernel,
        in_specs=[whole] * (2 + 2 * count + len(carries))
        + [pl.BlockSpec(memory_space=pl.ANY)] * len(after),
        out_specs=whole if more else [whole] * 2,
        out_shape=jax.ShapeDtypeStruct((len(HEADS_BY), rows + 8, HEAD_DIM), F32)
        if more
        else [
            jax.ShapeDtypeStruct((2, rows + 16, HEAD_DIM), BF),
            jax.ShapeDtypeStruct((1, rows + 16, HEAD_DIM), BF),
        ],
        scratch_shapes=[pltpu.VMEM((len(HEADS_BY), keys_total, 2 * HEAD_DIM), BF)],
        compiler_params=params(24),
        cost_estimate=pl.CostEstimate(
            flops=len(HEADS_BY) * rows * keys_total * HEAD_DIM * 8 if weighty else 10**6,
            bytes_accessed=8 * 2**20 if weighty else 10**4,
            transcendentals=0,
        ),
    )(*queries, *blocks[0], *blocks[1], *carries, *after)


def combine(parts_y, parts_x):
    packed = parts_y[0].shape[1]
    rows = packed - 16
    lines = rows // HEAD_DIM
    count = len(parts_y)
    heads = len(HEADS_BY)

    def kernel(*refs):
        out_ref = refs[-1]
        diagonal = lax.broadcasted_iota(jnp.int32, (HEAD_DIM, HEAD_DIM), 0) == lax.broadcasted_iota(
            jnp.int32, (HEAD_DIM, HEAD_DIM), 1
        )
        for h, (along, at) in enumerate(HEADS_BY):
            sources = refs[:count] if along == 1 else refs[count : 2 * count]
            tail = sources[0][at, rows : rows + 16].astype(F32)
            for ref in sources[1:]:
                tail = tail + ref[at, rows : rows + 16].astype(F32)
            for part in range(lines):
                place = slice(part * HEAD_DIM, (part + 1) * HEAD_DIM)
                numerator = sources[0][at, place].astype(F32)
                for ref in sources[1:]:
                    numerator = numerator + ref[at, place].astype(F32)
                total = tail[part : part + 1] + tail[lines + part : lines + part + 1]
                column = jnp.sum(jnp.where(diagonal, 1.0 / total, 0.0), axis=1, keepdims=True)
                out_ref[place, h * HEAD_DIM : (h + 1) * HEAD_DIM] = (numerator * column).astype(BF)

    return pl.pallas_call(
        kernel,
        out_shape=jax.ShapeDtypeStruct((rows, heads * HEAD_DIM), BF),
        compiler_params=params(16),
    )(*parts_y, *parts_x)


def attention(xs, ys, near_first, before):
    parts_y, parts_x = [None] * 4, [None] * 4
    after, carries, step = [], [None] * 4, 0
    if near_first:
        for k in (2, 1, 0):
            more = before(step, after[0] if after else None)
            carries[k] = attend(
                (xs[k], ys[k]), (xs[:3], ys[:3]), after + more, more=True, weighty=True
            )
            after = [carries[k]]
            step += 1
    for k in (3, 2, 1, 0):
        blocks = (xs, ys) if carries[k] is None else (xs[3:], ys[3:])
        more = before(step, after[0] if after else None)
        if k == 0:
            more = more + [parts_y[3], parts_x[3]]
        sums_y, sums_x = attend(
            (xs[k], ys[k]), blocks, after + more, carries[k], weighty=near_first
        )
        after = [sums_x]
        step += 1
        by = STEPS[k]
        parts_y[k] = shift_y(sums_y, -by) if by else sums_y
        parts_x[k] = shift_x(sums_x, -by) if by else sums_x
    return combine(parts_y, parts_x)


def held_until(array, other):
    return lax.optimization_barrier((array, other))[0]


def weight_copies(weight_refs, held_ref, sems):
    depth, width = held_ref.shape
    part = depth // 8
    half = width // 2
    copies = []
    for column in range(2):
        columns = slice(column * half, (column + 1) * half)
        for k in range(8):
            row, side = divmod(k, 2)
            source = weight_refs[side].at[row * part : (row + 1) * part, columns]
            place = held_ref.at[k * part : (k + 1) * part, columns]
            copies.append(pltpu.make_async_copy(source, place, sems.at[column * 8 + k]))
    return copies


def between_layers(places, blocks, weights, noisy, embed, gate, scale, shift, next_weight, query_gain, key_gain):
    rows, part = blocks[0].shape
    width = gate.shape[1]
    depth = 4 * part
    block = 512
    local = rows // 4
    kinds, _, channels = next_weight[0].shape
    heads = channels // HEAD_DIM

    def kernel(places_ref, *refs):
        block_refs = refs[:4]
        weight_refs = refs[4:6]
        noisy_ref, embed_ref, gate_ref, scale_ref, shift_ref = refs[6:11]
        next_refs = refs[11:13]
        qg_ref, kg_ref, x_ref, y_ref, own_ref = refs[13:18]
        held_ref, next_held_ref, side_ref, tokens_ref, sems = refs[18:]
        here = places_ref[4]

        def copies_in(section):
            return weight_copies(weight_refs if section == 0 else weight_refs[::-1], held_ref, sems)

        def next_copies_in(section):
            return [
                pltpu.make_async_copy(
                    next_refs[1 - section].at[j], next_held_ref.at[j], sems.at[16 + j]
                )
                for j in range(kinds)
            ]

        copies, next_copies = copies_in(0), next_copies_in(0)
        for section in range(2):

            @pl.when(here == section)
            def _():
                for copy in copies_in(section):
                    copy.start()

        for k in range(4):
            side_ref[:, pl.ds(pl.multiple_of(places_ref[k] * part, HEAD_DIM), part)] = block_refs[k][
                ...
            ]
        for column in range(2):
            for copy in copies[8 * column : 8 * column + 8]:
                copy.wait()
            if column == 0:
                for section in range(2):

                    @pl.when(here == section)
                    def _():
                        for copy in next_copies_in(section):
                            copy.start()

            @pl.loop(0, width // 2 // block)
            def _(n):
                place = pl.ds(pl.multiple_of(column * (width // 2) + n * block, block), block)
                update = jnp.dot(side_ref[...], held_ref[:, place], preferred_element_type=F32)
                base = jnp.dot(noisy_ref[...], embed_ref[:, place], preferred_element_type=F32)
                tokens_ref[:, place] = (
                    base.astype(BF).astype(F32) + gate_ref[:, place] * update
                ).astype(BF)

        own_ref[...] = tokens_ref[:local]

        @pl.loop(0, rows // 128)
        def _(n):
            place = pl.ds(pl.multiple_of(n * 128, 128), 128)
            values = tokens_ref[place].astype(F32)
            values = values - jnp.mean(values, axis=1, keepdims=True)
            spread = jnp.mean(values * values, axis=1, keepdims=True)
            tokens_ref[place] = (
                values * lax.rsqrt(spread + norm_eps) * (1.0 + scale_ref[...]) + shift_ref[...]
            ).astype(BF)

        for kind in range(kinds):
            next_copies[kind].wait()
            projected = jnp.dot(tokens_ref[...], next_held_ref[kind], preferred_element_type=F32)
            for h in range(heads):
                piece = projected[:, h * HEAD_DIM : (h + 1) * HEAD_DIM]
                if kind < 2:
                    piece = head_norm(piece, (qg_ref, kg_ref)[kind][...])
                else:
                    piece = piece.astype(BF)
                if (kind, h) in ALONG_X:
                    x_ref[ALONG_X.index((kind, h))] = piece
                else:
                    y_ref[ALONG_Y.index((kind, h))] = piece

    whole = pl.BlockSpec(memory_space=pltpu.VMEM)
    left = pl.BlockSpec(memory_space=pl.ANY)
    return pl.pallas_call(
        kernel,
        in_specs=[pl.BlockSpec(memory_space=pltpu.SMEM)]
        + [whole] * 4
        + [left] * 2
        + [whole] * 5
        + [left] * 2
        + [whole] * 2,
        out_specs=[whole] * 3,
        out_shape=[
            jax.ShapeDtypeStruct((len(ALONG_X), rows, HEAD_DIM), BF),
            jax.ShapeDtypeStruct((len(ALONG_Y), rows, HEAD_DIM), BF),
            jax.ShapeDtypeStruct((local, width), BF),
        ],
        scratch_shapes=[
            pltpu.VMEM((depth, width), BF),
            pltpu.VMEM(next_weight[0].shape, BF),
            pltpu.VMEM((rows, depth), BF),
            pltpu.VMEM((rows, width), BF),
            pltpu.SemaphoreType.DMA((16 + kinds,)),
        ],
        compiler_params=params(40),
        cost_estimate=pl.CostEstimate(
            flops=2 * rows * width * (depth + kinds * channels),
            bytes_accessed=10**4,
            transcendentals=0,
        ),
    )(places, *blocks, *weights, noisy, embed, gate, scale, shift, *next_weight, query_gain, key_gain)


def last_step(places, heads, weights, bases, gates):
    rows, depth = heads[0].shape
    width = gates.shape[1]
    block = 512

    part = depth // 4

    def kernel(places_ref, first_ref, second_ref, *refs):
        weight_refs = refs[:2]
        first_base_ref, second_base_ref, gates_ref, out_ref, held_ref, side_ref, sems = refs[2:]
        copies = weight_copies(weight_refs, held_ref, sems)
        for copy in copies:
            copy.start()
        for k in range(4):
            place = pl.ds(pl.multiple_of(places_ref[k] * part, HEAD_DIM), part)
            side_ref[:rows, place] = first_ref[:, k * part : (k + 1) * part]
            side_ref[rows:, place] = second_ref[:, k * part : (k + 1) * part]
        for column in range(2):
            for copy in copies[8 * column : 8 * column + 8]:
                copy.wait()

            @pl.loop(0, width // 2 // block)
            def _(n):
                place = pl.ds(pl.multiple_of(column * (width // 2) + n * block, block), block)
                update = jnp.dot(side_ref[...], held_ref[:, place], preferred_element_type=F32)
                for m, base_ref in enumerate((first_base_ref, second_base_ref)):
                    out_ref[m, :, place] = (
                        base_ref[:, place].astype(F32)
                        + gates_ref[m : m + 1, place] * update[m * rows : (m + 1) * rows]
                    ).astype(BF)

    whole = pl.BlockSpec(memory_space=pltpu.VMEM)
    return pl.pallas_call(
        kernel,
        in_specs=[pl.BlockSpec(memory_space=pltpu.SMEM)]
        + [whole] * 2
        + [pl.BlockSpec(memory_space=pl.ANY)] * 2
        + [whole] * 3,
        out_specs=whole,
        out_shape=jax.ShapeDtypeStruct((2, rows, width), BF),
        scratch_shapes=[
            pltpu.VMEM((depth, width), BF),
            pltpu.VMEM((2 * rows, depth), BF),
            pltpu.SemaphoreType.DMA((16,)),
        ],
        compiler_params=params(18),
    )(places, *heads, *weights, *bases, gates)


def per_device(
    latent,
    noise_field,
    timestep,
    embed_weight,
    modulate_weight,
    attend_weight,
    query_gain,
    key_gain,
    output_weight,
):
    batches = latent.shape[0]
    patch, width = embed_weight.shape
    local = latent.shape[1] * latent.shape[2] * latent.shape[3]
    section = lax.axis_index("section")
    row = lax.axis_index("row")
    first = section == 0

    def by_section(of_first, of_second):
        return jnp.where(first, of_first, of_second)

    def swapped(array):
        return lax.ppermute(array, "section", SWAP)

    level = signal_level(timestep)[:, None, None, None, None]
    noisy = (
        jnp.sqrt(level) * latent.astype(F32) + jnp.sqrt(1.0 - level) * noise_field.astype(F32)
    ).astype(BF)
    noisy = by_section(noisy[0], noisy[1]).reshape(local, patch)
    features = time_features(timestep, modulate_weight.shape[1]).astype(BF)
    mod_part = jnp.dot(features, modulate_weight[0], preferred_element_type=F32)

    out_own = output_weight[0]
    half = out_own.shape[0] // 2
    out_got = swapped(by_section(out_own[half:], out_own[:half]))
    attend_other = lax.ppermute(attend_weight[0], "section", [(1, 0)])
    out_part = by_section(out_own[:half], out_got)
    out_part_second = by_section(out_got, out_own[half:])

    centered = embed_weight.astype(F32)
    centered = centered - jnp.mean(centered, axis=1, keepdims=True)
    gram = (
        jnp.dot(centered, centered.T, preferred_element_type=F32, precision=lax.Precision.HIGHEST)
        / width
    )
    mod_rows = mod_part.size // patch
    packed = jnp.concatenate(
        [noisy.astype(F32), mod_part.reshape(mod_rows, patch), jnp.zeros((-mod_rows % 8, patch), F32)]
    )
    packed = gather(packed, shift_z)
    noisy_row = jnp.concatenate([block[:local] for block in packed]).astype(BF)
    mods = [block[local : local + mod_rows].reshape(batches, -1) for block in packed]

    def from_row(b):
        chosen = mods[0]
        for k in (1, 2, 3):
            chosen = jnp.where(row == (b + STEPS[k]) % 4, mods[k], chosen)
        return chosen

    modulation = jnp.concatenate([from_row(b) for b in range(4)], axis=1)
    shift_own = modulation[:, :width]
    scale_own = modulation[:, width : 2 * width]

    out_part, gram, noisy_row, scale_own = lax.optimization_barrier(
        (out_part, gram, noisy_row, scale_own)
    )
    out_first = lax.all_gather(out_part, "row", axis=0, tiled=True)

    noisy_x = gather(noisy_row, shift_x)
    noisy_y = gather(noisy_row, shift_y)

    mapped = map_weights(
        embed_weight, scale_own, shift_own, attend_weight[0], []
    )
    mapped_all = mapped
    kinds = mapped.shape[1]
    mapped_other = lax.ppermute(mapped[1], "section", [(0, 1)])
    mapped = by_section(mapped[0], mapped_other)
    bias = mapped[:, patch : patch + 1].astype(F32) + mapped[:, patch + 1 : patch + 2].astype(F32)
    mapped = mapped[:, :patch]

    gains = jnp.concatenate([query_gain, key_gain])
    small = jnp.concatenate([modulation.reshape(-1, patch), gains, jnp.zeros((6, patch), F32)])
    small_other = swapped(held_until(small, mapped_all))
    small_first = by_section(small, small_other)
    small_second = by_section(small_other, small)
    mod_rows_all = modulation.size // patch

    def unpack(array):
        mod = array[:mod_rows_all].reshape(batches, -1)
        mod = by_section(mod[:1], mod[1:])
        qg = array[mod_rows_all : mod_rows_all + 1] * QUERY_SCALE
        kg = array[mod_rows_all + 1 : mod_rows_all + 2]
        return mod[:, :width], mod[:, width : 2 * width], mod[:, 2 * width :], qg, kg

    _, _, gate_first, qg_first, kg_first = unpack(small_first)
    shift_second, scale_second, _, qg_second, kg_second = unpack(small_second)

    heads = kinds // 3
    gain_of = (qg_first, kg_first)

    def first_heads(blocks, along):
        weight = jnp.concatenate([mapped[kind * heads + h] for kind, h in along], axis=1)
        bias_row = jnp.concatenate([bias[kind * heads + h] for kind, h in along], axis=1)
        gains_here = jnp.concatenate([gain_of[kind] for kind, h in along if kind < 2])
        return [
            first_projection(block, gram, weight, bias_row, gains_here, [attend_other])
            for block in blocks
        ]

    out_first_other = []

    def before_first(step, sums):
        if step == 0:
            return [out_part_second]
        if step == 3:
            out_first_other.append(swapped(held_until(out_first, sums)))
        return []

    attended = attention(
        first_heads(noisy_x, ALONG_X), first_heads(noisy_y, ALONG_Y), False, before_first
    )

    blocks = gather(attended, shift_z)
    turned = []
    for block, by in zip(blocks, STEPS):
        order = [
            [k for k in range(4) if (by + STEPS[k] - STEPS[mine]) % 4 == 0][0] for mine in range(4)
        ]
        turned.append(jnp.concatenate([block[k * local : (k + 1) * local] for k in order]))
    out_part_second, blocks = lax.optimization_barrier((out_part_second, blocks))
    out_second = lax.all_gather(out_part_second, "row", axis=0, tiled=True)
    places = jnp.stack([(row - by) & 3 for by in STEPS] + [section]).astype(jnp.int32)
    along_x, along_y, result_first = between_layers(
        places,
        turned,
        (out_first, out_first_other[0]),
        noisy_row,
        embed_weight,
        gate_first,
        scale_second,
        shift_second,
        (attend_weight[0], attend_other),
        qg_second,
        kg_second,
    )
    result_other = swapped(result_first)

    out_second_other = []

    def before_second(step, sums):
        if step == 5:
            out_second_other.append(swapped(held_until(out_second, sums)))
        return [result_other] if step == 6 else []

    xs = [along_x] + [shift_x(along_x, by) for by in STEPS[1:3]]
    ys = [along_y] + [shift_y(along_y, by) for by in STEPS[1:3]]
    xs, ys = lax.optimization_barrier((xs, ys))
    xs.append(shift_x(xs[0], STEPS[3]))
    ys.append(shift_y(ys[0], STEPS[3]))
    attended = attention(xs, ys, True, before_second)
    mine = give_back([attended[k * local : (k + 1) * local] for k in range(4)], shift_z)
    mine = jnp.concatenate(mine, axis=1)
    mine_other = lax.ppermute(mine, "section", [(0, 1)])
    places_last = jnp.stack([(row + by) & 3 for by in STEPS]).astype(jnp.int32)
    gates = modulation[:, 2 * width :]

    def finish_first():
        return jnp.stack([result_first, result_other])

    def finish_second():
        return last_step(
            places_last,
            (mine_other, mine),
            (out_second_other[0], out_second),
            (result_other, result_first),
            gates,
        )

    result = lax.cond(first, finish_first, finish_second)
    return result.reshape(1, batches, latent.shape[1], latent.shape[2], latent.shape[3], width)


def solution(mesh):
    return jax.shard_map(
        per_device,
        mesh=mesh,
        in_specs=(
            P(None, "depth", "row", None, None),
            P(None, "depth", "row", None, None),
            P(),
            P(),
            P("section", None, "row"),
            P("section", None, None, "row"),
            P("section", None),
            P("section", None),
            P("section", "row", None),
        ),
        out_specs=P("section", None, "depth", "row", None, None),
        check_vma=False,
    )
```

```python
import math

import jax
import jax.numpy as jnp
from jax import lax
from jax.experimental import pallas as pl
from jax.experimental.pallas import tpu as pltpu
from jax.sharding import PartitionSpec as P

HEAD_DIM = 128
BF = jnp.bfloat16
F32 = jnp.float32

norm_eps = 1e-06
plan_steps = 1000.0
QUERY_SCALE = math.log2(math.e) / math.sqrt(HEAD_DIM)
SWAP = [(0, 1), (1, 0)]
STEPS = (0, 1, -1, 2)


def signal_level(timestep):
    phase = (timestep.astype(F32) / plan_steps + 0.008) / 1.008 * (math.pi / 2)
    return jnp.cos(phase) ** 2


def time_features(timestep, count):
    half = count // 2
    frequency = jnp.exp(-math.log(10000.0) * jnp.arange(half, dtype=F32) / half)
    angles = timestep.astype(F32)[:, None] * frequency[None, :]
    return jnp.concatenate([jnp.cos(angles), jnp.sin(angles)], axis=1)


def shift_x(array, by):
    return lax.ppermute(
        array, "depth", [(y * 4 + x, y * 4 + (x + by) % 4) for y in range(4) for x in range(4)]
    )


def shift_y(array, by):
    return lax.ppermute(
        array, "depth", [(y * 4 + x, (y + by) % 4 * 4 + x) for y in range(4) for x in range(4)]
    )


def shift_z(array, by):
    return lax.ppermute(array, "row", [(z, (z + by) % 4) for z in range(4)])


def gather(array, shift):
    return [array] + [shift(array, by) for by in STEPS[1:]]


def give_back(blocks, shift):
    return [blocks[0]] + [shift(block, -by) for block, by in zip(blocks[1:], STEPS[1:])]


def params(mib):
    return pltpu.CompilerParams(vmem_limit_bytes=mib * 2**20)


def head_norm(values, gain):
    factor = lax.rsqrt(jnp.mean(values * values, axis=1, keepdims=True) + norm_eps)
    return (values * factor * gain).astype(BF)


def map_weights(embed, scale, shift, weight, after):
    patch, width = embed.shape
    batches = scale.shape[0]
    kinds, _, channels = weight.shape
    heads = channels // HEAD_DIM

    def kernel(embed_ref, scale_ref, shift_ref, weight_ref, *refs):
        out_ref, sides_ref = refs[-2:]

        @pl.when(pl.program_id(0) == 0)
        def _():
            values = embed_ref[...].astype(F32)
            values = values - jnp.mean(values, axis=1, keepdims=True)
            for m in range(batches):
                sides_ref[m * patch : (m + 1) * patch] = (
                    values * (1.0 + scale_ref[m : m + 1])
                ).astype(BF)
            sides_ref[batches * patch :] = jnp.concatenate(
                [shift_ref[...], jnp.zeros((16 - batches, width), F32)]
            ).astype(BF)

        mapped = jnp.dot(sides_ref[...], weight_ref[0], preferred_element_type=F32)
        for m in range(batches):
            bias = mapped[batches * patch + m : batches * patch + m + 1]
            upper = bias.astype(BF).astype(F32)
            tail = jnp.concatenate([upper, bias - upper, jnp.zeros((14, channels), F32)]).astype(BF)
            for h in range(heads):
                part = slice(h * HEAD_DIM, (h + 1) * HEAD_DIM)
                out_ref[m, h, :patch] = mapped[m * patch : (m + 1) * patch, part].astype(BF)
                out_ref[m, h, patch:] = tail[:, part]

    return pl.pallas_call(
        kernel,
        grid=(kinds,),
        in_specs=[
            pl.BlockSpec((patch, width), lambda j: (0, 0)),
            pl.BlockSpec((batches, width), lambda j: (0, 0)),
            pl.BlockSpec((batches, width), lambda j: (0, 0)),
            pl.BlockSpec((1, width, channels), lambda j: (j, 0, 0)),
        ]
        + [pl.BlockSpec(memory_space=pl.ANY)] * len(after),
        out_specs=pl.BlockSpec((batches, heads, patch + 16, HEAD_DIM), lambda j: (0, j, 0, 0)),
        out_shape=jax.ShapeDtypeStruct((batches, kinds * heads, patch + 16, HEAD_DIM), BF),
        scratch_shapes=[pltpu.VMEM((batches * patch + 16, width), BF)],
        compiler_params=params(52),
        cost_estimate=pl.CostEstimate(
            flops=2 * batches * patch * width * kinds * channels,
            bytes_accessed=10**4,
            transcendentals=0,
        ),
    )(embed, scale, shift, weight, *after)


def first_projection(noisy, gram, weight, bias, gains, after):
    rows = noisy.shape[0]
    heads = weight.shape[1] // HEAD_DIM
    normed_heads = gains.shape[0]

    def kernel(noisy_ref, gram_ref, weight_ref, bias_ref, gains_ref, *refs):
        out_ref = refs[-1]
        values = noisy_ref[...].astype(F32)
        spread = jnp.sum(
            jnp.dot(
                values, gram_ref[...], preferred_element_type=F32, precision=lax.Precision.HIGHEST
            )
            * values,
            axis=1,
            keepdims=True,
        )
        scaled = (values * lax.rsqrt(spread + norm_eps)).astype(BF)
        projected = jnp.dot(scaled, weight_ref[...], preferred_element_type=F32) + bias_ref[...]
        for h in range(heads):
            part = projected[:, h * HEAD_DIM : (h + 1) * HEAD_DIM]
            if h < normed_heads:
                out_ref[h] = head_norm(part, gains_ref[h : h + 1])
            else:
                out_ref[h] = part.astype(BF)

    whole = pl.BlockSpec(memory_space=pltpu.VMEM)
    return pl.pallas_call(
        kernel,
        in_specs=[whole] * 5 + [pl.BlockSpec(memory_space=pl.ANY)] * len(after),
        out_specs=whole,
        out_shape=jax.ShapeDtypeStruct((heads, rows, HEAD_DIM), BF),
        compiler_params=params(16),
        cost_estimate=pl.CostEstimate(flops=10**6, bytes_accessed=10**4, transcendentals=0),
    )(noisy, gram, weight, bias, gains, *after)


ALONG_X = ((1, 0), (1, 2), (0, 1), (2, 0), (2, 2))
ALONG_Y = ((0, 0), (0, 2), (1, 1), (2, 1))
HEADS_BY = ((1, 0), (0, 0), (1, 1))


def attend(queries, blocks, after, carry=None, more=False, weighty=False):
    rows = queries[0].shape[1]
    key_rows = blocks[0][0].shape[1]
    count = len(blocks[0])
    keys_total = key_rows * count
    places = (ALONG_X, ALONG_Y)
    carries = [] if carry is None else [carry]

    def kernel(*refs):
        query_refs = refs[:2]
        block_refs = (refs[2 : 2 + count], refs[2 + count : 2 + 2 * count])
        out_refs = refs[-2:-1] if more else refs[-3:-1]
        wide_ref = refs[-1]
        diagonal = lax.broadcasted_iota(jnp.int32, (HEAD_DIM, HEAD_DIM), 0) == lax.broadcasted_iota(
            jnp.int32, (HEAD_DIM, HEAD_DIM), 1
        )
        for h, (along, out_place) in enumerate(HEADS_BY):
            query = query_refs[along][places[along].index((0, h))]
            key_at = places[1 - along].index((1, h))
            value_at = places[1 - along].index((2, h))
            sums = None
            for i, ref in enumerate(block_refs[1 - along]):
                wide_ref[h, i * key_rows : (i + 1) * key_rows, :HEAD_DIM] = ref[value_at]
                wide_ref[h, i * key_rows : (i + 1) * key_rows, HEAD_DIM:] = jnp.ones(
                    (key_rows, HEAD_DIM), BF
                )
            for i, ref in enumerate(block_refs[1 - along]):
                scores = lax.dot_general(
                    query, ref[key_at], (((1,), (1,)), ((), ())), preferred_element_type=F32
                )
                weights = jnp.exp2(scores).astype(BF)
                term = jnp.dot(
                    weights,
                    wide_ref[h, i * key_rows : (i + 1) * key_rows],
                    preferred_element_type=F32,
                )
                sums = term if sums is None else sums + term
            numerators = sums[:, :HEAD_DIM]
            lines = []
            for part in range(rows // HEAD_DIM):
                square = sums[part * HEAD_DIM : (part + 1) * HEAD_DIM, HEAD_DIM:]
                lines.append(jnp.sum(jnp.where(diagonal, square, 0.0), axis=0, keepdims=True))
            total = jnp.concatenate(lines, axis=0)
            if carry is not None:
                numerators = numerators + refs[2 + 2 * count][h, :rows]
                total = total + refs[2 + 2 * count][h, rows : rows + 4]
            if more:
                out_refs[0][h, :rows] = numerators
                out_refs[0][h, rows : rows + 8] = jnp.concatenate(
                    [total, jnp.zeros((4, HEAD_DIM), F32)], axis=0
                )
                continue
            out_ref = out_refs[1 - along]
            out_ref[out_place, :rows] = numerators.astype(BF)
            upper = total.astype(BF)
            lower = (total - upper.astype(F32)).astype(BF)
            out_ref[out_place, rows : rows + 16] = jnp.concatenate(
                [upper.astype(F32), lower.astype(F32), jnp.zeros((8, HEAD_DIM), F32)], axis=0
            ).astype(BF)

    whole = pl.BlockSpec(memory_space=pltpu.VMEM)
    return pl.pallas_call(
        kernel,
        in_specs=[whole] * (2 + 2 * count + len(carries))
        + [pl.BlockSpec(memory_space=pl.ANY)] * len(after),
        out_specs=whole if more else [whole] * 2,
        out_shape=jax.ShapeDtypeStruct((len(HEADS_BY), rows + 8, HEAD_DIM), F32)
        if more
        else [
            jax.ShapeDtypeStruct((2, rows + 16, HEAD_DIM), BF),
            jax.ShapeDtypeStruct((1, rows + 16, HEAD_DIM), BF),
        ],
        scratch_shapes=[pltpu.VMEM((len(HEADS_BY), keys_total, 2 * HEAD_DIM), BF)],
        compiler_params=params(24),
        cost_estimate=pl.CostEstimate(
            flops=len(HEADS_BY) * rows * keys_total * HEAD_DIM * 8 if weighty else 10**6,
            bytes_accessed=8 * 2**20 if weighty else 10**4,
            transcendentals=0,
        ),
    )(*queries, *blocks[0], *blocks[1], *carries, *after)


def combine(parts_y, parts_x):
    packed = parts_y[0].shape[1]
    rows = packed - 16
    lines = rows // HEAD_DIM
    count = len(parts_y)
    heads = len(HEADS_BY)

    def kernel(*refs):
        out_ref = refs[-1]
        diagonal = lax.broadcasted_iota(jnp.int32, (HEAD_DIM, HEAD_DIM), 0) == lax.broadcasted_iota(
            jnp.int32, (HEAD_DIM, HEAD_DIM), 1
        )
        for h, (along, at) in enumerate(HEADS_BY):
            sources = refs[:count] if along == 1 else refs[count : 2 * count]
            tail = sources[0][at, rows : rows + 16].astype(F32)
            for ref in sources[1:]:
                tail = tail + ref[at, rows : rows + 16].astype(F32)
            for part in range(lines):
                place = slice(part * HEAD_DIM, (part + 1) * HEAD_DIM)
                numerator = sources[0][at, place].astype(F32)
                for ref in sources[1:]:
                    numerator = numerator + ref[at, place].astype(F32)
                total = tail[part : part + 1] + tail[lines + part : lines + part + 1]
                column = jnp.sum(jnp.where(diagonal, 1.0 / total, 0.0), axis=1, keepdims=True)
                out_ref[place, h * HEAD_DIM : (h + 1) * HEAD_DIM] = (numerator * column).astype(BF)

    return pl.pallas_call(
        kernel,
        out_shape=jax.ShapeDtypeStruct((rows, heads * HEAD_DIM), BF),
        compiler_params=params(16),
    )(*parts_y, *parts_x)


def attention(xs, ys, near_first, before):
    parts_y, parts_x = [None] * 4, [None] * 4
    after, carries, step = [], [None] * 4, 0
    if near_first:
        for k in (2, 1, 0):
            more = before(step, after[0] if after else None)
            carries[k] = attend(
                (xs[k], ys[k]), (xs[:3], ys[:3]), after + more, more=True, weighty=True
            )
            after = [carries[k]]
            step += 1
    for k in (3, 2, 1, 0):
        blocks = (xs, ys) if carries[k] is None else (xs[3:], ys[3:])
        more = before(step, after[0] if after else None)
        if k == 0:
            more = more + [parts_y[3], parts_x[3]]
        sums_y, sums_x = attend(
            (xs[k], ys[k]), blocks, after + more, carries[k], weighty=near_first
        )
        after = [sums_x]
        step += 1
        by = STEPS[k]
        parts_y[k] = shift_y(sums_y, -by) if by else sums_y
        parts_x[k] = shift_x(sums_x, -by) if by else sums_x
    return combine(parts_y, parts_x)


def held_until(array, other):
    return lax.optimization_barrier((array, other))[0]


def weight_copies(weight_refs, held_ref, sems):
    depth, width = held_ref.shape
    part = depth // 8
    half = width // 2
    copies = []
    for column in range(2):
        columns = slice(column * half, (column + 1) * half)
        for k in range(8):
            row, side = divmod(k, 2)
            source = weight_refs[side].at[row * part : (row + 1) * part, columns]
            place = held_ref.at[k * part : (k + 1) * part, columns]
            copies.append(pltpu.make_async_copy(source, place, sems.at[column * 8 + k]))
    return copies


def between_layers(places, blocks, weights, noisy, embed, gate, scale, shift, next_weight, query_gain, key_gain):
    rows, part = blocks[0].shape
    width = gate.shape[1]
    depth = 4 * part
    block = 512
    local = rows // 4
    kinds, _, channels = next_weight[0].shape
    heads = channels // HEAD_DIM

    def kernel(places_ref, *refs):
        block_refs = refs[:4]
        weight_refs = refs[4:6]
        noisy_ref, embed_ref, gate_ref, scale_ref, shift_ref = refs[6:11]
        next_refs = refs[11:13]
        qg_ref, kg_ref, x_ref, y_ref, own_ref = refs[13:18]
        held_ref, next_held_ref, side_ref, tokens_ref, sems = refs[18:]
        here = places_ref[4]

        def copies_in(section):
            return weight_copies(weight_refs if section == 0 else weight_refs[::-1], held_ref, sems)

        def next_copies_in(section):
            return [
                pltpu.make_async_copy(
                    next_refs[1 - section].at[j], next_held_ref.at[j], sems.at[16 + j]
                )
                for j in range(kinds)
            ]

        copies, next_copies = copies_in(0), next_copies_in(0)
        for section in range(2):

            @pl.when(here == section)
            def _():
                for copy in copies_in(section):
                    copy.start()

        for k in range(4):
            side_ref[:, pl.ds(pl.multiple_of(places_ref[k] * part, HEAD_DIM), part)] = block_refs[k][
                ...
            ]
        for column in range(2):
            for copy in copies[8 * column : 8 * column + 8]:
                copy.wait()
            if column == 0:
                for section in range(2):

                    @pl.when(here == section)
                    def _():
                        for copy in next_copies_in(section):
                            copy.start()

            @pl.loop(0, width // 2 // block)
            def _(n):
                place = pl.ds(pl.multiple_of(column * (width // 2) + n * block, block), block)
                update = jnp.dot(side_ref[...], held_ref[:, place], preferred_element_type=F32)
                base = jnp.dot(noisy_ref[...], embed_ref[:, place], preferred_element_type=F32)
                tokens_ref[:, place] = (
                    base.astype(BF).astype(F32) + gate_ref[:, place] * update
                ).astype(BF)

        own_ref[...] = tokens_ref[:local]

        @pl.loop(0, rows // 128)
        def _(n):
            place = pl.ds(pl.multiple_of(n * 128, 128), 128)
            values = tokens_ref[place].astype(F32)
            values = values - jnp.mean(values, axis=1, keepdims=True)
            spread = jnp.mean(values * values, axis=1, keepdims=True)
            tokens_ref[place] = (
                values * lax.rsqrt(spread + norm_eps) * (1.0 + scale_ref[...]) + shift_ref[...]
            ).astype(BF)

        for kind in range(kinds):
            next_copies[kind].wait()
            projected = jnp.dot(tokens_ref[...], next_held_ref[kind], preferred_element_type=F32)
            for h in range(heads):
                piece = projected[:, h * HEAD_DIM : (h + 1) * HEAD_DIM]
                if kind < 2:
                    piece = head_norm(piece, (qg_ref, kg_ref)[kind][...])
                else:
                    piece = piece.astype(BF)
                if (kind, h) in ALONG_X:
                    x_ref[ALONG_X.index((kind, h))] = piece
                else:
                    y_ref[ALONG_Y.index((kind, h))] = piece

    whole = pl.BlockSpec(memory_space=pltpu.VMEM)
    left = pl.BlockSpec(memory_space=pl.ANY)
    return pl.pallas_call(
        kernel,
        in_specs=[pl.BlockSpec(memory_space=pltpu.SMEM)]
        + [whole] * 4
        + [left] * 2
        + [whole] * 5
        + [left] * 2
        + [whole] * 2,
        out_specs=[whole] * 3,
        out_shape=[
            jax.ShapeDtypeStruct((len(ALONG_X), rows, HEAD_DIM), BF),
            jax.ShapeDtypeStruct((len(ALONG_Y), rows, HEAD_DIM), BF),
            jax.ShapeDtypeStruct((local, width), BF),
        ],
        scratch_shapes=[
            pltpu.VMEM((depth, width), BF),
            pltpu.VMEM(next_weight[0].shape, BF),
            pltpu.VMEM((rows, depth), BF),
            pltpu.VMEM((rows, width), BF),
            pltpu.SemaphoreType.DMA((16 + kinds,)),
        ],
        compiler_params=params(52),
        cost_estimate=pl.CostEstimate(
            flops=2 * rows * width * (depth + kinds * channels),
            bytes_accessed=10**4,
            transcendentals=0,
        ),
    )(places, *blocks, *weights, noisy, embed, gate, scale, shift, *next_weight, query_gain, key_gain)


def last_step(places, heads, weights, bases, gates):
    rows, depth = heads[0].shape
    width = gates.shape[1]
    block = 512

    part = depth // 4

    def kernel(places_ref, first_ref, second_ref, *refs):
        weight_refs = refs[:2]
        first_base_ref, second_base_ref, gates_ref, out_ref, held_ref, side_ref, sems = refs[2:]
        copies = weight_copies(weight_refs, held_ref, sems)
        for copy in copies:
            copy.start()
        for k in range(4):
            place = pl.ds(pl.multiple_of(places_ref[k] * part, HEAD_DIM), part)
            side_ref[:rows, place] = first_ref[:, k * part : (k + 1) * part]
            side_ref[rows:, place] = second_ref[:, k * part : (k + 1) * part]
        for column in range(2):
            for copy in copies[8 * column : 8 * column + 8]:
                copy.wait()

            @pl.loop(0, width // 2 // block)
            def _(n):
                place = pl.ds(pl.multiple_of(column * (width // 2) + n * block, block), block)
                update = jnp.dot(side_ref[...], held_ref[:, place], preferred_element_type=F32)
                for m, base_ref in enumerate((first_base_ref, second_base_ref)):
                    out_ref[m, :, place] = (
                        base_ref[:, place].astype(F32)
                        + gates_ref[m : m + 1, place] * update[m * rows : (m + 1) * rows]
                    ).astype(BF)

    whole = pl.BlockSpec(memory_space=pltpu.VMEM)
    return pl.pallas_call(
        kernel,
        in_specs=[pl.BlockSpec(memory_space=pltpu.SMEM)]
        + [whole] * 2
        + [pl.BlockSpec(memory_space=pl.ANY)] * 2
        + [whole] * 3,
        out_specs=whole,
        out_shape=jax.ShapeDtypeStruct((2, rows, width), BF),
        scratch_shapes=[
            pltpu.VMEM((depth, width), BF),
            pltpu.VMEM((2 * rows, depth), BF),
            pltpu.SemaphoreType.DMA((16,)),
        ],
        compiler_params=params(52),
    )(places, *heads, *weights, *bases, gates)


def per_device(
    latent,
    noise_field,
    timestep,
    embed_weight,
    modulate_weight,
    attend_weight,
    query_gain,
    key_gain,
    output_weight,
):
    batches = latent.shape[0]
    patch, width = embed_weight.shape
    local = latent.shape[1] * latent.shape[2] * latent.shape[3]
    section = lax.axis_index("section")
    row = lax.axis_index("row")
    first = section == 0

    def by_section(of_first, of_second):
        return jnp.where(first, of_first, of_second)

    def swapped(array):
        return lax.ppermute(array, "section", SWAP)

    level = signal_level(timestep)[:, None, None, None, None]
    noisy = (
        jnp.sqrt(level) * latent.astype(F32) + jnp.sqrt(1.0 - level) * noise_field.astype(F32)
    ).astype(BF)
    noisy = by_section(noisy[0], noisy[1]).reshape(local, patch)
    features = time_features(timestep, modulate_weight.shape[1]).astype(BF)
    mod_part = jnp.dot(features, modulate_weight[0], preferred_element_type=F32)

    out_own = output_weight[0]
    half = out_own.shape[0] // 2
    out_got = swapped(by_section(out_own[half:], out_own[:half]))
    attend_other = lax.ppermute(attend_weight[0], "section", [(1, 0)])
    out_part = by_section(out_own[:half], out_got)
    out_part_second = by_section(out_got, out_own[half:])

    centered = embed_weight.astype(F32)
    centered = centered - jnp.mean(centered, axis=1, keepdims=True)
    gram = (
        jnp.dot(centered, centered.T, preferred_element_type=F32, precision=lax.Precision.HIGHEST)
        / width
    )
    mod_rows = mod_part.size // patch
    packed = jnp.concatenate(
        [noisy.astype(F32), mod_part.reshape(mod_rows, patch), jnp.zeros((-mod_rows % 8, patch), F32)]
    )
    packed = gather(packed, shift_z)
    noisy_row = jnp.concatenate([block[:local] for block in packed]).astype(BF)
    mods = [block[local : local + mod_rows].reshape(batches, -1) for block in packed]

    def from_row(b):
        chosen = mods[0]
        for k in (1, 2, 3):
            chosen = jnp.where(row == (b + STEPS[k]) % 4, mods[k], chosen)
        return chosen

    modulation = jnp.concatenate([from_row(b) for b in range(4)], axis=1)
    shift_own = modulation[:, :width]
    scale_own = modulation[:, width : 2 * width]

    out_part, gram, noisy_row, scale_own = lax.optimization_barrier(
        (out_part, gram, noisy_row, scale_own)
    )
    out_first = lax.all_gather(out_part, "row", axis=0, tiled=True)

    noisy_x = gather(noisy_row, shift_x)
    noisy_y = gather(noisy_row, shift_y)

    mapped = map_weights(
        embed_weight, scale_own, shift_own, attend_weight[0], []
    )
    mapped_all = mapped
    kinds = mapped.shape[1]
    mapped_other = lax.ppermute(mapped[1], "section", [(0, 1)])
    mapped = by_section(mapped[0], mapped_other)
    bias = mapped[:, patch : patch + 1].astype(F32) + mapped[:, patch + 1 : patch + 2].astype(F32)
    mapped = mapped[:, :patch]

    gains = jnp.concatenate([query_gain, key_gain])
    small = jnp.concatenate([modulation.reshape(-1, patch), gains, jnp.zeros((6, patch), F32)])
    small_other = swapped(held_until(small, mapped_all))
    small_first = by_section(small, small_other)
    small_second = by_section(small_other, small)
    mod_rows_all = modulation.size // patch

    def unpack(array):
        mod = array[:mod_rows_all].reshape(batches, -1)
        mod = by_section(mod[:1], mod[1:])
        qg = array[mod_rows_all : mod_rows_all + 1] * QUERY_SCALE
        kg = array[mod_rows_all + 1 : mod_rows_all + 2]
        return mod[:, :width], mod[:, width : 2 * width], mod[:, 2 * width :], qg, kg

    _, _, gate_first, qg_first, kg_first = unpack(small_first)
    shift_second, scale_second, _, qg_second, kg_second = unpack(small_second)

    heads = kinds // 3
    gain_of = (qg_first, kg_first)

    def first_heads(blocks, along):
        weight = jnp.concatenate([mapped[kind * heads + h] for kind, h in along], axis=1)
        bias_row = jnp.concatenate([bias[kind * heads + h] for kind, h in along], axis=1)
        gains_here = jnp.concatenate([gain_of[kind] for kind, h in along if kind < 2])
        return [
            first_projection(block, gram, weight, bias_row, gains_here, [attend_other])
            for block in blocks
        ]

    out_first_other = []

    def before_first(step, sums):
        if step == 0:
            return [out_part_second]
        if step == 3:
            out_first_other.append(swapped(held_until(out_first, sums)))
        return []

    attended = attention(
        first_heads(noisy_x, ALONG_X), first_heads(noisy_y, ALONG_Y), False, before_first
    )

    blocks = gather(attended, shift_z)
    turned = []
    for block, by in zip(blocks, STEPS):
        order = [
            [k for k in range(4) if (by + STEPS[k] - STEPS[mine]) % 4 == 0][0] for mine in range(4)
        ]
        turned.append(jnp.concatenate([block[k * local : (k + 1) * local] for k in order]))
    out_part_second, blocks = lax.optimization_barrier((out_part_second, blocks))
    out_second = lax.all_gather(out_part_second, "row", axis=0, tiled=True)
    places = jnp.stack([(row - by) & 3 for by in STEPS] + [section]).astype(jnp.int32)
    along_x, along_y, result_first = between_layers(
        places,
        turned,
        (out_first, out_first_other[0]),
        noisy_row,
        embed_weight,
        gate_first,
        scale_second,
        shift_second,
        (attend_weight[0], attend_other),
        qg_second,
        kg_second,
    )
    result_other = swapped(result_first)

    out_second_other = []

    def before_second(step, sums):
        if step == 5:
            out_second_other.append(swapped(held_until(out_second, sums)))
        return [result_other] if step == 6 else []

    xs = [along_x] + [shift_x(along_x, by) for by in STEPS[1:3]]
    ys = [along_y] + [shift_y(along_y, by) for by in STEPS[1:3]]
    xs, ys = lax.optimization_barrier((xs, ys))
    xs.append(shift_x(xs[0], STEPS[3]))
    ys.append(shift_y(ys[0], STEPS[3]))
    attended = attention(xs, ys, True, before_second)
    mine = give_back([attended[k * local : (k + 1) * local] for k in range(4)], shift_z)
    mine = jnp.concatenate(mine, axis=1)
    mine_other = lax.ppermute(mine, "section", [(0, 1)])
    places_last = jnp.stack([(row + by) & 3 for by in STEPS]).astype(jnp.int32)
    gates = modulation[:, 2 * width :]

    def finish_first():
        return jnp.stack([result_first, result_other])

    def finish_second():
        return last_step(
            places_last,
            (mine_other, mine),
            (out_second_other[0], out_second),
            (result_other, result_first),
            gates,
        )

    result = lax.cond(first, finish_first, finish_second)
    return result.reshape(1, batches, latent.shape[1], latent.shape[2], latent.shape[3], width)


def solution(mesh):
    return jax.shard_map(
        per_device,
        mesh=mesh,
        in_specs=(
            P(None, "depth", "row", None, None),
            P(None, "depth", "row", None, None),
            P(),
            P(),
            P("section", None, "row"),
            P("section", None, None, "row"),
            P("section", None),
            P("section", None),
            P("section", "row", None),
        ),
        out_specs=P("section", None, "depth", "row", None, None),
        check_vma=False,
    )
```

```python
import math

import jax
import jax.numpy as jnp
from jax import lax
from jax.experimental import pallas as pl
from jax.experimental.pallas import tpu as pltpu
from jax.sharding import PartitionSpec as P

HEAD_DIM = 128
BF = jnp.bfloat16
F32 = jnp.float32

norm_eps = 1e-06
plan_steps = 1000.0
QUERY_SCALE = math.log2(math.e) / math.sqrt(HEAD_DIM)
SWAP = [(0, 1), (1, 0)]
STEPS = (0, 1, -1, 2)


def signal_level(timestep):
    phase = (timestep.astype(F32) / plan_steps + 0.008) / 1.008 * (math.pi / 2)
    return jnp.cos(phase) ** 2


def time_features(timestep, count):
    half = count // 2
    frequency = jnp.exp(-math.log(10000.0) * jnp.arange(half, dtype=F32) / half)
    angles = timestep.astype(F32)[:, None] * frequency[None, :]
    return jnp.concatenate([jnp.cos(angles), jnp.sin(angles)], axis=1)


def shift_x(array, by):
    return lax.ppermute(
        array, "depth", [(y * 4 + x, y * 4 + (x + by) % 4) for y in range(4) for x in range(4)]
    )


def shift_y(array, by):
    return lax.ppermute(
        array, "depth", [(y * 4 + x, (y + by) % 4 * 4 + x) for y in range(4) for x in range(4)]
    )


def shift_z(array, by):
    return lax.ppermute(array, "row", [(z, (z + by) % 4) for z in range(4)])


def gather(array, shift):
    return [array] + [shift(array, by) for by in STEPS[1:]]


def give_back(blocks, shift):
    return [blocks[0]] + [shift(block, -by) for block, by in zip(blocks[1:], STEPS[1:])]


def params(mib):
    return pltpu.CompilerParams(vmem_limit_bytes=mib * 2**20)


def head_norm(values, gain):
    factor = lax.rsqrt(jnp.mean(values * values, axis=1, keepdims=True) + norm_eps)
    return (values * factor * gain).astype(BF)


def map_weights(embed, scale, shift, weight, after):
    patch, width = embed.shape
    batches = scale.shape[0]
    kinds, _, channels = weight.shape
    heads = channels // HEAD_DIM

    def kernel(embed_ref, scale_ref, shift_ref, weight_ref, *refs):
        out_ref, sides_ref = refs[-2:]

        @pl.when(pl.program_id(0) == 0)
        def _():
            values = embed_ref[...].astype(F32)
            values = values - jnp.mean(values, axis=1, keepdims=True)
            for m in range(batches):
                sides_ref[m * patch : (m + 1) * patch] = (
                    values * (1.0 + scale_ref[m : m + 1])
                ).astype(BF)
            sides_ref[batches * patch :] = jnp.concatenate(
                [shift_ref[...], jnp.zeros((16 - batches, width), F32)]
            ).astype(BF)

        mapped = jnp.dot(sides_ref[...], weight_ref[0], preferred_element_type=F32)
        for m in range(batches):
            bias = mapped[batches * patch + m : batches * patch + m + 1]
            upper = bias.astype(BF).astype(F32)
            tail = jnp.concatenate([upper, bias - upper, jnp.zeros((14, channels), F32)]).astype(BF)
            for h in range(heads):
                part = slice(h * HEAD_DIM, (h + 1) * HEAD_DIM)
                out_ref[m, h, :patch] = mapped[m * patch : (m + 1) * patch, part].astype(BF)
                out_ref[m, h, patch:] = tail[:, part]

    return pl.pallas_call(
        kernel,
        grid=(kinds,),
        in_specs=[
            pl.BlockSpec((patch, width), lambda j: (0, 0)),
            pl.BlockSpec((batches, width), lambda j: (0, 0)),
            pl.BlockSpec((batches, width), lambda j: (0, 0)),
            pl.BlockSpec((1, width, channels), lambda j: (j, 0, 0)),
        ]
        + [pl.BlockSpec(memory_space=pl.ANY)] * len(after),
        out_specs=pl.BlockSpec((batches, heads, patch + 16, HEAD_DIM), lambda j: (0, j, 0, 0)),
        out_shape=jax.ShapeDtypeStruct((batches, kinds * heads, patch + 16, HEAD_DIM), BF),
        scratch_shapes=[pltpu.VMEM((batches * patch + 16, width), BF)],
        compiler_params=params(18),
        cost_estimate=pl.CostEstimate(
            flops=2 * batches * patch * width * kinds * channels,
            bytes_accessed=10**4,
            transcendentals=0,
        ),
    )(embed, scale, shift, weight, *after)


def first_projection(noisy, gram, weight, bias, gains, after):
    rows = noisy.shape[0]
    heads = weight.shape[1] // HEAD_DIM
    normed_heads = gains.shape[0]

    def kernel(noisy_ref, gram_ref, weight_ref, bias_ref, gains_ref, *refs):
        out_ref = refs[-1]
        values = noisy_ref[...].astype(F32)
        spread = jnp.sum(
            jnp.dot(
                values, gram_ref[...], preferred_element_type=F32, precision=lax.Precision.HIGHEST
            )
            * values,
            axis=1,
            keepdims=True,
        )
        scaled = (values * lax.rsqrt(spread + norm_eps)).astype(BF)
        projected = jnp.dot(scaled, weight_ref[...], preferred_element_type=F32) + bias_ref[...]
        for h in range(heads):
            part = projected[:, h * HEAD_DIM : (h + 1) * HEAD_DIM]
            if h < normed_heads:
                out_ref[h] = head_norm(part, gains_ref[h : h + 1])
            else:
                out_ref[h] = part.astype(BF)

    whole = pl.BlockSpec(memory_space=pltpu.VMEM)
    return pl.pallas_call(
        kernel,
        in_specs=[whole] * 5 + [pl.BlockSpec(memory_space=pl.ANY)] * len(after),
        out_specs=whole,
        out_shape=jax.ShapeDtypeStruct((heads, rows, HEAD_DIM), BF),
        compiler_params=params(16),
        cost_estimate=pl.CostEstimate(flops=10**6, bytes_accessed=10**4, transcendentals=0),
    )(noisy, gram, weight, bias, gains, *after)


ALONG_X = ((1, 0), (1, 2), (0, 1), (2, 0), (2, 2))
ALONG_Y = ((0, 0), (0, 2), (1, 1), (2, 1))
HEADS_BY = ((1, 0), (0, 0), (1, 1))


def attend(queries, blocks, after, carry=None, more=False, weighty=False):
    rows = queries[0].shape[1]
    key_rows = blocks[0][0].shape[1]
    count = len(blocks[0])
    keys_total = key_rows * count
    places = (ALONG_X, ALONG_Y)
    carries = [] if carry is None else [carry]

    def kernel(*refs):
        query_refs = refs[:2]
        block_refs = (refs[2 : 2 + count], refs[2 + count : 2 + 2 * count])
        out_refs = refs[-2:-1] if more else refs[-3:-1]
        wide_ref = refs[-1]
        diagonal = lax.broadcasted_iota(jnp.int32, (HEAD_DIM, HEAD_DIM), 0) == lax.broadcasted_iota(
            jnp.int32, (HEAD_DIM, HEAD_DIM), 1
        )
        for h, (along, out_place) in enumerate(HEADS_BY):
            query = query_refs[along][places[along].index((0, h))]
            key_at = places[1 - along].index((1, h))
            value_at = places[1 - along].index((2, h))
            sums = None
            for i, ref in enumerate(block_refs[1 - along]):
                wide_ref[h, i * key_rows : (i + 1) * key_rows, :HEAD_DIM] = ref[value_at]
                wide_ref[h, i * key_rows : (i + 1) * key_rows, HEAD_DIM:] = jnp.ones(
                    (key_rows, HEAD_DIM), BF
                )
            for i, ref in enumerate(block_refs[1 - along]):
                scores = lax.dot_general(
                    query, ref[key_at], (((1,), (1,)), ((), ())), preferred_element_type=F32
                )
                weights = jnp.exp2(scores).astype(BF)
                term = jnp.dot(
                    weights,
                    wide_ref[h, i * key_rows : (i + 1) * key_rows],
                    preferred_element_type=F32,
                )
                sums = term if sums is None else sums + term
            numerators = sums[:, :HEAD_DIM]
            lines = []
            for part in range(rows // HEAD_DIM):
                square = sums[part * HEAD_DIM : (part + 1) * HEAD_DIM, HEAD_DIM:]
                lines.append(jnp.sum(jnp.where(diagonal, square, 0.0), axis=0, keepdims=True))
            total = jnp.concatenate(lines, axis=0)
            if carry is not None:
                numerators = numerators + refs[2 + 2 * count][h, :rows]
                total = total + refs[2 + 2 * count][h, rows : rows + 4]
            if more:
                out_refs[0][h, :rows] = numerators
                out_refs[0][h, rows : rows + 8] = jnp.concatenate(
                    [total, jnp.zeros((4, HEAD_DIM), F32)], axis=0
                )
                continue
            out_ref = out_refs[1 - along]
            out_ref[out_place, :rows] = numerators.astype(BF)
            upper = total.astype(BF)
            lower = (total - upper.astype(F32)).astype(BF)
            out_ref[out_place, rows : rows + 16] = jnp.concatenate(
                [upper.astype(F32), lower.astype(F32), jnp.zeros((8, HEAD_DIM), F32)], axis=0
            ).astype(BF)

    whole = pl.BlockSpec(memory_space=pltpu.VMEM)
    return pl.pallas_call(
        kernel,
        in_specs=[whole] * (2 + 2 * count + len(carries))
        + [pl.BlockSpec(memory_space=pl.ANY)] * len(after),
        out_specs=whole if more else [whole] * 2,
        out_shape=jax.ShapeDtypeStruct((len(HEADS_BY), rows + 8, HEAD_DIM), F32)
        if more
        else [
            jax.ShapeDtypeStruct((2, rows + 16, HEAD_DIM), BF),
            jax.ShapeDtypeStruct((1, rows + 16, HEAD_DIM), BF),
        ],
        scratch_shapes=[pltpu.VMEM((len(HEADS_BY), keys_total, 2 * HEAD_DIM), BF)],
        compiler_params=params(24),
        cost_estimate=pl.CostEstimate(
            flops=len(HEADS_BY) * rows * keys_total * HEAD_DIM * 8 if weighty else 10**6,
            bytes_accessed=8 * 2**20 if weighty else 10**4,
            transcendentals=0,
        ),
    )(*queries, *blocks[0], *blocks[1], *carries, *after)


def combine(parts_y, parts_x):
    packed = parts_y[0].shape[1]
    rows = packed - 16
    lines = rows // HEAD_DIM
    count = len(parts_y)
    heads = len(HEADS_BY)

    def kernel(*refs):
        out_ref = refs[-1]
        diagonal = lax.broadcasted_iota(jnp.int32, (HEAD_DIM, HEAD_DIM), 0) == lax.broadcasted_iota(
            jnp.int32, (HEAD_DIM, HEAD_DIM), 1
        )
        for h, (along, at) in enumerate(HEADS_BY):
            sources = refs[:count] if along == 1 else refs[count : 2 * count]
            tail = sources[0][at, rows : rows + 16].astype(F32)
            for ref in sources[1:]:
                tail = tail + ref[at, rows : rows + 16].astype(F32)
            for part in range(lines):
                place = slice(part * HEAD_DIM, (part + 1) * HEAD_DIM)
                numerator = sources[0][at, place].astype(F32)
                for ref in sources[1:]:
                    numerator = numerator + ref[at, place].astype(F32)
                total = tail[part : part + 1] + tail[lines + part : lines + part + 1]
                column = jnp.sum(jnp.where(diagonal, 1.0 / total, 0.0), axis=1, keepdims=True)
                out_ref[place, h * HEAD_DIM : (h + 1) * HEAD_DIM] = (numerator * column).astype(BF)

    return pl.pallas_call(
        kernel,
        out_shape=jax.ShapeDtypeStruct((rows, heads * HEAD_DIM), BF),
        compiler_params=params(16),
    )(*parts_y, *parts_x)


def attention(xs, ys, near_first, before):
    parts_y, parts_x = [None] * 4, [None] * 4
    after, carries, step = [], [None] * 4, 0
    if near_first:
        for k in (2, 1, 0):
            more = before(step, after[0] if after else None)
            carries[k] = attend(
                (xs[k], ys[k]), (xs[:3], ys[:3]), after + more, more=True, weighty=True
            )
            after = [carries[k]]
            step += 1
    for k in (3, 2, 1, 0):
        blocks = (xs, ys) if carries[k] is None else (xs[3:], ys[3:])
        more = before(step, after[0] if after else None)
        if k == 0:
            more = more + [parts_y[3], parts_x[3]]
        sums_y, sums_x = attend(
            (xs[k], ys[k]), blocks, after + more, carries[k], weighty=near_first
        )
        after = [sums_x]
        step += 1
        by = STEPS[k]
        parts_y[k] = shift_y(sums_y, -by) if by else sums_y
        parts_x[k] = shift_x(sums_x, -by) if by else sums_x
    return combine(parts_y, parts_x)


def held_until(array, other):
    return lax.optimization_barrier((array, other))[0]


def weight_copies(weight_refs, held_ref, sems):
    depth, width = held_ref.shape
    part = depth // 8
    half = width // 2
    copies = []
    for column in range(2):
        columns = slice(column * half, (column + 1) * half)
        for k in range(8):
            row, side = divmod(k, 2)
            source = weight_refs[side].at[row * part : (row + 1) * part, columns]
            place = held_ref.at[k * part : (k + 1) * part, columns]
            copies.append(pltpu.make_async_copy(source, place, sems.at[column * 8 + k]))
    return copies


def between_layers(places, blocks, weights, noisy, embed, gate, scale, shift, next_weight, query_gain, key_gain):
    rows, part = blocks[0].shape
    width = gate.shape[1]
    depth = 4 * part
    block = 512
    local = rows // 4
    kinds, _, channels = next_weight[0].shape
    heads = channels // HEAD_DIM

    def kernel(places_ref, *refs):
        block_refs = refs[:4]
        weight_refs = refs[4:6]
        noisy_ref, embed_ref, gate_ref, scale_ref, shift_ref = refs[6:11]
        next_refs = refs[11:13]
        qg_ref, kg_ref, x_ref, y_ref, own_ref = refs[13:18]
        held_ref, next_held_ref, side_ref, tokens_ref, sems = refs[18:]
        here = places_ref[4]

        def copies_in(section):
            return weight_copies(weight_refs if section == 0 else weight_refs[::-1], held_ref, sems)

        def next_copies_in(section):
            return [
                pltpu.make_async_copy(
                    next_refs[1 - section].at[j], next_held_ref.at[j], sems.at[16 + j]
                )
                for j in range(kinds)
            ]

        copies, next_copies = copies_in(0), next_copies_in(0)
        for section in range(2):

            @pl.when(here == section)
            def _():
                for copy in copies_in(section):
                    copy.start()

        for k in range(4):
            side_ref[:, pl.ds(pl.multiple_of(places_ref[k] * part, HEAD_DIM), part)] = block_refs[k][
                ...
            ]
        for column in range(2):
            for copy in copies[8 * column : 8 * column + 8]:
                copy.wait()
            if column == 0:
                for section in range(2):

                    @pl.when(here == section)
                    def _():
                        for copy in next_copies_in(section):
                            copy.start()

            @pl.loop(0, width // 2 // block)
            def _(n):
                place = pl.ds(pl.multiple_of(column * (width // 2) + n * block, block), block)
                update = jnp.dot(side_ref[...], held_ref[:, place], preferred_element_type=F32)
                base = jnp.dot(noisy_ref[...], embed_ref[:, place], preferred_element_type=F32)
                tokens_ref[:, place] = (
                    base.astype(BF).astype(F32) + gate_ref[:, place] * update
                ).astype(BF)

        own_ref[...] = tokens_ref[:local]

        @pl.loop(0, rows // 128)
        def _(n):
            place = pl.ds(pl.multiple_of(n * 128, 128), 128)
            values = tokens_ref[place].astype(F32)
            values = values - jnp.mean(values, axis=1, keepdims=True)
            spread = jnp.mean(values * values, axis=1, keepdims=True)
            tokens_ref[place] = (
                values * lax.rsqrt(spread + norm_eps) * (1.0 + scale_ref[...]) + shift_ref[...]
            ).astype(BF)

        for kind in range(kinds):
            next_copies[kind].wait()
            projected = jnp.dot(tokens_ref[...], next_held_ref[kind], preferred_element_type=F32)
            for h in range(heads):
                piece = projected[:, h * HEAD_DIM : (h + 1) * HEAD_DIM]
                if kind < 2:
                    piece = head_norm(piece, (qg_ref, kg_ref)[kind][...])
                else:
                    piece = piece.astype(BF)
                if (kind, h) in ALONG_X:
                    x_ref[ALONG_X.index((kind, h))] = piece
                else:
                    y_ref[ALONG_Y.index((kind, h))] = piece

    whole = pl.BlockSpec(memory_space=pltpu.VMEM)
    left = pl.BlockSpec(memory_space=pl.ANY)
    return pl.pallas_call(
        kernel,
        in_specs=[pl.BlockSpec(memory_space=pltpu.SMEM)]
        + [whole] * 4
        + [left] * 2
        + [whole] * 5
        + [left] * 2
        + [whole] * 2,
        out_specs=[whole] * 3,
        out_shape=[
            jax.ShapeDtypeStruct((len(ALONG_X), rows, HEAD_DIM), BF),
            jax.ShapeDtypeStruct((len(ALONG_Y), rows, HEAD_DIM), BF),
            jax.ShapeDtypeStruct((local, width), BF),
        ],
        scratch_shapes=[
            pltpu.VMEM((depth, width), BF),
            pltpu.VMEM(next_weight[0].shape, BF),
            pltpu.VMEM((rows, depth), BF),
            pltpu.VMEM((rows, width), BF),
            pltpu.SemaphoreType.DMA((16 + kinds,)),
        ],
        compiler_params=params(40),
        cost_estimate=pl.CostEstimate(
            flops=2 * rows * width * (depth + kinds * channels),
            bytes_accessed=10**4,
            transcendentals=0,
        ),
    )(places, *blocks, *weights, noisy, embed, gate, scale, shift, *next_weight, query_gain, key_gain)


def last_step(places, heads, weights, bases, gates):
    rows, depth = heads[0].shape
    width = gates.shape[1]
    block = 512

    part = depth // 4

    def kernel(places_ref, first_ref, second_ref, *refs):
        weight_refs = refs[:2]
        first_base_ref, second_base_ref, gates_ref, out_ref, held_ref, side_ref, sems = refs[2:]
        copies = weight_copies(weight_refs, held_ref, sems)
        for copy in copies:
            copy.start()
        for k in range(4):
            place = pl.ds(pl.multiple_of(places_ref[k] * part, HEAD_DIM), part)
            side_ref[:rows, place] = first_ref[:, k * part : (k + 1) * part]
            side_ref[rows:, place] = second_ref[:, k * part : (k + 1) * part]
        for column in range(2):
            for copy in copies[8 * column : 8 * column + 8]:
                copy.wait()

            @pl.loop(0, width // 2 // block)
            def _(n):
                place = pl.ds(pl.multiple_of(column * (width // 2) + n * block, block), block)
                update = jnp.dot(side_ref[...], held_ref[:, place], preferred_element_type=F32)
                for m, base_ref in enumerate((first_base_ref, second_base_ref)):
                    out_ref[m, :, place] = (
                        base_ref[:, place].astype(F32)
                        + gates_ref[m : m + 1, place] * update[m * rows : (m + 1) * rows]
                    ).astype(BF)

    whole = pl.BlockSpec(memory_space=pltpu.VMEM)
    return pl.pallas_call(
        kernel,
        in_specs=[pl.BlockSpec(memory_space=pltpu.SMEM)]
        + [whole] * 2
        + [pl.BlockSpec(memory_space=pl.ANY)] * 2
        + [whole] * 3,
        out_specs=whole,
        out_shape=jax.ShapeDtypeStruct((2, rows, width), BF),
        scratch_shapes=[
            pltpu.VMEM((depth, width), BF),
            pltpu.VMEM((2 * rows, depth), BF),
            pltpu.SemaphoreType.DMA((16,)),
        ],
        compiler_params=params(18),
    )(places, *heads, *weights, *bases, gates)


def per_device(
    latent,
    noise_field,
    timestep,
    embed_weight,
    modulate_weight,
    attend_weight,
    query_gain,
    key_gain,
    output_weight,
):
    batches = latent.shape[0]
    patch, width = embed_weight.shape
    local = latent.shape[1] * latent.shape[2] * latent.shape[3]
    section = lax.axis_index("section")
    row = lax.axis_index("row")
    first = section == 0

    def by_section(of_first, of_second):
        return jnp.where(first, of_first, of_second)

    def swapped(array):
        return lax.ppermute(array, "section", SWAP)

    level = signal_level(timestep)[:, None, None, None, None]
    noisy = (
        jnp.sqrt(level) * latent.astype(F32) + jnp.sqrt(1.0 - level) * noise_field.astype(F32)
    ).astype(BF)
    noisy = by_section(noisy[0], noisy[1]).reshape(local, patch)
    features = time_features(timestep, modulate_weight.shape[1]).astype(BF)
    mod_part = jnp.dot(features, modulate_weight[0], preferred_element_type=F32)

    out_own = output_weight[0]
    half = out_own.shape[0] // 2
    out_got = swapped(out_own)
    attend_other = lax.ppermute(attend_weight[0], "section", [(1, 0)])
    out_part = by_section(out_own[:half], out_got[half:])
    out_part_second = by_section(out_got[:half], out_own[half:])

    centered = embed_weight.astype(F32)
    centered = centered - jnp.mean(centered, axis=1, keepdims=True)
    gram = (
        jnp.dot(centered, centered.T, preferred_element_type=F32, precision=lax.Precision.HIGHEST)
        / width
    )
    mod_rows = mod_part.size // patch
    packed = jnp.concatenate(
        [noisy.astype(F32), mod_part.reshape(mod_rows, patch), jnp.zeros((-mod_rows % 8, patch), F32)]
    )
    packed = gather(packed, shift_z)
    noisy_row = jnp.concatenate([block[:local] for block in packed]).astype(BF)
    mods = [block[local : local + mod_rows].reshape(batches, -1) for block in packed]

    def from_row(b):
        chosen = mods[0]
        for k in (1, 2, 3):
            chosen = jnp.where(row == (b + STEPS[k]) % 4, mods[k], chosen)
        return chosen

    modulation = jnp.concatenate([from_row(b) for b in range(4)], axis=1)
    shift_own = modulation[:, :width]
    scale_own = modulation[:, width : 2 * width]

    out_part, gram, noisy_row, scale_own = lax.optimization_barrier(
        (out_part, gram, noisy_row, scale_own)
    )
    out_first = lax.all_gather(out_part, "row", axis=0, tiled=True)

    noisy_x = gather(noisy_row, shift_x)
    noisy_y = gather(noisy_row, shift_y)

    mapped = map_weights(
        embed_weight, scale_own, shift_own, attend_weight[0], []
    )
    mapped_all = mapped
    kinds = mapped.shape[1]
    mapped_other = lax.ppermute(mapped[1], "section", [(0, 1)])
    mapped = by_section(mapped[0], mapped_other)
    bias = mapped[:, patch : patch + 1].astype(F32) + mapped[:, patch + 1 : patch + 2].astype(F32)
    mapped = mapped[:, :patch]

    gains = jnp.concatenate([query_gain, key_gain])
    small = jnp.concatenate([modulation.reshape(-1, patch), gains, jnp.zeros((6, patch), F32)])
    small_other = swapped(held_until(small, mapped_all))
    small_first = by_section(small, small_other)
    small_second = by_section(small_other, small)
    mod_rows_all = modulation.size // patch

    def unpack(array):
        mod = array[:mod_rows_all].reshape(batches, -1)
        mod = by_section(mod[:1], mod[1:])
        qg = array[mod_rows_all : mod_rows_all + 1] * QUERY_SCALE
        kg = array[mod_rows_all + 1 : mod_rows_all + 2]
        return mod[:, :width], mod[:, width : 2 * width], mod[:, 2 * width :], qg, kg

    _, _, gate_first, qg_first, kg_first = unpack(small_first)
    shift_second, scale_second, _, qg_second, kg_second = unpack(small_second)

    heads = kinds // 3
    gain_of = (qg_first, kg_first)

    def first_heads(blocks, along):
        weight = jnp.concatenate([mapped[kind * heads + h] for kind, h in along], axis=1)
        bias_row = jnp.concatenate([bias[kind * heads + h] for kind, h in along], axis=1)
        gains_here = jnp.concatenate([gain_of[kind] for kind, h in along if kind < 2])
        return [
            first_projection(block, gram, weight, bias_row, gains_here, [attend_other])
            for block in blocks
        ]

    out_first_other = []

    def before_first(step, sums):
        if step < 3:
            return []
        out_first_other.append(swapped(held_until(out_first, sums)))
        return [out_part_second]

    attended = attention(
        first_heads(noisy_x, ALONG_X), first_heads(noisy_y, ALONG_Y), False, before_first
    )

    blocks = gather(attended, shift_z)
    turned = []
    for block, by in zip(blocks, STEPS):
        order = [
            [k for k in range(4) if (by + STEPS[k] - STEPS[mine]) % 4 == 0][0] for mine in range(4)
        ]
        turned.append(jnp.concatenate([block[k * local : (k + 1) * local] for k in order]))
    out_part_second, blocks = lax.optimization_barrier((out_part_second, blocks))
    out_second = lax.all_gather(out_part_second, "row", axis=0, tiled=True)
    places = jnp.stack([(row - by) & 3 for by in STEPS] + [section]).astype(jnp.int32)
    along_x, along_y, result_first = between_layers(
        places,
        turned,
        (out_first, out_first_other[0]),
        noisy_row,
        embed_weight,
        gate_first,
        scale_second,
        shift_second,
        (attend_weight[0], attend_other),
        qg_second,
        kg_second,
    )
    result_other = swapped(result_first)

    out_second_other = []

    def before_second(step, sums):
        if step == 5:
            out_second_other.append(swapped(held_until(out_second, sums)))
        return [result_other] if step == 6 else []

    xs = [along_x] + [shift_x(along_x, by) for by in STEPS[1:3]]
    ys = [along_y] + [shift_y(along_y, by) for by in STEPS[1:3]]
    xs, ys = lax.optimization_barrier((xs, ys))
    xs.append(shift_x(xs[0], STEPS[3]))
    ys.append(shift_y(ys[0], STEPS[3]))
    attended = attention(xs, ys, True, before_second)
    mine = give_back([attended[k * local : (k + 1) * local] for k in range(4)], shift_z)
    mine = jnp.concatenate(mine, axis=1)
    mine_other = lax.ppermute(mine, "section", [(0, 1)])
    places_last = jnp.stack([(row + by) & 3 for by in STEPS]).astype(jnp.int32)
    gates = modulation[:, 2 * width :]

    def finish_first():
        return jnp.stack([result_first, result_other])

    def finish_second():
        return last_step(
            places_last,
            (mine_other, mine),
            (out_second_other[0], out_second),
            (result_other, result_first),
            gates,
        )

    result = lax.cond(first, finish_first, finish_second)
    return result.reshape(1, batches, latent.shape[1], latent.shape[2], latent.shape[3], width)


def solution(mesh):
    return jax.shard_map(
        per_device,
        mesh=mesh,
        in_specs=(
            P(None, "depth", "row", None, None),
            P(None, "depth", "row", None, None),
            P(),
            P(),
            P("section", None, "row"),
            P("section", None, None, "row"),
            P("section", None),
            P("section", None),
            P("section", "row", None),
        ),
        out_specs=P("section", None, "depth", "row", None, None),
        check_vma=False,
    )
```

```python
import math

import jax
import jax.numpy as jnp
from jax import lax
from jax.experimental import pallas as pl
from jax.experimental.pallas import tpu as pltpu
from jax.sharding import PartitionSpec as P

HEAD_DIM = 128
BF = jnp.bfloat16
F32 = jnp.float32

norm_eps = 1e-06
plan_steps = 1000.0
QUERY_SCALE = math.log2(math.e) / math.sqrt(HEAD_DIM)
SWAP = [(0, 1), (1, 0)]
STEPS = (0, 1, -1, 2)


def signal_level(timestep):
    phase = (timestep.astype(F32) / plan_steps + 0.008) / 1.008 * (math.pi / 2)
    return jnp.cos(phase) ** 2


def time_features(timestep, count):
    half = count // 2
    frequency = jnp.exp(-math.log(10000.0) * jnp.arange(half, dtype=F32) / half)
    angles = timestep.astype(F32)[:, None] * frequency[None, :]
    return jnp.concatenate([jnp.cos(angles), jnp.sin(angles)], axis=1)


def shift_x(array, by):
    return lax.ppermute(
        array, "depth", [(y * 4 + x, y * 4 + (x + by) % 4) for y in range(4) for x in range(4)]
    )


def shift_y(array, by):
    return lax.ppermute(
        array, "depth", [(y * 4 + x, (y + by) % 4 * 4 + x) for y in range(4) for x in range(4)]
    )


def shift_z(array, by):
    return lax.ppermute(array, "row", [(z, (z + by) % 4) for z in range(4)])


def gather(array, shift):
    return [array] + [shift(array, by) for by in STEPS[1:]]


def give_back(blocks, shift):
    return [blocks[0]] + [shift(block, -by) for block, by in zip(blocks[1:], STEPS[1:])]


def params(mib):
    return pltpu.CompilerParams(vmem_limit_bytes=mib * 2**20)


def head_norm(values, gain):
    factor = lax.rsqrt(jnp.mean(values * values, axis=1, keepdims=True) + norm_eps)
    return (values * factor * gain).astype(BF)


def map_weights(embed, scale, shift, weight, after):
    patch, width = embed.shape
    batches = scale.shape[0]
    kinds, _, channels = weight.shape
    heads = channels // HEAD_DIM

    def kernel(embed_ref, scale_ref, shift_ref, weight_ref, *refs):
        out_ref, sides_ref = refs[-2:]

        @pl.when(pl.program_id(0) == 0)
        def _():
            values = embed_ref[...].astype(F32)
            values = values - jnp.mean(values, axis=1, keepdims=True)
            for m in range(batches):
                sides_ref[m * patch : (m + 1) * patch] = (
                    values * (1.0 + scale_ref[m : m + 1])
                ).astype(BF)
            sides_ref[batches * patch :] = jnp.concatenate(
                [shift_ref[...], jnp.zeros((16 - batches, width), F32)]
            ).astype(BF)

        mapped = jnp.dot(sides_ref[...], weight_ref[0], preferred_element_type=F32)
        for m in range(batches):
            bias = mapped[batches * patch + m : batches * patch + m + 1]
            upper = bias.astype(BF).astype(F32)
            tail = jnp.concatenate([upper, bias - upper, jnp.zeros((14, channels), F32)]).astype(BF)
            for h in range(heads):
                part = slice(h * HEAD_DIM, (h + 1) * HEAD_DIM)
                out_ref[m, h, :patch] = mapped[m * patch : (m + 1) * patch, part].astype(BF)
                out_ref[m, h, patch:] = tail[:, part]

    return pl.pallas_call(
        kernel,
        grid=(kinds,),
        in_specs=[
            pl.BlockSpec((patch, width), lambda j: (0, 0)),
            pl.BlockSpec((batches, width), lambda j: (0, 0)),
            pl.BlockSpec((batches, width), lambda j: (0, 0)),
            pl.BlockSpec((1, width, channels), lambda j: (j, 0, 0)),
        ]
        + [pl.BlockSpec(memory_space=pl.ANY)] * len(after),
        out_specs=pl.BlockSpec((batches, heads, patch + 16, HEAD_DIM), lambda j: (0, j, 0, 0)),
        out_shape=jax.ShapeDtypeStruct((batches, kinds * heads, patch + 16, HEAD_DIM), BF),
        scratch_shapes=[pltpu.VMEM((batches * patch + 16, width), BF)],
        compiler_params=params(18),
        cost_estimate=pl.CostEstimate(
            flops=2 * batches * patch * width * kinds * channels,
            bytes_accessed=10**4,
            transcendentals=0,
        ),
    )(embed, scale, shift, weight, *after)


def first_projection(noisy, gram, weight, bias, gains, after):
    rows = noisy.shape[0]
    heads = weight.shape[1] // HEAD_DIM
    normed_heads = gains.shape[0]

    def kernel(noisy_ref, gram_ref, weight_ref, bias_ref, gains_ref, *refs):
        out_ref = refs[-1]
        values = noisy_ref[...].astype(F32)
        spread = jnp.sum(
            jnp.dot(
                values, gram_ref[...], preferred_element_type=F32, precision=lax.Precision.HIGHEST
            )
            * values,
            axis=1,
            keepdims=True,
        )
        scaled = (values * lax.rsqrt(spread + norm_eps)).astype(BF)
        projected = jnp.dot(scaled, weight_ref[...], preferred_element_type=F32) + bias_ref[...]
        for h in range(heads):
            part = projected[:, h * HEAD_DIM : (h + 1) * HEAD_DIM]
            if h < normed_heads:
                out_ref[h] = head_norm(part, gains_ref[h : h + 1])
            else:
                out_ref[h] = part.astype(BF)

    whole = pl.BlockSpec(memory_space=pltpu.VMEM)
    return pl.pallas_call(
        kernel,
        in_specs=[whole] * 5 + [pl.BlockSpec(memory_space=pl.ANY)] * len(after),
        out_specs=whole,
        out_shape=jax.ShapeDtypeStruct((heads, rows, HEAD_DIM), BF),
        compiler_params=params(16),
        cost_estimate=pl.CostEstimate(flops=10**6, bytes_accessed=10**4, transcendentals=0),
    )(noisy, gram, weight, bias, gains, *after)


ALONG_X = ((1, 0), (1, 2), (0, 1), (2, 0), (2, 2))
ALONG_Y = ((0, 0), (0, 2), (1, 1), (2, 1))
HEADS_BY = ((1, 0), (0, 0), (1, 1))


def attend(queries, blocks, after, carry=None, more=False, weighty=False):
    rows = queries[0].shape[1]
    key_rows = blocks[0][0].shape[1]
    count = len(blocks[0])
    keys_total = key_rows * count
    places = (ALONG_X, ALONG_Y)
    carries = [] if carry is None else [carry]

    def kernel(*refs):
        query_refs = refs[:2]
        block_refs = (refs[2 : 2 + count], refs[2 + count : 2 + 2 * count])
        out_refs = refs[-2:-1] if more else refs[-3:-1]
        wide_ref = refs[-1]
        diagonal = lax.broadcasted_iota(jnp.int32, (HEAD_DIM, HEAD_DIM), 0) == lax.broadcasted_iota(
            jnp.int32, (HEAD_DIM, HEAD_DIM), 1
        )
        for h, (along, out_place) in enumerate(HEADS_BY):
            query = query_refs[along][places[along].index((0, h))]
            key_at = places[1 - along].index((1, h))
            value_at = places[1 - along].index((2, h))
            sums = None
            for i, ref in enumerate(block_refs[1 - along]):
                wide_ref[h, i * key_rows : (i + 1) * key_rows, :HEAD_DIM] = ref[value_at]
                wide_ref[h, i * key_rows : (i + 1) * key_rows, HEAD_DIM:] = jnp.ones(
                    (key_rows, HEAD_DIM), BF
                )
            for i, ref in enumerate(block_refs[1 - along]):
                scores = lax.dot_general(
                    query, ref[key_at], (((1,), (1,)), ((), ())), preferred_element_type=F32
                )
                weights = jnp.exp2(scores).astype(BF)
                term = jnp.dot(
                    weights,
                    wide_ref[h, i * key_rows : (i + 1) * key_rows],
                    preferred_element_type=F32,
                )
                sums = term if sums is None else sums + term
            numerators = sums[:, :HEAD_DIM]
            lines = []
            for part in range(rows // HEAD_DIM):
                square = sums[part * HEAD_DIM : (part + 1) * HEAD_DIM, HEAD_DIM:]
                lines.append(jnp.sum(jnp.where(diagonal, square, 0.0), axis=0, keepdims=True))
            total = jnp.concatenate(lines, axis=0)
            if carry is not None:
                numerators = numerators + refs[2 + 2 * count][h, :rows]
                total = total + refs[2 + 2 * count][h, rows : rows + 4]
            if more:
                out_refs[0][h, :rows] = numerators
                out_refs[0][h, rows : rows + 8] = jnp.concatenate(
                    [total, jnp.zeros((4, HEAD_DIM), F32)], axis=0
                )
                continue
            out_ref = out_refs[1 - along]
            out_ref[out_place, :rows] = numerators.astype(BF)
            upper = total.astype(BF)
            lower = (total - upper.astype(F32)).astype(BF)
            out_ref[out_place, rows : rows + 16] = jnp.concatenate(
                [upper.astype(F32), lower.astype(F32), jnp.zeros((8, HEAD_DIM), F32)], axis=0
            ).astype(BF)

    whole = pl.BlockSpec(memory_space=pltpu.VMEM)
    return pl.pallas_call(
        kernel,
        in_specs=[whole] * (2 + 2 * count + len(carries))
        + [pl.BlockSpec(memory_space=pl.ANY)] * len(after),
        out_specs=whole if more else [whole] * 2,
        out_shape=jax.ShapeDtypeStruct((len(HEADS_BY), rows + 8, HEAD_DIM), F32)
        if more
        else [
            jax.ShapeDtypeStruct((2, rows + 16, HEAD_DIM), BF),
            jax.ShapeDtypeStruct((1, rows + 16, HEAD_DIM), BF),
        ],
        scratch_shapes=[pltpu.VMEM((len(HEADS_BY), keys_total, 2 * HEAD_DIM), BF)],
        compiler_params=params(24),
        cost_estimate=pl.CostEstimate(
            flops=len(HEADS_BY) * rows * keys_total * HEAD_DIM * 8 if weighty else 10**6,
            bytes_accessed=8 * 2**20 if weighty else 10**4,
            transcendentals=0,
        ),
    )(*queries, *blocks[0], *blocks[1], *carries, *after)


def combine(parts_y, parts_x):
    packed = parts_y[0].shape[1]
    rows = packed - 16
    lines = rows // HEAD_DIM
    count = len(parts_y)
    heads = len(HEADS_BY)

    def kernel(*refs):
        out_ref = refs[-1]
        diagonal = lax.broadcasted_iota(jnp.int32, (HEAD_DIM, HEAD_DIM), 0) == lax.broadcasted_iota(
            jnp.int32, (HEAD_DIM, HEAD_DIM), 1
        )
        for h, (along, at) in enumerate(HEADS_BY):
            sources = refs[:count] if along == 1 else refs[count : 2 * count]
            tail = sources[0][at, rows : rows + 16].astype(F32)
            for ref in sources[1:]:
                tail = tail + ref[at, rows : rows + 16].astype(F32)
            for part in range(lines):
                place = slice(part * HEAD_DIM, (part + 1) * HEAD_DIM)
                numerator = sources[0][at, place].astype(F32)
                for ref in sources[1:]:
                    numerator = numerator + ref[at, place].astype(F32)
                total = tail[part : part + 1] + tail[lines + part : lines + part + 1]
                column = jnp.sum(jnp.where(diagonal, 1.0 / total, 0.0), axis=1, keepdims=True)
                out_ref[place, h * HEAD_DIM : (h + 1) * HEAD_DIM] = (numerator * column).astype(BF)

    return pl.pallas_call(
        kernel,
        out_shape=jax.ShapeDtypeStruct((rows, heads * HEAD_DIM), BF),
        compiler_params=params(16),
    )(*parts_y, *parts_x)


def attention(xs, ys, near_first, before):
    parts_y, parts_x = [None] * 4, [None] * 4
    after, carries, step = [], [None] * 4, 0
    if near_first:
        for k in (2, 1, 0):
            more = before(step, after[0] if after else None)
            carries[k] = attend(
                (xs[k], ys[k]), (xs[:3], ys[:3]), after + more, more=True, weighty=True
            )
            after = [carries[k]]
            step += 1
    for k in (3, 2, 1, 0):
        blocks = (xs, ys) if carries[k] is None else (xs[3:], ys[3:])
        more = before(step, after[0] if after else None)
        if k == 0:
            more = more + [parts_y[3], parts_x[3]]
        sums_y, sums_x = attend(
            (xs[k], ys[k]), blocks, after + more, carries[k], weighty=near_first
        )
        after = [sums_x]
        step += 1
        by = STEPS[k]
        parts_y[k] = shift_y(sums_y, -by) if by else sums_y
        parts_x[k] = shift_x(sums_x, -by) if by else sums_x
    return combine(parts_y, parts_x)


def held_until(array, other):
    return lax.optimization_barrier((array, other))[0]


def weight_copies(weight_refs, held_ref, sems):
    depth, width = held_ref.shape
    part = depth // 8
    half = width // 2
    copies = []
    for column in range(2):
        columns = slice(column * half, (column + 1) * half)
        for k in range(8):
            row, side = divmod(k, 2)
            source = weight_refs[side].at[row * part : (row + 1) * part, columns]
            place = held_ref.at[k * part : (k + 1) * part, columns]
            copies.append(pltpu.make_async_copy(source, place, sems.at[column * 8 + k]))
    return copies


def between_layers(places, blocks, weights, noisy, embed, gate, scale, shift, next_weight, query_gain, key_gain):
    rows, part = blocks[0].shape
    width = gate.shape[1]
    depth = 4 * part
    block = 512
    local = rows // 4
    kinds, _, channels = next_weight[0].shape
    heads = channels // HEAD_DIM

    def kernel(places_ref, *refs):
        block_refs = refs[:4]
        weight_refs = refs[4:6]
        noisy_ref, embed_ref, gate_ref, scale_ref, shift_ref = refs[6:11]
        next_refs = refs[11:13]
        qg_ref, kg_ref, x_ref, y_ref, own_ref = refs[13:18]
        held_ref, next_held_ref, side_ref, tokens_ref, sems = refs[18:]
        here = places_ref[4]

        def copies_in(section):
            return weight_copies(weight_refs if section == 0 else weight_refs[::-1], held_ref, sems)

        def next_copies_in(section):
            return [
                pltpu.make_async_copy(
                    next_refs[1 - section].at[j], next_held_ref.at[j], sems.at[16 + j]
                )
                for j in range(kinds)
            ]

        copies, next_copies = copies_in(0), next_copies_in(0)
        for section in range(2):

            @pl.when(here == section)
            def _():
                for copy in copies_in(section):
                    copy.start()

        for k in range(4):
            side_ref[:, pl.ds(pl.multiple_of(places_ref[k] * part, HEAD_DIM), part)] = block_refs[k][
                ...
            ]
        for column in range(2):
            for copy in copies[8 * column : 8 * column + 8]:
                copy.wait()
            if column == 0:
                for section in range(2):

                    @pl.when(here == section)
                    def _():
                        for copy in next_copies_in(section):
                            copy.start()

            @pl.loop(0, width // 2 // block)
            def _(n):
                place = pl.ds(pl.multiple_of(column * (width // 2) + n * block, block), block)
                update = jnp.dot(side_ref[...], held_ref[:, place], preferred_element_type=F32)
                base = jnp.dot(noisy_ref[...], embed_ref[:, place], preferred_element_type=F32)
                tokens_ref[:, place] = (
                    base.astype(BF).astype(F32) + gate_ref[:, place] * update
                ).astype(BF)

        own_ref[...] = tokens_ref[:local]

        @pl.loop(0, rows // 128)
        def _(n):
            place = pl.ds(pl.multiple_of(n * 128, 128), 128)
            values = tokens_ref[place].astype(F32)
            values = values - jnp.mean(values, axis=1, keepdims=True)
            spread = jnp.mean(values * values, axis=1, keepdims=True)
            tokens_ref[place] = (
                values * lax.rsqrt(spread + norm_eps) * (1.0 + scale_ref[...]) + shift_ref[...]
            ).astype(BF)

        for kind in range(kinds):
            next_copies[kind].wait()
            projected = jnp.dot(tokens_ref[...], next_held_ref[kind], preferred_element_type=F32)
            for h in range(heads):
                piece = projected[:, h * HEAD_DIM : (h + 1) * HEAD_DIM]
                if kind < 2:
                    piece = head_norm(piece, (qg_ref, kg_ref)[kind][...])
                else:
                    piece = piece.astype(BF)
                if (kind, h) in ALONG_X:
                    x_ref[ALONG_X.index((kind, h))] = piece
                else:
                    y_ref[ALONG_Y.index((kind, h))] = piece

    whole = pl.BlockSpec(memory_space=pltpu.VMEM)
    left = pl.BlockSpec(memory_space=pl.ANY)
    return pl.pallas_call(
        kernel,
        in_specs=[pl.BlockSpec(memory_space=pltpu.SMEM)]
        + [whole] * 4
        + [left] * 2
        + [whole] * 5
        + [left] * 2
        + [whole] * 2,
        out_specs=[whole] * 3,
        out_shape=[
            jax.ShapeDtypeStruct((len(ALONG_X), rows, HEAD_DIM), BF),
            jax.ShapeDtypeStruct((len(ALONG_Y), rows, HEAD_DIM), BF),
            jax.ShapeDtypeStruct((local, width), BF),
        ],
        scratch_shapes=[
            pltpu.VMEM((depth, width), BF),
            pltpu.VMEM(next_weight[0].shape, BF),
            pltpu.VMEM((rows, depth), BF),
            pltpu.VMEM((rows, width), BF),
            pltpu.SemaphoreType.DMA((16 + kinds,)),
        ],
        compiler_params=params(40),
        cost_estimate=pl.CostEstimate(
            flops=2 * rows * width * (depth + kinds * channels),
            bytes_accessed=10**4,
            transcendentals=0,
        ),
    )(places, *blocks, *weights, noisy, embed, gate, scale, shift, *next_weight, query_gain, key_gain)


def last_step(places, heads, weights, bases, gates):
    rows, depth = heads[0].shape
    width = gates.shape[1]
    block = 512

    part = depth // 4

    def kernel(places_ref, first_ref, second_ref, *refs):
        weight_refs = refs[:2]
        first_base_ref, second_base_ref, gates_ref, out_ref, held_ref, side_ref, sems = refs[2:]
        copies = weight_copies(weight_refs, held_ref, sems)
        for copy in copies:
            copy.start()
        for k in range(4):
            place = pl.ds(pl.multiple_of(places_ref[k] * part, HEAD_DIM), part)
            side_ref[:rows, place] = first_ref[:, k * part : (k + 1) * part]
            side_ref[rows:, place] = second_ref[:, k * part : (k + 1) * part]
        for column in range(2):
            for copy in copies[8 * column : 8 * column + 8]:
                copy.wait()

            @pl.loop(0, width // 2 // block)
            def _(n):
                place = pl.ds(pl.multiple_of(column * (width // 2) + n * block, block), block)
                update = jnp.dot(side_ref[...], held_ref[:, place], preferred_element_type=F32)
                for m, base_ref in enumerate((first_base_ref, second_base_ref)):
                    out_ref[m, :, place] = (
                        base_ref[:, place].astype(F32)
                        + gates_ref[m : m + 1, place] * update[m * rows : (m + 1) * rows]
                    ).astype(BF)

    whole = pl.BlockSpec(memory_space=pltpu.VMEM)
    return pl.pallas_call(
        kernel,
        in_specs=[pl.BlockSpec(memory_space=pltpu.SMEM)]
        + [whole] * 2
        + [pl.BlockSpec(memory_space=pl.ANY)] * 2
        + [whole] * 3,
        out_specs=whole,
        out_shape=jax.ShapeDtypeStruct((2, rows, width), BF),
        scratch_shapes=[
            pltpu.VMEM((depth, width), BF),
            pltpu.VMEM((2 * rows, depth), BF),
            pltpu.SemaphoreType.DMA((16,)),
        ],
        compiler_params=params(18),
    )(places, *heads, *weights, *bases, gates)


def per_device(
    latent,
    noise_field,
    timestep,
    embed_weight,
    modulate_weight,
    attend_weight,
    query_gain,
    key_gain,
    output_weight,
):
    batches = latent.shape[0]
    patch, width = embed_weight.shape
    local = latent.shape[1] * latent.shape[2] * latent.shape[3]
    section = lax.axis_index("section")
    row = lax.axis_index("row")
    first = section == 0

    def by_section(of_first, of_second):
        return jnp.where(first, of_first, of_second)

    def swapped(array):
        return lax.ppermute(array, "section", SWAP)

    level = signal_level(timestep)[:, None, None, None, None]
    noisy = (
        jnp.sqrt(level) * latent.astype(F32) + jnp.sqrt(1.0 - level) * noise_field.astype(F32)
    ).astype(BF)
    noisy = by_section(noisy[0], noisy[1]).reshape(local, patch)
    features = time_features(timestep, modulate_weight.shape[1]).astype(BF)
    mod_part = jnp.dot(features, modulate_weight[0], preferred_element_type=F32)

    out_own = output_weight[0]
    half = out_own.shape[0] // 2
    out_got = swapped(out_own)
    attend_other = lax.ppermute(attend_weight[0], "section", [(1, 0)])
    out_part = by_section(out_own[:half], out_got[half:])
    out_part_second = by_section(out_got[:half], out_own[half:])

    centered = embed_weight.astype(F32)
    centered = centered - jnp.mean(centered, axis=1, keepdims=True)
    gram = (
        jnp.dot(centered, centered.T, preferred_element_type=F32, precision=lax.Precision.HIGHEST)
        / width
    )
    mod_rows = mod_part.size // patch
    packed = jnp.concatenate(
        [noisy.astype(F32), mod_part.reshape(mod_rows, patch), jnp.zeros((-mod_rows % 8, patch), F32)]
    )
    packed = gather(packed, shift_z)
    noisy_row = jnp.concatenate([block[:local] for block in packed]).astype(BF)
    mods = [block[local : local + mod_rows].reshape(batches, -1) for block in packed]

    def from_row(b):
        chosen = mods[0]
        for k in (1, 2, 3):
            chosen = jnp.where(row == (b + STEPS[k]) % 4, mods[k], chosen)
        return chosen

    modulation = jnp.concatenate([from_row(b) for b in range(4)], axis=1)
    shift_own = modulation[:, :width]
    scale_own = modulation[:, width : 2 * width]

    out_part, gram, noisy_row, scale_own = lax.optimization_barrier(
        (out_part, gram, noisy_row, scale_own)
    )
    out_first = lax.all_gather(out_part, "row", axis=0, tiled=True)

    noisy_x = gather(noisy_row, shift_x)
    noisy_y = gather(noisy_row, shift_y)

    mapped = map_weights(
        embed_weight, scale_own, shift_own, attend_weight[0], []
    )
    mapped_all = mapped
    kinds = mapped.shape[1]
    mapped_other = lax.ppermute(mapped[1], "section", [(0, 1)])
    mapped = by_section(mapped[0], mapped_other)
    bias = mapped[:, patch : patch + 1].astype(F32) + mapped[:, patch + 1 : patch + 2].astype(F32)
    mapped = mapped[:, :patch]

    gains = jnp.concatenate([query_gain, key_gain])
    small = jnp.concatenate([modulation.reshape(-1, patch), gains, jnp.zeros((6, patch), F32)])
    small_other = swapped(held_until(small, mapped_all))
    small_first = by_section(small, small_other)
    small_second = by_section(small_other, small)
    mod_rows_all = modulation.size // patch

    def unpack(array):
        mod = array[:mod_rows_all].reshape(batches, -1)
        mod = by_section(mod[:1], mod[1:])
        qg = array[mod_rows_all : mod_rows_all + 1] * QUERY_SCALE
        kg = array[mod_rows_all + 1 : mod_rows_all + 2]
        return mod[:, :width], mod[:, width : 2 * width], mod[:, 2 * width :], qg, kg

    _, _, gate_first, qg_first, kg_first = unpack(small_first)
    shift_second, scale_second, _, qg_second, kg_second = unpack(small_second)

    heads = kinds // 3
    gain_of = (qg_first, kg_first)

    def first_heads(blocks, along):
        weight = jnp.concatenate([mapped[kind * heads + h] for kind, h in along], axis=1)
        bias_row = jnp.concatenate([bias[kind * heads + h] for kind, h in along], axis=1)
        gains_here = jnp.concatenate([gain_of[kind] for kind, h in along if kind < 2])
        return [
            first_projection(block, gram, weight, bias_row, gains_here, [attend_other])
            for block in blocks
        ]

    out_first_other = []

    def before_first(step, sums):
        if step == 3:
            out_first_other.append(swapped(held_until(out_first, sums)))
        return []

    attended = attention(
        first_heads(noisy_x, ALONG_X), first_heads(noisy_y, ALONG_Y), False, before_first
    )

    blocks = gather(attended, shift_z)
    turned = []
    for block, by in zip(blocks, STEPS):
        order = [
            [k for k in range(4) if (by + STEPS[k] - STEPS[mine]) % 4 == 0][0] for mine in range(4)
        ]
        turned.append(jnp.concatenate([block[k * local : (k + 1) * local] for k in order]))
    out_part_second, blocks = lax.optimization_barrier((out_part_second, blocks))
    out_second = lax.all_gather(out_part_second, "row", axis=0, tiled=True)
    places = jnp.stack([(row - by) & 3 for by in STEPS] + [section]).astype(jnp.int32)
    along_x, along_y, result_first = between_layers(
        places,
        turned,
        (out_first, out_first_other[0]),
        noisy_row,
        embed_weight,
        gate_first,
        scale_second,
        shift_second,
        (attend_weight[0], attend_other),
        qg_second,
        kg_second,
    )
    result_other = swapped(result_first)

    out_second_other = []

    def before_second(step, sums):
        if step == 5:
            out_second_other.append(swapped(held_until(out_second, sums)))
        return []

    xs = [along_x] + [shift_x(along_x, by) for by in STEPS[1:3]]
    ys = [along_y] + [shift_y(along_y, by) for by in STEPS[1:3]]
    xs, ys = lax.optimization_barrier((xs, ys))
    xs.append(shift_x(xs[0], STEPS[3]))
    ys.append(shift_y(ys[0], STEPS[3]))
    attended = attention(xs, ys, True, before_second)
    mine = give_back([attended[k * local : (k + 1) * local] for k in range(4)], shift_z)
    mine = jnp.concatenate(mine, axis=1)
    mine_other = lax.ppermute(mine, "section", [(0, 1)])
    places_last = jnp.stack([(row + by) & 3 for by in STEPS]).astype(jnp.int32)
    gates = modulation[:, 2 * width :]

    def finish_first():
        return jnp.stack([result_first, result_other])

    def finish_second():
        return last_step(
            places_last,
            (mine_other, mine),
            (out_second_other[0], out_second),
            (result_other, result_first),
            gates,
        )

    result = lax.cond(first, finish_first, finish_second)
    return result.reshape(1, batches, latent.shape[1], latent.shape[2], latent.shape[3], width)


def solution(mesh):
    return jax.shard_map(
        per_device,
        mesh=mesh,
        in_specs=(
            P(None, "depth", "row", None, None),
            P(None, "depth", "row", None, None),
            P(),
            P(),
            P("section", None, "row"),
            P("section", None, None, "row"),
            P("section", None),
            P("section", None),
            P("section", "row", None),
        ),
        out_specs=P("section", None, "depth", "row", None, None),
        check_vma=False,
    )
```

```python
import math

import jax
import jax.numpy as jnp
from jax import lax
from jax.experimental import pallas as pl
from jax.experimental.pallas import tpu as pltpu
from jax.sharding import PartitionSpec as P

HEAD_DIM = 128
BF = jnp.bfloat16
F32 = jnp.float32

norm_eps = 1e-06
plan_steps = 1000.0
QUERY_SCALE = math.log2(math.e) / math.sqrt(HEAD_DIM)
SWAP = [(0, 1), (1, 0)]
STEPS = (0, 1, -1, 2)


def signal_level(timestep):
    phase = (timestep.astype(F32) / plan_steps + 0.008) / 1.008 * (math.pi / 2)
    return jnp.cos(phase) ** 2


def time_features(timestep, count):
    half = count // 2
    frequency = jnp.exp(-math.log(10000.0) * jnp.arange(half, dtype=F32) / half)
    angles = timestep.astype(F32)[:, None] * frequency[None, :]
    return jnp.concatenate([jnp.cos(angles), jnp.sin(angles)], axis=1)


def shift_x(array, by):
    return lax.ppermute(
        array, "depth", [(y * 4 + x, y * 4 + (x + by) % 4) for y in range(4) for x in range(4)]
    )


def shift_y(array, by):
    return lax.ppermute(
        array, "depth", [(y * 4 + x, (y + by) % 4 * 4 + x) for y in range(4) for x in range(4)]
    )


def shift_z(array, by):
    return lax.ppermute(array, "row", [(z, (z + by) % 4) for z in range(4)])


def gather(array, shift):
    return [array] + [shift(array, by) for by in STEPS[1:]]


def give_back(blocks, shift):
    return [blocks[0]] + [shift(block, -by) for block, by in zip(blocks[1:], STEPS[1:])]


def params(mib):
    return pltpu.CompilerParams(vmem_limit_bytes=mib * 2**20)


def head_norm(values, gain):
    factor = lax.rsqrt(jnp.mean(values * values, axis=1, keepdims=True) + norm_eps)
    return (values * factor * gain).astype(BF)


def map_weights(embed, scale, shift, weight, after):
    patch, width = embed.shape
    batches = scale.shape[0]
    kinds, _, channels = weight.shape
    heads = channels // HEAD_DIM

    def kernel(embed_ref, scale_ref, shift_ref, weight_ref, *refs):
        out_ref, sides_ref = refs[-2:]

        @pl.when(pl.program_id(0) == 0)
        def _():
            values = embed_ref[...].astype(F32)
            values = values - jnp.mean(values, axis=1, keepdims=True)
            for m in range(batches):
                sides_ref[m * patch : (m + 1) * patch] = (
                    values * (1.0 + scale_ref[m : m + 1])
                ).astype(BF)
            sides_ref[batches * patch :] = jnp.concatenate(
                [shift_ref[...], jnp.zeros((16 - batches, width), F32)]
            ).astype(BF)

        mapped = jnp.dot(sides_ref[...], weight_ref[0], preferred_element_type=F32)
        for m in range(batches):
            bias = mapped[batches * patch + m : batches * patch + m + 1]
            upper = bias.astype(BF).astype(F32)
            tail = jnp.concatenate([upper, bias - upper, jnp.zeros((14, channels), F32)]).astype(BF)
            for h in range(heads):
                part = slice(h * HEAD_DIM, (h + 1) * HEAD_DIM)
                out_ref[m, h, :patch] = mapped[m * patch : (m + 1) * patch, part].astype(BF)
                out_ref[m, h, patch:] = tail[:, part]

    return pl.pallas_call(
        kernel,
        grid=(kinds,),
        in_specs=[
            pl.BlockSpec((patch, width), lambda j: (0, 0)),
            pl.BlockSpec((batches, width), lambda j: (0, 0)),
            pl.BlockSpec((batches, width), lambda j: (0, 0)),
            pl.BlockSpec((1, width, channels), lambda j: (j, 0, 0)),
        ]
        + [pl.BlockSpec(memory_space=pl.ANY)] * len(after),
        out_specs=pl.BlockSpec((batches, heads, patch + 16, HEAD_DIM), lambda j: (0, j, 0, 0)),
        out_shape=jax.ShapeDtypeStruct((batches, kinds * heads, patch + 16, HEAD_DIM), BF),
        scratch_shapes=[pltpu.VMEM((batches * patch + 16, width), BF)],
        compiler_params=params(18),
        cost_estimate=pl.CostEstimate(
            flops=2 * batches * patch * width * kinds * channels,
            bytes_accessed=10**4,
            transcendentals=0,
        ),
    )(embed, scale, shift, weight, *after)


def first_projection(noisy, gram, weight, bias, gains, after):
    rows = noisy.shape[0]
    heads = weight.shape[1] // HEAD_DIM
    normed_heads = gains.shape[0]

    def kernel(noisy_ref, gram_ref, weight_ref, bias_ref, gains_ref, *refs):
        out_ref = refs[-1]
        values = noisy_ref[...].astype(F32)
        spread = jnp.sum(
            jnp.dot(
                values, gram_ref[...], preferred_element_type=F32, precision=lax.Precision.HIGHEST
            )
            * values,
            axis=1,
            keepdims=True,
        )
        scaled = (values * lax.rsqrt(spread + norm_eps)).astype(BF)
        projected = jnp.dot(scaled, weight_ref[...], preferred_element_type=F32) + bias_ref[...]
        for h in range(heads):
            part = projected[:, h * HEAD_DIM : (h + 1) * HEAD_DIM]
            if h < normed_heads:
                out_ref[h] = head_norm(part, gains_ref[h : h + 1])
            else:
                out_ref[h] = part.astype(BF)

    whole = pl.BlockSpec(memory_space=pltpu.VMEM)
    return pl.pallas_call(
        kernel,
        in_specs=[whole] * 5 + [pl.BlockSpec(memory_space=pl.ANY)] * len(after),
        out_specs=whole,
        out_shape=jax.ShapeDtypeStruct((heads, rows, HEAD_DIM), BF),
        compiler_params=params(16),
        cost_estimate=pl.CostEstimate(flops=10**6, bytes_accessed=10**4, transcendentals=0),
    )(noisy, gram, weight, bias, gains, *after)


ALONG_X = ((1, 0), (1, 2), (0, 1), (2, 0), (2, 2))
ALONG_Y = ((0, 0), (0, 2), (1, 1), (2, 1))
HEADS_BY = ((1, 0), (0, 0), (1, 1))


def attend(queries, blocks, after, carry=None, more=False, weighty=False):
    rows = queries[0].shape[1]
    key_rows = blocks[0][0].shape[1]
    count = len(blocks[0])
    keys_total = key_rows * count
    places = (ALONG_X, ALONG_Y)
    carries = [] if carry is None else [carry]

    def kernel(*refs):
        query_refs = refs[:2]
        block_refs = (refs[2 : 2 + count], refs[2 + count : 2 + 2 * count])
        out_refs = refs[-2:-1] if more else refs[-3:-1]
        wide_ref = refs[-1]
        diagonal = lax.broadcasted_iota(jnp.int32, (HEAD_DIM, HEAD_DIM), 0) == lax.broadcasted_iota(
            jnp.int32, (HEAD_DIM, HEAD_DIM), 1
        )
        for h, (along, out_place) in enumerate(HEADS_BY):
            query = query_refs[along][places[along].index((0, h))]
            key_at = places[1 - along].index((1, h))
            value_at = places[1 - along].index((2, h))
            sums = None
            for i, ref in enumerate(block_refs[1 - along]):
                wide_ref[h, i * key_rows : (i + 1) * key_rows, :HEAD_DIM] = ref[value_at]
                wide_ref[h, i * key_rows : (i + 1) * key_rows, HEAD_DIM:] = jnp.ones(
                    (key_rows, HEAD_DIM), BF
                )
            for i, ref in enumerate(block_refs[1 - along]):
                scores = lax.dot_general(
                    query, ref[key_at], (((1,), (1,)), ((), ())), preferred_element_type=F32
                )
                weights = jnp.exp2(scores).astype(BF)
                term = jnp.dot(
                    weights,
                    wide_ref[h, i * key_rows : (i + 1) * key_rows],
                    preferred_element_type=F32,
                )
                sums = term if sums is None else sums + term
            numerators = sums[:, :HEAD_DIM]
            lines = []
            for part in range(rows // HEAD_DIM):
                square = sums[part * HEAD_DIM : (part + 1) * HEAD_DIM, HEAD_DIM:]
                lines.append(jnp.sum(jnp.where(diagonal, square, 0.0), axis=0, keepdims=True))
            total = jnp.concatenate(lines, axis=0)
            if carry is not None:
                numerators = numerators + refs[2 + 2 * count][h, :rows]
                total = total + refs[2 + 2 * count][h, rows : rows + 4]
            if more:
                out_refs[0][h, :rows] = numerators
                out_refs[0][h, rows : rows + 8] = jnp.concatenate(
                    [total, jnp.zeros((4, HEAD_DIM), F32)], axis=0
                )
                continue
            out_ref = out_refs[1 - along]
            out_ref[out_place, :rows] = numerators.astype(BF)
            upper = total.astype(BF)
            lower = (total - upper.astype(F32)).astype(BF)
            out_ref[out_place, rows : rows + 16] = jnp.concatenate(
                [upper.astype(F32), lower.astype(F32), jnp.zeros((8, HEAD_DIM), F32)], axis=0
            ).astype(BF)

    whole = pl.BlockSpec(memory_space=pltpu.VMEM)
    return pl.pallas_call(
        kernel,
        in_specs=[whole] * (2 + 2 * count + len(carries))
        + [pl.BlockSpec(memory_space=pl.ANY)] * len(after),
        out_specs=whole if more else [whole] * 2,
        out_shape=jax.ShapeDtypeStruct((len(HEADS_BY), rows + 8, HEAD_DIM), F32)
        if more
        else [
            jax.ShapeDtypeStruct((2, rows + 16, HEAD_DIM), BF),
            jax.ShapeDtypeStruct((1, rows + 16, HEAD_DIM), BF),
        ],
        scratch_shapes=[pltpu.VMEM((len(HEADS_BY), keys_total, 2 * HEAD_DIM), BF)],
        compiler_params=params(24),
        cost_estimate=pl.CostEstimate(
            flops=len(HEADS_BY) * rows * keys_total * HEAD_DIM * 8 if weighty else 10**6,
            bytes_accessed=8 * 2**20 if weighty else 10**4,
            transcendentals=0,
        ),
    )(*queries, *blocks[0], *blocks[1], *carries, *after)


def combine(parts_y, parts_x):
    packed = parts_y[0].shape[1]
    rows = packed - 16
    lines = rows // HEAD_DIM
    count = len(parts_y)
    heads = len(HEADS_BY)

    def kernel(*refs):
        out_ref = refs[-1]
        diagonal = lax.broadcasted_iota(jnp.int32, (HEAD_DIM, HEAD_DIM), 0) == lax.broadcasted_iota(
            jnp.int32, (HEAD_DIM, HEAD_DIM), 1
        )
        for h, (along, at) in enumerate(HEADS_BY):
            sources = refs[:count] if along == 1 else refs[count : 2 * count]
            tail = sources[0][at, rows : rows + 16].astype(F32)
            for ref in sources[1:]:
                tail = tail + ref[at, rows : rows + 16].astype(F32)
            for part in range(lines):
                place = slice(part * HEAD_DIM, (part + 1) * HEAD_DIM)
                numerator = sources[0][at, place].astype(F32)
                for ref in sources[1:]:
                    numerator = numerator + ref[at, place].astype(F32)
                total = tail[part : part + 1] + tail[lines + part : lines + part + 1]
                column = jnp.sum(jnp.where(diagonal, 1.0 / total, 0.0), axis=1, keepdims=True)
                out_ref[place, h * HEAD_DIM : (h + 1) * HEAD_DIM] = (numerator * column).astype(BF)

    return pl.pallas_call(
        kernel,
        out_shape=jax.ShapeDtypeStruct((rows, heads * HEAD_DIM), BF),
        compiler_params=params(16),
    )(*parts_y, *parts_x)


def attention(xs, ys, near_first, before):
    parts_y, parts_x = [None] * 4, [None] * 4
    after, carries, step = [], [None] * 4, 0
    if near_first:
        for k in (2, 1, 0):
            more = before(step, after[0] if after else None)
            carries[k] = attend(
                (xs[k], ys[k]), (xs[:3], ys[:3]), after + more, more=True, weighty=True
            )
            after = [carries[k]]
            step += 1
    for k in (3, 2, 1, 0):
        blocks = (xs, ys) if carries[k] is None else (xs[3:], ys[3:])
        more = before(step, after[0] if after else None)
        if k == 0:
            more = more + [parts_y[3], parts_x[3]]
        sums_y, sums_x = attend(
            (xs[k], ys[k]), blocks, after + more, carries[k], weighty=near_first
        )
        after = [sums_x]
        step += 1
        by = STEPS[k]
        parts_y[k] = shift_y(sums_y, -by) if by else sums_y
        parts_x[k] = shift_x(sums_x, -by) if by else sums_x
    return combine(parts_y, parts_x)


def held_until(array, other):
    return lax.optimization_barrier((array, other))[0]


def weight_copies(weight_refs, held_ref, sems):
    depth, width = held_ref.shape
    part = depth // 8
    half = width // 2
    copies = []
    for column in range(2):
        columns = slice(column * half, (column + 1) * half)
        for k in range(8):
            row, side = divmod(k, 2)
            source = weight_refs[side].at[row * part : (row + 1) * part, columns]
            place = held_ref.at[k * part : (k + 1) * part, columns]
            copies.append(pltpu.make_async_copy(source, place, sems.at[column * 8 + k]))
    return copies


def between_layers(places, blocks, weights, noisy, embed, gate, scale, shift, next_weight, query_gain, key_gain):
    rows, part = blocks[0].shape
    width = gate.shape[1]
    depth = 4 * part
    block = 512
    local = rows // 4
    kinds, _, channels = next_weight[0].shape
    heads = channels // HEAD_DIM

    def kernel(places_ref, *refs):
        block_refs = refs[:4]
        weight_refs = refs[4:6]
        noisy_ref, embed_ref, gate_ref, scale_ref, shift_ref = refs[6:11]
        next_refs = refs[11:13]
        qg_ref, kg_ref, x_ref, y_ref, own_ref = refs[13:18]
        held_ref, next_held_ref, side_ref, tokens_ref, sems = refs[18:]
        here = places_ref[4]

        def copies_in(section):
            return weight_copies(weight_refs if section == 0 else weight_refs[::-1], held_ref, sems)

        def next_copies_in(section):
            return [
                pltpu.make_async_copy(
                    next_refs[1 - section].at[j], next_held_ref.at[j], sems.at[16 + j]
                )
                for j in range(kinds)
            ]

        copies, next_copies = copies_in(0), next_copies_in(0)
        for section in range(2):

            @pl.when(here == section)
            def _():
                for copy in copies_in(section):
                    copy.start()

        for k in range(4):
            side_ref[:, pl.ds(pl.multiple_of(places_ref[k] * part, HEAD_DIM), part)] = block_refs[k][
                ...
            ]
        for column in range(2):
            for copy in copies[8 * column : 8 * column + 8]:
                copy.wait()
            if column == 0:
                for section in range(2):

                    @pl.when(here == section)
                    def _():
                        for copy in next_copies_in(section):
                            copy.start()

            @pl.loop(0, width // 2 // block)
            def _(n):
                place = pl.ds(pl.multiple_of(column * (width // 2) + n * block, block), block)
                update = jnp.dot(side_ref[...], held_ref[:, place], preferred_element_type=F32)
                base = jnp.dot(noisy_ref[...], embed_ref[:, place], preferred_element_type=F32)
                tokens_ref[:, place] = (
                    base.astype(BF).astype(F32) + gate_ref[:, place] * update
                ).astype(BF)

        own_ref[...] = tokens_ref[:local]

        @pl.loop(0, rows // 128)
        def _(n):
            place = pl.ds(pl.multiple_of(n * 128, 128), 128)
            values = tokens_ref[place].astype(F32)
            values = values - jnp.mean(values, axis=1, keepdims=True)
            spread = jnp.mean(values * values, axis=1, keepdims=True)
            tokens_ref[place] = (
                values * lax.rsqrt(spread + norm_eps) * (1.0 + scale_ref[...]) + shift_ref[...]
            ).astype(BF)

        for kind in range(kinds):
            next_copies[kind].wait()
            projected = jnp.dot(tokens_ref[...], next_held_ref[kind], preferred_element_type=F32)
            for h in range(heads):
                piece = projected[:, h * HEAD_DIM : (h + 1) * HEAD_DIM]
                if kind < 2:
                    piece = head_norm(piece, (qg_ref, kg_ref)[kind][...])
                else:
                    piece = piece.astype(BF)
                if (kind, h) in ALONG_X:
                    x_ref[ALONG_X.index((kind, h))] = piece
                else:
                    y_ref[ALONG_Y.index((kind, h))] = piece

    whole = pl.BlockSpec(memory_space=pltpu.VMEM)
    left = pl.BlockSpec(memory_space=pl.ANY)
    return pl.pallas_call(
        kernel,
        in_specs=[pl.BlockSpec(memory_space=pltpu.SMEM)]
        + [whole] * 4
        + [left] * 2
        + [whole] * 5
        + [left] * 2
        + [whole] * 2,
        out_specs=[whole] * 3,
        out_shape=[
            jax.ShapeDtypeStruct((len(ALONG_X), rows, HEAD_DIM), BF),
            jax.ShapeDtypeStruct((len(ALONG_Y), rows, HEAD_DIM), BF),
            jax.ShapeDtypeStruct((local, width), BF),
        ],
        scratch_shapes=[
            pltpu.VMEM((depth, width), BF),
            pltpu.VMEM(next_weight[0].shape, BF),
            pltpu.VMEM((rows, depth), BF),
            pltpu.VMEM((rows, width), BF),
            pltpu.SemaphoreType.DMA((16 + kinds,)),
        ],
        compiler_params=params(40),
        cost_estimate=pl.CostEstimate(
            flops=2 * rows * width * (depth + kinds * channels),
            bytes_accessed=10**4,
            transcendentals=0,
        ),
    )(places, *blocks, *weights, noisy, embed, gate, scale, shift, *next_weight, query_gain, key_gain)


def last_step(places, heads, weights, bases, gates):
    rows, depth = heads[0].shape
    width = gates.shape[1]
    block = 512

    part = depth // 4

    def kernel(places_ref, first_ref, second_ref, *refs):
        weight_refs = refs[:2]
        first_base_ref, second_base_ref, gates_ref, out_ref, held_ref, side_ref, sems = refs[2:]
        copies = weight_copies(weight_refs, held_ref, sems)
        for copy in copies:
            copy.start()
        for k in range(4):
            place = pl.ds(pl.multiple_of(places_ref[k] * part, HEAD_DIM), part)
            side_ref[:rows, place] = first_ref[:, k * part : (k + 1) * part]
            side_ref[rows:, place] = second_ref[:, k * part : (k + 1) * part]
        for column in range(2):
            for copy in copies[8 * column : 8 * column + 8]:
                copy.wait()

            @pl.loop(0, width // 2 // block)
            def _(n):
                place = pl.ds(pl.multiple_of(column * (width // 2) + n * block, block), block)
                update = jnp.dot(side_ref[...], held_ref[:, place], preferred_element_type=F32)
                for m, base_ref in enumerate((first_base_ref, second_base_ref)):
                    out_ref[m, :, place] = (
                        base_ref[:, place].astype(F32)
                        + gates_ref[m : m + 1, place] * update[m * rows : (m + 1) * rows]
                    ).astype(BF)

    whole = pl.BlockSpec(memory_space=pltpu.VMEM)
    return pl.pallas_call(
        kernel,
        in_specs=[pl.BlockSpec(memory_space=pltpu.SMEM)]
        + [whole] * 2
        + [pl.BlockSpec(memory_space=pl.ANY)] * 2
        + [whole] * 3,
        out_specs=whole,
        out_shape=jax.ShapeDtypeStruct((2, rows, width), BF),
        scratch_shapes=[
            pltpu.VMEM((depth, width), BF),
            pltpu.VMEM((2 * rows, depth), BF),
            pltpu.SemaphoreType.DMA((16,)),
        ],
        compiler_params=params(52),
    )(places, *heads, *weights, *bases, gates)


def per_device(
    latent,
    noise_field,
    timestep,
    embed_weight,
    modulate_weight,
    attend_weight,
    query_gain,
    key_gain,
    output_weight,
):
    batches = latent.shape[0]
    patch, width = embed_weight.shape
    local = latent.shape[1] * latent.shape[2] * latent.shape[3]
    section = lax.axis_index("section")
    row = lax.axis_index("row")
    first = section == 0

    def by_section(of_first, of_second):
        return jnp.where(first, of_first, of_second)

    def swapped(array):
        return lax.ppermute(array, "section", SWAP)

    level = signal_level(timestep)[:, None, None, None, None]
    noisy = (
        jnp.sqrt(level) * latent.astype(F32) + jnp.sqrt(1.0 - level) * noise_field.astype(F32)
    ).astype(BF)
    noisy = by_section(noisy[0], noisy[1]).reshape(local, patch)
    features = time_features(timestep, modulate_weight.shape[1]).astype(BF)
    mod_part = jnp.dot(features, modulate_weight[0], preferred_element_type=F32)

    out_own = output_weight[0]
    half = out_own.shape[0] // 2
    out_got = swapped(out_own)
    attend_other = lax.ppermute(attend_weight[0], "section", [(1, 0)])
    out_part = by_section(out_own[:half], out_got[half:])
    out_part_second = by_section(out_got[:half], out_own[half:])

    centered = embed_weight.astype(F32)
    centered = centered - jnp.mean(centered, axis=1, keepdims=True)
    gram = (
        jnp.dot(centered, centered.T, preferred_element_type=F32, precision=lax.Precision.HIGHEST)
        / width
    )
    mod_rows = mod_part.size // patch
    packed = jnp.concatenate(
        [noisy.astype(F32), mod_part.reshape(mod_rows, patch), jnp.zeros((-mod_rows % 8, patch), F32)]
    )
    packed = gather(packed, shift_z)
    noisy_row = jnp.concatenate([block[:local] for block in packed]).astype(BF)
    mods = [block[local : local + mod_rows].reshape(batches, -1) for block in packed]

    def from_row(b):
        chosen = mods[0]
        for k in (1, 2, 3):
            chosen = jnp.where(row == (b + STEPS[k]) % 4, mods[k], chosen)
        return chosen

    modulation = jnp.concatenate([from_row(b) for b in range(4)], axis=1)
    shift_own = modulation[:, :width]
    scale_own = modulation[:, width : 2 * width]

    out_part, gram, noisy_row, scale_own = lax.optimization_barrier(
        (out_part, gram, noisy_row, scale_own)
    )
    out_first = lax.all_gather(out_part, "row", axis=0, tiled=True)

    noisy_x = gather(noisy_row, shift_x)
    noisy_y = gather(noisy_row, shift_y)

    mapped = map_weights(
        embed_weight, scale_own, shift_own, attend_weight[0], []
    )
    mapped_all = mapped
    kinds = mapped.shape[1]
    mapped_other = lax.ppermute(mapped[1], "section", [(0, 1)])
    mapped = by_section(mapped[0], mapped_other)
    bias = mapped[:, patch : patch + 1].astype(F32) + mapped[:, patch + 1 : patch + 2].astype(F32)
    mapped = mapped[:, :patch]

    gains = jnp.concatenate([query_gain, key_gain])
    small = jnp.concatenate([modulation.reshape(-1, patch), gains, jnp.zeros((6, patch), F32)])
    small_other = swapped(held_until(small, mapped_all))
    small_first = by_section(small, small_other)
    small_second = by_section(small_other, small)
    mod_rows_all = modulation.size // patch

    def unpack(array):
        mod = array[:mod_rows_all].reshape(batches, -1)
        mod = by_section(mod[:1], mod[1:])
        qg = array[mod_rows_all : mod_rows_all + 1] * QUERY_SCALE
        kg = array[mod_rows_all + 1 : mod_rows_all + 2]
        return mod[:, :width], mod[:, width : 2 * width], mod[:, 2 * width :], qg, kg

    _, _, gate_first, qg_first, kg_first = unpack(small_first)
    shift_second, scale_second, _, qg_second, kg_second = unpack(small_second)

    heads = kinds // 3
    gain_of = (qg_first, kg_first)

    def first_heads(blocks, along):
        weight = jnp.concatenate([mapped[kind * heads + h] for kind, h in along], axis=1)
        bias_row = jnp.concatenate([bias[kind * heads + h] for kind, h in along], axis=1)
        gains_here = jnp.concatenate([gain_of[kind] for kind, h in along if kind < 2])
        return [
            first_projection(block, gram, weight, bias_row, gains_here, [attend_other])
            for block in blocks
        ]

    out_first_other = []

    def before_first(step, sums):
        if step == 3:
            out_first_other.append(swapped(held_until(out_first, sums)))
        return []

    attended = attention(
        first_heads(noisy_x, ALONG_X), first_heads(noisy_y, ALONG_Y), False, before_first
    )

    blocks = gather(attended, shift_z)
    turned = []
    for block, by in zip(blocks, STEPS):
        order = [
            [k for k in range(4) if (by + STEPS[k] - STEPS[mine]) % 4 == 0][0] for mine in range(4)
        ]
        turned.append(jnp.concatenate([block[k * local : (k + 1) * local] for k in order]))
    out_part_second, blocks = lax.optimization_barrier((out_part_second, blocks))
    out_second = lax.all_gather(out_part_second, "row", axis=0, tiled=True)
    places = jnp.stack([(row - by) & 3 for by in STEPS] + [section]).astype(jnp.int32)
    along_x, along_y, result_first = between_layers(
        places,
        turned,
        (out_first, out_first_other[0]),
        noisy_row,
        embed_weight,
        gate_first,
        scale_second,
        shift_second,
        (attend_weight[0], attend_other),
        qg_second,
        kg_second,
    )
    result_other = swapped(result_first)

    out_second_other = []

    def before_second(step, sums):
        if step == 5:
            out_second_other.append(swapped(held_until(out_second, sums)))
        return []

    xs = [along_x] + [shift_x(along_x, by) for by in STEPS[1:3]]
    ys = [along_y] + [shift_y(along_y, by) for by in STEPS[1:3]]
    xs, ys = lax.optimization_barrier((xs, ys))
    xs.append(shift_x(xs[0], STEPS[3]))
    ys.append(shift_y(ys[0], STEPS[3]))
    attended = attention(xs, ys, True, before_second)
    mine = give_back([attended[k * local : (k + 1) * local] for k in range(4)], shift_z)
    mine = jnp.concatenate(mine, axis=1)
    mine_other = lax.ppermute(mine, "section", [(0, 1)])
    places_last = jnp.stack([(row + by) & 3 for by in STEPS]).astype(jnp.int32)
    gates = modulation[:, 2 * width :]

    def finish_first():
        return jnp.stack([result_first, result_other])

    def finish_second():
        return last_step(
            places_last,
            (mine_other, mine),
            (out_second_other[0], out_second),
            (result_other, result_first),
            gates,
        )

    result = lax.cond(first, finish_first, finish_second)
    return result.reshape(1, batches, latent.shape[1], latent.shape[2], latent.shape[3], width)


def solution(mesh):
    return jax.shard_map(
        per_device,
        mesh=mesh,
        in_specs=(
            P(None, "depth", "row", None, None),
            P(None, "depth", "row", None, None),
            P(),
            P(),
            P("section", None, "row"),
            P("section", None, None, "row"),
            P("section", None),
            P("section", None),
            P("section", "row", None),
        ),
        out_specs=P("section", None, "depth", "row", None, None),
        check_vma=False,
    )
```
